32 devices in a mesh: dp: 4 (over y, core), seq: 8 (over z, x).
Axes of the slice: x: 2, y: 2, z: 4, core: 2. Of those that a mesh axis runs over, the one named last changes fastest.
Arguments:
- inputs: bfloat16 [4, 2048, 512], P('dp', 'seq'), may hold values from -12 to 12
- lengths: int32 [4], P('dp'), may hold values from 1793 to 2048
- labels: int32 [4], P('dp'), may hold values from 0 to 1
- norm_gain: float32 [2, 512], replicated, may hold values from 0.5 to 1.5
- norm_bias: float32 [2, 512], replicated, may hold values from -4 to 4
- b_proj: float32 [2, 512, 768], P(None, 'dp'), may hold values from -0.25 to 0.25
- rate: float32 [2, 384], P(None, 'seq'), may hold values from 0.00024414062 to 0.05
- phase: float32 [2, 384], P(None, 'seq'), may hold values from -3.140625 to 3.140625
- c_proj: float32 [2, 4, 384, 512], P(None, None, 'seq', 'dp'), may hold values from -0.15625 to 0.15625
- skip: float32 [2, 512], replicated, may hold values from 0.5 to 1.5
- glu_weight: float32 [2, 512, 512], P(None, 'dp'), may hold values from -0.25 to 0.25
- glu_bias: float32 [2, 512], replicated, may hold values from -6 to 6
- class_weight: float32 [512, 2], replicated, may hold values from -0.5 to 0.5
- class_bias: float32 [2], replicated, may hold values from -6 to 6
Outputs:
- loss_mean: float32 [], replicated
- grad_inputs: float32 [4, 2048, 512], P('dp', 'seq')
- grad_norm_gain: float32 [2, 512], replicated
- grad_norm_bias: float32 [2, 512], replicated
- grad_b_proj: float32 [2, 512, 768], P(None, 'dp')
- grad_rate: float32 [2, 384], P(None, 'seq')
- grad_phase: float32 [2, 384], P(None, 'seq')
- grad_c_proj: float32 [2, 4, 384, 512], P(None, None, 'seq', 'dp')
- grad_skip: float32 [2, 512], replicated
- grad_glu_weight: float32 [2, 512, 512], P(None, 'dp')
- grad_glu_bias: float32 [2, 512], replicated
- grad_class_weight: float32 [512, 2], replicated
- grad_class_bias: float32 [2], replicated
The draws below stay inside these ranges and needn't reach their ends.
All inputs are finite; a program needn't handle non-finite values.
Results may differ from the reference program's by a relative error of at most 0.0128.
The reference program's roundings to bfloat16 on the way count: a program that leaves them out, or rounds other values in their place, can miss the bound.
Values may be sent and summed in bfloat16 or wider, within the bound.
A program may use at most 192 MiB of HBM per device.

```python
import math
import jax
import jax.numpy as jnp
from jax import lax

H = 512
P_SIZE = 384
K = 2
LAYERS = 2
TOK_DEV = 256
SEQ_LEN = 2048
BATCH = 4


def draw_inputs(key, part):
    key_center, key_noise = jax.random.split(jax.random.fold_in(key, 11))
    center = jax.random.normal(key_center, (BATCH, 1, H), jnp.float32)
    noise = 0.8 * jax.random.normal(key_noise, (BATCH, SEQ_LEN, H), jnp.float32)
    return jnp.clip(center + noise, -12.0, 12.0).astype(jnp.bfloat16)


def plant(drawn, stream_key, smallest, largest):
    longest = drawn.shape.index(max(drawn.shape))
    spots = []
    for shift in (0, 1):
        where = [jax.random.randint(jax.random.fold_in(stream_key, axis), (), 0, length) for axis, length in enumerate(drawn.shape)]
        where[longest] = (where[longest] + shift) % drawn.shape[longest]
        spots.append(tuple(where))
    return drawn.at[spots[0]].set(smallest).at[spots[1]].set(largest)


def levels(stream_key, extent, shards, low, top_value):
    def one(position, blocks):
        heights = jax.random.uniform(jax.random.fold_in(jax.random.fold_in(stream_key, 6), position), (blocks,), jnp.float32, low / len(shards), top_value / len(shards))
        return jnp.repeat(jnp.exp(heights), extent[position] // blocks).reshape((-1,) + (1,) * (len(extent) - position - 1))

    level = one(*shards[0])
    for cut in shards[1:]:
        level = level * one(*cut)
    return level


def centred(stream_key, shape, scale, most, cuts=(), kind=jnp.bfloat16):
    entries = scale * jax.random.normal(stream_key, shape, jnp.float32)
    if cuts:
        entries = entries * levels(stream_key, shape, cuts, -0.22, 0.18)
    return jnp.clip(entries, -most, most).astype(kind)


def setup_inputs(seed: int = 0) -> dict:
    streams_of = jax.random.split(jax.random.key(seed), 15)
    inputs = draw_inputs(jax.random.fold_in(streams_of[14], 71), 0)
    lengths = plant(jax.random.randint(streams_of[1], (BATCH,), SEQ_LEN - TOK_DEV + 1, SEQ_LEN + 1), jax.random.fold_in(streams_of[1], 1), SEQ_LEN - TOK_DEV + 1, SEQ_LEN).astype(jnp.int32)
    labels = plant(jax.random.randint(streams_of[2], (BATCH,), 0, K), jax.random.fold_in(streams_of[2], 1), 0, K - 1).astype(jnp.int32)
    norm_gain = jnp.clip(1.0 + 0.1 * jax.random.normal(streams_of[3], (LAYERS, H), jnp.float32), 0.5, 1.5)
    norm_bias = centred(streams_of[4], (LAYERS, H), 0.3, 4.0, (), jnp.float32)
    b_proj = centred(streams_of[5], (LAYERS, H, 2 * P_SIZE), H ** -0.5, 0.25, ((1, 4),), jnp.float32)
    rate = jnp.clip(jnp.exp(math.log(0.05) - 5.322034 * jax.random.uniform(streams_of[6], (LAYERS, P_SIZE), jnp.float32) ** levels(streams_of[6], (LAYERS, P_SIZE), ((1, 8),), -0.2, 0.2)), 0.00024414062, 0.05)
    phase = jnp.clip(jax.random.uniform(streams_of[7], (LAYERS, P_SIZE), jnp.float32, -3.140625, 3.140625), -3.140625, 3.140625)
    c_proj = centred(streams_of[8], (LAYERS, 4, P_SIZE, H), (4 * P_SIZE) ** -0.5, 0.15625, ((2, 8), (3, 4)), jnp.float32)
    skip = jnp.clip(jax.random.uniform(streams_of[9], (LAYERS, H), jnp.float32, 0.5, 1.5), 0.5, 1.5)
    glu_weight = centred(streams_of[10], (LAYERS, H, H), H ** -0.5, 0.25, ((1, 4),), jnp.float32)
    glu_bias = centred(streams_of[11], (LAYERS, H), 0.5, 6.0, (), jnp.float32)
    class_weight = centred(streams_of[12], (H, K), (H // 4) ** -0.5, 0.5, (), jnp.float32)
    class_bias = centred(streams_of[13], (K,), 0.5, 6.0, (), jnp.float32)
    return dict(inputs=inputs, lengths=lengths, labels=labels, norm_gain=norm_gain, norm_bias=norm_bias, b_proj=b_proj, rate=rate, phase=phase, c_proj=c_proj, skip=skip, glu_weight=glu_weight, glu_bias=glu_bias, class_weight=class_weight, class_bias=class_bias)


@jax.custom_vjp
def low(v):
    return lax.optimization_barrier(v.astype(jnp.bfloat16)).astype(jnp.float32)

@jax.custom_vjp
def low_back(v):
    return v

def low_keep(v):
    return (low(v), None)

def low_pass(kept, grad):
    return (grad,)

def back_keep(v):
    return (v, None)

def back_low(kept, grad):
    return (low(grad),)
low.defvjp(low_keep, low_pass)
low_back.defvjp(back_keep, back_low)

def dot_high(left, right):
    return jnp.dot(left, right, precision=lax.Precision.HIGHEST, preferred_element_type=jnp.float32)

def norm_apply(stream, gain_row, bias_row):
    center = stream - lax.optimization_barrier(jnp.mean(stream, axis=1, keepdims=True))
    spread = lax.optimization_barrier(jnp.mean(center * center, axis=1, keepdims=True))
    return center * lax.rsqrt(spread + 1e-05) * gain_row + bias_row

def combine_steps(earlier, later):
    ea_re, ea_im, eb_re, eb_im = earlier
    la_re, la_im, lb_re, lb_im = later
    return (la_re * ea_re - la_im * ea_im, la_re * ea_im + la_im * ea_re, la_re * eb_re - la_im * eb_im + lb_re, la_re * eb_im + la_im * eb_re + lb_im)

def scan_states(values, rate_row, phase_row):
    decay_mag = jnp.exp(-rate_row)
    lam_re = decay_mag * jnp.cos(phase_row)
    lam_im = decay_mag * jnp.sin(phase_row)
    in_scale = jnp.sqrt(-jnp.expm1(-2.0 * rate_row))
    drive_re = values[:, 0, :] * in_scale
    drive_im = values[:, 1, :] * in_scale
    full_re = jnp.broadcast_to(lam_re, drive_re.shape)
    full_im = jnp.broadcast_to(lam_im, drive_re.shape)
    forward = lax.associative_scan(combine_steps, (full_re, full_im, drive_re, drive_im), axis=0)
    backward = lax.associative_scan(combine_steps, (full_re, full_im, drive_re, drive_im), reverse=True, axis=0)
    return jnp.stack([forward[2], forward[3], backward[2], backward[3]], axis=1)

def s5_layer(stream, params):
    gain_row, bias_row, b_mat, rate_row, phase_row, c_mat, skip_row, glu_mat, glu_row = params
    normed = norm_apply(stream, gain_row, bias_row)
    drive = low(low_back(dot_high(low(normed), low(b_mat))))
    feat = low(scan_states(drive.reshape(-1, 2, P_SIZE), rate_row, phase_row)).reshape(-1, 4 * P_SIZE)
    mixed = low_back(dot_high(feat, low(c_mat).reshape(4 * P_SIZE, H)))
    pre_act = mixed + skip_row * normed
    gelu_out = jax.nn.gelu(pre_act, approximate=True)
    gate_pre = low_back(dot_high(low(gelu_out), low(glu_mat)) + glu_row)
    return stream + gelu_out * jax.nn.sigmoid(gate_pre)

def reference(inputs, lengths, labels, norm_gain, norm_bias, b_proj, rate, phase, c_proj, skip, glu_weight, glu_bias, class_weight, class_bias):
    start_stream = inputs.astype(jnp.float32)

    def objective(first, gain_all, bias_all, b_all, rate_all, phase_all, c_all, skip_all, glu_all, glub_all, head_w, head_b):

        def one_seq(stream, length, label):
            for layer_idx in range(LAYERS):
                params = (gain_all[layer_idx], bias_all[layer_idx], b_all[layer_idx], rate_all[layer_idx], phase_all[layer_idx], c_all[layer_idx], skip_all[layer_idx], glu_all[layer_idx], glub_all[layer_idx])
                stream = s5_layer(stream, params)
            positions = jnp.arange(stream.shape[0], dtype=jnp.int32)
            valid_mask = (positions < length).astype(jnp.float32)
            length_f = length.astype(jnp.float32)
            pooled = lax.optimization_barrier(jnp.sum(stream * valid_mask[:, None], axis=0)) / length_f
            logits = dot_high(pooled[None, :], head_w)[0] + head_b
            onehot = (jnp.arange(K, dtype=jnp.int32) == label).astype(jnp.float32)
            cross_ent = jax.nn.logsumexp(logits) - jnp.sum(onehot * logits)
            return (length_f * cross_ent, cross_ent)
        checked = jax.checkpoint(one_seq)

        def step_fn(running, item):
            weighted, cross_ent = checked(item[0], item[1], item[2])
            return (running + weighted, cross_ent)
        total, cross_all = lax.scan(step_fn, jnp.zeros((), jnp.float32), (first, lengths, labels))
        return (total, jnp.mean(cross_all))
    primals = (start_stream, norm_gain, norm_bias, b_proj, rate, phase, c_proj, skip, glu_weight, glu_bias, class_weight, class_bias)
    total, back_fn, loss_mean = jax.vjp(objective, *primals, has_aux=True)
    grads = back_fn(jnp.ones((), jnp.float32))
    return (loss_mean, grads[0], grads[1], grads[2], grads[3], grads[4], grads[5], grads[6], grads[7], grads[8], grads[9], grads[10], grads[11])
```

```python
from functools import partial

import jax
import jax.numpy as jnp
from jax import lax
from jax.experimental import pallas as pl
from jax.experimental.pallas import tpu as pltpu
from jax.sharding import PartitionSpec as P

MESH = pl.DeviceIdType.MESH
F32 = jnp.float32
BF16 = jnp.bfloat16
CHUNKS = 8
TILE = 32
GELU_A = 0.7978845608028654
GELU_B = 0.044715


def mm_nn(left, right):
    return lax.dot_general(left, right, (((1,), (0,)), ((), ())), preferred_element_type=F32)


def mm_nt(left, right):
    return lax.dot_general(left, right, (((1,), (1,)), ((), ())), preferred_element_type=F32)


def mm_tn(left, right):
    return lax.dot_general(left, right, (((0,), (0,)), ((), ())), preferred_element_type=F32)


def cmul(a_re, a_im, b_re, b_im):
    return a_re * b_re - a_im * b_im, a_re * b_im + a_im * b_re


def fold8(value):
    total = value[0:8]
    for first in range(8, value.shape[0], 8):
        total = total + value[first : first + 8]
    return total


def model_kernel(
    dims,
    len_ref,
    lab_ref,
    x_ref,
    gain_ref,
    bias_ref,
    skip_ref,
    glub_ref,
    tab_ref,
    cw_ref,
    cb_ref,
    b_ref,
    glu_ref,
    c_ref,
    gin_ref,
    small_ref,
    bgrad_ref,
    glugrad_ref,
    cgrad_ref,
    stream,
    xhat,
    rstd,
    nlow,
    drive,
    caus,
    anti,
    feat,
    gelu_out,
    gelu_low,
    gelu_der,
    sig,
    wide,
    temp,
    mix,
    mlow,
    ggrad,
    dlow,
    perm,
    send_buf,
    recv_buf,
    send_sem,
    recv_sem,
):
    layers, tok, width, states, classes, ndp, nseq = dims
    steps = tok // CHUNKS
    me = lax.axis_index("seq")
    p = states

    barrier = pltpu.get_barrier_semaphore()

    def greet(k, carry):
        peer = lax.rem(me + k, nseq)
        pl.semaphore_signal(barrier, inc=1, device_id={"seq": peer}, device_id_type=MESH)
        return carry

    lax.fori_loop(1, nseq, greet, 0)

    def row_loop(body, init, unroll=1):
        def step(k, carry):
            rows = pl.ds(pl.multiple_of(k * TILE, TILE), TILE)
            return body(rows, k * TILE, carry)

        return lax.fori_loop(0, tok // TILE, step, init, unroll=unroll)

    def exchange_copy(slot, peer, origin):
        return pltpu.make_async_remote_copy(
            src_ref=send_buf.at[slot],
            dst_ref=recv_buf.at[slot, origin],
            send_sem=send_sem.at[slot, peer],
            recv_sem=recv_sem.at[slot, origin],
            device_id={"seq": peer},
            device_id_type=MESH,
        )

    def exchange_start(slot):
        def one(k, carry):
            exchange_copy(slot, lax.rem(me + k, nseq), me).start()
            return carry

        lax.fori_loop(1, nseq, one, 0)

    def exchange_wait(slot):
        def one(k, carry):
            peer = lax.rem(me + k, nseq)
            exchange_copy(slot, peer, me).wait_send()
            exchange_copy(slot, peer, peer).wait_recv()
            return carry

        lax.fori_loop(1, nseq, one, 0)

    sub = lax.broadcasted_iota(jnp.int32, (CHUNKS, p), 0)

    def layer_powers(layer, conj):
        lam_re = tab_ref[layer, 0:1, :]
        lam_im = tab_ref[layer, 1:2, :]
        if conj:
            lam_im = -lam_im
        pw_re, pw_im = lam_re, lam_im
        count = 1
        while count < steps:
            pw_re, pw_im = cmul(pw_re, pw_im, pw_re, pw_im)
            count *= 2
        jumps = [(pw_re, pw_im)]
        for _ in range(3):
            pw_re, pw_im = cmul(pw_re, pw_im, pw_re, pw_im)
            jumps.append((pw_re, pw_im))
        return lam_re, lam_im, jumps

    def jump_table(jumps, index):
        re = jnp.ones((CHUNKS, p), F32)
        im = jnp.zeros((CHUNKS, p), F32)
        for bit in range(3):
            new_re, new_im = cmul(re, im, jumps[bit][0], jumps[bit][1])
            has = (index & (1 << bit)) != 0
            re = jnp.where(has, new_re, re)
            im = jnp.where(has, new_im, im)
        return re, im

    def local_ends(src, first_c, first_a, lam_re, lam_im):
        zero = jnp.zeros((CHUNKS, p), F32)
        l_re = jnp.broadcast_to(lam_re, (CHUNKS, p))
        l_im = jnp.broadcast_to(lam_im, (CHUNKS, p))

        def step(j, carry):
            e_re, e_im, f_re, f_im = carry
            up = pl.ds(pl.multiple_of(j * CHUNKS, CHUNKS), CHUNKS)
            down = pl.ds(pl.multiple_of((steps - 1 - j) * CHUNKS, CHUNKS), CHUNKS)
            e_re, e_im = cmul(l_re, l_im, e_re, e_im)
            f_re, f_im = cmul(l_re, l_im, f_re, f_im)
            return (
                e_re + src[up, first_c : first_c + p],
                e_im + src[up, first_c + p : first_c + 2 * p],
                f_re + src[down, first_a : first_a + p],
                f_im + src[down, first_a + p : first_a + 2 * p],
            )

        return lax.fori_loop(0, steps, step, (zero,) * 4, unroll=4)

    def local_prefix(ends, jumps):
        e_re, e_im, f_re, f_im = ends
        for bit in range(3):
            shift = 1 << bit
            j_re, j_im = jumps[bit]
            s_re = jnp.where(sub >= shift, pltpu.roll(e_re, shift, 0), 0.0)
            s_im = jnp.where(sub >= shift, pltpu.roll(e_im, shift, 0), 0.0)
            a_re, a_im = cmul(j_re, j_im, s_re, s_im)
            e_re, e_im = e_re + a_re, e_im + a_im
            s_re = jnp.where(sub < CHUNKS - shift, pltpu.roll(f_re, CHUNKS - shift, 0), 0.0)
            s_im = jnp.where(sub < CHUNKS - shift, pltpu.roll(f_im, CHUNKS - shift, 0), 0.0)
            a_re, a_im = cmul(j_re, j_im, s_re, s_im)
            f_re, f_im = f_re + a_re, f_im + a_im
        return e_re, e_im, f_re, f_im

    def send_totals(slot, prefix):
        e_re, e_im, f_re, f_im = prefix
        send_buf[slot, 0:1, 0:p] = e_re[CHUNKS - 1 : CHUNKS]
        send_buf[slot, 1:2, 0:p] = e_im[CHUNKS - 1 : CHUNKS]
        send_buf[slot, 2:3, 0:p] = f_re[0:1]
        send_buf[slot, 3:4, 0:p] = f_im[0:1]
        exchange_start(slot)

    def chunk_carries(slot, prefix, jumps):
        e_re, e_im, f_re, f_im = prefix
        d_re, d_im = jumps[3]
        zero = jnp.zeros((1, p), F32)

        def step(k, carry):
            c_re, c_im, a_re, a_im = carry
            n_re, n_im = cmul(d_re, d_im, c_re, c_im)
            use = k < me
            c_re = jnp.where(use, n_re + recv_buf[slot, k, 0:1, 0:p], c_re)
            c_im = jnp.where(use, n_im + recv_buf[slot, k, 1:2, 0:p], c_im)
            back = nseq - 1 - k
            n_re, n_im = cmul(d_re, d_im, a_re, a_im)
            use = back > me
            a_re = jnp.where(use, n_re + recv_buf[slot, back, 2:3, 0:p], a_re)
            a_im = jnp.where(use, n_im + recv_buf[slot, back, 3:4, 0:p], a_im)
            return c_re, c_im, a_re, a_im

        c_re, c_im, a_re, a_im = lax.fori_loop(0, nseq, step, (zero,) * 4)
        t_re, t_im = jump_table(jumps, sub)
        g_re, g_im = cmul(t_re, t_im, c_re, c_im)
        in_c_re = g_re + jnp.where(sub >= 1, pltpu.roll(e_re, 1, 0), 0.0)
        in_c_im = g_im + jnp.where(sub >= 1, pltpu.roll(e_im, 1, 0), 0.0)
        t_re, t_im = jump_table(jumps, CHUNKS - 1 - sub)
        g_re, g_im = cmul(t_re, t_im, a_re, a_im)
        in_a_re = g_re + jnp.where(sub < CHUNKS - 1, pltpu.roll(f_re, CHUNKS - 1, 0), 0.0)
        in_a_im = g_im + jnp.where(sub < CHUNKS - 1, pltpu.roll(f_im, CHUNKS - 1, 0), 0.0)
        return in_c_re, in_c_im, in_a_re, in_a_im

    for col in range(0, width, 128):
        perm[col // 128] = x_ref[:, col : col + 128].astype(F32)

        def place(j, carry, col=col):
            rows = pl.ds(pl.multiple_of(j * CHUNKS, CHUNKS), CHUNKS)
            stream[rows, col : col + 128] = perm[col // 128, pl.ds(j, CHUNKS, stride=steps), :]
            return carry

        lax.fori_loop(0, steps, place, 0, unroll=4)

    for layer in range(layers):
        gain = gain_ref[layer : layer + 1, :]
        bias = bias_ref[layer : layer + 1, :]
        skip = skip_ref[layer : layer + 1, :]

        def norm_rows(rows, first, carry, layer=layer, gain=gain, bias=bias):
            value = stream[rows, :]
            center = value - jnp.mean(value, axis=1, keepdims=True)
            spread = jnp.mean(center * center, axis=1, keepdims=True)
            inv = lax.rsqrt(spread + 1e-05)
            hat = center * inv
            xhat[layer, rows, :] = hat
            rstd[layer, rows, :] = inv
            nlow[layer, rows, :] = (hat * gain + bias).astype(BF16)
            return carry

        row_loop(norm_rows, 0)

        in_scale = tab_ref[layer, 2:3, :]
        for col in range(0, 2 * p, 256):
            part = mm_nn(nlow[layer], b_ref[layer, :, col : col + 256])
            for half in range(col, col + 256, 128):
                scale_col = half % p
                drive[layer, :, half : half + 128] = (
                    part[:, half - col : half - col + 128].astype(BF16).astype(F32)
                    * in_scale[:, scale_col : scale_col + 128]
                )

        lam_re, lam_im, jumps = layer_powers(layer, False)
        ends = local_ends(drive.at[layer], 0, 0, lam_re, lam_im)
        prefix = local_prefix(ends, jumps)
        if layer == 0:
            pl.semaphore_wait(barrier, nseq - 1)
        send_totals(layer, prefix)
        exchange_wait(layer)
        carries = chunk_carries(layer, prefix, jumps)
        caus[layer, 0:CHUNKS, 0:p] = carries[0]
        caus[layer, 0:CHUNKS, p : 2 * p] = carries[1]
        anti[layer, tok : tok + CHUNKS, 0:p] = carries[2]
        anti[layer, tok : tok + CHUNKS, p : 2 * p] = carries[3]
        l_re = jnp.broadcast_to(lam_re, (CHUNKS, p))
        l_im = jnp.broadcast_to(lam_im, (CHUNKS, p))

        def state_pair(k, carry, layer=layer, l_re=l_re, l_im=l_im):
            s_re, s_im, r_re, r_im = carry
            first = pl.multiple_of(k * 2 * CHUNKS, 2 * CHUNKS)
            kept_re, kept_im = [], []
            for half in range(2):
                rows = pl.ds(first + half * CHUNKS, CHUNKS)
                s_re, s_im = cmul(l_re, l_im, s_re, s_im)
                s_re = s_re + drive[layer, rows, 0:p]
                s_im = s_im + drive[layer, rows, p : 2 * p]
                after = pl.ds(first + (half + 1) * CHUNKS, CHUNKS)
                caus[layer, after, 0:p] = s_re
                caus[layer, after, p : 2 * p] = s_im
                kept_re.append(s_re)
                kept_im.append(s_im)
            both = pl.ds(first, 2 * CHUNKS)
            feat[layer, both, 0:p] = jnp.concatenate(kept_re, axis=0).astype(BF16)
            feat[layer, both, p : 2 * p] = jnp.concatenate(kept_im, axis=0).astype(BF16)
            last = pl.multiple_of(tok - (k + 1) * 2 * CHUNKS, 2 * CHUNKS)
            kept_re, kept_im = [], []
            for half in (1, 0):
                rows = pl.ds(last + half * CHUNKS, CHUNKS)
                r_re, r_im = cmul(l_re, l_im, r_re, r_im)
                r_re = r_re + drive[layer, rows, 0:p]
                r_im = r_im + drive[layer, rows, p : 2 * p]
                anti[layer, rows, 0:p] = r_re
                anti[layer, rows, p : 2 * p] = r_im
                kept_re.insert(0, r_re)
                kept_im.insert(0, r_im)
            both = pl.ds(last, 2 * CHUNKS)
            feat[layer, both, 2 * p : 3 * p] = jnp.concatenate(kept_re, axis=0).astype(BF16)
            feat[layer, both, 3 * p : 4 * p] = jnp.concatenate(kept_im, axis=0).astype(BF16)
            return s_re, s_im, r_re, r_im

        lax.fori_loop(0, steps // 2, state_pair, carries, unroll=2)

        for col in range(0, width, 256):
            temp[:, col : col + 256] = mm_nn(feat[layer], c_ref[layer, :, col : col + 256])

        def act_rows(rows, first, carry, layer=layer, gain=gain, bias=bias, skip=skip):
            pre = temp[rows, :] + skip * (xhat[layer, rows, :] * gain + bias)
            square = pre * pre
            th = jnp.tanh(GELU_A * pre * (1.0 + GELU_B * square))
            cdf = 0.5 * (1.0 + th)
            out = pre * cdf
            gelu_out[layer, rows, :] = out
            gelu_low[layer, rows, :] = out.astype(BF16)
            gelu_der[layer, rows, :] = cdf + 0.5 * pre * (1.0 - th * th) * (
                GELU_A * (1.0 + 3.0 * GELU_B * square)
            )
            return carry

        row_loop(act_rows, 0)
        for col in range(0, width, 256):
            temp[:, col : col + 256] = mm_nn(gelu_low[layer], glu_ref[layer, :, col : col + 256])
        glu_bias = glub_ref[layer : layer + 1, :]
        last_layer = layer == layers - 1

        def gate_rows(rows, first, carry, layer=layer, glu_bias=glu_bias, last_layer=last_layer):
            gate = 1.0 / (1.0 + jnp.exp(-(temp[rows, :] + glu_bias)))
            sig[layer, rows, :] = gate
            new = stream[rows, :] + gelu_out[layer, rows, :] * gate
            if not last_layer:
                stream[rows, :] = new
                return carry
            return carry + fold8(new * row_mask(first))

        def row_mask(first):
            row = first + lax.broadcasted_iota(jnp.int32, (TILE, 1), 0)
            position = me * tok + (row & (CHUNKS - 1)) * steps + (row >> 3)
            return jnp.where(position < len_ref[0], 1.0, 0.0).astype(F32)

        pooled_part = row_loop(gate_rows, jnp.zeros((CHUNKS, width), F32) if last_layer else 0)

    pool_slot = 2 * layers
    own_sum = jnp.sum(pooled_part, axis=0, keepdims=True)
    send_buf[pool_slot, 0:1, :] = own_sum
    exchange_start(pool_slot)
    exchange_wait(pool_slot)

    def add_pool(k, total):
        return total + jnp.where(k == me, 0.0, recv_buf[pool_slot, k, 0:1, :])

    pooled_sum = lax.fori_loop(0, nseq, add_pool, own_sum)
    len_row = jnp.full((1, 1), len_ref[0], jnp.int32).astype(F32)
    pooled = pooled_sum / len_row
    logit = [
        jnp.sum(pooled * cw_ref[k : k + 1, :], axis=1, keepdims=True) + cb_ref[k : k + 1, :]
        for k in range(classes)
    ]
    top = logit[0]
    for k in range(1, classes):
        top = jnp.maximum(top, logit[k])
    expo = [jnp.exp(v - top) for v in logit]
    norm = expo[0]
    for k in range(1, classes):
        norm = norm + expo[k]
    hot = [jnp.where(lab_ref[0] == k, 1.0, 0.0).astype(F32) for k in range(classes)]
    cross = top + jnp.log(norm)
    for k in range(classes):
        cross = cross - hot[k] * logit[k]
    lgrad = [len_row * (expo[k] / norm - hot[k]) for k in range(classes)]
    pooled_grad = lgrad[0] * cw_ref[0:1, :]
    for k in range(1, classes):
        pooled_grad = pooled_grad + lgrad[k] * cw_ref[k : k + 1, :]
    grad_row = pooled_grad / len_row
    once = jnp.where(me == 0, 1.0, 0.0).astype(F32)
    small_ref[...] = jnp.zeros_like(small_ref)
    head_row = 6 * layers
    lane = lax.broadcasted_iota(jnp.int32, (1, width), 1)
    bias_line = jnp.zeros((1, width), F32)
    for k in range(classes):
        small_ref[head_row + k : head_row + k + 1, :] = pooled * lgrad[k] * once
        bias_line = jnp.where(lane == k, lgrad[k] * once, bias_line)
    bias_line = jnp.where(lane == classes, cross * once, bias_line)
    small_ref[head_row + classes : head_row + classes + 1, :] = bias_line

    grad = stream

    def first_grad(rows, first, carry):
        grad[rows, :] = row_mask(first) * grad_row
        return carry

    row_loop(first_grad, 0)

    for layer in reversed(range(layers)):
        gain = gain_ref[layer : layer + 1, :]
        bias = bias_ref[layer : layer + 1, :]
        skip = skip_ref[layer : layer + 1, :]
        zero_sum = jnp.zeros((CHUNKS, width), F32)

        def gate_back(rows, first, total, layer=layer):
            gate = sig[layer, rows, :]
            low = (grad[rows, :] * gelu_out[layer, rows, :] * gate * (1.0 - gate)).astype(BF16)
            ggrad[rows, :] = low
            return total + fold8(low.astype(F32))

        total = row_loop(gate_back, zero_sum)
        small_ref[3 * layers + layer : 3 * layers + layer + 1, :] = jnp.sum(
            total, axis=0, keepdims=True
        )
        for col in range(0, width, 256):
            temp[:, col : col + 256] = mm_nt(ggrad[...], glu_ref[layer, col : col + 256, :])

        def mix_back(rows, first, total, layer=layer, gain=gain, bias=bias):
            act = grad[rows, :] * sig[layer, rows, :] + temp[rows, :]
            value = act * gelu_der[layer, rows, :]
            mix[rows, :] = value
            mlow[rows, :] = value.astype(BF16)
            return total + fold8(value * (xhat[layer, rows, :] * gain + bias))

        total = row_loop(mix_back, zero_sum)
        small_ref[2 * layers + layer : 2 * layers + layer + 1, :] = jnp.sum(
            total, axis=0, keepdims=True
        )
        for col in range(0, 4 * p, 256):
            wide[:, col : col + 256] = mm_nt(mlow[...], c_ref[layer, col : col + 256, :])

        lam_re, lam_im, jumps = layer_powers(layer, True)
        ends = local_ends(wide, 2 * p, 0, lam_re, lam_im)
        prefix = local_prefix(ends, jumps)
        slot = layers + layer
        send_totals(slot, prefix)
        for col in range(0, 4 * p, 256):
            cgrad_ref[layer, col : col + 256, :] = mm_tn(
                feat[layer, :, col : col + 256], mlow[...]
            ).astype(BF16)
        for col in range(0, width, 256):
            glugrad_ref[layer, col : col + 256, :] = mm_tn(
                gelu_low[layer, :, col : col + 256], ggrad[...]
            ).astype(BF16)
        exchange_wait(slot)
        carries = chunk_carries(slot, prefix, jumps)
        l_re = jnp.broadcast_to(lam_re, (CHUNKS, p))
        l_im = jnp.broadcast_to(lam_im, (CHUNKS, p))
        zero = jnp.zeros((CHUNKS, p), F32)

        def anti_grad(j, carry, layer=layer, l_re=l_re, l_im=l_im):
            r_re, r_im, d_re, d_im = carry
            rows = pl.ds(pl.multiple_of(j * CHUNKS, CHUNKS), CHUNKS)
            after = pl.ds(pl.multiple_of((j + 1) * CHUNKS, CHUNKS), CHUNKS)
            r_re, r_im = cmul(l_re, l_im, r_re, r_im)
            r_re = r_re + wide[rows, 2 * p : 3 * p]
            r_im = r_im + wide[rows, 3 * p : 4 * p]
            wide[rows, 2 * p : 3 * p] = r_re
            wide[rows, 3 * p : 4 * p] = r_im
            q_re = anti[layer, after, 0:p]
            q_im = anti[layer, after, p : 2 * p]
            return r_re, r_im, d_re + (r_re * q_re + r_im * q_im), d_im + (r_im * q_re - r_re * q_im)

        _, _, d_re, d_im = lax.fori_loop(
            0, steps, anti_grad, (carries[0], carries[1], zero, zero), unroll=4
        )
        in_scale = jnp.broadcast_to(tab_ref[layer, 2:3, :], (CHUNKS, p))

        def caus_grad(k, carry, layer=layer, l_re=l_re, l_im=l_im, in_scale=in_scale):
            a_re, a_im, d_re, d_im, s_sum = carry
            last = pl.multiple_of(tok - (k + 1) * 2 * CHUNKS, 2 * CHUNKS)
            kept_re, kept_im = [], []
            for half in (1, 0):
                rows = pl.ds(last + half * CHUNKS, CHUNKS)
                a_re, a_im = cmul(l_re, l_im, a_re, a_im)
                a_re = a_re + wide[rows, 0:p]
                a_im = a_im + wide[rows, p : 2 * p]
                q_re = caus[layer, rows, 0:p]
                q_im = caus[layer, rows, p : 2 * p]
                d_re = d_re + (a_re * q_re + a_im * q_im)
                d_im = d_im + (a_im * q_re - a_re * q_im)
                t_re = a_re + wide[rows, 2 * p : 3 * p]
                t_im = a_im + wide[rows, 3 * p : 4 * p]
                s_sum = s_sum + (
                    t_re * drive[layer, rows, 0:p] + t_im * drive[layer, rows, p : 2 * p]
                )
                kept_re.insert(0, t_re * in_scale)
                kept_im.insert(0, t_im * in_scale)
            both = pl.ds(last, 2 * CHUNKS)
            dlow[both, 0:p] = jnp.concatenate(kept_re, axis=0).astype(BF16)
            dlow[both, p : 2 * p] = jnp.concatenate(kept_im, axis=0).astype(BF16)
            return a_re, a_im, d_re, d_im, s_sum

        _, _, d_re, d_im, s_sum = lax.fori_loop(
            0, steps // 2, caus_grad, (carries[2], carries[3], d_re, d_im, zero), unroll=2
        )
        d_re = jnp.sum(d_re, axis=0, keepdims=True)
        d_im = jnp.sum(d_im, axis=0, keepdims=True)
        s_sum = jnp.sum(s_sum, axis=0, keepdims=True) / tab_ref[layer, 2:3, :]
        true_re = tab_ref[layer, 0:1, :]
        true_im = tab_ref[layer, 1:2, :]
        row = 4 * layers + layer
        small_ref[row : row + 1, 0:p] = (
            s_sum * tab_ref[layer, 3:4, :] - d_re * true_re - d_im * true_im
        )
        row = 5 * layers + layer
        small_ref[row : row + 1, 0:p] = d_im * true_re - d_re * true_im

        for col in range(0, width, 256):
            bgrad_ref[layer, col : col + 256, :] = mm_tn(
                nlow[layer, :, col : col + 256], dlow[...]
            ).astype(BF16)
            temp[:, col : col + 256] = mm_nt(dlow[...], b_ref[layer, col : col + 256, :])

        def norm_back(rows, first, carry, layer=layer, gain=gain, skip=skip):
            gain_sum, bias_sum = carry
            ngrad = mix[rows, :] * skip + temp[rows, :]
            hat = xhat[layer, rows, :]
            q = ngrad * gain
            mean_q = jnp.mean(q, axis=1, keepdims=True)
            mean_x = jnp.mean(q * hat, axis=1, keepdims=True)
            grad[rows, :] = grad[rows, :] + (q - mean_q - hat * mean_x) * rstd[layer, rows, :]
            return gain_sum + fold8(ngrad * hat), bias_sum + fold8(ngrad)

        gain_sum, bias_sum = row_loop(norm_back, (zero_sum, zero_sum))
        small_ref[layer : layer + 1, :] = jnp.sum(gain_sum, axis=0, keepdims=True)
        small_ref[layers + layer : layers + layer + 1, :] = jnp.sum(bias_sum, axis=0, keepdims=True)

    for col in range(0, width, 128):
        perm[col // 128] = grad[:, col : col + 128]

        def unplace(k, carry, col=col):
            first = k * CHUNKS
            chunk = first // steps
            rows = pl.ds((first - chunk * steps) * CHUNKS + chunk, CHUNKS, stride=CHUNKS)
            out = pl.ds(pl.multiple_of(first, CHUNKS), CHUNKS)
            gin_ref[out, col : col + 128] = perm[col // 128, rows, :]
            return carry

        lax.fori_loop(0, steps, unplace, 0, unroll=4)


def run_model(dims, operands):
    layers, tok, width, states, classes, ndp, nseq = dims
    vmem = pl.BlockSpec(memory_space=pltpu.VMEM)
    smem = pl.BlockSpec(memory_space=pltpu.SMEM)
    small_rows = -(-(6 * layers + classes + 1) // 8) * 8
    slots = 2 * layers + 1
    per_layer = lambda cols, kind, rows=tok: pltpu.VMEM((layers, rows, cols), kind)
    return pl.pallas_call(
        partial(model_kernel, dims),
        out_shape=(
            jax.ShapeDtypeStruct((tok, width), F32),
            jax.ShapeDtypeStruct((small_rows, width), F32),
            jax.ShapeDtypeStruct((layers, width, 2 * states), BF16),
            jax.ShapeDtypeStruct((layers, width, width), BF16),
            jax.ShapeDtypeStruct((layers, 4 * states, width), BF16),
        ),
        in_specs=[smem, smem] + [vmem] * 11,
        out_specs=[vmem] * 5,
        scratch_shapes=[
            pltpu.VMEM((tok, width), F32),
            per_layer(width, F32),
            per_layer(1, F32),
            per_layer(width, BF16),
            per_layer(2 * states, F32),
            per_layer(2 * states, F32, tok + CHUNKS),
            per_layer(2 * states, F32, tok + CHUNKS),
            per_layer(4 * states, BF16),
            per_layer(width, F32),
            per_layer(width, BF16),
            per_layer(width, F32),
            per_layer(width, F32),
            pltpu.VMEM((tok, 4 * states), F32),
            pltpu.VMEM((tok, width), F32),
            pltpu.VMEM((tok, width), F32),
            pltpu.VMEM((tok, width), BF16),
            pltpu.VMEM((tok, width), BF16),
            pltpu.VMEM((tok, 2 * states), BF16),
            pltpu.VMEM((width // 128, tok, 128), F32),
            pltpu.VMEM((slots, 8, width), F32),
            pltpu.VMEM((slots, nseq, 8, width), F32),
            pltpu.SemaphoreType.DMA((slots, nseq)),
            pltpu.SemaphoreType.DMA((slots, nseq)),
        ],
        compiler_params=pltpu.CompilerParams(
            collective_id=0, has_side_effects=True, vmem_limit_bytes=56 * 1024 * 1024
        ),
        cost_estimate=pl.CostEstimate(
            flops=6 * layers * tok * width * (6 * states + width),
            bytes_accessed=16 * 1024 * 1024,
            transcendentals=2 * layers * tok * width,
        ),
    )(*operands)


def per_device(
    inputs,
    lengths,
    labels,
    norm_gain,
    norm_bias,
    b_proj,
    rate,
    phase,
    c_proj,
    skip,
    glu_weight,
    glu_bias,
    class_weight,
    class_bias,
):
    layers, width = norm_gain.shape
    tok = inputs.shape[1]
    ndp = lax.axis_size("dp")
    nseq = lax.axis_size("seq")
    states = c_proj.shape[2] * nseq
    classes = class_bias.shape[0]
    dims = (layers, tok, width, states, classes, ndp, nseq)
    b_full = lax.all_gather(b_proj.astype(BF16), "dp", axis=1, tiled=True)
    g_full = lax.all_gather(glu_weight.astype(BF16), "dp", axis=1, tiled=True)
    c_half = lax.all_gather(c_proj.astype(BF16), "dp", axis=3, tiled=True)
    c_full = lax.all_gather(c_half, "seq", axis=2, tiled=True)
    c_full = c_full.reshape(layers, 4 * states, width)
    decay = jnp.exp(-rate)
    in_scale = jnp.sqrt(-jnp.expm1(-2.0 * rate))
    table = jnp.stack(
        [
            decay * jnp.cos(phase),
            decay * jnp.sin(phase),
            in_scale,
            jnp.exp(-2.0 * rate) / in_scale,
        ],
        axis=1,
    )
    table = lax.all_gather(table, "seq", axis=2, tiled=True)
    grad_inputs, small, b_grad, g_grad, c_grad = run_model(
        dims,
        (
            lengths,
            labels,
            inputs[0],
            norm_gain,
            norm_bias,
            skip,
            glu_bias,
            table,
            class_weight.T,
            class_bias[:, None],
            b_full,
            g_full,
            c_full,
        ),
    )
    b_share = lax.psum_scatter(b_grad, "dp", scatter_dimension=1, tiled=True)
    g_share = lax.psum_scatter(g_grad, "dp", scatter_dimension=1, tiled=True)
    b_share = lax.psum(b_share, "seq").astype(F32)
    g_share = lax.psum(g_share, "seq").astype(F32)
    c_grad = c_grad.reshape(layers, 4, states, width)
    c_share = lax.psum_scatter(c_grad, "seq", scatter_dimension=2, tiled=True)
    c_share = lax.psum_scatter(c_share, "dp", scatter_dimension=3, tiled=True).astype(F32)
    small = lax.psum(small, ("dp", "seq"))
    own = lax.axis_index("seq") * (states // nseq)

    def state_rows(first):
        return lax.dynamic_slice(small[first : first + layers], (0, own), (layers, states // nseq))

    head = 6 * layers
    return (
        small[head + classes, classes] / ndp,
        grad_inputs[None],
        small[0:layers],
        small[layers : 2 * layers],
        b_share,
        state_rows(4 * layers),
        state_rows(5 * layers),
        c_share,
        small[2 * layers : 3 * layers],
        g_share,
        small[3 * layers : 4 * layers],
        small[head : head + classes].T,
        small[head + classes, 0:classes],
    )


def solution(mesh):
    return jax.shard_map(
        per_device,
        mesh=mesh,
        in_specs=(
            P("dp", "seq", None),
            P("dp"),
            P("dp"),
            P(),
            P(),
            P(None, "dp", None),
            P(None, "seq"),
            P(None, "seq"),
            P(None, None, "seq", "dp"),
            P(),
            P(None, "dp", None),
            P(),
            P(),
            P(),
        ),
        out_specs=(
            P(),
            P("dp", "seq", None),
            P(),
            P(),
            P(None, "dp", None),
            P(None, "seq"),
            P(None, "seq"),
            P(None, None, "seq", "dp"),
            P(),
            P(None, "dp", None),
            P(),
            P(),
            P(),
        ),
        check_vma=False,
    )
```

```python
from functools import partial
from typing import Any, NamedTuple

import jax
import jax.numpy as jnp
from jax import lax
from jax.experimental import pallas as pl
from jax.experimental.pallas import tpu as pltpu
from jax.sharding import PartitionSpec as P

MESH = pl.DeviceIdType.MESH
F32 = jnp.float32
BF16 = jnp.bfloat16
CHUNKS = 8
TILE = 32
GELU_A = 0.7978845608028654
GELU_B = 0.044715


def mm_nn(left, right):
    return lax.dot_general(left, right, (((1,), (0,)), ((), ())), preferred_element_type=F32)


def mm_nt(left, right):
    return lax.dot_general(left, right, (((1,), (1,)), ((), ())), preferred_element_type=F32)


def mm_tn(left, right):
    return lax.dot_general(left, right, (((0,), (0,)), ((), ())), preferred_element_type=F32)


def cmul(a_re, a_im, b_re, b_im):
    return a_re * b_re - a_im * b_im, a_re * b_im + a_im * b_re


def fold8(value):
    total = value[0:8]
    for first in range(8, value.shape[0], 8):
        total = total + value[first : first + 8]
    return total


class Operands(NamedTuple):
    len: Any
    lab: Any
    x: Any
    gain: Any
    bias: Any
    skip: Any
    glub: Any
    tab_in: Any
    cw: Any
    cb: Any
    b_in: Any
    glu_in: Any
    c_in: Any


class Results(NamedTuple):
    gin: Any
    small_out: Any
    b_out: Any
    glu_out: Any
    c_out: Any


class Local(NamedTuple):
    stream: Any
    xhat: Any
    rstd: Any
    nlow: Any
    drive: Any
    caus: Any
    anti: Any
    feat: Any
    gelu_out: Any
    gelu_low: Any
    gelu_der: Any
    sig: Any
    wide: Any
    temp: Any
    mix: Any
    mlow: Any
    ggrad: Any
    dlow: Any
    perm: Any
    send_buf: Any
    recv_buf: Any
    send_sem: Any
    recv_sem: Any


class Shared(NamedTuple):
    tab: Any
    tab_recv: Any
    b_buf: Any
    glu_buf: Any
    c_buf: Any
    ssem: Any
    rsem: Any
    small: Any
    small_core: Any
    small_y: Any
    small_sum: Any
    small_recv: Any


class RowGrad(NamedTuple):
    snd1: Any
    rcv1: Any
    acc: Any
    snd2: Any
    rcv2: Any
    acc2: Any
    snd3: Any
    rcv3: Any
    full: Any


class ColGrad(NamedTuple):
    snd1: Any
    rcv1: Any
    acc: Any
    snd2: Any
    rcv2: Any
    acc2: Any
    snd3: Any
    rcv3: Any
    acc3: Any
    snd4: Any
    rcv4: Any


def take(refs, kind):
    count = len(kind._fields)
    return kind(*refs[:count]), refs[count:]


def model_kernel(dims, inside, *refs):
    layers, tok, width, states, classes, ndp, nseq = dims
    I, refs = take(refs, Operands)
    O, refs = take(refs, Results)
    L, refs = take(refs, Local)
    if inside:
        S, refs = take(refs, Shared)
        BG, refs = take(refs, RowGrad)
        GG, refs = take(refs, RowGrad)
        CG, refs = take(refs, ColGrad)
        tab_ref, b_ref, glu_ref, c_ref, small_ref = S.tab, S.b_buf, S.glu_buf, S.c_buf, S.small
    else:
        tab_ref, b_ref, glu_ref, c_ref, small_ref = I.tab_in, I.b_in, I.glu_in, I.c_in, O.small_out
    len_ref, lab_ref, x_ref = I.len, I.lab, I.x
    gain_ref, bias_ref, skip_ref, glub_ref = I.gain, I.bias, I.skip, I.glub
    cw_ref, cb_ref, gin_ref = I.cw, I.cb, O.gin
    stream, xhat, rstd, nlow, drive = L.stream, L.xhat, L.rstd, L.nlow, L.drive
    caus, anti, feat, gelu_out, gelu_low = L.caus, L.anti, L.feat, L.gelu_out, L.gelu_low
    gelu_der, sig, wide, temp, mix = L.gelu_der, L.sig, L.wide, L.temp, L.mix
    mlow, ggrad, dlow, perm = L.mlow, L.ggrad, L.dlow, L.perm
    send_buf, recv_buf = L.send_buf, L.recv_buf
    send_sem, recv_sem = L.send_sem, L.recv_sem
    steps = tok // CHUNKS
    half_cols = width // 2
    me = lax.axis_index("seq")
    my_dp = lax.axis_index("dp")
    p = states
    core, yy = lax.rem(my_dp, 2), my_dp // 2
    xx, zz = lax.rem(me, 2), me // 2
    ny, nz = ndp // 2, nseq // 2
    own_half = core if inside else 0

    barrier = pltpu.get_barrier_semaphore()

    def greet(k, carry):
        peer = lax.rem(me + k, nseq)
        pl.semaphore_signal(barrier, inc=1, device_id={"seq": peer}, device_id_type=MESH)
        return carry

    lax.fori_loop(1, nseq, greet, 0)
    greeted = nseq - 1
    sibling = {"dp": 2 * yy + 1 - core}
    y_peer = {"dp": 2 * (1 - yy) + core}
    x_peer = {"seq": 2 * zz + 1 - xx}
    if inside:
        for peer in (sibling, y_peer):
            pl.semaphore_signal(barrier, inc=1, device_id=peer, device_id_type=MESH)
        greeted += 2

    used = [0]

    def new_sems(count):
        first = used[0]
        used[0] += count
        return first

    def remote(src, dst, sem, peer):
        return pltpu.make_async_remote_copy(
            src_ref=src,
            dst_ref=dst,
            send_sem=S.ssem.at[sem],
            recv_sem=S.rsem.at[sem],
            device_id=peer,
            device_id_type=MESH,
        )

    def seq_loop(body):
        def one(k, carry):
            body(k)
            return carry

        lax.fori_loop(1, nseq, one, 0)

    def cast_rows(dst, src, rows, step, extra=None):
        def one(k, carry):
            part = pl.ds(pl.multiple_of(k * step, step), step)
            value = src[part, :].astype(F32)
            if extra is not None:
                value = value + extra[part, :].astype(F32)
            dst[part, :] = value.astype(dst.dtype)
            return carry

        lax.fori_loop(0, rows // step, one, 0)

    def row_loop(body, init, unroll=1):
        def step(k, carry):
            rows = pl.ds(pl.multiple_of(k * TILE, TILE), TILE)
            return body(rows, k * TILE, carry)

        return lax.fori_loop(0, tok // TILE, step, init, unroll=unroll)

    def exchange_copy(slot, peer, origin):
        return pltpu.make_async_remote_copy(
            src_ref=send_buf.at[slot],
            dst_ref=recv_buf.at[slot, origin],
            send_sem=send_sem.at[slot, peer],
            recv_sem=recv_sem.at[slot, origin],
            device_id={"seq": peer},
            device_id_type=MESH,
        )

    def exchange_start(slot):
        def one(k, carry):
            exchange_copy(slot, lax.rem(me + k, nseq), me).start()
            return carry

        lax.fori_loop(1, nseq, one, 0)

    def exchange_wait(slot):
        def one(k, carry):
            peer = lax.rem(me + k, nseq)
            exchange_copy(slot, peer, me).wait_send()
            exchange_copy(slot, peer, peer).wait_recv()
            return carry

        lax.fori_loop(1, nseq, one, 0)

    sub = lax.broadcasted_iota(jnp.int32, (CHUNKS, p), 0)

    def layer_powers(layer, conj):
        lam_re = tab_ref[layer, 0:1, :]
        lam_im = tab_ref[layer, 1:2, :]
        if conj:
            lam_im = -lam_im
        pw_re, pw_im = lam_re, lam_im
        count = 1
        while count < steps:
            pw_re, pw_im = cmul(pw_re, pw_im, pw_re, pw_im)
            count *= 2
        jumps = [(pw_re, pw_im)]
        for _ in range(3):
            pw_re, pw_im = cmul(pw_re, pw_im, pw_re, pw_im)
            jumps.append((pw_re, pw_im))
        return lam_re, lam_im, jumps

    def jump_table(jumps, index):
        re = jnp.ones((CHUNKS, p), F32)
        im = jnp.zeros((CHUNKS, p), F32)
        for bit in range(3):
            new_re, new_im = cmul(re, im, jumps[bit][0], jumps[bit][1])
            has = (index & (1 << bit)) != 0
            re = jnp.where(has, new_re, re)
            im = jnp.where(has, new_im, im)
        return re, im

    def local_ends(src, first_c, first_a, lam_re, lam_im):
        zero = jnp.zeros((CHUNKS, p), F32)
        l_re = jnp.broadcast_to(lam_re, (CHUNKS, p))
        l_im = jnp.broadcast_to(lam_im, (CHUNKS, p))

        def step(j, carry):
            e_re, e_im, f_re, f_im = carry
            up = pl.ds(pl.multiple_of(j * CHUNKS, CHUNKS), CHUNKS)
            down = pl.ds(pl.multiple_of((steps - 1 - j) * CHUNKS, CHUNKS), CHUNKS)
            e_re, e_im = cmul(l_re, l_im, e_re, e_im)
            f_re, f_im = cmul(l_re, l_im, f_re, f_im)
            return (
                e_re + src[up, first_c : first_c + p],
                e_im + src[up, first_c + p : first_c + 2 * p],
                f_re + src[down, first_a : first_a + p],
                f_im + src[down, first_a + p : first_a + 2 * p],
            )

        return lax.fori_loop(0, steps, step, (zero,) * 4, unroll=4)

    def local_prefix(ends, jumps):
        e_re, e_im, f_re, f_im = ends
        for bit in range(3):
            shift = 1 << bit
            j_re, j_im = jumps[bit]
            s_re = jnp.where(sub >= shift, pltpu.roll(e_re, shift, 0), 0.0)
            s_im = jnp.where(sub >= shift, pltpu.roll(e_im, shift, 0), 0.0)
            a_re, a_im = cmul(j_re, j_im, s_re, s_im)
            e_re, e_im = e_re + a_re, e_im + a_im
            s_re = jnp.where(sub < CHUNKS - shift, pltpu.roll(f_re, CHUNKS - shift, 0), 0.0)
            s_im = jnp.where(sub < CHUNKS - shift, pltpu.roll(f_im, CHUNKS - shift, 0), 0.0)
            a_re, a_im = cmul(j_re, j_im, s_re, s_im)
            f_re, f_im = f_re + a_re, f_im + a_im
        return e_re, e_im, f_re, f_im

    def send_totals(slot, prefix):
        e_re, e_im, f_re, f_im = prefix
        send_buf[slot, 0:1, 0:p] = e_re[CHUNKS - 1 : CHUNKS]
        send_buf[slot, 1:2, 0:p] = e_im[CHUNKS - 1 : CHUNKS]
        send_buf[slot, 2:3, 0:p] = f_re[0:1]
        send_buf[slot, 3:4, 0:p] = f_im[0:1]
        exchange_start(slot)

    def chunk_carries(slot, prefix, jumps):
        e_re, e_im, f_re, f_im = prefix
        d_re, d_im = jumps[3]
        zero = jnp.zeros((1, p), F32)

        def step(k, carry):
            c_re, c_im, a_re, a_im = carry
            n_re, n_im = cmul(d_re, d_im, c_re, c_im)
            use = k < me
            c_re = jnp.where(use, n_re + recv_buf[slot, k, 0:1, 0:p], c_re)
            c_im = jnp.where(use, n_im + recv_buf[slot, k, 1:2, 0:p], c_im)
            back = nseq - 1 - k
            n_re, n_im = cmul(d_re, d_im, a_re, a_im)
            use = back > me
            a_re = jnp.where(use, n_re + recv_buf[slot, back, 2:3, 0:p], a_re)
            a_im = jnp.where(use, n_im + recv_buf[slot, back, 3:4, 0:p], a_im)
            return c_re, c_im, a_re, a_im

        c_re, c_im, a_re, a_im = lax.fori_loop(0, nseq, step, (zero,) * 4)
        t_re, t_im = jump_table(jumps, sub)
        g_re, g_im = cmul(t_re, t_im, c_re, c_im)
        in_c_re = g_re + jnp.where(sub >= 1, pltpu.roll(e_re, 1, 0), 0.0)
        in_c_im = g_im + jnp.where(sub >= 1, pltpu.roll(e_im, 1, 0), 0.0)
        t_re, t_im = jump_table(jumps, CHUNKS - 1 - sub)
        g_re, g_im = cmul(t_re, t_im, a_re, a_im)
        in_a_re = g_re + jnp.where(sub < CHUNKS - 1, pltpu.roll(f_re, CHUNKS - 1, 0), 0.0)
        in_a_im = g_im + jnp.where(sub < CHUNKS - 1, pltpu.roll(f_im, CHUNKS - 1, 0), 0.0)
        return in_c_re, in_c_im, in_a_re, in_a_im

    def half_blocks(half):
        blocks = []
        for first in range(0, half_cols, 128):
            if inside:
                at = (2 * (first // part_cols) + half) * part_cols + first % part_cols
            else:
                at = half * half_cols + first
            if not isinstance(at, int):
                at = pl.multiple_of(at, 128)
            blocks.append((first, pl.ds(at, 128)))
        return blocks

    def put_line(line, row):
        for col in range(0, width, 128):
            at = line * (width // 128) + col // 128
            small_ref[at : at + 1, :] = row[:, col : col + 128]

    part_cols = width // ndp
    rows_dp = width // ndp
    share = p // nseq

    def c_block(layer, half, z, x):
        return c_ref.at[layer, half, :, z, x]

    def own_rows(index):
        return pl.ds(pl.multiple_of(index * rows_dp, 16), rows_dp)

    def cast_c(layer):
        cols = pl.ds(pl.multiple_of(yy * part_cols, 128), part_cols)
        c_ref[layer, core, :, zz, xx, :, cols] = I.c_in[layer].astype(BF16)

    def cast_b(layer):
        b_ref[layer, own_rows(my_dp), :] = I.b_in[layer].astype(BF16)

    def cast_glu(layer):
        glu_ref[layer, own_rows(my_dp), :] = I.glu_in[layer].astype(BF16)

    copies = {}

    def start(name, copy):
        copies[name] = copy
        copy.start()

    def finish(name):
        copies.pop(name).wait()

    def c_stage_y(layer):
        cols = pl.ds(pl.multiple_of(yy * part_cols, 128), part_cols)
        block = c_ref.at[layer, core, :, zz, xx, :, cols]
        start((0, layer), remote(block, block, new_sems(1), y_peer))

    def c_stage_z(layer):
        finish((0, layer))
        block = c_block(layer, core, zz, xx)
        for k in range(1, nz):
            peer = {"seq": 2 * lax.rem(zz + k, nz) + xx}
            start((1, layer, k), remote(block, block, new_sems(1), peer))
        start((2, layer, 0), remote(block, block, new_sems(1), x_peer))

    def c_stage_x(layer):
        for k in range(1, nz):
            finish((1, layer, k))
            block = c_block(layer, core, lax.rem(zz + nz - k, nz), xx)
            start((2, layer, k), remote(block, block, new_sems(1), x_peer))
        block = c_ref.at[layer, core, :, :, xx]
        start((3, layer, 0), remote(block, block, new_sems(1), sibling))

    def c_stage_core(layer):
        for k in range(nz):
            finish((2, layer, k))
        block = c_ref.at[layer, core, :, :, 1 - xx]
        start((3, layer, 1), remote(block, block, new_sems(1), sibling))

    def c_stage_end(layer):
        for part in range(2):
            finish((3, layer, part))

    def row_stage_y(ref, layer):
        block = ref.at[layer, own_rows(my_dp), :]
        start((id(ref), 0, layer), remote(block, block, new_sems(1), y_peer))
        start((id(ref), 1, layer), remote(block, block, new_sems(1), sibling))

    def row_stage_core(ref, layer):
        finish((id(ref), 0, layer))
        block = ref.at[layer, own_rows(2 * (1 - yy) + core), :]
        start((id(ref), 2, layer), remote(block, block, new_sems(1), sibling))

    def row_stage_end(ref, layer):
        finish((id(ref), 1, layer))
        finish((id(ref), 2, layer))

    def table_stage():
        own = I.tab_in
        S.tab_recv[me] = own[...]
        sems = new_sems(nseq)

        def copy(k, origin, peer):
            return remote(own, S.tab_recv.at[origin], sems + k, {"seq": peer})

        seq_loop(lambda k: copy(k, me, lax.rem(me + k, nseq)).start())
        return copy

    def table_end(copy):
        def one(k):
            copy(k, me, lax.rem(me + k, nseq)).wait_send()
            copy(k, lax.rem(me + nseq - k, nseq), me).wait_recv()

        seq_loop(one)
        lane = lax.broadcasted_iota(jnp.int32, (8, 128), 1)
        tiles = [jnp.zeros((8, 128), F32) for _ in range(p // 128)]
        for q in range(nseq):
            tile, first = (q * share) // 128, (q * share) % 128
            piece = S.tab_recv[q]
            if first:
                piece = pltpu.roll(piece, first, 1)
            here = (lane >= first) & (lane < first + share)
            tiles[tile] = jnp.where(here, piece, tiles[tile])
            if first + share > 128:
                tiles[tile + 1] = jnp.where(lane < first + share - 128, piece, tiles[tile + 1])
        for layer in range(layers):
            for tile in range(p // 128):
                tab_ref[layer, 0:4, tile * 128 : tile * 128 + 128] = tiles[tile][
                    4 * layer : 4 * layer + 4
                ]

    if inside:
        cast_c(0)
        cast_b(0)
        pl.semaphore_wait(barrier, greeted)
        c_stage_y(0)
        row_stage_y(b_ref, 0)
        table_copy = table_stage()
        for layer in range(layers):
            if layer:
                cast_c(layer)
                cast_b(layer)
            cast_glu(layer)
    else:
        pl.semaphore_wait(barrier, greeted)

    for col in range(0, width, 128):
        perm[col // 128] = x_ref[:, col : col + 128].astype(F32)

        def place(j, carry, col=col):
            rows = pl.ds(pl.multiple_of(j * CHUNKS, CHUNKS), CHUNKS)
            stream[rows, col : col + 128] = perm[col // 128, pl.ds(j, CHUNKS, stride=steps), :]
            return carry

        lax.fori_loop(0, steps, place, 0, unroll=4)

    for layer in range(layers):
        gain = gain_ref[layer : layer + 1, :]
        bias = bias_ref[layer : layer + 1, :]
        skip = skip_ref[layer : layer + 1, :]

        def norm_rows(rows, first, carry, layer=layer, gain=gain, bias=bias):
            value = stream[rows, :]
            center = value - jnp.mean(value, axis=1, keepdims=True)
            spread = jnp.mean(center * center, axis=1, keepdims=True)
            inv = lax.rsqrt(spread + 1e-05)
            hat = center * inv
            xhat[layer, rows, :] = hat
            rstd[layer, rows, :] = inv
            nlow[layer, rows, :] = (hat * gain + bias).astype(BF16)
            return carry

        row_loop(norm_rows, 0)

        if inside:
            if layer == 0:
                table_end(table_copy)
                c_stage_z(0)
                row_stage_core(b_ref, 0)
                row_stage_y(glu_ref, 0)
            row_stage_end(b_ref, layer)
        in_scale = tab_ref[layer, 2:3, :]
        for col in range(0, 2 * p, 256):
            part = mm_nn(nlow[layer], b_ref[layer, :, col : col + 256])
            for half in range(col, col + 256, 128):
                scale_col = half % p
                drive[layer, :, half : half + 128] = (
                    part[:, half - col : half - col + 128].astype(BF16).astype(F32)
                    * in_scale[:, scale_col : scale_col + 128]
                )

        lam_re, lam_im, jumps = layer_powers(layer, False)
        ends = local_ends(drive.at[layer], 0, 0, lam_re, lam_im)
        prefix = local_prefix(ends, jumps)
        send_totals(layer, prefix)
        if inside and layer == 0:
            for later in range(1, layers):
                c_stage_y(later)
                row_stage_y(b_ref, later)
                row_stage_y(glu_ref, later)
        exchange_wait(layer)
        carries = chunk_carries(layer, prefix, jumps)
        caus[layer, 0:CHUNKS, 0:p] = carries[0]
        caus[layer, 0:CHUNKS, p : 2 * p] = carries[1]
        anti[layer, tok : tok + CHUNKS, 0:p] = carries[2]
        anti[layer, tok : tok + CHUNKS, p : 2 * p] = carries[3]
        l_re = jnp.broadcast_to(lam_re, (CHUNKS, p))
        l_im = jnp.broadcast_to(lam_im, (CHUNKS, p))

        def state_pair(k, carry, layer=layer, l_re=l_re, l_im=l_im):
            s_re, s_im, r_re, r_im = carry
            first = pl.multiple_of(k * 2 * CHUNKS, 2 * CHUNKS)
            kept_re, kept_im = [], []
            for half in range(2):
                rows = pl.ds(first + half * CHUNKS, CHUNKS)
                s_re, s_im = cmul(l_re, l_im, s_re, s_im)
                s_re = s_re + drive[layer, rows, 0:p]
                s_im = s_im + drive[layer, rows, p : 2 * p]
                after = pl.ds(first + (half + 1) * CHUNKS, CHUNKS)
                caus[layer, after, 0:p] = s_re
                caus[layer, after, p : 2 * p] = s_im
                kept_re.append(s_re)
                kept_im.append(s_im)
            both = pl.ds(first, 2 * CHUNKS)
            feat[layer, both, 0:p] = jnp.concatenate(kept_re, axis=0).astype(BF16)
            feat[layer, both, p : 2 * p] = jnp.concatenate(kept_im, axis=0).astype(BF16)
            last = pl.multiple_of(tok - (k + 1) * 2 * CHUNKS, 2 * CHUNKS)
            kept_re, kept_im = [], []
            for half in (1, 0):
                rows = pl.ds(last + half * CHUNKS, CHUNKS)
                r_re, r_im = cmul(l_re, l_im, r_re, r_im)
                r_re = r_re + drive[layer, rows, 0:p]
                r_im = r_im + drive[layer, rows, p : 2 * p]
                anti[layer, rows, 0:p] = r_re
                anti[layer, rows, p : 2 * p] = r_im
                kept_re.insert(0, r_re)
                kept_im.insert(0, r_im)
            both = pl.ds(last, 2 * CHUNKS)
            feat[layer, both, 2 * p : 3 * p] = jnp.concatenate(kept_re, axis=0).astype(BF16)
            feat[layer, both, 3 * p : 4 * p] = jnp.concatenate(kept_im, axis=0).astype(BF16)
            return s_re, s_im, r_re, r_im

        lax.fori_loop(0, steps // 2, state_pair, carries, unroll=2)

        if inside and layer == 0:
            c_stage_x(0)
            row_stage_core(glu_ref, 0)
            for later in range(1, layers):
                c_stage_z(later)
                row_stage_core(b_ref, later)
                row_stage_core(glu_ref, later)
        if inside:
            c_stage_core(layer)
        for turn in range(2):
            half = (1 - own_half) if turn else own_half
            if inside and turn:
                c_stage_end(layer)
            part = mm_nn(feat[layer], c_ref[layer, half].reshape(4 * p, half_cols))
            for first, block in half_blocks(half):
                temp[:, block] = part[:, first : first + 128]

        if inside and layer == 0:
            for later in range(1, layers):
                c_stage_x(later)
        if inside:
            row_stage_end(glu_ref, layer)
        def act_rows(rows, first, carry, layer=layer, gain=gain, bias=bias, skip=skip):
            pre = temp[rows, :] + skip * (xhat[layer, rows, :] * gain + bias)
            square = pre * pre
            th = jnp.tanh(GELU_A * pre * (1.0 + GELU_B * square))
            cdf = 0.5 * (1.0 + th)
            out = pre * cdf
            gelu_out[layer, rows, :] = out
            gelu_low[layer, rows, :] = out.astype(BF16)
            gelu_der[layer, rows, :] = cdf + 0.5 * pre * (1.0 - th * th) * (
                GELU_A * (1.0 + 3.0 * GELU_B * square)
            )
            return carry

        row_loop(act_rows, 0)
        for col in range(0, width, 256):
            temp[:, col : col + 256] = mm_nn(gelu_low[layer], glu_ref[layer, :, col : col + 256])
        glu_bias = glub_ref[layer : layer + 1, :]
        last_layer = layer == layers - 1

        def gate_rows(rows, first, carry, layer=layer, glu_bias=glu_bias, last_layer=last_layer):
            gate = 1.0 / (1.0 + jnp.exp(-(temp[rows, :] + glu_bias)))
            sig[layer, rows, :] = gate
            new = stream[rows, :] + gelu_out[layer, rows, :] * gate
            if not last_layer:
                stream[rows, :] = new
                return carry
            return carry + fold8(new * row_mask(first))

        def row_mask(first):
            row = first + lax.broadcasted_iota(jnp.int32, (TILE, 1), 0)
            position = me * tok + (row & (CHUNKS - 1)) * steps + (row >> 3)
            return jnp.where(position < len_ref[0], 1.0, 0.0).astype(F32)

        pooled_part = row_loop(gate_rows, jnp.zeros((CHUNKS, width), F32) if last_layer else 0)

    pool_slot = 2 * layers
    own_sum = jnp.sum(pooled_part, axis=0, keepdims=True)
    send_buf[pool_slot, 0:1, :] = own_sum
    exchange_start(pool_slot)
    exchange_wait(pool_slot)

    def add_pool(k, total):
        return total + jnp.where(k == me, 0.0, recv_buf[pool_slot, k, 0:1, :])

    pooled_sum = lax.fori_loop(0, nseq, add_pool, own_sum)
    len_row = jnp.full((1, 1), len_ref[0], jnp.int32).astype(F32)
    pooled = pooled_sum / len_row
    logit = [
        jnp.sum(pooled * cw_ref[k : k + 1, :], axis=1, keepdims=True) + cb_ref[k : k + 1, :]
        for k in range(classes)
    ]
    top = logit[0]
    for k in range(1, classes):
        top = jnp.maximum(top, logit[k])
    expo = [jnp.exp(v - top) for v in logit]
    norm = expo[0]
    for k in range(1, classes):
        norm = norm + expo[k]
    hot = [jnp.where(lab_ref[0] == k, 1.0, 0.0).astype(F32) for k in range(classes)]
    cross = top + jnp.log(norm)
    for k in range(classes):
        cross = cross - hot[k] * logit[k]
    lgrad = [len_row * (expo[k] / norm - hot[k]) for k in range(classes)]
    pooled_grad = lgrad[0] * cw_ref[0:1, :]
    for k in range(1, classes):
        pooled_grad = pooled_grad + lgrad[k] * cw_ref[k : k + 1, :]
    grad_row = pooled_grad / len_row
    once = jnp.where(me == 0, 1.0, 0.0).astype(F32)
    small_ref[...] = jnp.zeros(small_ref.shape, F32)
    head_row = 6 * layers
    lane = lax.broadcasted_iota(jnp.int32, (1, width), 1)
    bias_line = jnp.zeros((1, width), F32)
    for k in range(classes):
        put_line(head_row + k, pooled * lgrad[k] * once)
        bias_line = jnp.where(lane == k, lgrad[k] * once, bias_line)
    bias_line = jnp.where(lane == classes, cross * once, bias_line)
    put_line(head_row + classes, bias_line)

    def c_grad_start(layer):
        for half, own in ((1 - core, False), (core, True)):
            for col in range(0, 4 * p, 2 * p):
                value = mm_tn(feat[layer, :, col : col + 2 * p], mlow[half])
                if own:
                    CG.acc[layer, col : col + 2 * p, :] = value
                else:
                    CG.snd1[layer, col : col + 2 * p, :] = value.astype(BF16)
            if not own:
                copy = remote(CG.snd1.at[layer], CG.rcv1.at[layer], new_sems(1), sibling)
                start((4, layer), copy)

    def c_grad_y(layer):
        finish((4, layer))
        acc, rcv = CG.acc.at[layer], CG.rcv1.at[layer]
        away = pl.ds(pl.multiple_of((1 - yy) * part_cols, 128), part_cols)
        keep = pl.ds(pl.multiple_of(yy * part_cols, 128), part_cols)
        cast_rows(CG.snd2.at[layer], acc.at[:, away], 4 * p, 128, rcv.at[:, away])
        copy = remote(CG.snd2.at[layer], CG.rcv2.at[layer], new_sems(1), y_peer)
        start((5, layer), copy)
        cast_rows(CG.acc2.at[layer], acc.at[:, keep], 4 * p, 128, rcv.at[:, keep])

    def c_grad_x(layer):
        finish((5, layer))

        def total(group):
            rows = pl.ds(pl.multiple_of(group * share, 16), share)
            return CG.acc2[layer, rows, :] + CG.rcv2[layer, rows, :].astype(F32)

        def away(k, carry):
            CG.snd3[layer, k] = total(2 * k + 1 - xx).astype(BF16)
            return carry

        def keep(k, carry):
            CG.acc3[layer, k] = total(2 * k + xx)
            return carry

        lax.fori_loop(0, 4 * nz, away, 0)
        copy = remote(CG.snd3.at[layer], CG.rcv3.at[layer], new_sems(1), x_peer)
        start((6, layer), copy)
        lax.fori_loop(0, 4 * nz, keep, 0)

    def c_grad_z(layer):
        finish((6, layer))

        def total(k, carry):
            plane, z = k // nz, lax.rem(k, nz)
            value = CG.acc3[layer, k] + CG.rcv3[layer, k].astype(F32)
            CG.acc3[layer, k] = value
            CG.snd4[layer, z, plane] = value.astype(BF16)
            return carry

        lax.fori_loop(0, 4 * nz, total, 0)
        for k in range(1, nz):
            peer = lax.rem(zz + k, nz)
            copy = remote(
                CG.snd4.at[layer, peer],
                CG.rcv4.at[layer, k],
                new_sems(1),
                {"seq": 2 * peer + xx},
            )
            start((7, layer, k), copy)

    def c_grad_end(layer):
        for k in range(1, nz):
            finish((7, layer, k))
        for plane in range(4):
            value = CG.acc3[layer, plane * nz + zz]
            for k in range(1, nz):
                value = value + CG.rcv4[layer, k, plane].astype(F32)
            O.c_out[layer, plane] = value

    def row_grad_start(G, layer, left, right):
        for y in range(ny):
            block = left[layer, :, own_rows(2 * y + 1 - core)]
            G.snd1[layer, y] = mm_tn(block, right[...]).astype(BF16)
        copy = remote(G.snd1.at[layer], G.rcv1.at[layer], new_sems(1), sibling)
        start((id(G), 0, layer), copy)
        for y in range(ny):
            block = left[layer, :, own_rows(2 * y + core)]
            G.acc[layer, y] = mm_tn(block, right[...])

    def row_grad_y(G, layer):
        finish((id(G), 0, layer))
        acc, rcv = G.acc.at[layer], G.rcv1.at[layer]
        cast_rows(G.snd2.at[layer], acc.at[1 - yy], rows_dp, 32, rcv.at[1 - yy])
        copy = remote(G.snd2.at[layer], G.rcv2.at[layer], new_sems(1), y_peer)
        start((id(G), 1, layer), copy)
        cast_rows(G.acc2.at[layer], acc.at[yy], rows_dp, 32, rcv.at[yy])

    piece = rows_dp // nseq

    def piece_rows(q):
        return pl.ds(pl.multiple_of(q * piece, 16), piece)

    def row_grad_scatter(G, layer):
        finish((id(G), 1, layer))
        acc, snd = G.acc2.at[layer], G.snd3.at[layer]
        cast_rows(acc, acc, rows_dp, 32, G.rcv2.at[layer])
        cast_rows(snd, acc, rows_dp, 32)
        sems = new_sems(nseq)

        def copy(k):
            peer = lax.rem(me + k, nseq)
            return remote(
                snd.at[piece_rows(peer), :],
                G.rcv3.at[layer, k],
                sems + k,
                {"seq": peer},
            )

        copies[(id(G), 2, layer)] = copy
        seq_loop(lambda k: copy(k).start())

    def row_grad_gather(G, layer):
        scattered = copies.pop((id(G), 2, layer))
        seq_loop(lambda k: scattered(k).wait())
        value = G.acc2[layer, piece_rows(me), :]
        for k in range(1, nseq):
            value = value + G.rcv3[layer, k].astype(F32)
        full = G.full.at[layer]
        full[piece_rows(me), :] = value.astype(BF16)
        sems = new_sems(nseq)

        def copy(k, origin, peer):
            block = piece_rows(origin)
            return remote(full.at[block, :], full.at[block, :], sems + k, {"seq": peer})

        copies[(id(G), 3, layer)] = copy
        seq_loop(lambda k: copy(k, me, lax.rem(me + k, nseq)).start())

    def row_grad_end(G, layer):
        copy = copies.pop((id(G), 3, layer))

        def one(k):
            copy(k, me, lax.rem(me + k, nseq)).wait_send()
            copy(k, lax.rem(me + nseq - k, nseq), me).wait_recv()

        seq_loop(one)
        out = O.b_out if G is BG else O.glu_out
        cast_rows(out.at[layer], G.full.at[layer], rows_dp, 32)

    small_rows = small_ref.shape[0]
    small_piece = small_rows // nseq

    def small_start():
        start((8, 0), remote(small_ref, S.small_core, new_sems(1), sibling))

    def small_y():
        finish((8, 0))
        S.small_sum[0] = small_ref[...] + S.small_core[...]
        start((8, 1), remote(S.small_sum.at[0], S.small_y, new_sems(1), y_peer))

    def small_part(q):
        return pl.ds(pl.multiple_of(q * small_piece, 8), small_piece)

    def small_scatter():
        finish((8, 1))
        S.small_sum[1] = S.small_sum[0] + S.small_y[...]
        sems = new_sems(nseq)

        def copy(k):
            peer = lax.rem(me + k, nseq)
            return remote(
                S.small_sum.at[1, small_part(peer), :],
                S.small_recv.at[k],
                sems + k,
                {"seq": peer},
            )

        copies[(8, 2)] = copy
        seq_loop(lambda k: copy(k).start())

    def small_gather():
        scattered = copies.pop((8, 2))
        seq_loop(lambda k: scattered(k).wait())
        value = S.small_sum[1, small_part(me), :]
        for k in range(1, nseq):
            value = value + S.small_recv[k]
        full = S.small_sum.at[2]
        full[small_part(me), :] = value
        sems = new_sems(nseq)

        def copy(k, origin, peer):
            block = full.at[small_part(origin), :]
            return remote(block, block, sems + k, {"seq": peer})

        copies[(8, 3)] = copy
        seq_loop(lambda k: copy(k, me, lax.rem(me + k, nseq)).start())

    def small_end():
        copy = copies.pop((8, 3))

        def one(k):
            copy(k, me, lax.rem(me + k, nseq)).wait_send()
            copy(k, lax.rem(me + nseq - k, nseq), me).wait_recv()

        seq_loop(one)
        O.small_out[...] = S.small_sum[2]

    grad = stream

    def first_grad(rows, first, carry):
        grad[rows, :] = row_mask(first) * grad_row
        return carry

    row_loop(first_grad, 0)

    for layer in reversed(range(layers)):
        gain = gain_ref[layer : layer + 1, :]
        bias = bias_ref[layer : layer + 1, :]
        skip = skip_ref[layer : layer + 1, :]
        zero_sum = jnp.zeros((CHUNKS, width), F32)

        def gate_back(rows, first, total, layer=layer):
            gate = sig[layer, rows, :]
            low = (grad[rows, :] * gelu_out[layer, rows, :] * gate * (1.0 - gate)).astype(BF16)
            ggrad[rows, :] = low
            return total + fold8(low.astype(F32))

        total = row_loop(gate_back, zero_sum)
        put_line(3 * layers + layer, jnp.sum(total, axis=0, keepdims=True))
        for col in range(0, width, 256):
            temp[:, col : col + 256] = mm_nt(ggrad[...], glu_ref[layer, col : col + 256, :])

        def mix_back(rows, first, total, layer=layer, gain=gain, bias=bias):
            act = grad[rows, :] * sig[layer, rows, :] + temp[rows, :]
            value = act * gelu_der[layer, rows, :]
            mix[rows, :] = value
            for h in range(2):
                for first, block in half_blocks(h):
                    at = block.start
                    mlow[h, rows, first : first + 128] = value[:, at : at + 128].astype(BF16)
            return total + fold8(value * (xhat[layer, rows, :] * gain + bias))

        total = row_loop(mix_back, zero_sum)
        put_line(2 * layers + layer, jnp.sum(total, axis=0, keepdims=True))
        if inside and layer < layers - 1:
            c_grad_z(layer + 1)
            row_grad_scatter(BG, layer + 1)
            row_grad_gather(GG, layer + 1)
        for plane in range(0, 4, 2):
            rows = [c_ref[layer, h, plane : plane + 2].reshape(2 * p, half_cols) for h in range(2)]
            wide[:, plane * p : (plane + 2) * p] = mm_nt(mlow[0], rows[0]) + mm_nt(mlow[1], rows[1])

        lam_re, lam_im, jumps = layer_powers(layer, True)
        ends = local_ends(wide, 2 * p, 0, lam_re, lam_im)
        prefix = local_prefix(ends, jumps)
        slot = layers + layer
        send_totals(slot, prefix)
        if inside:
            c_grad_start(layer)
            row_grad_start(GG, layer, gelu_low, ggrad)
        else:
            for h in range(2):
                for col in range(0, 4 * p, 2 * p):
                    O.c_out[layer, col : col + 2 * p, h * half_cols : (h + 1) * half_cols] = mm_tn(
                        feat[layer, :, col : col + 2 * p], mlow[h]
                    ).astype(BF16)
            for col in range(0, width, 256):
                O.glu_out[layer, col : col + 256, :] = mm_tn(
                    gelu_low[layer, :, col : col + 256], ggrad[...]
                ).astype(BF16)
        exchange_wait(slot)
        carries = chunk_carries(slot, prefix, jumps)
        l_re = jnp.broadcast_to(lam_re, (CHUNKS, p))
        l_im = jnp.broadcast_to(lam_im, (CHUNKS, p))
        zero = jnp.zeros((CHUNKS, p), F32)

        def anti_grad(j, carry, layer=layer, l_re=l_re, l_im=l_im):
            r_re, r_im, d_re, d_im = carry
            rows = pl.ds(pl.multiple_of(j * CHUNKS, CHUNKS), CHUNKS)
            after = pl.ds(pl.multiple_of((j + 1) * CHUNKS, CHUNKS), CHUNKS)
            r_re, r_im = cmul(l_re, l_im, r_re, r_im)
            r_re = r_re + wide[rows, 2 * p : 3 * p]
            r_im = r_im + wide[rows, 3 * p : 4 * p]
            wide[rows, 2 * p : 3 * p] = r_re
            wide[rows, 3 * p : 4 * p] = r_im
            q_re = anti[layer, after, 0:p]
            q_im = anti[layer, after, p : 2 * p]
            return r_re, r_im, d_re + (r_re * q_re + r_im * q_im), d_im + (r_im * q_re - r_re * q_im)

        _, _, d_re, d_im = lax.fori_loop(
            0, steps, anti_grad, (carries[0], carries[1], zero, zero), unroll=4
        )
        in_scale = jnp.broadcast_to(tab_ref[layer, 2:3, :], (CHUNKS, p))

        def caus_grad(k, carry, layer=layer, l_re=l_re, l_im=l_im, in_scale=in_scale):
            a_re, a_im, d_re, d_im, s_sum = carry
            last = pl.multiple_of(tok - (k + 1) * 2 * CHUNKS, 2 * CHUNKS)
            kept_re, kept_im = [], []
            for half in (1, 0):
                rows = pl.ds(last + half * CHUNKS, CHUNKS)
                a_re, a_im = cmul(l_re, l_im, a_re, a_im)
                a_re = a_re + wide[rows, 0:p]
                a_im = a_im + wide[rows, p : 2 * p]
                q_re = caus[layer, rows, 0:p]
                q_im = caus[layer, rows, p : 2 * p]
                d_re = d_re + (a_re * q_re + a_im * q_im)
                d_im = d_im + (a_im * q_re - a_re * q_im)
                t_re = a_re + wide[rows, 2 * p : 3 * p]
                t_im = a_im + wide[rows, 3 * p : 4 * p]
                s_sum = s_sum + (
                    t_re * drive[layer, rows, 0:p] + t_im * drive[layer, rows, p : 2 * p]
                )
                kept_re.insert(0, t_re * in_scale)
                kept_im.insert(0, t_im * in_scale)
            both = pl.ds(last, 2 * CHUNKS)
            dlow[both, 0:p] = jnp.concatenate(kept_re, axis=0).astype(BF16)
            dlow[both, p : 2 * p] = jnp.concatenate(kept_im, axis=0).astype(BF16)
            return a_re, a_im, d_re, d_im, s_sum

        _, _, d_re, d_im, s_sum = lax.fori_loop(
            0, steps // 2, caus_grad, (carries[2], carries[3], d_re, d_im, zero), unroll=2
        )
        d_re = jnp.sum(d_re, axis=0, keepdims=True)
        d_im = jnp.sum(d_im, axis=0, keepdims=True)
        s_sum = jnp.sum(s_sum, axis=0, keepdims=True) / tab_ref[layer, 2:3, :]
        true_re = tab_ref[layer, 0:1, :]
        true_im = tab_ref[layer, 1:2, :]
        pad = jnp.zeros((1, width - p), F32)
        rate_part = s_sum * tab_ref[layer, 3:4, :] - d_re * true_re - d_im * true_im
        put_line(4 * layers + layer, jnp.concatenate([rate_part, pad], axis=1))
        phase_part = d_im * true_re - d_re * true_im
        put_line(5 * layers + layer, jnp.concatenate([phase_part, pad], axis=1))

        if inside and layer < layers - 1:
            c_grad_end(layer + 1)
            row_grad_gather(BG, layer + 1)
            row_grad_end(GG, layer + 1)
        if inside:
            row_grad_start(BG, layer, nlow, dlow)
            c_grad_y(layer)
            row_grad_y(GG, layer)
        else:
            for col in range(0, width, 256):
                O.b_out[layer, col : col + 256, :] = mm_tn(
                    nlow[layer, :, col : col + 256], dlow[...]
                ).astype(BF16)
        for col in range(0, width, 256):
            temp[:, col : col + 256] = mm_nt(dlow[...], b_ref[layer, col : col + 256, :])

        def norm_back(rows, first, carry, layer=layer, gain=gain, skip=skip):
            gain_sum, bias_sum = carry
            ngrad = mix[rows, :] * skip + temp[rows, :]
            hat = xhat[layer, rows, :]
            q = ngrad * gain
            mean_q = jnp.mean(q, axis=1, keepdims=True)
            mean_x = jnp.mean(q * hat, axis=1, keepdims=True)
            grad[rows, :] = grad[rows, :] + (q - mean_q - hat * mean_x) * rstd[layer, rows, :]
            return gain_sum + fold8(ngrad * hat), bias_sum + fold8(ngrad)

        gain_sum, bias_sum = row_loop(norm_back, (zero_sum, zero_sum))
        put_line(layer, jnp.sum(gain_sum, axis=0, keepdims=True))
        put_line(layers + layer, jnp.sum(bias_sum, axis=0, keepdims=True))
        if inside:
            row_grad_y(BG, layer)
            c_grad_x(layer)
            row_grad_scatter(GG, layer)

    if inside:
        small_start()
    for col in range(0, width, 128):
        perm[col // 128] = grad[:, col : col + 128]

        def unplace(k, carry, col=col):
            first = k * CHUNKS
            chunk = first // steps
            rows = pl.ds((first - chunk * steps) * CHUNKS + chunk, CHUNKS, stride=CHUNKS)
            out = pl.ds(pl.multiple_of(first, CHUNKS), CHUNKS)
            gin_ref[out, col : col + 128] = perm[col // 128, rows, :]
            return carry

        lax.fori_loop(0, steps, unplace, 0, unroll=4)

    if inside:
        if layers > 1:
            row_grad_end(BG, 1)
        small_y()
        c_grad_z(0)
        row_grad_scatter(BG, 0)
        row_grad_gather(GG, 0)
        small_scatter()
        c_grad_end(0)
        row_grad_gather(BG, 0)
        small_gather()
        row_grad_end(GG, 0)
        row_grad_end(BG, 0)
        small_end()


def run_model(dims, inside, operands):
    layers, tok, width, states, classes, ndp, nseq = dims
    vmem = pl.BlockSpec(memory_space=pltpu.VMEM)
    smem = pl.BlockSpec(memory_space=pltpu.SMEM)
    lines = -(-(6 * layers + classes + 1) // 8) * 8
    small_shape = (lines * width // 128, 128)
    slots = 2 * layers + 1
    share, rows_dp = states // nseq, width // ndp
    per_layer = lambda cols, kind, rows=tok: pltpu.VMEM((layers, rows, cols), kind)
    if inside:
        b_shape, g_shape = (layers, rows_dp, 2 * states), (layers, rows_dp, width)
        c_shape, kind = (layers, 4, share, width // ndp), F32
    else:
        b_shape, g_shape = (layers, width, 2 * states), (layers, width, width)
        c_shape, kind = (layers, 4 * states, width), BF16
    scratch = [
        pltpu.VMEM((tok, width), F32),
        per_layer(width, F32),
        per_layer(1, F32),
        per_layer(width, BF16),
        per_layer(2 * states, F32),
        per_layer(2 * states, F32, tok + CHUNKS),
        per_layer(2 * states, F32, tok + CHUNKS),
        per_layer(4 * states, BF16),
        per_layer(width, F32),
        per_layer(width, BF16),
        per_layer(width, F32),
        per_layer(width, F32),
        pltpu.VMEM((tok, 4 * states), F32),
        pltpu.VMEM((tok, width), F32),
        pltpu.VMEM((tok, width), F32),
        pltpu.VMEM((2, tok, width // 2), BF16),
        pltpu.VMEM((tok, width), BF16),
        pltpu.VMEM((tok, 2 * states), BF16),
        pltpu.VMEM((width // 128, tok, 128), F32),
        pltpu.VMEM((slots, 8, width), F32),
        pltpu.VMEM((slots, nseq, 8, width), F32),
        pltpu.SemaphoreType.DMA((slots, nseq)),
        pltpu.SemaphoreType.DMA((slots, nseq)),
    ]
    if inside:
        ny, nz, part, half = ndp // 2, nseq // 2, width // ndp, width // 2
        copies = 64 + layers * (24 + 4 * nseq + 2 * nz) + 4 * nseq
        scratch += [
            pltpu.VMEM((layers, 8, states), F32),
            pltpu.VMEM((nseq, 8, 128), F32),
            per_layer(2 * states, BF16, width),
            per_layer(width, BF16, width),
            pltpu.VMEM((layers, 2, 4, nz, 2, share, half), BF16),
            pltpu.SemaphoreType.DMA((copies,)),
            pltpu.SemaphoreType.DMA((copies,)),
            pltpu.VMEM(small_shape, F32),
            pltpu.VMEM(small_shape, F32),
            pltpu.VMEM(small_shape, F32),
            pltpu.VMEM((3,) + small_shape, F32),
            pltpu.VMEM((nseq, small_shape[0] // nseq, 128), F32),
        ]
        for cols in (2 * states, width):
            scratch += [
                pltpu.VMEM((layers, ny, rows_dp, cols), BF16),
                pltpu.VMEM((layers, ny, rows_dp, cols), BF16),
                pltpu.VMEM((layers, ny, rows_dp, cols), F32),
                per_layer(cols, BF16, rows_dp),
                per_layer(cols, BF16, rows_dp),
                per_layer(cols, F32, rows_dp),
                per_layer(cols, BF16, rows_dp),
                pltpu.VMEM((layers, nseq, rows_dp // nseq, cols), BF16),
                per_layer(cols, BF16, rows_dp),
            ]
        scratch += [
            per_layer(half, BF16, 4 * states),
            per_layer(half, BF16, 4 * states),
            per_layer(half, F32, 4 * states),
            per_layer(part, BF16, 4 * states),
            per_layer(part, BF16, 4 * states),
            per_layer(part, F32, 4 * states),
            pltpu.VMEM((layers, 4 * nz, share, part), BF16),
            pltpu.VMEM((layers, 4 * nz, share, part), BF16),
            pltpu.VMEM((layers, 4 * nz, share, part), F32),
            pltpu.VMEM((layers, nz, 4, share, part), BF16),
            pltpu.VMEM((layers, nz, 4, share, part), BF16),
        ]
    return pl.pallas_call(
        partial(model_kernel, dims, inside),
        out_shape=(
            jax.ShapeDtypeStruct((tok, width), F32),
            jax.ShapeDtypeStruct(small_shape, F32),
            jax.ShapeDtypeStruct(b_shape, kind),
            jax.ShapeDtypeStruct(g_shape, kind),
            jax.ShapeDtypeStruct(c_shape, kind),
        ),
        in_specs=[smem, smem] + [vmem] * 11,
        out_specs=[vmem] * 5,
        scratch_shapes=scratch,
        compiler_params=pltpu.CompilerParams(
            collective_id=0, has_side_effects=True, vmem_limit_bytes=60 * 1024 * 1024
        ),
        cost_estimate=pl.CostEstimate(
            flops=6 * layers * tok * width * (6 * states + width),
            bytes_accessed=16 * 1024 * 1024,
            transcendentals=2 * layers * tok * width,
        ),
    )(*operands)


def per_device(
    inputs,
    lengths,
    labels,
    norm_gain,
    norm_bias,
    b_proj,
    rate,
    phase,
    c_proj,
    skip,
    glu_weight,
    glu_bias,
    class_weight,
    class_bias,
):
    layers, width = norm_gain.shape
    tok = inputs.shape[1]
    ndp = lax.axis_size("dp")
    nseq = lax.axis_size("seq")
    states = c_proj.shape[2] * nseq
    classes = class_bias.shape[0]
    dims = (layers, tok, width, states, classes, ndp, nseq)
    share = states // nseq
    inside = (
        ndp == 4
        and nseq % 2 == 0
        and share % 16 == 0
        and (width // ndp) % 128 == 0
        and (width // ndp) % (16 * nseq) == 0
        and 4 * layers == 8
    )
    decay = jnp.exp(-rate)
    in_scale = jnp.sqrt(-jnp.expm1(-2.0 * rate))
    rows = [
        decay * jnp.cos(phase),
        decay * jnp.sin(phase),
        in_scale,
        jnp.exp(-2.0 * rate) / in_scale,
    ]
    table = jnp.stack(rows, axis=1)
    if inside:
        table = jnp.pad(table.reshape(4 * layers, share), ((0, 0), (0, 128 - share)))
        weights = (b_proj, glu_weight, c_proj)
    else:
        table = lax.all_gather(table, "seq", axis=2, tiled=True)
        b_full = lax.all_gather(b_proj.astype(BF16), "dp", axis=1, tiled=True)
        g_full = lax.all_gather(glu_weight.astype(BF16), "dp", axis=1, tiled=True)
        c_half = lax.all_gather(c_proj.astype(BF16), "dp", axis=3, tiled=True)
        c_full = lax.all_gather(c_half, "seq", axis=2, tiled=True)
        c_full = c_full.reshape(layers, 4, states, 2, width // 2)
        c_full = jnp.moveaxis(c_full, 3, 1)
        weights = (b_full, g_full, c_full)
    grad_inputs, small, b_grad, g_grad, c_grad = run_model(
        dims,
        inside,
        (
            lengths,
            labels,
            inputs[0],
            norm_gain,
            norm_bias,
            skip,
            glu_bias,
            table,
            class_weight.T,
            class_bias[:, None],
        )
        + weights,
    )
    if inside:
        b_share, g_share, c_share = b_grad, g_grad, c_grad
    else:
        b_share = lax.psum_scatter(b_grad, "dp", scatter_dimension=1, tiled=True)
        g_share = lax.psum_scatter(g_grad, "dp", scatter_dimension=1, tiled=True)
        b_share = lax.psum(b_share, "seq").astype(F32)
        g_share = lax.psum(g_share, "seq").astype(F32)
        c_grad = c_grad.reshape(layers, 4, states, width)
        c_share = lax.psum_scatter(c_grad, "seq", scatter_dimension=2, tiled=True)
        c_share = lax.psum_scatter(c_share, "dp", scatter_dimension=3, tiled=True).astype(F32)
        small = lax.psum(small, ("dp", "seq"))
    small = small.reshape(-1, width)
    own = lax.axis_index("seq") * (states // nseq)

    def state_rows(first):
        return lax.dynamic_slice(small[first : first + layers], (0, own), (layers, states // nseq))

    head = 6 * layers
    return (
        small[head + classes, classes] / ndp,
        grad_inputs[None],
        small[0:layers],
        small[layers : 2 * layers],
        b_share,
        state_rows(4 * layers),
        state_rows(5 * layers),
        c_share,
        small[2 * layers : 3 * layers],
        g_share,
        small[3 * layers : 4 * layers],
        small[head : head + classes].T,
        small[head + classes, 0:classes],
    )


def solution(mesh):
    return jax.shard_map(
        per_device,
        mesh=mesh,
        in_specs=(
            P("dp", "seq", None),
            P("dp"),
            P("dp"),
            P(),
            P(),
            P(None, "dp", None),
            P(None, "seq"),
            P(None, "seq"),
            P(None, None, "seq", "dp"),
            P(),
            P(None, "dp", None),
            P(),
            P(),
            P(),
        ),
        out_specs=(
            P(),
            P("dp", "seq", None),
            P(),
            P(),
            P(None, "dp", None),
            P(None, "seq"),
            P(None, "seq"),
            P(None, None, "seq", "dp"),
            P(),
            P(None, "dp", None),
            P(),
            P(),
            P(),
        ),
        check_vma=False,
    )
```

```python
from functools import partial
from typing import Any, NamedTuple

import jax
import jax.numpy as jnp
from jax import lax
from jax.experimental import pallas as pl
from jax.experimental.pallas import tpu as pltpu
from jax.sharding import PartitionSpec as P

MESH = pl.DeviceIdType.MESH
F32 = jnp.float32
BF16 = jnp.bfloat16
CHUNKS = 8
TILE = 32
GELU_A = 0.7978845608028654
GELU_B = 0.044715


def mm_nn(left, right):
    return lax.dot_general(left, right, (((1,), (0,)), ((), ())), preferred_element_type=F32)


def mm_nt(left, right):
    return lax.dot_general(left, right, (((1,), (1,)), ((), ())), preferred_element_type=F32)


def mm_tn(left, right):
    return lax.dot_general(left, right, (((0,), (0,)), ((), ())), preferred_element_type=F32)


def cmul(a_re, a_im, b_re, b_im):
    return a_re * b_re - a_im * b_im, a_re * b_im + a_im * b_re


def fold8(value):
    total = value[0:8]
    for first in range(8, value.shape[0], 8):
        total = total + value[first : first + 8]
    return total


class Operands(NamedTuple):
    len: Any
    lab: Any
    x: Any
    gain: Any
    bias: Any
    skip: Any
    glub: Any
    tab_in: Any
    cw: Any
    cb: Any
    b_in: Any
    glu_in: Any
    c_in: Any


class Results(NamedTuple):
    gin: Any
    small_out: Any
    b_out: Any
    glu_out: Any
    c_out: Any


class Local(NamedTuple):
    stream: Any
    xhat: Any
    rstd: Any
    nlow: Any
    drive: Any
    caus: Any
    anti: Any
    feat: Any
    gelu_out: Any
    gelu_low: Any
    gelu_der: Any
    sig: Any
    wide: Any
    temp: Any
    mix: Any
    mlow: Any
    ggrad: Any
    dlow: Any
    perm: Any
    send_buf: Any
    recv_buf: Any
    send_sem: Any
    recv_sem: Any


class Shared(NamedTuple):
    tab: Any
    tab_recv: Any
    b_buf: Any
    glu_buf: Any
    c_buf: Any
    ssem: Any
    rsem: Any
    small: Any
    small_core: Any
    small_y: Any
    small_sum: Any
    small_recv: Any


class RowGrad(NamedTuple):
    snd1: Any
    rcv1: Any
    acc: Any
    snd2: Any
    rcv2: Any
    acc2: Any
    snd3: Any
    rcv3: Any
    acc3: Any
    snd4: Any
    rcv4: Any
    full: Any


class ColGrad(NamedTuple):
    snd1: Any
    rcv1: Any
    acc: Any
    snd2a: Any
    rcv2a: Any
    acc2a: Any
    snd2b: Any
    rcv2b: Any
    acc2b: Any
    snd3: Any
    rcv3: Any
    acc3: Any
    snd4: Any
    rcv4: Any


def take(refs, kind):
    count = len(kind._fields)
    return kind(*refs[:count]), refs[count:]


def model_kernel(dims, inside, *refs):
    layers, tok, width, states, classes, ndp, nseq = dims
    I, refs = take(refs, Operands)
    O, refs = take(refs, Results)
    L, refs = take(refs, Local)
    if inside:
        S, refs = take(refs, Shared)
        BG, refs = take(refs, RowGrad)
        GG, refs = take(refs, RowGrad)
        CG, refs = take(refs, ColGrad)
        tab_ref, b_ref, glu_ref, c_ref, small_ref = S.tab, S.b_buf, S.glu_buf, S.c_buf, S.small
    else:
        tab_ref, b_ref, glu_ref, c_ref, small_ref = I.tab_in, I.b_in, I.glu_in, I.c_in, O.small_out
    len_ref, lab_ref, x_ref = I.len, I.lab, I.x
    gain_ref, bias_ref, skip_ref, glub_ref = I.gain, I.bias, I.skip, I.glub
    cw_ref, cb_ref, gin_ref = I.cw, I.cb, O.gin
    stream, xhat, rstd, nlow, drive = L.stream, L.xhat, L.rstd, L.nlow, L.drive
    caus, anti, feat, gelu_out, gelu_low = L.caus, L.anti, L.feat, L.gelu_out, L.gelu_low
    gelu_der, sig, wide, temp, mix = L.gelu_der, L.sig, L.wide, L.temp, L.mix
    mlow, ggrad, dlow, perm = L.mlow, L.ggrad, L.dlow, L.perm
    send_buf, recv_buf = L.send_buf, L.recv_buf
    send_sem, recv_sem = L.send_sem, L.recv_sem
    steps = tok // CHUNKS
    half_cols = width // 2
    me = lax.axis_index("seq")
    my_dp = lax.axis_index("dp")
    p = states
    core, yy = lax.rem(my_dp, 2), my_dp // 2
    xx, zz = lax.rem(me, 2), me // 2
    ny, nz = ndp // 2, nseq // 2
    own_half = core if inside else 0

    barrier = pltpu.get_barrier_semaphore()

    def greet(k, carry):
        peer = lax.rem(me + k, nseq)
        pl.semaphore_signal(barrier, inc=1, device_id={"seq": peer}, device_id_type=MESH)
        return carry

    lax.fori_loop(1, nseq, greet, 0)
    greeted = nseq - 1
    sibling = {"dp": 2 * yy + 1 - core}
    y_peer = {"dp": 2 * (1 - yy) + core}
    x_peer = {"seq": 2 * zz + 1 - xx}
    if inside:
        for peer in (sibling, y_peer):
            pl.semaphore_signal(barrier, inc=1, device_id=peer, device_id_type=MESH)
        greeted += 2

    used = [0]

    def new_sems(count):
        first = used[0]
        used[0] += count
        return first

    def remote(src, dst, sem, peer):
        return pltpu.make_async_remote_copy(
            src_ref=src,
            dst_ref=dst,
            send_sem=S.ssem.at[sem],
            recv_sem=S.rsem.at[sem],
            device_id=peer,
            device_id_type=MESH,
        )

    def seq_loop(body):
        def one(k, carry):
            body(k)
            return carry

        lax.fori_loop(1, nseq, one, 0)

    def cast_rows(dst, src, rows, step, extra=None):
        def one(k, carry):
            part = pl.ds(pl.multiple_of(k * step, step), step)
            value = src[part, :].astype(F32)
            if extra is not None:
                value = value + extra[part, :].astype(F32)
            dst[part, :] = value.astype(dst.dtype)
            return carry

        lax.fori_loop(0, rows // step, one, 0)

    def row_loop(body, init, unroll=1):
        def step(k, carry):
            rows = pl.ds(pl.multiple_of(k * TILE, TILE), TILE)
            return body(rows, k * TILE, carry)

        return lax.fori_loop(0, tok // TILE, step, init, unroll=unroll)

    def exchange_start(slot):
        def one(k, carry):
            pltpu.make_async_remote_copy(
                src_ref=send_buf.at[slot],
                dst_ref=recv_buf.at[slot, k],
                send_sem=send_sem.at[slot],
                recv_sem=recv_sem.at[slot],
                device_id={"seq": lax.rem(me + k, nseq)},
                device_id_type=MESH,
            ).start()
            return carry

        lax.fori_loop(1, nseq, one, 0)

    def exchange_wait(slot):
        arrived = recv_buf.at[slot, pl.ds(1, nseq - 1)]
        pltpu.make_async_remote_copy(
            src_ref=arrived,
            dst_ref=arrived,
            send_sem=send_sem.at[slot],
            recv_sem=recv_sem.at[slot],
            device_id={"seq": lax.rem(me + 1, nseq)},
            device_id_type=MESH,
        ).wait()

    def from_rank(q):
        return lax.rem(me - q + nseq, nseq)

    sub = lax.broadcasted_iota(jnp.int32, (CHUNKS, p), 0)

    def layer_powers(layer, conj):
        lam_re = tab_ref[layer, 0:1, :]
        lam_im = tab_ref[layer, 1:2, :]
        if conj:
            lam_im = -lam_im
        pw_re, pw_im = lam_re, lam_im
        count = 1
        while count < steps:
            pw_re, pw_im = cmul(pw_re, pw_im, pw_re, pw_im)
            count *= 2
        jumps = [(pw_re, pw_im)]
        for _ in range(3):
            pw_re, pw_im = cmul(pw_re, pw_im, pw_re, pw_im)
            jumps.append((pw_re, pw_im))
        return lam_re, lam_im, jumps

    def jump_table(jumps, index):
        re = jnp.ones((CHUNKS, p), F32)
        im = jnp.zeros((CHUNKS, p), F32)
        for bit in range(3):
            new_re, new_im = cmul(re, im, jumps[bit][0], jumps[bit][1])
            has = (index & (1 << bit)) != 0
            re = jnp.where(has, new_re, re)
            im = jnp.where(has, new_im, im)
        return re, im

    def local_ends(src, first_c, first_a, lam_re, lam_im):
        zero = jnp.zeros((CHUNKS, p), F32)
        l_re = jnp.broadcast_to(lam_re, (CHUNKS, p))
        l_im = jnp.broadcast_to(lam_im, (CHUNKS, p))

        def step(j, carry):
            e_re, e_im, f_re, f_im = carry
            up = pl.ds(pl.multiple_of(j * CHUNKS, CHUNKS), CHUNKS)
            down = pl.ds(pl.multiple_of((steps - 1 - j) * CHUNKS, CHUNKS), CHUNKS)
            e_re, e_im = cmul(l_re, l_im, e_re, e_im)
            f_re, f_im = cmul(l_re, l_im, f_re, f_im)
            return (
                e_re + src[up, first_c : first_c + p],
                e_im + src[up, first_c + p : first_c + 2 * p],
                f_re + src[down, first_a : first_a + p],
                f_im + src[down, first_a + p : first_a + 2 * p],
            )

        return lax.fori_loop(0, steps, step, (zero,) * 4, unroll=4)

    def local_prefix(ends, jumps):
        e_re, e_im, f_re, f_im = ends
        for bit in range(3):
            shift = 1 << bit
            j_re, j_im = jumps[bit]
            s_re = jnp.where(sub >= shift, pltpu.roll(e_re, shift, 0), 0.0)
            s_im = jnp.where(sub >= shift, pltpu.roll(e_im, shift, 0), 0.0)
            a_re, a_im = cmul(j_re, j_im, s_re, s_im)
            e_re, e_im = e_re + a_re, e_im + a_im
            s_re = jnp.where(sub < CHUNKS - shift, pltpu.roll(f_re, CHUNKS - shift, 0), 0.0)
            s_im = jnp.where(sub < CHUNKS - shift, pltpu.roll(f_im, CHUNKS - shift, 0), 0.0)
            a_re, a_im = cmul(j_re, j_im, s_re, s_im)
            f_re, f_im = f_re + a_re, f_im + a_im
        return e_re, e_im, f_re, f_im

    def send_totals(slot, prefix):
        e_re, e_im, f_re, f_im = prefix
        send_buf[slot, 0:1, 0:p] = e_re[CHUNKS - 1 : CHUNKS]
        send_buf[slot, 1:2, 0:p] = e_im[CHUNKS - 1 : CHUNKS]
        send_buf[slot, 2:3, 0:p] = f_re[0:1]
        send_buf[slot, 3:4, 0:p] = f_im[0:1]
        exchange_start(slot)

    def chunk_carries(slot, prefix, jumps):
        e_re, e_im, f_re, f_im = prefix
        d_re, d_im = jumps[3]
        zero = jnp.zeros((1, p), F32)

        def step(k, carry):
            c_re, c_im, a_re, a_im = carry
            n_re, n_im = cmul(d_re, d_im, c_re, c_im)
            use = k < me
            c_re = jnp.where(use, n_re + recv_buf[slot, from_rank(k), 0:1, 0:p], c_re)
            c_im = jnp.where(use, n_im + recv_buf[slot, from_rank(k), 1:2, 0:p], c_im)
            back = nseq - 1 - k
            n_re, n_im = cmul(d_re, d_im, a_re, a_im)
            use = back > me
            a_re = jnp.where(use, n_re + recv_buf[slot, from_rank(back), 2:3, 0:p], a_re)
            a_im = jnp.where(use, n_im + recv_buf[slot, from_rank(back), 3:4, 0:p], a_im)
            return c_re, c_im, a_re, a_im

        c_re, c_im, a_re, a_im = lax.fori_loop(0, nseq, step, (zero,) * 4)
        t_re, t_im = jump_table(jumps, sub)
        g_re, g_im = cmul(t_re, t_im, c_re, c_im)
        in_c_re = g_re + jnp.where(sub >= 1, pltpu.roll(e_re, 1, 0), 0.0)
        in_c_im = g_im + jnp.where(sub >= 1, pltpu.roll(e_im, 1, 0), 0.0)
        t_re, t_im = jump_table(jumps, CHUNKS - 1 - sub)
        g_re, g_im = cmul(t_re, t_im, a_re, a_im)
        in_a_re = g_re + jnp.where(sub < CHUNKS - 1, pltpu.roll(f_re, CHUNKS - 1, 0), 0.0)
        in_a_im = g_im + jnp.where(sub < CHUNKS - 1, pltpu.roll(f_im, CHUNKS - 1, 0), 0.0)
        return in_c_re, in_c_im, in_a_re, in_a_im

    def half_blocks(half):
        blocks = []
        for first in range(0, half_cols, 128):
            if inside:
                at = (2 * (first // part_cols) + half) * part_cols + first % part_cols
            else:
                at = half * half_cols + first
            if not isinstance(at, int):
                at = pl.multiple_of(at, 128)
            blocks.append((first, pl.ds(at, 128)))
        return blocks

    def put_line(line, row):
        for col in range(0, width, 128):
            at = line * (width // 128) + col // 128
            small_ref[at : at + 1, :] = row[:, col : col + 128]

    part_cols = width // ndp
    rows_dp = width // ndp
    share = p // nseq

    def own_rows(index):
        return pl.ds(pl.multiple_of(index * rows_dp, 16), rows_dp)

    def cast_c(layer):
        cols = pl.ds(pl.multiple_of(yy * part_cols, 128), part_cols)
        c_ref[layer, core, :, zz, xx, :, cols] = I.c_in[layer].astype(BF16)

    def cast_b(layer):
        b_ref[layer, own_rows(my_dp), :] = I.b_in[layer].astype(BF16)

    def cast_glu(layer):
        glu_ref[layer, own_rows(my_dp), :] = I.glu_in[layer].astype(BF16)

    copies, sem_of = {}, {}

    def start(name, copy):
        copies[name] = copy
        copy.start()

    def finish(name):
        copies.pop(name).wait()

    def y_cols(y):
        return pl.ds(pl.multiple_of(y * part_cols, 128), part_cols)

    def start_all(name, total, pairs):
        if name not in copies:
            sem_of[name] = new_sems(1)
            copies[name] = remote(total, total, sem_of[name], x_peer)
        for block, peer in pairs:
            remote(block, block, sem_of[name], peer).start()

    def z_peers():
        return [{"seq": 2 * lax.rem(zz + k, nz) + xx} for k in range(1, nz)]

    def c_piece(layer, z, x, y):
        return c_ref.at[layer, core, :, z, x, :, y_cols(y)]

    def c_spread(layer, y):
        block = c_piece(layer, zz, xx, y)
        total = c_ref.at[layer, core, :, pl.ds(0, nz - 1), xx, :, y_cols(y)]
        own = y is yy
        start_all((1 if own else 2, layer), total, [(block, peer) for peer in z_peers()])
        start_all((3, layer), c_ref.at[layer, core, :, :, xx], [(block, x_peer)])

    def c_stage_0(layer):
        block = c_piece(layer, zz, xx, yy)
        start((0, layer), remote(block, block, new_sems(1), y_peer))
        c_spread(layer, yy)

    other_y = 1 - yy

    def c_stage_1(layer):
        finish((0, layer))
        c_spread(layer, other_y)

    def c_pass(layer, y):
        finish((1 if y is yy else 2, layer))
        blocks = [c_piece(layer, lax.rem(zz + k, nz), xx, y) for k in range(1, nz)]
        start_all((3, layer), c_ref.at[layer, core, :, :, xx], [(block, x_peer) for block in blocks])

    def c_stage_2(layer):
        c_pass(layer, yy)

    def c_stage_3(layer):
        c_pass(layer, other_y)
        block = c_ref.at[layer, core, :, :, xx]
        start((4, layer), remote(block, block, new_sems(1), sibling))

    def c_stage_4(layer):
        finish((3, layer))
        block = c_ref.at[layer, core, :, :, 1 - xx]
        start((5, layer), remote(block, block, new_sems(1), sibling))

    def c_stage_5(layer):
        finish((4, layer))
        finish((5, layer))

    def row_stage_y(ref, layer):
        block = ref.at[layer, own_rows(my_dp), :]
        start((id(ref), 0, layer), remote(block, block, new_sems(1), y_peer))
        total = ref.at[layer, pl.ds(0, 2 * rows_dp), :]
        start_all((id(ref), 1, layer), total, [(block, sibling)])

    def row_stage_core(ref, layer):
        finish((id(ref), 0, layer))
        block = ref.at[layer, own_rows(2 * (1 - yy) + core), :]
        start_all((id(ref), 1, layer), ref.at[layer, pl.ds(0, 2 * rows_dp), :], [(block, sibling)])

    def row_stage_end(ref, layer):
        finish((id(ref), 1, layer))

    def table_stage():
        own, every = I.tab_in, S.tab_recv
        every[0] = own[...]
        arrived = every.at[pl.ds(1, nseq - 1)]
        sem = new_sems(1)
        total = remote(arrived, arrived, sem, x_peer)

        def one(k):
            remote(own, every.at[k], sem, {"seq": lax.rem(me + k, nseq)}).start()

        seq_loop(one)
        return total

    def table_end(total):
        total.wait()
        lane = lax.broadcasted_iota(jnp.int32, (8, 128), 1)
        tiles = [jnp.zeros((8, 128), F32) for _ in range(p // 128)]
        for q in range(nseq):
            tile, first = (q * share) // 128, (q * share) % 128
            piece = S.tab_recv[from_rank(q)]
            if first:
                piece = pltpu.roll(piece, first, 1)
            here = (lane >= first) & (lane < first + share)
            tiles[tile] = jnp.where(here, piece, tiles[tile])
            if first + share > 128:
                tiles[tile + 1] = jnp.where(lane < first + share - 128, piece, tiles[tile + 1])
        for layer in range(layers):
            for tile in range(p // 128):
                tab_ref[layer, 0:4, tile * 128 : tile * 128 + 128] = tiles[tile][
                    4 * layer : 4 * layer + 4
                ]

    if inside:
        for layer in range(layers):
            cast_c(layer)
        cast_b(0)
        pl.semaphore_wait(barrier, greeted)
        c_stage_0(0)
        row_stage_y(b_ref, 0)
        table_copy = table_stage()
        for layer in range(layers):
            if layer:
                cast_b(layer)
            cast_glu(layer)
    else:
        pl.semaphore_wait(barrier, greeted)

    for col in range(0, width, 128):
        perm[col // 128] = x_ref[:, col : col + 128].astype(F32)

        def place(j, carry, col=col):
            rows = pl.ds(pl.multiple_of(j * CHUNKS, CHUNKS), CHUNKS)
            stream[rows, col : col + 128] = perm[col // 128, pl.ds(j, CHUNKS, stride=steps), :]
            return carry

        lax.fori_loop(0, steps, place, 0, unroll=4)

    for layer in range(layers):
        gain = gain_ref[layer : layer + 1, :]
        bias = bias_ref[layer : layer + 1, :]
        skip = skip_ref[layer : layer + 1, :]

        def norm_rows(rows, first, carry, layer=layer, gain=gain, bias=bias):
            value = stream[rows, :]
            center = value - jnp.mean(value, axis=1, keepdims=True)
            spread = jnp.mean(center * center, axis=1, keepdims=True)
            inv = lax.rsqrt(spread + 1e-05)
            hat = center * inv
            xhat[layer, rows, :] = hat
            rstd[layer, rows, :] = inv
            nlow[layer, rows, :] = (hat * gain + bias).astype(BF16)
            return carry

        if inside and layer == 0:
            c_stage_1(0)
        row_loop(norm_rows, 0)

        if inside:
            if layer == 0:
                c_stage_2(0)
                c_stage_0(1)
                row_stage_y(glu_ref, 0)
                table_end(table_copy)
                row_stage_core(b_ref, 0)
            row_stage_end(b_ref, layer)
        in_scale = tab_ref[layer, 2:3, :]
        for col in range(0, 2 * p, 256):
            part = mm_nn(nlow[layer], b_ref[layer, :, col : col + 256])
            for half in range(col, col + 256, 128):
                scale_col = half % p
                drive[layer, :, half : half + 128] = (
                    part[:, half - col : half - col + 128].astype(BF16).astype(F32)
                    * in_scale[:, scale_col : scale_col + 128]
                )

        lam_re, lam_im, jumps = layer_powers(layer, False)
        ends = local_ends(drive.at[layer], 0, 0, lam_re, lam_im)
        prefix = local_prefix(ends, jumps)
        send_totals(layer, prefix)
        if inside and layer == 0:
            c_stage_1(1)
            c_stage_3(0)
            row_stage_y(b_ref, 1)
        elif inside:
            c_stage_4(1)
            row_stage_core(glu_ref, 1)
        exchange_wait(layer)
        carries = chunk_carries(layer, prefix, jumps)
        caus[layer, 0:CHUNKS, 0:p] = carries[0]
        caus[layer, 0:CHUNKS, p : 2 * p] = carries[1]
        anti[layer, tok : tok + CHUNKS, 0:p] = carries[2]
        anti[layer, tok : tok + CHUNKS, p : 2 * p] = carries[3]
        l_re = jnp.broadcast_to(lam_re, (CHUNKS, p))
        l_im = jnp.broadcast_to(lam_im, (CHUNKS, p))

        def state_pair(k, carry, layer=layer, l_re=l_re, l_im=l_im):
            s_re, s_im, r_re, r_im = carry
            first = pl.multiple_of(k * 2 * CHUNKS, 2 * CHUNKS)
            kept_re, kept_im = [], []
            for half in range(2):
                rows = pl.ds(first + half * CHUNKS, CHUNKS)
                s_re, s_im = cmul(l_re, l_im, s_re, s_im)
                s_re = s_re + drive[layer, rows, 0:p]
                s_im = s_im + drive[layer, rows, p : 2 * p]
                after = pl.ds(first + (half + 1) * CHUNKS, CHUNKS)
                caus[layer, after, 0:p] = s_re
                caus[layer, after, p : 2 * p] = s_im
                kept_re.append(s_re)
                kept_im.append(s_im)
            both = pl.ds(first, 2 * CHUNKS)
            feat[layer, both, 0:p] = jnp.concatenate(kept_re, axis=0).astype(BF16)
            feat[layer, both, p : 2 * p] = jnp.concatenate(kept_im, axis=0).astype(BF16)
            last = pl.multiple_of(tok - (k + 1) * 2 * CHUNKS, 2 * CHUNKS)
            kept_re, kept_im = [], []
            for half in (1, 0):
                rows = pl.ds(last + half * CHUNKS, CHUNKS)
                r_re, r_im = cmul(l_re, l_im, r_re, r_im)
                r_re = r_re + drive[layer, rows, 0:p]
                r_im = r_im + drive[layer, rows, p : 2 * p]
                anti[layer, rows, 0:p] = r_re
                anti[layer, rows, p : 2 * p] = r_im
                kept_re.insert(0, r_re)
                kept_im.insert(0, r_im)
            both = pl.ds(last, 2 * CHUNKS)
            feat[layer, both, 2 * p : 3 * p] = jnp.concatenate(kept_re, axis=0).astype(BF16)
            feat[layer, both, 3 * p : 4 * p] = jnp.concatenate(kept_im, axis=0).astype(BF16)
            return s_re, s_im, r_re, r_im

        lax.fori_loop(0, steps // 2, state_pair, carries, unroll=2)

        if inside and layer == 0:
            c_stage_4(0)
            row_stage_core(glu_ref, 0)
            c_stage_2(1)
            row_stage_y(glu_ref, 1)
        for turn in range(2):
            half = (1 - own_half) if turn else own_half
            if inside and turn:
                c_stage_5(layer)
            part = mm_nn(feat[layer], c_ref[layer, half].reshape(4 * p, half_cols))
            for first, block in half_blocks(half):
                temp[:, block] = part[:, first : first + 128]

        if inside:
            row_stage_end(glu_ref, layer)
        def act_rows(rows, first, carry, layer=layer, gain=gain, bias=bias, skip=skip):
            pre = temp[rows, :] + skip * (xhat[layer, rows, :] * gain + bias)
            square = pre * pre
            th = jnp.tanh(GELU_A * pre * (1.0 + GELU_B * square))
            cdf = 0.5 * (1.0 + th)
            out = pre * cdf
            gelu_out[layer, rows, :] = out
            gelu_low[layer, rows, :] = out.astype(BF16)
            gelu_der[layer, rows, :] = cdf + 0.5 * pre * (1.0 - th * th) * (
                GELU_A * (1.0 + 3.0 * GELU_B * square)
            )
            return carry

        row_loop(act_rows, 0)
        for col in range(0, width, 256):
            temp[:, col : col + 256] = mm_nn(gelu_low[layer], glu_ref[layer, :, col : col + 256])
        if inside and layer == 0:
            c_stage_3(1)
            row_stage_core(b_ref, 1)
        glu_bias = glub_ref[layer : layer + 1, :]
        last_layer = layer == layers - 1

        def gate_rows(rows, first, carry, layer=layer, glu_bias=glu_bias, last_layer=last_layer):
            gate = 1.0 / (1.0 + jnp.exp(-(temp[rows, :] + glu_bias)))
            sig[layer, rows, :] = gate
            new = stream[rows, :] + gelu_out[layer, rows, :] * gate
            if not last_layer:
                stream[rows, :] = new
                return carry
            return carry + fold8(new * row_mask(first))

        def row_mask(first):
            row = first + lax.broadcasted_iota(jnp.int32, (TILE, 1), 0)
            position = me * tok + (row & (CHUNKS - 1)) * steps + (row >> 3)
            return jnp.where(position < len_ref[0], 1.0, 0.0).astype(F32)

        pooled_part = row_loop(gate_rows, jnp.zeros((CHUNKS, width), F32) if last_layer else 0)

    pool_slot = 2 * layers
    own_sum = jnp.sum(pooled_part, axis=0, keepdims=True)
    send_buf[pool_slot, 0:1, :] = own_sum
    exchange_start(pool_slot)
    exchange_wait(pool_slot)

    def add_pool(k, total):
        return total + jnp.where(k == me, 0.0, recv_buf[pool_slot, from_rank(k), 0:1, :])

    pooled_sum = lax.fori_loop(0, nseq, add_pool, own_sum)
    len_row = jnp.full((1, 1), len_ref[0], jnp.int32).astype(F32)
    pooled = pooled_sum / len_row
    logit = [
        jnp.sum(pooled * cw_ref[k : k + 1, :], axis=1, keepdims=True) + cb_ref[k : k + 1, :]
        for k in range(classes)
    ]
    top = logit[0]
    for k in range(1, classes):
        top = jnp.maximum(top, logit[k])
    expo = [jnp.exp(v - top) for v in logit]
    norm = expo[0]
    for k in range(1, classes):
        norm = norm + expo[k]
    hot = [jnp.where(lab_ref[0] == k, 1.0, 0.0).astype(F32) for k in range(classes)]
    cross = top + jnp.log(norm)
    for k in range(classes):
        cross = cross - hot[k] * logit[k]
    lgrad = [len_row * (expo[k] / norm - hot[k]) for k in range(classes)]
    pooled_grad = lgrad[0] * cw_ref[0:1, :]
    for k in range(1, classes):
        pooled_grad = pooled_grad + lgrad[k] * cw_ref[k : k + 1, :]
    grad_row = pooled_grad / len_row
    once = jnp.where(me == 0, 1.0, 0.0).astype(F32)
    small_ref[...] = jnp.zeros(small_ref.shape, F32)
    head_row = 6 * layers
    lane = lax.broadcasted_iota(jnp.int32, (1, width), 1)
    bias_line = jnp.zeros((1, width), F32)
    for k in range(classes):
        put_line(head_row + k, pooled * lgrad[k] * once)
        bias_line = jnp.where(lane == k, lgrad[k] * once, bias_line)
    bias_line = jnp.where(lane == classes, cross * once, bias_line)
    put_line(head_row + classes, bias_line)

    groups = 4 * nz

    def loop(count, body):
        def one(k, carry):
            body(k)
            return carry

        lax.fori_loop(0, count, one, 0)

    def c_grad_start(layer, part):
        rows = feat[layer, :, part * 2 * p : (part + 1) * 2 * p]
        value = mm_tn(rows, mlow[1 - core]).reshape(groups, share, half_cols)
        CG.snd1[layer, part] = value.astype(BF16)
        copy = remote(CG.snd1.at[layer, part], CG.rcv1.at[layer, part], new_sems(1), sibling)
        start((6, layer, part), copy)
        CG.acc[layer, part] = mm_tn(rows, mlow[core]).reshape(groups, share, half_cols)

    def c_grad_first(layer, part):
        finish((6, layer, part))
        acc, rcv = CG.acc.at[layer, part], CG.rcv1.at[layer, part]
        if part == 0:

            def put(dst, cols):
                def one(g):
                    value = acc[g, :, cols] + rcv[g, :, cols].astype(F32)
                    dst[layer, g] = value.astype(dst.dtype)

                loop(groups, one)

            put(CG.snd2a, y_cols(1 - yy))
            copy = remote(CG.snd2a.at[layer], CG.rcv2a.at[layer], new_sems(1), y_peer)
            start((7, layer, part), copy)
            put(CG.acc2a, y_cols(yy))
        else:

            def put(dst, x):
                def one(h):
                    value = acc[2 * h + x] + rcv[2 * h + x].astype(F32)
                    dst[layer, h] = value.astype(dst.dtype)

                loop(groups // 2, one)

            put(CG.snd2b, 1 - xx)
            copy = remote(CG.snd2b.at[layer], CG.rcv2b.at[layer], new_sems(1), x_peer)
            start((7, layer, part), copy)
            put(CG.acc2b, xx)

    def c_grad_second(layer, part):
        finish((7, layer, part))
        if part == 0:

            def put(dst, x):
                def one(h):
                    value = CG.acc2a[layer, 2 * h + x] + CG.rcv2a[layer, 2 * h + x].astype(F32)
                    dst[layer, part, h] = value.astype(dst.dtype)

                loop(groups // 2, one)

            away, keep, peer = 1 - xx, xx, x_peer
        else:

            def put(dst, cols):
                def one(h):
                    value = CG.acc2b[layer, h, :, cols] + CG.rcv2b[layer, h, :, cols].astype(F32)
                    dst[layer, part, h] = value.astype(dst.dtype)

                loop(groups // 2, one)

            away, keep, peer = y_cols(1 - yy), y_cols(yy), y_peer
        put(CG.snd3, away)
        copy = remote(CG.snd3.at[layer, part], CG.rcv3.at[layer, part], new_sems(1), peer)
        start((8, layer, part), copy)
        put(CG.acc3, keep)

    def spread_z(name, src, dst):
        arrived = dst.at[pl.ds(1, nz - 1)]
        sem = new_sems(1)
        copies[name] = remote(arrived, arrived, sem, x_peer)
        for k in range(1, nz):
            peer = lax.rem(zz + k, nz)
            remote(src(peer), dst.at[k], sem, {"seq": 2 * peer + xx}).start()

    def c_grad_third(layer, part):
        finish((8, layer, part))

        def one(h):
            value = CG.acc3[layer, part, h] + CG.rcv3[layer, part, h].astype(F32)
            CG.acc3[layer, part, h] = value
            CG.snd4[layer, part, lax.rem(h, nz), h // nz] = value.astype(BF16)

        loop(groups // 2, one)
        snd = CG.snd4.at[layer, part]
        spread_z((9, layer, part), lambda peer: snd.at[peer], CG.rcv4.at[layer, part])

    def c_grad_end(layer, part):
        finish((9, layer, part))
        for plane in range(2):
            value = CG.acc3[layer, part, plane * nz + zz]
            for k in range(1, nz):
                value = value + CG.rcv4[layer, part, k, plane].astype(F32)
            O.c_out[layer, 2 * part + plane] = value

    def row_grad_start(G, layer, left, right):
        for y in range(ny):
            block = left[layer, :, own_rows(2 * y + 1 - core)]
            G.snd1[layer, y] = mm_tn(block, right[...]).astype(BF16)
        copy = remote(G.snd1.at[layer], G.rcv1.at[layer], new_sems(1), sibling)
        start((id(G), 0, layer), copy)
        for y in range(ny):
            block = left[layer, :, own_rows(2 * y + core)]
            G.acc[layer, y] = mm_tn(block, right[...])

    def row_grad_y(G, layer):
        finish((id(G), 0, layer))
        acc, rcv = G.acc.at[layer], G.rcv1.at[layer]
        cast_rows(G.snd2.at[layer], acc.at[1 - yy], rows_dp, 32, rcv.at[1 - yy])
        copy = remote(G.snd2.at[layer], G.rcv2.at[layer], new_sems(1), y_peer)
        start((id(G), 1, layer), copy)
        cast_rows(G.acc2.at[layer], acc.at[yy], rows_dp, 32, rcv.at[yy])

    piece = rows_dp // nseq

    def row_grad_x(G, layer):
        finish((id(G), 1, layer))

        def put(dst, x):
            def one(z):
                rows = pl.ds(pl.multiple_of((2 * z + x) * piece, 16), piece)
                value = G.acc2[layer, rows, :] + G.rcv2[layer, rows, :].astype(F32)
                dst[layer, z] = value.astype(dst.dtype)

            loop(nz, one)

        put(G.snd3, 1 - xx)
        start((id(G), 2, layer), remote(G.snd3.at[layer], G.rcv3.at[layer], new_sems(1), x_peer))
        put(G.acc3, xx)

    def row_grad_z(G, layer):
        finish((id(G), 2, layer))

        def one(z):
            value = G.acc3[layer, z] + G.rcv3[layer, z].astype(F32)
            G.acc3[layer, z] = value
            G.snd4[layer, z] = value.astype(BF16)

        loop(nz, one)
        snd = G.snd4.at[layer]
        spread_z((id(G), 3, layer), lambda peer: snd.at[peer], G.rcv4.at[layer])

    def row_grad_back_z(G, layer):
        finish((id(G), 3, layer))
        value = G.acc3[layer, zz]
        for k in range(1, nz):
            value = value + G.rcv4[layer, k].astype(F32)
        G.full[layer, zz, xx] = value.astype(BF16)
        block = G.full.at[layer, zz, xx]
        total = G.full.at[layer, pl.ds(0, nz - 1), xx]
        start_all((id(G), 4, layer), total, [(block, peer) for peer in z_peers()])

    def row_grad_back_x(G, layer):
        finish((id(G), 4, layer))
        block = G.full.at[layer, :, xx]
        start((id(G), 5, layer), remote(block, block, new_sems(1), x_peer))

    def row_grad_end(G, layer):
        finish((id(G), 5, layer))
        out = O.b_out if G is BG else O.glu_out

        def one(z):
            for x in range(2):
                rows = pl.ds(pl.multiple_of((2 * z + x) * piece, 16), piece)
                out[layer, rows, :] = G.full[layer, z, x].astype(F32)

        loop(nz, one)

    small_rows = small_ref.shape[0]
    small_piece = small_rows // nseq

    def small_start():
        start((8, 0), remote(small_ref, S.small_core, new_sems(1), sibling))

    def small_y():
        finish((8, 0))
        S.small_sum[0] = small_ref[...] + S.small_core[...]
        start((8, 1), remote(S.small_sum.at[0], S.small_y, new_sems(1), y_peer))

    def small_part(q):
        return pl.ds(pl.multiple_of(q * small_piece, 8), small_piece)

    def small_spread(name, src, dst, wait_ref):
        sem = new_sems(1)
        copies[name] = remote(wait_ref, wait_ref, sem, x_peer)

        def one(k):
            peer = lax.rem(me + k, nseq)
            remote(src(peer), dst(k), sem, {"seq": peer}).start()

        seq_loop(one)

    def small_scatter():
        finish((8, 1))
        S.small_sum[1] = S.small_sum[0] + S.small_y[...]
        small_spread(
            (8, 2),
            lambda peer: S.small_sum.at[1, small_part(peer), :],
            lambda k: S.small_recv.at[k],
            S.small_recv.at[pl.ds(1, nseq - 1)],
        )

    def small_gather():
        finish((8, 2))
        value = S.small_sum[1, small_part(me), :]
        for k in range(1, nseq):
            value = value + S.small_recv[k]
        S.small_sum[2, small_part(me), :] = value
        block = S.small_sum.at[2, small_part(me), :]
        small_spread(
            (8, 3), lambda peer: block, lambda k: block, S.small_recv.at[pl.ds(1, nseq - 1)]
        )

    def small_end():
        finish((8, 3))
        O.small_out[...] = S.small_sum[2]

    grad = stream

    def first_grad(rows, first, carry):
        grad[rows, :] = row_mask(first) * grad_row
        return carry

    row_loop(first_grad, 0)

    for layer in reversed(range(layers)):
        gain = gain_ref[layer : layer + 1, :]
        bias = bias_ref[layer : layer + 1, :]
        skip = skip_ref[layer : layer + 1, :]
        zero_sum = jnp.zeros((CHUNKS, width), F32)

        def gate_back(rows, first, total, layer=layer):
            gate = sig[layer, rows, :]
            low = (grad[rows, :] * gelu_out[layer, rows, :] * gate * (1.0 - gate)).astype(BF16)
            ggrad[rows, :] = low
            return total + fold8(low.astype(F32))

        total = row_loop(gate_back, zero_sum)
        if inside:
            row_grad_start(GG, layer, gelu_low, ggrad)
        put_line(3 * layers + layer, jnp.sum(total, axis=0, keepdims=True))
        for col in range(0, width, 256):
            temp[:, col : col + 256] = mm_nt(ggrad[...], glu_ref[layer, col : col + 256, :])

        def mix_back(rows, first, total, layer=layer, gain=gain, bias=bias):
            act = grad[rows, :] * sig[layer, rows, :] + temp[rows, :]
            value = act * gelu_der[layer, rows, :]
            mix[rows, :] = value
            for h in range(2):
                for first, block in half_blocks(h):
                    at = block.start
                    mlow[h, rows, first : first + 128] = value[:, at : at + 128].astype(BF16)
            return total + fold8(value * (xhat[layer, rows, :] * gain + bias))

        total = row_loop(mix_back, zero_sum)
        put_line(2 * layers + layer, jnp.sum(total, axis=0, keepdims=True))
        if inside:
            row_grad_y(GG, layer)
        for plane in range(0, 4, 2):
            rows = [c_ref[layer, h, plane : plane + 2].reshape(2 * p, half_cols) for h in range(2)]
            wide[:, plane * p : (plane + 2) * p] = mm_nt(mlow[0], rows[0]) + mm_nt(mlow[1], rows[1])

        lam_re, lam_im, jumps = layer_powers(layer, True)
        ends = local_ends(wide, 2 * p, 0, lam_re, lam_im)
        prefix = local_prefix(ends, jumps)
        slot = layers + layer
        send_totals(slot, prefix)
        if inside:
            for part in range(2):
                c_grad_start(layer, part)
            if layer < layers - 1:
                c_grad_second(layer + 1, 1)
                row_grad_x(BG, layer + 1)
        else:
            for h in range(2):
                for col in range(0, 4 * p, 2 * p):
                    O.c_out[layer, col : col + 2 * p, h * half_cols : (h + 1) * half_cols] = mm_tn(
                        feat[layer, :, col : col + 2 * p], mlow[h]
                    ).astype(BF16)
            for col in range(0, width, 256):
                O.glu_out[layer, col : col + 256, :] = mm_tn(
                    gelu_low[layer, :, col : col + 256], ggrad[...]
                ).astype(BF16)
        if inside and layer == layers - 1:
            for part in range(2):
                c_grad_first(layer, part)
        exchange_wait(slot)
        carries = chunk_carries(slot, prefix, jumps)
        l_re = jnp.broadcast_to(lam_re, (CHUNKS, p))
        l_im = jnp.broadcast_to(lam_im, (CHUNKS, p))
        zero = jnp.zeros((CHUNKS, p), F32)

        def anti_grad(j, carry, layer=layer, l_re=l_re, l_im=l_im):
            r_re, r_im, d_re, d_im = carry
            rows = pl.ds(pl.multiple_of(j * CHUNKS, CHUNKS), CHUNKS)
            after = pl.ds(pl.multiple_of((j + 1) * CHUNKS, CHUNKS), CHUNKS)
            r_re, r_im = cmul(l_re, l_im, r_re, r_im)
            r_re = r_re + wide[rows, 2 * p : 3 * p]
            r_im = r_im + wide[rows, 3 * p : 4 * p]
            wide[rows, 2 * p : 3 * p] = r_re
            wide[rows, 3 * p : 4 * p] = r_im
            q_re = anti[layer, after, 0:p]
            q_im = anti[layer, after, p : 2 * p]
            return r_re, r_im, d_re + (r_re * q_re + r_im * q_im), d_im + (r_im * q_re - r_re * q_im)

        _, _, d_re, d_im = lax.fori_loop(
            0, steps, anti_grad, (carries[0], carries[1], zero, zero), unroll=4
        )
        in_scale = jnp.broadcast_to(tab_ref[layer, 2:3, :], (CHUNKS, p))

        def caus_grad(k, carry, layer=layer, l_re=l_re, l_im=l_im, in_scale=in_scale):
            a_re, a_im, d_re, d_im, s_sum = carry
            last = pl.multiple_of(tok - (k + 1) * 2 * CHUNKS, 2 * CHUNKS)
            kept_re, kept_im = [], []
            for half in (1, 0):
                rows = pl.ds(last + half * CHUNKS, CHUNKS)
                a_re, a_im = cmul(l_re, l_im, a_re, a_im)
                a_re = a_re + wide[rows, 0:p]
                a_im = a_im + wide[rows, p : 2 * p]
                q_re = caus[layer, rows, 0:p]
                q_im = caus[layer, rows, p : 2 * p]
                d_re = d_re + (a_re * q_re + a_im * q_im)
                d_im = d_im + (a_im * q_re - a_re * q_im)
                t_re = a_re + wide[rows, 2 * p : 3 * p]
                t_im = a_im + wide[rows, 3 * p : 4 * p]
                s_sum = s_sum + (
                    t_re * drive[layer, rows, 0:p] + t_im * drive[layer, rows, p : 2 * p]
                )
                kept_re.insert(0, t_re * in_scale)
                kept_im.insert(0, t_im * in_scale)
            both = pl.ds(last, 2 * CHUNKS)
            dlow[both, 0:p] = jnp.concatenate(kept_re, axis=0).astype(BF16)
            dlow[both, p : 2 * p] = jnp.concatenate(kept_im, axis=0).astype(BF16)
            return a_re, a_im, d_re, d_im, s_sum

        _, _, d_re, d_im, s_sum = lax.fori_loop(
            0, steps // 2, caus_grad, (carries[2], carries[3], d_re, d_im, zero), unroll=2
        )
        d_re = jnp.sum(d_re, axis=0, keepdims=True)
        d_im = jnp.sum(d_im, axis=0, keepdims=True)
        s_sum = jnp.sum(s_sum, axis=0, keepdims=True) / tab_ref[layer, 2:3, :]
        true_re = tab_ref[layer, 0:1, :]
        true_im = tab_ref[layer, 1:2, :]
        pad = jnp.zeros((1, width - p), F32)
        rate_part = s_sum * tab_ref[layer, 3:4, :] - d_re * true_re - d_im * true_im
        put_line(4 * layers + layer, jnp.concatenate([rate_part, pad], axis=1))
        phase_part = d_im * true_re - d_re * true_im
        put_line(5 * layers + layer, jnp.concatenate([phase_part, pad], axis=1))

        if inside:
            row_grad_start(BG, layer, nlow, dlow)
        else:
            for col in range(0, width, 256):
                O.b_out[layer, col : col + 256, :] = mm_tn(
                    nlow[layer, :, col : col + 256], dlow[...]
                ).astype(BF16)
        for col in range(0, width, 256):
            temp[:, col : col + 256] = mm_nt(dlow[...], b_ref[layer, col : col + 256, :])

        def norm_back(rows, first, carry, layer=layer, gain=gain, skip=skip):
            gain_sum, bias_sum = carry
            ngrad = mix[rows, :] * skip + temp[rows, :]
            hat = xhat[layer, rows, :]
            q = ngrad * gain
            mean_q = jnp.mean(q, axis=1, keepdims=True)
            mean_x = jnp.mean(q * hat, axis=1, keepdims=True)
            grad[rows, :] = grad[rows, :] + (q - mean_q - hat * mean_x) * rstd[layer, rows, :]
            return gain_sum + fold8(ngrad * hat), bias_sum + fold8(ngrad)

        gain_sum, bias_sum = row_loop(norm_back, (zero_sum, zero_sum))
        put_line(layer, jnp.sum(gain_sum, axis=0, keepdims=True))
        put_line(layers + layer, jnp.sum(bias_sum, axis=0, keepdims=True))
        if inside:
            row_grad_y(BG, layer)
            if layer == layers - 1:
                row_grad_x(GG, layer)
                c_grad_second(layer, 0)

    if inside:
        small_start()
        for part in range(2):
            c_grad_first(0, part)
        row_grad_z(GG, 1)
        c_grad_third(1, 0)
        row_grad_x(GG, 0)
        small_y()
    for col in range(0, width, 128):
        perm[col // 128] = grad[:, col : col + 128]

        def unplace(k, carry, col=col):
            first = k * CHUNKS
            chunk = first // steps
            rows = pl.ds((first - chunk * steps) * CHUNKS + chunk, CHUNKS, stride=CHUNKS)
            out = pl.ds(pl.multiple_of(first, CHUNKS), CHUNKS)
            gin_ref[out, col : col + 128] = perm[col // 128, rows, :]
            return carry

        lax.fori_loop(0, steps, unplace, 0, unroll=4)

    if inside:
        c_grad_third(1, 1)
        row_grad_z(BG, 1)
        row_grad_x(BG, 0)
        small_scatter()
        row_grad_back_z(GG, 1)
        row_grad_z(GG, 0)
        c_grad_second(0, 0)
        c_grad_second(0, 1)
        row_grad_z(BG, 0)
        small_gather()
        row_grad_back_z(BG, 1)
        row_grad_back_x(GG, 1)
        row_grad_back_z(GG, 0)
        row_grad_back_z(BG, 0)
        c_grad_third(0, 0)
        c_grad_third(0, 1)
        row_grad_back_x(BG, 1)
        row_grad_back_x(GG, 0)
        row_grad_back_x(BG, 0)
        c_grad_end(1, 0)
        c_grad_end(1, 1)
        row_grad_end(GG, 1)
        small_end()
        row_grad_end(BG, 1)
        row_grad_end(GG, 0)
        c_grad_end(0, 0)
        c_grad_end(0, 1)
        row_grad_end(BG, 0)


def run_model(dims, inside, operands):
    layers, tok, width, states, classes, ndp, nseq = dims
    vmem = pl.BlockSpec(memory_space=pltpu.VMEM)
    smem = pl.BlockSpec(memory_space=pltpu.SMEM)
    lines = -(-(6 * layers + classes + 1) // 8) * 8
    small_shape = (lines * width // 128, 128)
    slots = 2 * layers + 1
    share, rows_dp = states // nseq, width // ndp
    per_layer = lambda cols, kind, rows=tok: pltpu.VMEM((layers, rows, cols), kind)
    if inside:
        b_shape, g_shape = (layers, rows_dp, 2 * states), (layers, rows_dp, width)
        c_shape, kind = (layers, 4, share, width // ndp), F32
    else:
        b_shape, g_shape = (layers, width, 2 * states), (layers, width, width)
        c_shape, kind = (layers, 4 * states, width), BF16
    scratch = [
        pltpu.VMEM((tok, width), F32),
        per_layer(width, F32),
        per_layer(1, F32),
        per_layer(width, BF16),
        per_layer(2 * states, F32),
        per_layer(2 * states, F32, tok + CHUNKS),
        per_layer(2 * states, F32, tok + CHUNKS),
        per_layer(4 * states, BF16),
        per_layer(width, F32),
        per_layer(width, BF16),
        per_layer(width, F32),
        per_layer(width, F32),
        pltpu.VMEM((tok, 4 * states), F32),
        pltpu.VMEM((tok, width), F32),
        pltpu.VMEM((tok, width), F32),
        pltpu.VMEM((2, tok, width // 2), BF16),
        pltpu.VMEM((tok, width), BF16),
        pltpu.VMEM((tok, 2 * states), BF16),
        pltpu.VMEM((width // 128, tok, 128), F32),
        pltpu.VMEM((slots, 8, width), F32),
        pltpu.VMEM((slots, nseq, 8, width), F32),
        pltpu.SemaphoreType.DMA((slots,)),
        pltpu.SemaphoreType.DMA((slots,)),
    ]
    if inside:
        ny, nz, part, half = ndp // 2, nseq // 2, width // ndp, width // 2
        copies = 68
        scratch += [
            pltpu.VMEM((layers, 8, states), F32),
            pltpu.VMEM((nseq, 8, 128), F32),
            per_layer(2 * states, BF16, width),
            per_layer(width, BF16, width),
            pltpu.VMEM((layers, 2, 4, nz, 2, share, half), BF16),
            pltpu.SemaphoreType.DMA((copies,)),
            pltpu.SemaphoreType.DMA((copies,)),
            pltpu.VMEM(small_shape, F32),
            pltpu.VMEM(small_shape, F32),
            pltpu.VMEM(small_shape, F32),
            pltpu.VMEM((3,) + small_shape, F32),
            pltpu.VMEM((nseq, small_shape[0] // nseq, 128), F32),
        ]
        for cols in (2 * states, width):
            scratch += [
                pltpu.VMEM((layers, ny, rows_dp, cols), BF16),
                pltpu.VMEM((layers, ny, rows_dp, cols), BF16),
                pltpu.VMEM((layers, ny, rows_dp, cols), F32),
                per_layer(cols, BF16, rows_dp),
                per_layer(cols, BF16, rows_dp),
                per_layer(cols, F32, rows_dp),
                pltpu.VMEM((layers, nz, rows_dp // nseq, cols), BF16),
                pltpu.VMEM((layers, nz, rows_dp // nseq, cols), BF16),
                pltpu.VMEM((layers, nz, rows_dp // nseq, cols), F32),
                pltpu.VMEM((layers, nz, rows_dp // nseq, cols), BF16),
                pltpu.VMEM((layers, nz, rows_dp // nseq, cols), BF16),
                pltpu.VMEM((layers, nz, 2, rows_dp // nseq, cols), BF16),
            ]
        scratch += [
            pltpu.VMEM((layers, 2, 4 * nz, share, half), BF16),
            pltpu.VMEM((layers, 2, 4 * nz, share, half), BF16),
            pltpu.VMEM((layers, 2, 4 * nz, share, half), F32),
            pltpu.VMEM((layers, 4 * nz, share, part), BF16),
            pltpu.VMEM((layers, 4 * nz, share, part), BF16),
            pltpu.VMEM((layers, 4 * nz, share, part), F32),
            pltpu.VMEM((layers, 2 * nz, share, half), BF16),
            pltpu.VMEM((layers, 2 * nz, share, half), BF16),
            pltpu.VMEM((layers, 2 * nz, share, half), F32),
            pltpu.VMEM((layers, 2, 2 * nz, share, part), BF16),
            pltpu.VMEM((layers, 2, 2 * nz, share, part), BF16),
            pltpu.VMEM((layers, 2, 2 * nz, share, part), F32),
            pltpu.VMEM((layers, 2, nz, 2, share, part), BF16),
            pltpu.VMEM((layers, 2, nz, 2, share, part), BF16),
        ]
    return pl.pallas_call(
        partial(model_kernel, dims, inside),
        out_shape=(
            jax.ShapeDtypeStruct((tok, width), F32),
            jax.ShapeDtypeStruct(small_shape, F32),
            jax.ShapeDtypeStruct(b_shape, kind),
            jax.ShapeDtypeStruct(g_shape, kind),
            jax.ShapeDtypeStruct(c_shape, kind),
        ),
        in_specs=[smem, smem] + [vmem] * 11,
        out_specs=[vmem] * 5,
        scratch_shapes=scratch,
        compiler_params=pltpu.CompilerParams(
            collective_id=0, has_side_effects=True, vmem_limit_bytes=60 * 1024 * 1024
        ),
        cost_estimate=pl.CostEstimate(
            flops=6 * layers * tok * width * (6 * states + width),
            bytes_accessed=16 * 1024 * 1024,
            transcendentals=2 * layers * tok * width,
        ),
    )(*operands)


def per_device(
    inputs,
    lengths,
    labels,
    norm_gain,
    norm_bias,
    b_proj,
    rate,
    phase,
    c_proj,
    skip,
    glu_weight,
    glu_bias,
    class_weight,
    class_bias,
):
    layers, width = norm_gain.shape
    tok = inputs.shape[1]
    ndp = lax.axis_size("dp")
    nseq = lax.axis_size("seq")
    states = c_proj.shape[2] * nseq
    classes = class_bias.shape[0]
    dims = (layers, tok, width, states, classes, ndp, nseq)
    share = states // nseq
    inside = (
        ndp == 4
        and nseq % 2 == 0
        and share % 16 == 0
        and (width // ndp) % 128 == 0
        and (width // ndp) % (16 * nseq) == 0
        and 4 * layers == 8
    )
    decay = jnp.exp(-rate)
    in_scale = jnp.sqrt(-jnp.expm1(-2.0 * rate))
    rows = [
        decay * jnp.cos(phase),
        decay * jnp.sin(phase),
        in_scale,
        jnp.exp(-2.0 * rate) / in_scale,
    ]
    table = jnp.stack(rows, axis=1)
    if inside:
        table = jnp.pad(table.reshape(4 * layers, share), ((0, 0), (0, 128 - share)))
        weights = (b_proj, glu_weight, c_proj)
    else:
        table = lax.all_gather(table, "seq", axis=2, tiled=True)
        b_full = lax.all_gather(b_proj.astype(BF16), "dp", axis=1, tiled=True)
        g_full = lax.all_gather(glu_weight.astype(BF16), "dp", axis=1, tiled=True)
        c_half = lax.all_gather(c_proj.astype(BF16), "dp", axis=3, tiled=True)
        c_full = lax.all_gather(c_half, "seq", axis=2, tiled=True)
        c_full = c_full.reshape(layers, 4, states, 2, width // 2)
        c_full = jnp.moveaxis(c_full, 3, 1)
        weights = (b_full, g_full, c_full)
    grad_inputs, small, b_grad, g_grad, c_grad = run_model(
        dims,
        inside,
        (
            lengths,
            labels,
            inputs[0],
            norm_gain,
            norm_bias,
            skip,
            glu_bias,
            table,
            class_weight.T,
            class_bias[:, None],
        )
        + weights,
    )
    if inside:
        b_share, g_share, c_share = b_grad, g_grad, c_grad
    else:
        b_share = lax.psum_scatter(b_grad, "dp", scatter_dimension=1, tiled=True)
        g_share = lax.psum_scatter(g_grad, "dp", scatter_dimension=1, tiled=True)
        b_share = lax.psum(b_share, "seq").astype(F32)
        g_share = lax.psum(g_share, "seq").astype(F32)
        c_grad = c_grad.reshape(layers, 4, states, width)
        c_share = lax.psum_scatter(c_grad, "seq", scatter_dimension=2, tiled=True)
        c_share = lax.psum_scatter(c_share, "dp", scatter_dimension=3, tiled=True).astype(F32)
        small = lax.psum(small, ("dp", "seq"))
    small = small.reshape(-1, width)
    own = lax.axis_index("seq") * (states // nseq)

    def state_rows(first):
        return lax.dynamic_slice(small[first : first + layers], (0, own), (layers, states // nseq))

    head = 6 * layers
    return (
        small[head + classes, classes] / ndp,
        grad_inputs[None],
        small[0:layers],
        small[layers : 2 * layers],
        b_share,
        state_rows(4 * layers),
        state_rows(5 * layers),
        c_share,
        small[2 * layers : 3 * layers],
        g_share,
        small[3 * layers : 4 * layers],
        small[head : head + classes].T,
        small[head + classes, 0:classes],
    )


def solution(mesh):
    return jax.shard_map(
        per_device,
        mesh=mesh,
        in_specs=(
            P("dp", "seq", None),
            P("dp"),
            P("dp"),
            P(),
            P(),
            P(None, "dp", None),
            P(None, "seq"),
            P(None, "seq"),
            P(None, None, "seq", "dp"),
            P(),
            P(None, "dp", None),
            P(),
            P(),
            P(),
        ),
        out_specs=(
            P(),
            P("dp", "seq", None),
            P(),
            P(),
            P(None, "dp", None),
            P(None, "seq"),
            P(None, "seq"),
            P(None, None, "seq", "dp"),
            P(),
            P(None, "dp", None),
            P(),
            P(),
            P(),
        ),
        check_vma=False,
    )
```

```python
from functools import partial
from typing import Any, NamedTuple

import jax
import jax.numpy as jnp
from jax import lax
from jax.experimental import pallas as pl
from jax.experimental.pallas import tpu as pltpu
from jax.sharding import PartitionSpec as P

MESH = pl.DeviceIdType.MESH
F32 = jnp.float32
BF16 = jnp.bfloat16
CHUNKS = 8
TILE = 32
GELU_A = 0.7978845608028654
GELU_B = 0.044715


def mm_nn(left, right):
    return lax.dot_general(left, right, (((1,), (0,)), ((), ())), preferred_element_type=F32)


def mm_nt(left, right):
    return lax.dot_general(left, right, (((1,), (1,)), ((), ())), preferred_element_type=F32)


def mm_tn(left, right):
    return lax.dot_general(left, right, (((0,), (0,)), ((), ())), preferred_element_type=F32)


def cmul(a_re, a_im, b_re, b_im):
    return a_re * b_re - a_im * b_im, a_re * b_im + a_im * b_re


def fold8(value):
    total = value[0:8]
    for first in range(8, value.shape[0], 8):
        total = total + value[first : first + 8]
    return total


class Operands(NamedTuple):
    len: Any
    lab: Any
    cb: Any
    x: Any
    gain: Any
    bias: Any
    skip: Any
    glub: Any
    rate: Any
    phase: Any
    cw: Any
    b_in: Any
    glu_in: Any
    c_in: Any


class Results(NamedTuple):
    gin: Any
    small_out: Any
    b_out: Any
    glu_out: Any
    c_out: Any


class Local(NamedTuple):
    stream: Any
    xhat: Any
    rstd: Any
    nlow: Any
    drive: Any
    caus: Any
    anti: Any
    feat: Any
    gelu_out: Any
    gelu_low: Any
    gelu_der: Any
    sig: Any
    wide: Any
    temp: Any
    mix: Any
    mlow: Any
    ggrad: Any
    dlow: Any
    perm: Any
    send_buf: Any
    recv_buf: Any
    send_sem: Any
    recv_sem: Any


class Shared(NamedTuple):
    tab: Any
    tab_recv: Any
    b_buf: Any
    glu_buf: Any
    c_buf: Any
    ssem: Any
    rsem: Any
    small: Any
    small_core: Any
    small_y: Any
    small_sum: Any
    small_recv: Any


class RowGrad(NamedTuple):
    snd1: Any
    rcv1: Any
    acc: Any
    snd2: Any
    rcv2: Any
    acc2: Any
    snd3: Any
    rcv3: Any
    acc3: Any
    snd4: Any
    rcv4: Any
    full: Any


class ColGrad(NamedTuple):
    snd1: Any
    rcv1: Any
    acc: Any
    snd2a: Any
    rcv2a: Any
    acc2a: Any
    snd2b: Any
    rcv2b: Any
    acc2b: Any
    snd3: Any
    rcv3: Any
    acc3: Any
    snd4: Any
    rcv4: Any


def take(refs, kind):
    count = len(kind._fields)
    return kind(*refs[:count]), refs[count:]


def model_kernel(dims, inside, *refs):
    layers, tok, width, states, classes, ndp, nseq = dims
    I, refs = take(refs, Operands)
    O, refs = take(refs, Results)
    L, refs = take(refs, Local)
    if inside:
        S, refs = take(refs, Shared)
        BG, refs = take(refs, RowGrad)
        GG, refs = take(refs, RowGrad)
        CG, refs = take(refs, ColGrad)
        tab_ref, b_ref, glu_ref, c_ref, small_ref = S.tab, S.b_buf, S.glu_buf, S.c_buf, S.small
    else:
        tab_ref, b_ref, glu_ref, c_ref, small_ref = I.rate, I.b_in, I.glu_in, I.c_in, O.small_out
    len_ref, lab_ref, x_ref = I.len, I.lab, I.x
    gain_ref, bias_ref, skip_ref, glub_ref = I.gain, I.bias, I.skip, I.glub
    cw_ref, cb_ref, gin_ref = I.cw, I.cb, O.gin
    stream, xhat, rstd, nlow, drive = L.stream, L.xhat, L.rstd, L.nlow, L.drive
    caus, anti, feat, gelu_out, gelu_low = L.caus, L.anti, L.feat, L.gelu_out, L.gelu_low
    gelu_der, sig, wide, temp, mix = L.gelu_der, L.sig, L.wide, L.temp, L.mix
    mlow, ggrad, dlow, perm = L.mlow, L.ggrad, L.dlow, L.perm
    send_buf, recv_buf = L.send_buf, L.recv_buf
    send_sem, recv_sem = L.send_sem, L.recv_sem
    steps = tok // CHUNKS
    half_cols = width // 2
    me = lax.axis_index("seq")
    my_dp = lax.axis_index("dp")
    p = states
    core, yy = lax.rem(my_dp, 2), my_dp // 2
    xx, zz = lax.rem(me, 2), me // 2
    ny, nz = ndp // 2, nseq // 2
    own_half = core if inside else 0

    barrier = pltpu.get_barrier_semaphore()

    def greet(k, carry):
        peer = lax.rem(me + k, nseq)
        pl.semaphore_signal(barrier, inc=1, device_id={"seq": peer}, device_id_type=MESH)
        return carry

    lax.fori_loop(1, nseq, greet, 0)
    greeted = nseq - 1
    sibling = {"dp": 2 * yy + 1 - core}
    y_peer = {"dp": 2 * (1 - yy) + core}
    x_peer = {"seq": 2 * zz + 1 - xx}
    if inside:
        for peer in (sibling, y_peer):
            pl.semaphore_signal(barrier, inc=1, device_id=peer, device_id_type=MESH)
        greeted += 2

    used = [0]

    def new_sems(count):
        first = used[0]
        used[0] += count
        return first

    def remote(src, dst, sem, peer):
        return pltpu.make_async_remote_copy(
            src_ref=src,
            dst_ref=dst,
            send_sem=S.ssem.at[sem],
            recv_sem=S.rsem.at[sem],
            device_id=peer,
            device_id_type=MESH,
        )

    def seq_loop(body):
        def one(k, carry):
            body(k)
            return carry

        lax.fori_loop(1, nseq, one, 0)

    def cast_rows(dst, src, rows, step, extra=None):
        def one(k, carry):
            part = pl.ds(pl.multiple_of(k * step, step), step)
            value = src[part, :].astype(F32)
            if extra is not None:
                value = value + extra[part, :].astype(F32)
            dst[part, :] = value.astype(dst.dtype)
            return carry

        lax.fori_loop(0, rows // step, one, 0)

    def row_loop(body, init, unroll=1):
        def step(k, carry):
            rows = pl.ds(pl.multiple_of(k * TILE, TILE), TILE)
            return body(rows, k * TILE, carry)

        return lax.fori_loop(0, tok // TILE, step, init, unroll=unroll)

    def exchange_start(slot):
        def one(k, carry):
            peer = lax.rem(me + k, nseq)
            pltpu.make_async_remote_copy(
                src_ref=send_buf.at[slot, (peer - me + nseq) // nseq],
                dst_ref=recv_buf.at[slot, k],
                send_sem=send_sem.at[slot],
                recv_sem=recv_sem.at[slot],
                device_id={"seq": peer},
                device_id_type=MESH,
            ).start()
            return carry

        lax.fori_loop(1, nseq, one, 0)

    def exchange_wait(slot):
        arrived = recv_buf.at[slot, pl.ds(1, nseq - 1)]
        pltpu.make_async_remote_copy(
            src_ref=arrived,
            dst_ref=arrived,
            send_sem=send_sem.at[slot],
            recv_sem=recv_sem.at[slot],
            device_id={"seq": lax.rem(me + 1, nseq)},
            device_id_type=MESH,
        ).wait()

    def from_rank(q):
        return lax.rem(me - q + nseq, nseq)

    sub = lax.broadcasted_iota(jnp.int32, (CHUNKS, p), 0)

    def layer_powers(layer, conj):
        lam_re = tab_ref[layer, 0:1, :]
        lam_im = tab_ref[layer, 1:2, :]
        if conj:
            lam_im = -lam_im
        pw_re, pw_im = lam_re, lam_im
        count = 1
        while count < steps:
            pw_re, pw_im = cmul(pw_re, pw_im, pw_re, pw_im)
            count *= 2
        jumps = [(pw_re, pw_im)]
        for _ in range(3):
            pw_re, pw_im = cmul(pw_re, pw_im, pw_re, pw_im)
            jumps.append((pw_re, pw_im))
        return lam_re, lam_im, jumps

    def jump_table(jumps, index):
        re = jnp.ones((CHUNKS, p), F32)
        im = jnp.zeros((CHUNKS, p), F32)
        for bit in range(3):
            new_re, new_im = cmul(re, im, jumps[bit][0], jumps[bit][1])
            has = (index & (1 << bit)) != 0
            re = jnp.where(has, new_re, re)
            im = jnp.where(has, new_im, im)
        return re, im

    def local_ends(src, first_c, first_a, lam_re, lam_im):
        zero = jnp.zeros((CHUNKS, p), F32)
        l_re = jnp.broadcast_to(lam_re, (CHUNKS, p))
        l_im = jnp.broadcast_to(lam_im, (CHUNKS, p))

        def step(j, carry):
            e_re, e_im, f_re, f_im = carry
            up = pl.ds(pl.multiple_of(j * CHUNKS, CHUNKS), CHUNKS)
            down = pl.ds(pl.multiple_of((steps - 1 - j) * CHUNKS, CHUNKS), CHUNKS)
            e_re, e_im = cmul(l_re, l_im, e_re, e_im)
            f_re, f_im = cmul(l_re, l_im, f_re, f_im)
            return (
                e_re + src[up, first_c : first_c + p],
                e_im + src[up, first_c + p : first_c + 2 * p],
                f_re + src[down, first_a : first_a + p],
                f_im + src[down, first_a + p : first_a + 2 * p],
            )

        return lax.fori_loop(0, steps, step, (zero,) * 4, unroll=4)

    def local_prefix(ends, jumps):
        e_re, e_im, f_re, f_im = ends
        for bit in range(3):
            shift = 1 << bit
            j_re, j_im = jumps[bit]
            s_re = jnp.where(sub >= shift, pltpu.roll(e_re, shift, 0), 0.0)
            s_im = jnp.where(sub >= shift, pltpu.roll(e_im, shift, 0), 0.0)
            a_re, a_im = cmul(j_re, j_im, s_re, s_im)
            e_re, e_im = e_re + a_re, e_im + a_im
            s_re = jnp.where(sub < CHUNKS - shift, pltpu.roll(f_re, CHUNKS - shift, 0), 0.0)
            s_im = jnp.where(sub < CHUNKS - shift, pltpu.roll(f_im, CHUNKS - shift, 0), 0.0)
            a_re, a_im = cmul(j_re, j_im, s_re, s_im)
            f_re, f_im = f_re + a_re, f_im + a_im
        return e_re, e_im, f_re, f_im

    def send_totals(slot, prefix):
        e_re, e_im, f_re, f_im = prefix
        last, first = slice(CHUNKS - 1, CHUNKS), slice(0, 1)
        for tile in range(p // 128):
            cols = slice(tile * 128, tile * 128 + 128)
            for row, value, part, at in (
                (tile, e_re, 1, last),
                (p // 128 + tile, e_im, 1, last),
                (tile, f_re, 0, first),
                (p // 128 + tile, f_im, 0, first),
            ):
                send_buf[slot, part, row : row + 1, :] = value[at, cols]
        exchange_start(slot)

    def chunk_carries(slot, prefix, jumps):
        e_re, e_im, f_re, f_im = prefix
        d_re, d_im = jumps[3]
        zero = jnp.zeros((1, p), F32)

        def arrived(q, first):
            rows = range(first, first + p // 128)
            return jnp.concatenate([recv_buf[slot, from_rank(q), r : r + 1, :] for r in rows], axis=1)

        def step(k, carry):
            c_re, c_im, a_re, a_im = carry
            n_re, n_im = cmul(d_re, d_im, c_re, c_im)
            use = k < me
            c_re = jnp.where(use, n_re + arrived(k, 0), c_re)
            c_im = jnp.where(use, n_im + arrived(k, p // 128), c_im)
            back = nseq - 1 - k
            n_re, n_im = cmul(d_re, d_im, a_re, a_im)
            use = back > me
            a_re = jnp.where(use, n_re + arrived(back, 0), a_re)
            a_im = jnp.where(use, n_im + arrived(back, p // 128), a_im)
            return c_re, c_im, a_re, a_im

        c_re, c_im, a_re, a_im = lax.fori_loop(0, nseq, step, (zero,) * 4)
        t_re, t_im = jump_table(jumps, sub)
        g_re, g_im = cmul(t_re, t_im, c_re, c_im)
        in_c_re = g_re + jnp.where(sub >= 1, pltpu.roll(e_re, 1, 0), 0.0)
        in_c_im = g_im + jnp.where(sub >= 1, pltpu.roll(e_im, 1, 0), 0.0)
        t_re, t_im = jump_table(jumps, CHUNKS - 1 - sub)
        g_re, g_im = cmul(t_re, t_im, a_re, a_im)
        in_a_re = g_re + jnp.where(sub < CHUNKS - 1, pltpu.roll(f_re, CHUNKS - 1, 0), 0.0)
        in_a_im = g_im + jnp.where(sub < CHUNKS - 1, pltpu.roll(f_im, CHUNKS - 1, 0), 0.0)
        return in_c_re, in_c_im, in_a_re, in_a_im

    def half_blocks(half):
        blocks = []
        for first in range(0, half_cols, 128):
            if inside:
                at = (2 * (first // part_cols) + half) * part_cols + first % part_cols
            else:
                at = half * half_cols + first
            if not isinstance(at, int):
                at = pl.multiple_of(at, 128)
            blocks.append((first, pl.ds(at, 128)))
        return blocks

    def put_line(line, row):
        for col in range(0, width, 128):
            at = line * (width // 128) + col // 128
            small_ref[at : at + 1, :] = row[:, col : col + 128]

    part_cols = width // ndp
    rows_dp = width // ndp
    share = p // nseq

    def own_rows(index):
        return pl.ds(pl.multiple_of(index * rows_dp, 16), rows_dp)

    def cast_c(layer):
        cols = pl.ds(pl.multiple_of(yy * part_cols, 128), part_cols)
        c_ref[layer, core, :, zz, xx, :, cols] = I.c_in[layer].astype(BF16)

    def cast_b(layer):
        b_ref[layer, own_rows(my_dp), :] = I.b_in[layer].astype(BF16)

    def cast_glu(layer):
        glu_ref[layer, own_rows(my_dp), :] = I.glu_in[layer].astype(BF16)

    copies, sem_of = {}, {}

    def start(name, copy):
        copies[name] = copy
        copy.start()

    def finish(name):
        copies.pop(name).wait()

    def y_cols(y):
        return pl.ds(pl.multiple_of(y * part_cols, 128), part_cols)

    def start_all(name, total, pairs):
        if name not in copies:
            sem_of[name] = new_sems(1)
            copies[name] = remote(total, total, sem_of[name], x_peer)
        for block, peer in pairs:
            remote(block, block, sem_of[name], peer).start()

    def z_peers():
        return [{"seq": 2 * lax.rem(zz + k, nz) + xx} for k in range(1, nz)]

    def c_piece(layer, z, x, y):
        return c_ref.at[layer, core, :, z, x, :, y_cols(y)]

    def c_spread(layer, y):
        block = c_piece(layer, zz, xx, y)
        total = c_ref.at[layer, core, :, pl.ds(0, nz - 1), xx, :, y_cols(y)]
        own = y is yy
        start_all((1 if own else 2, layer), total, [(block, peer) for peer in z_peers()])
        start_all((3, layer), c_ref.at[layer, core, :, :, xx], [(block, x_peer)])

    def c_stage_0(layer):
        block = c_piece(layer, zz, xx, yy)
        start((0, layer), remote(block, block, new_sems(1), y_peer))

    other_y = 1 - yy

    def c_stage_1(layer):
        finish((0, layer))
        c_spread(layer, other_y)

    def c_pass(layer, y):
        finish((1 if y is yy else 2, layer))
        blocks = [c_piece(layer, lax.rem(zz + k, nz), xx, y) for k in range(1, nz)]
        start_all((3, layer), c_ref.at[layer, core, :, :, xx], [(block, x_peer) for block in blocks])

    def c_stage_2(layer):
        c_pass(layer, yy)

    def c_stage_3(layer):
        c_pass(layer, other_y)
        block = c_ref.at[layer, core, :, :, xx]
        start((4, layer), remote(block, block, new_sems(1), sibling))

    def c_stage_4(layer):
        finish((3, layer))
        block = c_ref.at[layer, core, :, :, 1 - xx]
        start((5, layer), remote(block, block, new_sems(1), sibling))

    def c_stage_5(layer):
        finish((4, layer))
        finish((5, layer))

    def row_stage_y(ref, layer):
        block = ref.at[layer, own_rows(my_dp), :]
        start((id(ref), 0, layer), remote(block, block, new_sems(1), y_peer))
        total = ref.at[layer, pl.ds(0, 2 * rows_dp), :]
        start_all((id(ref), 1, layer), total, [(block, sibling)])

    def row_stage_core(ref, layer):
        finish((id(ref), 0, layer))
        block = ref.at[layer, own_rows(2 * (1 - yy) + core), :]
        start_all((id(ref), 1, layer), ref.at[layer, pl.ds(0, 2 * rows_dp), :], [(block, sibling)])

    def row_stage_end(ref, layer):
        finish((id(ref), 1, layer))

    def table_stage():
        every, own = S.tab_recv, S.tab_recv.at[0]
        rate, phase = I.rate[...], I.phase[...]
        decay = jnp.exp(-rate)
        twice = 2.0 * rate
        series = 1.0 - twice / 7.0
        for term in (6.0, 5.0, 4.0, 3.0, 2.0):
            series = 1.0 - series * (twice / term)
        loss = jnp.where(twice < 0.25, twice * series, 1.0 - jnp.exp(-twice))
        in_scale = jnp.sqrt(loss)
        every[0] = jnp.zeros((8, 128), F32)
        parts = (decay * jnp.cos(phase), decay * jnp.sin(phase), in_scale, jnp.exp(-twice) / in_scale)
        for row, value in enumerate(parts):
            for layer in range(layers):
                at = 4 * layer + row
                every[0, at : at + 1, 0:share] = value[layer : layer + 1]
        arrived = every.at[pl.ds(1, nseq - 1)]
        sem = new_sems(1)
        total = remote(arrived, arrived, sem, x_peer)

        def one(k):
            remote(own, every.at[k], sem, {"seq": lax.rem(me + k, nseq)}).start()

        seq_loop(one)
        return total

    def table_end(total):
        total.wait()
        lane = lax.broadcasted_iota(jnp.int32, (8, 128), 1)
        tiles = [jnp.zeros((8, 128), F32) for _ in range(p // 128)]
        for q in range(nseq):
            tile, first = (q * share) // 128, (q * share) % 128
            piece = S.tab_recv[from_rank(q)]
            if first:
                piece = pltpu.roll(piece, first, 1)
            here = (lane >= first) & (lane < first + share)
            tiles[tile] = jnp.where(here, piece, tiles[tile])
            if first + share > 128:
                tiles[tile + 1] = jnp.where(lane < first + share - 128, piece, tiles[tile + 1])
        for layer in range(layers):
            for tile in range(p // 128):
                tab_ref[layer, 0:4, tile * 128 : tile * 128 + 128] = tiles[tile][
                    4 * layer : 4 * layer + 4
                ]

    if inside:
        for layer in range(layers):
            cast_c(layer)
        cast_b(0)
        pl.semaphore_wait(barrier, greeted)
        c_stage_0(0)
        c_spread(0, yy)
        row_stage_y(b_ref, 0)
        c_stage_0(1)
        table_copy = table_stage()
        for layer in range(layers):
            if layer:
                cast_b(layer)
            cast_glu(layer)
    else:
        pl.semaphore_wait(barrier, greeted)

    for col in range(0, width, 128):
        perm[col // 128] = x_ref[:, col : col + 128].astype(F32)

        def place(j, carry, col=col):
            rows = pl.ds(pl.multiple_of(j * CHUNKS, CHUNKS), CHUNKS)
            stream[rows, col : col + 128] = perm[col // 128, pl.ds(j, CHUNKS, stride=steps), :]
            return carry

        lax.fori_loop(0, steps, place, 0, unroll=4)

    for layer in range(layers):
        gain = gain_ref[layer : layer + 1, :]
        bias = bias_ref[layer : layer + 1, :]
        skip = skip_ref[layer : layer + 1, :]

        def norm_rows(rows, first, carry, layer=layer, gain=gain, bias=bias):
            value = stream[rows, :]
            center = value - jnp.mean(value, axis=1, keepdims=True)
            spread = jnp.mean(center * center, axis=1, keepdims=True)
            inv = lax.rsqrt(spread + 1e-05)
            hat = center * inv
            xhat[layer, rows, :] = hat
            rstd[layer, rows, :] = inv
            nlow[layer, rows, :] = (hat * gain + bias).astype(BF16)
            return carry

        if inside and layer == 0:
            c_stage_1(0)
        row_loop(norm_rows, 0)

        if inside:
            if layer == 0:
                c_stage_2(0)
                row_stage_y(glu_ref, 0)
                table_end(table_copy)
                row_stage_core(b_ref, 0)
            row_stage_end(b_ref, layer)
        in_scale = tab_ref[layer, 2:3, :]
        for col in range(0, 2 * p, 256):
            part = mm_nn(nlow[layer], b_ref[layer, :, col : col + 256])
            for half in range(col, col + 256, 128):
                scale_col = half % p
                drive[layer, :, half : half + 128] = (
                    part[:, half - col : half - col + 128].astype(BF16).astype(F32)
                    * in_scale[:, scale_col : scale_col + 128]
                )

        lam_re, lam_im, jumps = layer_powers(layer, False)
        ends = local_ends(drive.at[layer], 0, 0, lam_re, lam_im)
        prefix = local_prefix(ends, jumps)
        send_totals(layer, prefix)
        if inside and layer == 0:
            c_spread(1, yy)
            c_stage_3(0)
            c_stage_1(1)
            row_stage_y(b_ref, 1)
        elif inside:
            c_stage_4(1)
            row_stage_core(glu_ref, 1)
        exchange_wait(layer)
        carries = chunk_carries(layer, prefix, jumps)
        caus[layer, 0:CHUNKS, 0:p] = carries[0]
        caus[layer, 0:CHUNKS, p : 2 * p] = carries[1]
        anti[layer, tok : tok + CHUNKS, 0:p] = carries[2]
        anti[layer, tok : tok + CHUNKS, p : 2 * p] = carries[3]
        l_re = jnp.broadcast_to(lam_re, (CHUNKS, p))
        l_im = jnp.broadcast_to(lam_im, (CHUNKS, p))

        def state_pair(k, carry, layer=layer, l_re=l_re, l_im=l_im):
            s_re, s_im, r_re, r_im = carry
            first = pl.multiple_of(k * 2 * CHUNKS, 2 * CHUNKS)
            kept_re, kept_im = [], []
            for half in range(2):
                rows = pl.ds(first + half * CHUNKS, CHUNKS)
                s_re, s_im = cmul(l_re, l_im, s_re, s_im)
                s_re = s_re + drive[layer, rows, 0:p]
                s_im = s_im + drive[layer, rows, p : 2 * p]
                after = pl.ds(first + (half + 1) * CHUNKS, CHUNKS)
                caus[layer, after, 0:p] = s_re
                caus[layer, after, p : 2 * p] = s_im
                kept_re.append(s_re)
                kept_im.append(s_im)
            both = pl.ds(first, 2 * CHUNKS)
            feat[layer, both, 0:p] = jnp.concatenate(kept_re, axis=0).astype(BF16)
            feat[layer, both, p : 2 * p] = jnp.concatenate(kept_im, axis=0).astype(BF16)
            last = pl.multiple_of(tok - (k + 1) * 2 * CHUNKS, 2 * CHUNKS)
            kept_re, kept_im = [], []
            for half in (1, 0):
                rows = pl.ds(last + half * CHUNKS, CHUNKS)
                r_re, r_im = cmul(l_re, l_im, r_re, r_im)
                r_re = r_re + drive[layer, rows, 0:p]
                r_im = r_im + drive[layer, rows, p : 2 * p]
                anti[layer, rows, 0:p] = r_re
                anti[layer, rows, p : 2 * p] = r_im
                kept_re.insert(0, r_re)
                kept_im.insert(0, r_im)
            both = pl.ds(last, 2 * CHUNKS)
            feat[layer, both, 2 * p : 3 * p] = jnp.concatenate(kept_re, axis=0).astype(BF16)
            feat[layer, both, 3 * p : 4 * p] = jnp.concatenate(kept_im, axis=0).astype(BF16)
            return s_re, s_im, r_re, r_im

        lax.fori_loop(0, steps // 2, state_pair, carries, unroll=2)

        if inside and layer == 0:
            c_stage_4(0)
            row_stage_core(glu_ref, 0)
            c_stage_2(1)
            row_stage_y(glu_ref, 1)
        for turn in range(2):
            half = (1 - own_half) if turn else own_half
            if inside and turn:
                c_stage_5(layer)
            part = mm_nn(feat[layer], c_ref[layer, half].reshape(4 * p, half_cols))
            for first, block in half_blocks(half):
                temp[:, block] = part[:, first : first + 128]

        if inside:
            row_stage_end(glu_ref, layer)
        def act_rows(rows, first, carry, layer=layer, gain=gain, bias=bias, skip=skip):
            pre = temp[rows, :] + skip * (xhat[layer, rows, :] * gain + bias)
            square = pre * pre
            th = jnp.tanh(GELU_A * pre * (1.0 + GELU_B * square))
            cdf = 0.5 * (1.0 + th)
            out = pre * cdf
            gelu_out[layer, rows, :] = out
            gelu_low[layer, rows, :] = out.astype(BF16)
            gelu_der[layer, rows, :] = cdf + 0.5 * pre * (1.0 - th * th) * (
                GELU_A * (1.0 + 3.0 * GELU_B * square)
            )
            return carry

        row_loop(act_rows, 0)
        for col in range(0, width, 256):
            temp[:, col : col + 256] = mm_nn(gelu_low[layer], glu_ref[layer, :, col : col + 256])
        if inside and layer == 0:
            c_stage_3(1)
            row_stage_core(b_ref, 1)
        glu_bias = glub_ref[layer : layer + 1, :]
        last_layer = layer == layers - 1

        def gate_rows(rows, first, carry, layer=layer, glu_bias=glu_bias, last_layer=last_layer):
            gate = 1.0 / (1.0 + jnp.exp(-(temp[rows, :] + glu_bias)))
            sig[layer, rows, :] = gate
            new = stream[rows, :] + gelu_out[layer, rows, :] * gate
            if not last_layer:
                stream[rows, :] = new
                return carry
            return carry + fold8(new * row_mask(first))

        def row_mask(first):
            row = first + lax.broadcasted_iota(jnp.int32, (TILE, 1), 0)
            position = me * tok + (row & (CHUNKS - 1)) * steps + (row >> 3)
            return jnp.where(position < len_ref[0], 1.0, 0.0).astype(F32)

        pooled_part = row_loop(gate_rows, jnp.zeros((CHUNKS, width), F32) if last_layer else 0)

    pool_slot = 2 * layers
    own_sum = jnp.sum(pooled_part, axis=0, keepdims=True)
    for part in range(2):
        for tile in range(width // 128):
            cols = slice(tile * 128, tile * 128 + 128)
            send_buf[pool_slot, part, tile : tile + 1, :] = own_sum[:, cols]
    exchange_start(pool_slot)
    exchange_wait(pool_slot)

    def add_pool(k, total):
        rows = [recv_buf[pool_slot, from_rank(k), r : r + 1, :] for r in range(width // 128)]
        return total + jnp.where(k == me, 0.0, jnp.concatenate(rows, axis=1))

    pooled_sum = lax.fori_loop(0, nseq, add_pool, own_sum)
    len_row = jnp.full((1, 1), len_ref[0], jnp.int32).astype(F32)
    pooled = pooled_sum / len_row
    logit = [
        jnp.sum(pooled * cw_ref[k : k + 1, :], axis=1, keepdims=True) + jnp.full((1, 1), cb_ref[k], F32)
        for k in range(classes)
    ]
    top = logit[0]
    for k in range(1, classes):
        top = jnp.maximum(top, logit[k])
    expo = [jnp.exp(v - top) for v in logit]
    norm = expo[0]
    for k in range(1, classes):
        norm = norm + expo[k]
    hot = [jnp.where(lab_ref[0] == k, 1.0, 0.0).astype(F32) for k in range(classes)]
    cross = top + jnp.log(norm)
    for k in range(classes):
        cross = cross - hot[k] * logit[k]
    lgrad = [len_row * (expo[k] / norm - hot[k]) for k in range(classes)]
    pooled_grad = lgrad[0] * cw_ref[0:1, :]
    for k in range(1, classes):
        pooled_grad = pooled_grad + lgrad[k] * cw_ref[k : k + 1, :]
    grad_row = pooled_grad / len_row
    once = jnp.where(me == 0, 1.0, 0.0).astype(F32)
    small_ref[...] = jnp.zeros(small_ref.shape, F32)
    head_row = 6 * layers
    lane = lax.broadcasted_iota(jnp.int32, (1, width), 1)
    bias_line = jnp.zeros((1, width), F32)
    for k in range(classes):
        put_line(head_row + k, pooled * lgrad[k] * once)
        bias_line = jnp.where(lane == k, lgrad[k] * once, bias_line)
    bias_line = jnp.where(lane == classes, cross * once, bias_line)
    put_line(head_row + classes, bias_line)

    groups = 4 * nz

    def loop(count, body):
        def one(k, carry):
            body(k)
            return carry

        lax.fori_loop(0, count, one, 0)

    def c_grad_start(layer, part):
        rows = feat[layer, :, part * 2 * p : (part + 1) * 2 * p]
        value = mm_tn(rows, mlow[1 - core]).reshape(groups, share, half_cols)
        CG.snd1[layer, part] = value.astype(BF16)
        copy = remote(CG.snd1.at[layer, part], CG.rcv1.at[layer, part], new_sems(1), sibling)
        start((6, layer, part), copy)
        CG.acc[layer, part] = mm_tn(rows, mlow[core]).reshape(groups, share, half_cols)

    def c_grad_first(layer, part):
        finish((6, layer, part))
        acc, rcv = CG.acc.at[layer, part], CG.rcv1.at[layer, part]
        if part == 0:

            def put(dst, cols):
                def one(g):
                    value = acc[g, :, cols] + rcv[g, :, cols].astype(F32)
                    dst[layer, g] = value.astype(dst.dtype)

                loop(groups, one)

            put(CG.snd2a, y_cols(1 - yy))
            copy = remote(CG.snd2a.at[layer], CG.rcv2a.at[layer], new_sems(1), y_peer)
            start((7, layer, part), copy)
            put(CG.acc2a, y_cols(yy))
        else:

            def put(dst, x):
                def one(h):
                    value = acc[2 * h + x] + rcv[2 * h + x].astype(F32)
                    dst[layer, h] = value.astype(dst.dtype)

                loop(groups // 2, one)

            put(CG.snd2b, 1 - xx)
            copy = remote(CG.snd2b.at[layer], CG.rcv2b.at[layer], new_sems(1), x_peer)
            start((7, layer, part), copy)
            put(CG.acc2b, xx)

    def c_grad_second(layer, part):
        finish((7, layer, part))
        if part == 0:

            def put(dst, x):
                def one(h):
                    value = CG.acc2a[layer, 2 * h + x] + CG.rcv2a[layer, 2 * h + x].astype(F32)
                    dst[layer, part, h] = value.astype(dst.dtype)

                loop(groups // 2, one)

            away, keep, peer = 1 - xx, xx, x_peer
        else:

            def put(dst, cols):
                def one(h):
                    value = CG.acc2b[layer, h, :, cols] + CG.rcv2b[layer, h, :, cols].astype(F32)
                    dst[layer, part, h] = value.astype(dst.dtype)

                loop(groups // 2, one)

            away, keep, peer = y_cols(1 - yy), y_cols(yy), y_peer
        put(CG.snd3, away)
        copy = remote(CG.snd3.at[layer, part], CG.rcv3.at[layer, part], new_sems(1), peer)
        start((8, layer, part), copy)
        put(CG.acc3, keep)

    def spread_z(name, src, dst):
        arrived = dst.at[pl.ds(1, nz - 1)]
        sem = new_sems(1)
        copies[name] = remote(arrived, arrived, sem, x_peer)
        for k in range(1, nz):
            peer = lax.rem(zz + k, nz)
            remote(src(peer), dst.at[k], sem, {"seq": 2 * peer + xx}).start()

    def c_grad_third(layer, part):
        finish((8, layer, part))

        def one(h):
            value = CG.acc3[layer, part, h] + CG.rcv3[layer, part, h].astype(F32)
            CG.acc3[layer, part, h] = value
            CG.snd4[layer, part, lax.rem(h, nz), h // nz] = value.astype(BF16)

        loop(groups // 2, one)
        snd = CG.snd4.at[layer, part]
        spread_z((9, layer, part), lambda peer: snd.at[peer], CG.rcv4.at[layer, part])

    def c_grad_end(layer, part):
        finish((9, layer, part))
        for plane in range(2):
            value = CG.acc3[layer, part, plane * nz + zz]
            for k in range(1, nz):
                value = value + CG.rcv4[layer, part, k, plane].astype(F32)
            O.c_out[layer, 2 * part + plane] = value

    def row_grad_start(G, layer, left, right):
        for y in range(ny):
            block = left[layer, :, own_rows(2 * y + 1 - core)]
            G.snd1[layer, y] = mm_tn(block, right[...]).astype(BF16)
        copy = remote(G.snd1.at[layer], G.rcv1.at[layer], new_sems(1), sibling)
        start((id(G), 0, layer), copy)
        for y in range(ny):
            block = left[layer, :, own_rows(2 * y + core)]
            G.acc[layer, y] = mm_tn(block, right[...])

    def row_grad_y(G, layer):
        finish((id(G), 0, layer))
        acc, rcv = G.acc.at[layer], G.rcv1.at[layer]
        cast_rows(G.snd2.at[layer], acc.at[1 - yy], rows_dp, 32, rcv.at[1 - yy])
        copy = remote(G.snd2.at[layer], G.rcv2.at[layer], new_sems(1), y_peer)
        start((id(G), 1, layer), copy)
        cast_rows(G.acc2.at[layer], acc.at[yy], rows_dp, 32, rcv.at[yy])

    piece = rows_dp // nseq

    def row_grad_x(G, layer):
        finish((id(G), 1, layer))

        def put(dst, x):
            def one(z):
                rows = pl.ds(pl.multiple_of((2 * z + x) * piece, 16), piece)
                value = G.acc2[layer, rows, :] + G.rcv2[layer, rows, :].astype(F32)
                dst[layer, z] = value.astype(dst.dtype)

            loop(nz, one)

        put(G.snd3, 1 - xx)
        start((id(G), 2, layer), remote(G.snd3.at[layer], G.rcv3.at[layer], new_sems(1), x_peer))
        put(G.acc3, xx)

    def row_grad_z(G, layer):
        finish((id(G), 2, layer))

        def one(z):
            value = G.acc3[layer, z] + G.rcv3[layer, z].astype(F32)
            G.acc3[layer, z] = value
            G.snd4[layer, z] = value.astype(BF16)

        loop(nz, one)
        snd = G.snd4.at[layer]
        spread_z((id(G), 3, layer), lambda peer: snd.at[peer], G.rcv4.at[layer])

    def row_grad_back_z(G, layer):
        finish((id(G), 3, layer))
        value = G.acc3[layer, zz]
        for k in range(1, nz):
            value = value + G.rcv4[layer, k].astype(F32)
        G.full[layer, zz, xx] = value.astype(BF16)
        block = G.full.at[layer, zz, xx]
        total = G.full.at[layer, pl.ds(0, nz - 1), xx]
        start_all((id(G), 4, layer), total, [(block, peer) for peer in z_peers()])

    def row_grad_back_x(G, layer):
        finish((id(G), 4, layer))
        block = G.full.at[layer, :, xx]
        start((id(G), 5, layer), remote(block, block, new_sems(1), x_peer))

    def row_grad_end(G, layer):
        finish((id(G), 5, layer))
        out = O.b_out if G is BG else O.glu_out

        def one(z):
            for x in range(2):
                rows = pl.ds(pl.multiple_of((2 * z + x) * piece, 16), piece)
                out[layer, rows, :] = G.full[layer, z, x].astype(F32)

        loop(nz, one)

    small_rows = small_ref.shape[0]
    small_piece = small_rows // nseq

    def small_start():
        start((8, 0), remote(small_ref, S.small_core, new_sems(1), sibling))

    def small_y():
        finish((8, 0))
        S.small_sum[0] = small_ref[...] + S.small_core[...]
        start((8, 1), remote(S.small_sum.at[0], S.small_y, new_sems(1), y_peer))

    def small_part(q):
        return pl.ds(pl.multiple_of(q * small_piece, 8), small_piece)

    def small_spread(name, src, dst, wait_ref):
        sem = new_sems(1)
        copies[name] = remote(wait_ref, wait_ref, sem, x_peer)

        def one(k):
            peer = lax.rem(me + k, nseq)
            remote(src(peer), dst(k), sem, {"seq": peer}).start()

        seq_loop(one)

    def small_scatter():
        finish((8, 1))
        S.small_sum[1] = S.small_sum[0] + S.small_y[...]
        small_spread(
            (8, 2),
            lambda peer: S.small_sum.at[1, small_part(peer), :],
            lambda k: S.small_recv.at[k],
            S.small_recv.at[pl.ds(1, nseq - 1)],
        )

    def small_gather():
        finish((8, 2))
        value = S.small_sum[1, small_part(me), :]
        for k in range(1, nseq):
            value = value + S.small_recv[k]
        S.small_sum[2, small_part(me), :] = value
        block = S.small_sum.at[2, small_part(me), :]
        small_spread(
            (8, 3), lambda peer: block, lambda k: block, S.small_recv.at[pl.ds(1, nseq - 1)]
        )

    def small_end():
        finish((8, 3))
        O.small_out[...] = S.small_sum[2]

    grad = stream

    def first_grad(rows, first, carry):
        grad[rows, :] = row_mask(first) * grad_row
        return carry

    row_loop(first_grad, 0)

    for layer in reversed(range(layers)):
        gain = gain_ref[layer : layer + 1, :]
        bias = bias_ref[layer : layer + 1, :]
        skip = skip_ref[layer : layer + 1, :]
        zero_sum = jnp.zeros((CHUNKS, width), F32)

        def gate_back(rows, first, total, layer=layer):
            gate = sig[layer, rows, :]
            low = (grad[rows, :] * gelu_out[layer, rows, :] * gate * (1.0 - gate)).astype(BF16)
            ggrad[rows, :] = low
            return total + fold8(low.astype(F32))

        total = row_loop(gate_back, zero_sum)
        if inside:
            if layer < layers - 1:
                row_grad_y(BG, layer + 1)
            row_grad_start(GG, layer, gelu_low, ggrad)
        put_line(3 * layers + layer, jnp.sum(total, axis=0, keepdims=True))
        for col in range(0, width, 256):
            temp[:, col : col + 256] = mm_nt(ggrad[...], glu_ref[layer, col : col + 256, :])

        def mix_back(rows, first, total, layer=layer, gain=gain, bias=bias):
            act = grad[rows, :] * sig[layer, rows, :] + temp[rows, :]
            value = act * gelu_der[layer, rows, :]
            mix[rows, :] = value
            for h in range(2):
                for first, block in half_blocks(h):
                    at = block.start
                    mlow[h, rows, first : first + 128] = value[:, at : at + 128].astype(BF16)
            return total + fold8(value * (xhat[layer, rows, :] * gain + bias))

        total = row_loop(mix_back, zero_sum)
        put_line(2 * layers + layer, jnp.sum(total, axis=0, keepdims=True))
        for plane in range(0, 4, 2):
            rows = [c_ref[layer, h, plane : plane + 2].reshape(2 * p, half_cols) for h in range(2)]
            wide[:, plane * p : (plane + 2) * p] = mm_nt(mlow[0], rows[0]) + mm_nt(mlow[1], rows[1])

        lam_re, lam_im, jumps = layer_powers(layer, True)
        ends = local_ends(wide, 2 * p, 0, lam_re, lam_im)
        prefix = local_prefix(ends, jumps)
        slot = layers + layer
        send_totals(slot, prefix)
        if inside and layer == layers - 1:
            c_grad_start(layer, 0)
            row_grad_y(GG, layer)
            c_grad_start(layer, 1)
            c_grad_first(layer, 0)
        elif inside:
            row_grad_y(GG, layer)
            c_grad_second(layer + 1, 0)
            for part in range(2):
                c_grad_start(layer, part)
            row_grad_z(GG, layer + 1)
            c_grad_second(layer + 1, 1)
        else:
            for h in range(2):
                for col in range(0, 4 * p, 2 * p):
                    O.c_out[layer, col : col + 2 * p, h * half_cols : (h + 1) * half_cols] = mm_tn(
                        feat[layer, :, col : col + 2 * p], mlow[h]
                    ).astype(BF16)
            for col in range(0, width, 256):
                O.glu_out[layer, col : col + 256, :] = mm_tn(
                    gelu_low[layer, :, col : col + 256], ggrad[...]
                ).astype(BF16)
        exchange_wait(slot)
        carries = chunk_carries(slot, prefix, jumps)
        l_re = jnp.broadcast_to(lam_re, (CHUNKS, p))
        l_im = jnp.broadcast_to(lam_im, (CHUNKS, p))
        zero = jnp.zeros((CHUNKS, p), F32)

        def anti_grad(j, carry, layer=layer, l_re=l_re, l_im=l_im):
            r_re, r_im, d_re, d_im = carry
            rows = pl.ds(pl.multiple_of(j * CHUNKS, CHUNKS), CHUNKS)
            after = pl.ds(pl.multiple_of((j + 1) * CHUNKS, CHUNKS), CHUNKS)
            r_re, r_im = cmul(l_re, l_im, r_re, r_im)
            r_re = r_re + wide[rows, 2 * p : 3 * p]
            r_im = r_im + wide[rows, 3 * p : 4 * p]
            wide[rows, 2 * p : 3 * p] = r_re
            wide[rows, 3 * p : 4 * p] = r_im
            q_re = anti[layer, after, 0:p]
            q_im = anti[layer, after, p : 2 * p]
            return r_re, r_im, d_re + (r_re * q_re + r_im * q_im), d_im + (r_im * q_re - r_re * q_im)

        _, _, d_re, d_im = lax.fori_loop(
            0, steps, anti_grad, (carries[0], carries[1], zero, zero), unroll=4
        )
        in_scale = jnp.broadcast_to(tab_ref[layer, 2:3, :], (CHUNKS, p))

        def caus_grad(k, carry, layer=layer, l_re=l_re, l_im=l_im, in_scale=in_scale):
            a_re, a_im, d_re, d_im, s_sum = carry
            last = pl.multiple_of(tok - (k + 1) * 2 * CHUNKS, 2 * CHUNKS)
            kept_re, kept_im = [], []
            for half in (1, 0):
                rows = pl.ds(last + half * CHUNKS, CHUNKS)
                a_re, a_im = cmul(l_re, l_im, a_re, a_im)
                a_re = a_re + wide[rows, 0:p]
                a_im = a_im + wide[rows, p : 2 * p]
                q_re = caus[layer, rows, 0:p]
                q_im = caus[layer, rows, p : 2 * p]
                d_re = d_re + (a_re * q_re + a_im * q_im)
                d_im = d_im + (a_im * q_re - a_re * q_im)
                t_re = a_re + wide[rows, 2 * p : 3 * p]
                t_im = a_im + wide[rows, 3 * p : 4 * p]
                s_sum = s_sum + (
                    t_re * drive[layer, rows, 0:p] + t_im * drive[layer, rows, p : 2 * p]
                )
                kept_re.insert(0, t_re * in_scale)
                kept_im.insert(0, t_im * in_scale)
            both = pl.ds(last, 2 * CHUNKS)
            dlow[both, 0:p] = jnp.concatenate(kept_re, axis=0).astype(BF16)
            dlow[both, p : 2 * p] = jnp.concatenate(kept_im, axis=0).astype(BF16)
            return a_re, a_im, d_re, d_im, s_sum

        _, _, d_re, d_im, s_sum = lax.fori_loop(
            0, steps // 2, caus_grad, (carries[2], carries[3], d_re, d_im, zero), unroll=2
        )
        d_re = jnp.sum(d_re, axis=0, keepdims=True)
        d_im = jnp.sum(d_im, axis=0, keepdims=True)
        s_sum = jnp.sum(s_sum, axis=0, keepdims=True) / tab_ref[layer, 2:3, :]
        true_re = tab_ref[layer, 0:1, :]
        true_im = tab_ref[layer, 1:2, :]
        pad = jnp.zeros((1, width - p), F32)
        rate_part = s_sum * tab_ref[layer, 3:4, :] - d_re * true_re - d_im * true_im
        put_line(4 * layers + layer, jnp.concatenate([rate_part, pad], axis=1))
        phase_part = d_im * true_re - d_re * true_im
        put_line(5 * layers + layer, jnp.concatenate([phase_part, pad], axis=1))

        if inside:
            if layer == layers - 1:
                c_grad_first(layer, 1)
            row_grad_start(BG, layer, nlow, dlow)
            if layer == layers - 1:
                row_grad_x(GG, layer)
            else:
                row_grad_x(BG, layer + 1)
                c_grad_third(layer + 1, 0)
        else:
            for col in range(0, width, 256):
                O.b_out[layer, col : col + 256, :] = mm_tn(
                    nlow[layer, :, col : col + 256], dlow[...]
                ).astype(BF16)
        for col in range(0, width, 256):
            temp[:, col : col + 256] = mm_nt(dlow[...], b_ref[layer, col : col + 256, :])

        def norm_back(rows, first, carry, layer=layer, gain=gain, skip=skip):
            gain_sum, bias_sum = carry
            ngrad = mix[rows, :] * skip + temp[rows, :]
            hat = xhat[layer, rows, :]
            q = ngrad * gain
            mean_q = jnp.mean(q, axis=1, keepdims=True)
            mean_x = jnp.mean(q * hat, axis=1, keepdims=True)
            grad[rows, :] = grad[rows, :] + (q - mean_q - hat * mean_x) * rstd[layer, rows, :]
            return gain_sum + fold8(ngrad * hat), bias_sum + fold8(ngrad)

        gain_sum, bias_sum = row_loop(norm_back, (zero_sum, zero_sum))
        put_line(layer, jnp.sum(gain_sum, axis=0, keepdims=True))
        put_line(layers + layer, jnp.sum(bias_sum, axis=0, keepdims=True))
        if inside and layer == 0:
            row_grad_y(BG, layer)

    plan = []
    if inside:
        plan = [
            partial(row_grad_x, GG, 0),
            small_start,
            partial(row_grad_back_z, GG, 1),
            small_y,
            partial(c_grad_first, 0, 1),
            partial(row_grad_z, BG, 1),
            partial(c_grad_third, 1, 1),
            partial(c_grad_first, 0, 0),
            partial(row_grad_z, GG, 0),
            partial(row_grad_x, BG, 0),
            partial(row_grad_back_z, BG, 1),
            small_scatter,
            partial(row_grad_z, BG, 0),
            partial(c_grad_second, 0, 0),
            partial(row_grad_back_z, GG, 0),
            small_gather,
            partial(c_grad_second, 0, 1),
            partial(row_grad_back_x, BG, 1),
            partial(row_grad_back_z, BG, 0),
            partial(c_grad_end, 1, 1),
            partial(c_grad_third, 0, 0),
            partial(c_grad_end, 1, 0),
            partial(row_grad_back_x, GG, 1),
            small_end,
            partial(row_grad_back_x, GG, 0),
            partial(c_grad_third, 0, 1),
            partial(row_grad_back_x, BG, 0),
            partial(row_grad_end, GG, 1),
            partial(row_grad_end, BG, 1),
            partial(row_grad_end, GG, 0),
            partial(c_grad_end, 0, 0),
            partial(c_grad_end, 0, 1),
            partial(row_grad_end, BG, 0),
        ]
    for stage in plan[:4]:
        stage()
    for col in range(0, width, 128):
        perm[col // 128] = grad[:, col : col + 128]

        def unplace(k, carry, col=col):
            first = k * CHUNKS
            chunk = first // steps
            rows = pl.ds((first - chunk * steps) * CHUNKS + chunk, CHUNKS, stride=CHUNKS)
            out = pl.ds(pl.multiple_of(first, CHUNKS), CHUNKS)
            gin_ref[out, col : col + 128] = perm[col // 128, rows, :]
            return carry

        lax.fori_loop(0, steps, unplace, 0, unroll=4)

    for stage in plan[4:]:
        stage()


def run_model(dims, inside, operands):
    layers, tok, width, states, classes, ndp, nseq = dims
    vmem = pl.BlockSpec(memory_space=pltpu.VMEM)
    smem = pl.BlockSpec(memory_space=pltpu.SMEM)
    lines = -(-(6 * layers + classes + 1) // 8) * 8
    small_shape = (lines * width // 128, 128)
    slots = 2 * layers + 1
    share, rows_dp = states // nseq, width // ndp
    per_layer = lambda cols, kind, rows=tok: pltpu.VMEM((layers, rows, cols), kind)
    if inside:
        b_shape, g_shape = (layers, rows_dp, 2 * states), (layers, rows_dp, width)
        c_shape, kind = (layers, 4, share, width // ndp), F32
    else:
        b_shape, g_shape = (layers, width, 2 * states), (layers, width, width)
        c_shape, kind = (layers, 4 * states, width), BF16
    scratch = [
        pltpu.VMEM((tok, width), F32),
        per_layer(width, F32),
        per_layer(1, F32),
        per_layer(width, BF16),
        per_layer(2 * states, F32),
        per_layer(2 * states, F32, tok + CHUNKS),
        per_layer(2 * states, F32, tok + CHUNKS),
        per_layer(4 * states, BF16),
        per_layer(width, F32),
        per_layer(width, BF16),
        per_layer(width, F32),
        per_layer(width, F32),
        pltpu.VMEM((tok, 4 * states), F32),
        pltpu.VMEM((tok, width), F32),
        pltpu.VMEM((tok, width), F32),
        pltpu.VMEM((2, tok, width // 2), BF16),
        pltpu.VMEM((tok, width), BF16),
        pltpu.VMEM((tok, 2 * states), BF16),
        pltpu.VMEM((width // 128, tok, 128), F32),
        pltpu.VMEM((slots, 2, 8, 128), F32),
        pltpu.VMEM((slots, nseq, 8, 128), F32),
        pltpu.SemaphoreType.DMA((slots,)),
        pltpu.SemaphoreType.DMA((slots,)),
    ]
    if inside:
        ny, nz, part, half = ndp // 2, nseq // 2, width // ndp, width // 2
        copies = 68
        scratch += [
            pltpu.VMEM((layers, 8, states), F32),
            pltpu.VMEM((nseq, 8, 128), F32),
            per_layer(2 * states, BF16, width),
            per_layer(width, BF16, width),
            pltpu.VMEM((layers, 2, 4, nz, 2, share, half), BF16),
            pltpu.SemaphoreType.DMA((copies,)),
            pltpu.SemaphoreType.DMA((copies,)),
            pltpu.VMEM(small_shape, F32),
            pltpu.VMEM(small_shape, F32),
            pltpu.VMEM(small_shape, F32),
            pltpu.VMEM((3,) + small_shape, F32),
            pltpu.VMEM((nseq, small_shape[0] // nseq, 128), F32),
        ]
        for cols in (2 * states, width):
            scratch += [
                pltpu.VMEM((layers, ny, rows_dp, cols), BF16),
                pltpu.VMEM((layers, ny, rows_dp, cols), BF16),
                pltpu.VMEM((layers, ny, rows_dp, cols), F32),
                per_layer(cols, BF16, rows_dp),
                per_layer(cols, BF16, rows_dp),
                per_layer(cols, F32, rows_dp),
                pltpu.VMEM((layers, nz, rows_dp // nseq, cols), BF16),
                pltpu.VMEM((layers, nz, rows_dp // nseq, cols), BF16),
                pltpu.VMEM((layers, nz, rows_dp // nseq, cols), F32),
                pltpu.VMEM((layers, nz, rows_dp // nseq, cols), BF16),
                pltpu.VMEM((layers, nz, rows_dp // nseq, cols), BF16),
                pltpu.VMEM((layers, nz, 2, rows_dp // nseq, cols), BF16),
            ]
        scratch += [
            pltpu.VMEM((layers, 2, 4 * nz, share, half), BF16),
            pltpu.VMEM((layers, 2, 4 * nz, share, half), BF16),
            pltpu.VMEM((layers, 2, 4 * nz, share, half), F32),
            pltpu.VMEM((layers, 4 * nz, share, part), BF16),
            pltpu.VMEM((layers, 4 * nz, share, part), BF16),
            pltpu.VMEM((layers, 4 * nz, share, part), F32),
            pltpu.VMEM((layers, 2 * nz, share, half), BF16),
            pltpu.VMEM((layers, 2 * nz, share, half), BF16),
            pltpu.VMEM((layers, 2 * nz, share, half), F32),
            pltpu.VMEM((layers, 2, 2 * nz, share, part), BF16),
            pltpu.VMEM((layers, 2, 2 * nz, share, part), BF16),
            pltpu.VMEM((layers, 2, 2 * nz, share, part), F32),
            pltpu.VMEM((layers, 2, nz, 2, share, part), BF16),
            pltpu.VMEM((layers, 2, nz, 2, share, part), BF16),
        ]
    return pl.pallas_call(
        partial(model_kernel, dims, inside),
        out_shape=(
            jax.ShapeDtypeStruct((tok, width), F32),
            jax.ShapeDtypeStruct(small_shape, F32),
            jax.ShapeDtypeStruct(b_shape, kind),
            jax.ShapeDtypeStruct(g_shape, kind),
            jax.ShapeDtypeStruct(c_shape, kind),
        ),
        in_specs=[smem] * 3 + [vmem] * 11,
        out_specs=[vmem] * 5,
        scratch_shapes=scratch,
        compiler_params=pltpu.CompilerParams(
            collective_id=0, has_side_effects=True, vmem_limit_bytes=60 * 1024 * 1024
        ),
        cost_estimate=pl.CostEstimate(
            flops=6 * layers * tok * width * (6 * states + width),
            bytes_accessed=16 * 1024 * 1024,
            transcendentals=2 * layers * tok * width,
        ),
    )(*operands)


def finish_kernel(dims, *refs):
    layers, tok, width, states, classes, ndp, nseq = dims
    small = refs[4]
    loss, gain, bias, rate, phase, skip, glub, head_w, head_b = refs[9:18]
    tiles = width // 128

    def line(row, count=tiles):
        parts = [small[row * tiles + t : row * tiles + t + 1, :] for t in range(count)]
        return jnp.concatenate(parts, axis=1)

    for layer in range(layers):
        at = slice(layer, layer + 1)
        gain[at, :] = line(layer)
        bias[at, :] = line(layers + layer)
        skip[at, :] = line(2 * layers + layer)
        glub[at, :] = line(3 * layers + layer)
    share = states // nseq
    me = lax.axis_index("seq")
    for first, out in ((4 * layers, rate), (5 * layers, phase)):
        every = jnp.concatenate([line(first + layer) for layer in range(layers)], axis=0)
        mine = every[:, 0:share]
        for q in range(1, nseq):
            mine = jnp.where(me == q, every[:, q * share : (q + 1) * share], mine)
        out[...] = mine
    head = 6 * layers
    for k in range(classes):
        head_w[k : k + 1, :] = line(head + k)
    last = line(head + classes)
    head_b[...] = last[:, 0:classes]
    loss[...] = last[:, classes : classes + 1] / ndp
    for k in range(4):
        source, target = refs[k], refs[5 + k]
        step = 16

        def move(i, carry, source=source, target=target, step=step):
            rows = pl.ds(pl.multiple_of(i * step, step), step)
            target[rows, :] = source[rows, :]
            return carry

        lax.fori_loop(0, source.shape[0] // step, move, 0, unroll=4)


def finish_outputs(dims, grad_inputs, small, b_grad, g_grad, c_grad):
    layers, tok, width, states, classes, ndp, nseq = dims
    vmem = pl.BlockSpec(memory_space=pltpu.VMEM)
    large = [a.reshape(-1, a.shape[-1]) for a in (grad_inputs, b_grad, g_grad, c_grad)]
    share = states // nseq
    rows = (layers, width)
    shapes = [(1, 1), rows, rows, (layers, share), (layers, share), rows, rows, (classes, width)]
    shapes.append((1, classes))
    results = pl.pallas_call(
        partial(finish_kernel, dims),
        out_shape=[jax.ShapeDtypeStruct(a.shape, F32) for a in large]
        + [jax.ShapeDtypeStruct(shape, F32) for shape in shapes],
        in_specs=[vmem] * 5,
        out_specs=[vmem] * 13,
        compiler_params=pltpu.CompilerParams(vmem_limit_bytes=16 * 1024 * 1024),
    )(*large, small)
    gin, b_share, g_share, c_share, loss, gain, bias, rate, phase, skip, glub, head_w, head_b = results
    return (
        loss.reshape(()),
        gin.reshape((1,) + grad_inputs.shape),
        gain,
        bias,
        b_share.reshape(b_grad.shape),
        rate,
        phase,
        c_share.reshape(c_grad.shape),
        skip,
        g_share.reshape(g_grad.shape),
        glub,
        head_w.T,
        head_b.reshape(classes),
    )


def per_device(
    inputs,
    lengths,
    labels,
    norm_gain,
    norm_bias,
    b_proj,
    rate,
    phase,
    c_proj,
    skip,
    glu_weight,
    glu_bias,
    class_weight,
    class_bias,
):
    layers, width = norm_gain.shape
    tok = inputs.shape[1]
    ndp = lax.axis_size("dp")
    nseq = lax.axis_size("seq")
    states = c_proj.shape[2] * nseq
    classes = class_bias.shape[0]
    dims = (layers, tok, width, states, classes, ndp, nseq)
    share = states // nseq
    inside = (
        ndp == 4
        and nseq % 2 == 0
        and share % 16 == 0
        and (width // ndp) % 128 == 0
        and (width // ndp) % (16 * nseq) == 0
        and 4 * layers == 8
    )
    if inside:
        tables = (rate, phase)
        weights = (b_proj, glu_weight, c_proj)
    else:
        decay = jnp.exp(-rate)
        in_scale = jnp.sqrt(-jnp.expm1(-2.0 * rate))
        rows = [
            decay * jnp.cos(phase),
            decay * jnp.sin(phase),
            in_scale,
            jnp.exp(-2.0 * rate) / in_scale,
        ]
        table = lax.all_gather(jnp.stack(rows, axis=1), "seq", axis=2, tiled=True)
        tables = (table, phase)
        b_full = lax.all_gather(b_proj.astype(BF16), "dp", axis=1, tiled=True)
        g_full = lax.all_gather(glu_weight.astype(BF16), "dp", axis=1, tiled=True)
        c_half = lax.all_gather(c_proj.astype(BF16), "dp", axis=3, tiled=True)
        c_full = lax.all_gather(c_half, "seq", axis=2, tiled=True)
        c_full = c_full.reshape(layers, 4, states, 2, width // 2)
        c_full = jnp.moveaxis(c_full, 3, 1)
        weights = (b_full, g_full, c_full)
    grad_inputs, small, b_grad, g_grad, c_grad = run_model(
        dims,
        inside,
        (
            lengths,
            labels,
            class_bias,
            inputs[0],
            norm_gain,
            norm_bias,
            skip,
            glu_bias,
            *tables,
            class_weight.T,
            *weights,
        ),
    )
    if inside:
        return finish_outputs(dims, grad_inputs, small, b_grad, g_grad, c_grad)
    else:
        b_share = lax.psum_scatter(b_grad, "dp", scatter_dimension=1, tiled=True)
        g_share = lax.psum_scatter(g_grad, "dp", scatter_dimension=1, tiled=True)
        b_share = lax.psum(b_share, "seq").astype(F32)
        g_share = lax.psum(g_share, "seq").astype(F32)
        c_grad = c_grad.reshape(layers, 4, states, width)
        c_share = lax.psum_scatter(c_grad, "seq", scatter_dimension=2, tiled=True)
        c_share = lax.psum_scatter(c_share, "dp", scatter_dimension=3, tiled=True).astype(F32)
        small = lax.psum(small, ("dp", "seq"))
    small = small.reshape(-1, width)
    own = lax.axis_index("seq") * (states // nseq)

    def state_rows(first):
        return lax.dynamic_slice(small[first : first + layers], (0, own), (layers, states // nseq))

    head = 6 * layers
    return (
        small[head + classes, classes] / ndp,
        grad_inputs[None],
        small[0:layers],
        small[layers : 2 * layers],
        b_share,
        state_rows(4 * layers),
        state_rows(5 * layers),
        c_share,
        small[2 * layers : 3 * layers],
        g_share,
        small[3 * layers : 4 * layers],
        small[head : head + classes].T,
        small[head + classes, 0:classes],
    )


def solution(mesh):
    return jax.shard_map(
        per_device,
        mesh=mesh,
        in_specs=(
            P("dp", "seq", None),
            P("dp"),
            P("dp"),
            P(),
            P(),
            P(None, "dp", None),
            P(None, "seq"),
            P(None, "seq"),
            P(None, None, "seq", "dp"),
            P(),
            P(None, "dp", None),
            P(),
            P(),
            P(),
        ),
        out_specs=(
            P(),
            P("dp", "seq", None),
            P(),
            P(),
            P(None, "dp", None),
            P(None, "seq"),
            P(None, "seq"),
            P(None, None, "seq", "dp"),
            P(),
            P(None, "dp", None),
            P(),
            P(),
            P(),
        ),
        check_vma=False,
    )
```

```python
from functools import partial
from typing import Any, NamedTuple

import jax
import jax.numpy as jnp
from jax import lax
from jax.experimental import pallas as pl
from jax.experimental.pallas import tpu as pltpu
from jax.sharding import PartitionSpec as P

MESH = pl.DeviceIdType.MESH
F32 = jnp.float32
BF16 = jnp.bfloat16
CHUNKS = 8
TILE = 32
GELU_A = 0.7978845608028654
GELU_B = 0.044715


def mm_nn(left, right):
    return lax.dot_general(left, right, (((1,), (0,)), ((), ())), preferred_element_type=F32)


def mm_nt(left, right):
    return lax.dot_general(left, right, (((1,), (1,)), ((), ())), preferred_element_type=F32)


def mm_tn(left, right):
    return lax.dot_general(left, right, (((0,), (0,)), ((), ())), preferred_element_type=F32)


def cmul(a_re, a_im, b_re, b_im):
    return a_re * b_re - a_im * b_im, a_re * b_im + a_im * b_re


def fold8(value):
    total = value[0:8]
    for first in range(8, value.shape[0], 8):
        total = total + value[first : first + 8]
    return total


class Operands(NamedTuple):
    len: Any
    lab: Any
    cb: Any
    x: Any
    gain: Any
    bias: Any
    skip: Any
    glub: Any
    rate: Any
    phase: Any
    cw: Any
    b_in: Any
    glu_in: Any
    c_in: Any


class Results(NamedTuple):
    gin: Any
    small_out: Any
    b_out: Any
    glu_out: Any
    c_out: Any


class Local(NamedTuple):
    stream: Any
    xhat: Any
    rstd: Any
    nlow: Any
    drive: Any
    caus: Any
    anti: Any
    feat: Any
    gelu_out: Any
    gelu_low: Any
    gelu_der: Any
    sig: Any
    wide: Any
    temp: Any
    mix: Any
    mlow: Any
    ggrad: Any
    dlow: Any
    perm: Any
    send_buf: Any
    recv_buf: Any
    send_sem: Any
    recv_sem: Any


class Shared(NamedTuple):
    tab: Any
    tab_recv: Any
    b_buf: Any
    glu_buf: Any
    c_buf: Any
    ssem: Any
    rsem: Any
    small: Any
    small_core: Any
    small_y: Any
    small_sum: Any
    small_recv: Any


class RowGrad(NamedTuple):
    snd1: Any
    rcv1: Any
    acc: Any
    snd2: Any
    rcv2: Any
    acc2: Any
    snd3: Any
    rcv3: Any
    acc3: Any
    snd4: Any
    rcv4: Any
    full: Any


class ColGrad(NamedTuple):
    snd1: Any
    rcv1: Any
    acc: Any
    snd2a: Any
    rcv2a: Any
    acc2a: Any
    snd2b: Any
    rcv2b: Any
    acc2b: Any
    snd3: Any
    rcv3: Any
    acc3: Any
    snd4: Any
    rcv4: Any


def take(refs, kind):
    count = len(kind._fields)
    return kind(*refs[:count]), refs[count:]


def model_kernel(dims, inside, *refs):
    layers, tok, width, states, classes, ndp, nseq = dims
    given, refs = take(refs, Operands)
    O, refs = take(refs, Results)
    fetched, refs = refs[: len(given) - 3], refs[len(given) - 3 :]
    fetch_sem, refs = refs[0], refs[1:]
    I = Operands(*given[:3], *fetched)
    L, refs = take(refs, Local)
    if inside:
        S, refs = take(refs, Shared)
        BG, refs = take(refs, RowGrad)
        GG, refs = take(refs, RowGrad)
        CG, refs = take(refs, ColGrad)
        tab_ref, b_ref, glu_ref, c_ref, small_ref = S.tab, S.b_buf, S.glu_buf, S.c_buf, S.small
    else:
        tab_ref, b_ref, glu_ref, c_ref, small_ref = I.rate, I.b_in, I.glu_in, I.c_in, O.small_out
    len_ref, lab_ref, x_ref = I.len, I.lab, I.x
    gain_ref, bias_ref, skip_ref, glub_ref = I.gain, I.bias, I.skip, I.glub
    cw_ref, cb_ref, gin_ref = I.cw, I.cb, O.gin
    stream, xhat, rstd, nlow, drive = L.stream, L.xhat, L.rstd, L.nlow, L.drive
    caus, anti, feat, gelu_out, gelu_low = L.caus, L.anti, L.feat, L.gelu_out, L.gelu_low
    gelu_der, sig, wide, temp, mix = L.gelu_der, L.sig, L.wide, L.temp, L.mix
    mlow, ggrad, dlow, perm = L.mlow, L.ggrad, L.dlow, L.perm
    send_buf, recv_buf = L.send_buf, L.recv_buf
    send_sem, recv_sem = L.send_sem, L.recv_sem
    steps = tok // CHUNKS
    half_cols = width // 2
    me = lax.axis_index("seq")
    my_dp = lax.axis_index("dp")
    p = states
    core, yy = lax.rem(my_dp, 2), my_dp // 2
    xx, zz = lax.rem(me, 2), me // 2
    ny, nz = ndp // 2, nseq // 2
    own_half = core if inside else 0

    barrier = pltpu.get_barrier_semaphore()

    def greet(k, carry):
        peer = lax.rem(me + k, nseq)
        pl.semaphore_signal(barrier, inc=1, device_id={"seq": peer}, device_id_type=MESH)
        return carry

    lax.fori_loop(1, nseq, greet, 0)
    greeted = nseq - 1
    sibling = {"dp": 2 * yy + 1 - core}
    y_peer = {"dp": 2 * (1 - yy) + core}
    x_peer = {"seq": 2 * zz + 1 - xx}
    if inside:
        for peer in (sibling, y_peer):
            pl.semaphore_signal(barrier, inc=1, device_id=peer, device_id_type=MESH)
        greeted += 2

    fetches = [
        pltpu.make_async_copy(src, dst, fetch_sem.at[k])
        for k, (src, dst) in enumerate(zip(given[3:], fetched))
    ]
    for fetch in reversed(fetches):
        fetch.start()

    used = [0]

    def new_sems(count):
        first = used[0]
        used[0] += count
        return first

    def remote(src, dst, sem, peer):
        return pltpu.make_async_remote_copy(
            src_ref=src,
            dst_ref=dst,
            send_sem=S.ssem.at[sem],
            recv_sem=S.rsem.at[sem],
            device_id=peer,
            device_id_type=MESH,
        )

    def seq_loop(body):
        def one(k, carry):
            body(k)
            return carry

        lax.fori_loop(1, nseq, one, 0)

    def cast_rows(dst, src, rows, step, extra=None):
        def one(k, carry):
            part = pl.ds(pl.multiple_of(k * step, step), step)
            value = src[part, :].astype(F32)
            if extra is not None:
                value = value + extra[part, :].astype(F32)
            dst[part, :] = value.astype(dst.dtype)
            return carry

        lax.fori_loop(0, rows // step, one, 0, unroll=4)

    def row_loop(body, init, unroll=2):
        def step(k, carry):
            rows = pl.ds(pl.multiple_of(k * TILE, TILE), TILE)
            return body(rows, k * TILE, carry)

        return lax.fori_loop(0, tok // TILE, step, init, unroll=unroll)

    def exchange_start(slot):
        def one(k, carry):
            peer = lax.rem(me + k, nseq)
            pltpu.make_async_remote_copy(
                src_ref=send_buf.at[slot, (peer - me + nseq) // nseq],
                dst_ref=recv_buf.at[slot, k],
                send_sem=send_sem.at[slot],
                recv_sem=recv_sem.at[slot],
                device_id={"seq": peer},
                device_id_type=MESH,
            ).start()
            return carry

        lax.fori_loop(1, nseq, one, 0)

    def exchange_wait(slot):
        arrived = recv_buf.at[slot, pl.ds(1, nseq - 1)]
        pltpu.make_async_remote_copy(
            src_ref=arrived,
            dst_ref=arrived,
            send_sem=send_sem.at[slot],
            recv_sem=recv_sem.at[slot],
            device_id={"seq": lax.rem(me + 1, nseq)},
            device_id_type=MESH,
        ).wait()

    def from_rank(q):
        return lax.rem(me - q + nseq, nseq)

    sub = lax.broadcasted_iota(jnp.int32, (CHUNKS, p), 0)

    def layer_powers(layer, conj):
        lam_re = tab_ref[layer, 0:1, :]
        lam_im = tab_ref[layer, 1:2, :]
        if conj:
            lam_im = -lam_im
        pw_re, pw_im = lam_re, lam_im
        count = 1
        while count < steps:
            pw_re, pw_im = cmul(pw_re, pw_im, pw_re, pw_im)
            count *= 2
        jumps = [(pw_re, pw_im)]
        for _ in range(3):
            pw_re, pw_im = cmul(pw_re, pw_im, pw_re, pw_im)
            jumps.append((pw_re, pw_im))
        return lam_re, lam_im, jumps

    def jump_table(jumps, index):
        re = jnp.ones((CHUNKS, p), F32)
        im = jnp.zeros((CHUNKS, p), F32)
        for bit in range(3):
            new_re, new_im = cmul(re, im, jumps[bit][0], jumps[bit][1])
            has = (index & (1 << bit)) != 0
            re = jnp.where(has, new_re, re)
            im = jnp.where(has, new_im, im)
        return re, im

    def local_ends(src, first_c, first_a, lam_re, lam_im):
        zero = jnp.zeros((CHUNKS, p), F32)
        l_re = jnp.broadcast_to(lam_re, (CHUNKS, p))
        l_im = jnp.broadcast_to(lam_im, (CHUNKS, p))

        def step(j, carry):
            e_re, e_im, f_re, f_im = carry
            up = pl.ds(pl.multiple_of(j * CHUNKS, CHUNKS), CHUNKS)
            down = pl.ds(pl.multiple_of((steps - 1 - j) * CHUNKS, CHUNKS), CHUNKS)
            e_re, e_im = cmul(l_re, l_im, e_re, e_im)
            f_re, f_im = cmul(l_re, l_im, f_re, f_im)
            return (
                e_re + src[up, first_c : first_c + p],
                e_im + src[up, first_c + p : first_c + 2 * p],
                f_re + src[down, first_a : first_a + p],
                f_im + src[down, first_a + p : first_a + 2 * p],
            )

        return lax.fori_loop(0, steps, step, (zero,) * 4, unroll=4)

    def local_prefix(ends, jumps):
        e_re, e_im, f_re, f_im = ends
        for bit in range(3):
            shift = 1 << bit
            j_re, j_im = jumps[bit]
            s_re = jnp.where(sub >= shift, pltpu.roll(e_re, shift, 0), 0.0)
            s_im = jnp.where(sub >= shift, pltpu.roll(e_im, shift, 0), 0.0)
            a_re, a_im = cmul(j_re, j_im, s_re, s_im)
            e_re, e_im = e_re + a_re, e_im + a_im
            s_re = jnp.where(sub < CHUNKS - shift, pltpu.roll(f_re, CHUNKS - shift, 0), 0.0)
            s_im = jnp.where(sub < CHUNKS - shift, pltpu.roll(f_im, CHUNKS - shift, 0), 0.0)
            a_re, a_im = cmul(j_re, j_im, s_re, s_im)
            f_re, f_im = f_re + a_re, f_im + a_im
        return e_re, e_im, f_re, f_im

    def send_totals(slot, prefix):
        e_re, e_im, f_re, f_im = prefix
        last, first = slice(CHUNKS - 1, CHUNKS), slice(0, 1)
        for tile in range(p // 128):
            cols = slice(tile * 128, tile * 128 + 128)
            for row, value, part, at in (
                (tile, e_re, 1, last),
                (p // 128 + tile, e_im, 1, last),
                (tile, f_re, 0, first),
                (p // 128 + tile, f_im, 0, first),
            ):
                send_buf[slot, part, row : row + 1, :] = value[at, cols]
        exchange_start(slot)

    def chunk_carries(slot, prefix, jumps):
        e_re, e_im, f_re, f_im = prefix
        d_re, d_im = jumps[3]
        zero = jnp.zeros((1, p), F32)

        def arrived(q, first):
            rows = range(first, first + p // 128)
            return jnp.concatenate([recv_buf[slot, from_rank(q), r : r + 1, :] for r in rows], axis=1)

        def step(k, carry):
            c_re, c_im, a_re, a_im = carry
            n_re, n_im = cmul(d_re, d_im, c_re, c_im)
            use = k < me
            c_re = jnp.where(use, n_re + arrived(k, 0), c_re)
            c_im = jnp.where(use, n_im + arrived(k, p // 128), c_im)
            back = nseq - 1 - k
            n_re, n_im = cmul(d_re, d_im, a_re, a_im)
            use = back > me
            a_re = jnp.where(use, n_re + arrived(back, 0), a_re)
            a_im = jnp.where(use, n_im + arrived(back, p // 128), a_im)
            return c_re, c_im, a_re, a_im

        c_re, c_im, a_re, a_im = lax.fori_loop(0, nseq, step, (zero,) * 4)
        t_re, t_im = jump_table(jumps, sub)
        g_re, g_im = cmul(t_re, t_im, c_re, c_im)
        in_c_re = g_re + jnp.where(sub >= 1, pltpu.roll(e_re, 1, 0), 0.0)
        in_c_im = g_im + jnp.where(sub >= 1, pltpu.roll(e_im, 1, 0), 0.0)
        t_re, t_im = jump_table(jumps, CHUNKS - 1 - sub)
        g_re, g_im = cmul(t_re, t_im, a_re, a_im)
        in_a_re = g_re + jnp.where(sub < CHUNKS - 1, pltpu.roll(f_re, CHUNKS - 1, 0), 0.0)
        in_a_im = g_im + jnp.where(sub < CHUNKS - 1, pltpu.roll(f_im, CHUNKS - 1, 0), 0.0)
        return in_c_re, in_c_im, in_a_re, in_a_im

    def half_blocks(half):
        blocks = []
        for first in range(0, half_cols, 128):
            if inside:
                at = (2 * (first // part_cols) + half) * part_cols + first % part_cols
            else:
                at = half * half_cols + first
            if not isinstance(at, int):
                at = pl.multiple_of(at, 128)
            blocks.append((first, pl.ds(at, 128)))
        return blocks

    def put_line(line, row):
        for col in range(0, width, 128):
            at = line * (width // 128) + col // 128
            small_ref[at : at + 1, :] = row[:, col : col + 128]

    part_cols = width // ndp
    rows_dp = width // ndp
    share = p // nseq

    def own_rows(index):
        return pl.ds(pl.multiple_of(index * rows_dp, 16), rows_dp)

    def cast_c(layer):
        cols = pl.ds(pl.multiple_of(yy * part_cols, 128), part_cols)
        c_ref[layer, core, :, zz, xx, :, cols] = I.c_in[layer].astype(BF16)

    def cast_b(layer):
        b_ref[layer, own_rows(my_dp), :] = I.b_in[layer].astype(BF16)

    def cast_glu(layer):
        glu_ref[layer, own_rows(my_dp), :] = I.glu_in[layer].astype(BF16)

    copies, sem_of = {}, {}

    def start(name, copy):
        copies[name] = copy
        copy.start()

    def finish(name):
        copies.pop(name).wait()

    def ensure(name):
        if name in copies:
            finish(name)

    def y_cols(y):
        return pl.ds(pl.multiple_of(y * part_cols, 128), part_cols)

    def start_all(name, total, pairs):
        if name not in copies:
            sem_of[name] = new_sems(1)
            copies[name] = remote(total, total, sem_of[name], x_peer)
        for block, peer in pairs:
            remote(block, block, sem_of[name], peer).start()

    def z_peers():
        return [{"seq": 2 * lax.rem(zz + k, nz) + xx} for k in range(1, nz)]

    front, back = pl.ds(0, 2), pl.ds(2, 2)
    other_y = 1 - yy

    def c_piece(layer, planes, z, x, y):
        return c_ref.at[layer, core, planes, z, x, :, y_cols(y)]

    def c_to_z(name, layer, planes, y):
        total = c_ref.at[layer, core, planes, pl.ds(0, nz - 1), xx, :, y_cols(y)]
        block = c_piece(layer, planes, zz, xx, y)
        start_all((name, layer), total, [(block, peer) for peer in z_peers()])

    def c_to_x(layer, planes, y, others):
        if planes is front:
            name, total = 3, c_ref.at[layer, core, planes, :, xx]
        else:
            name, total = 13, c_ref.at[layer, core, planes, :, xx, :, y_cols(yy)]
        ranks = [lax.rem(zz + k, nz) for k in range(1, nz)] if others else [zz]
        pairs = [(c_piece(layer, planes, z, xx, y), x_peer) for z in ranks]
        start_all((name, layer), total, pairs)

    def one_copy(name, layer, block, peer):
        start((name, layer), remote(block, block, new_sems(1), peer))

    def cya(layer):
        one_copy(0, layer, c_piece(layer, front, zz, xx, yy), y_peer)

    def spoa(layer):
        c_to_z(1, layer, front, yy)

    def xoa(layer):
        c_to_x(layer, front, yy, False)

    def spta(layer):
        ensure((0, layer))
        c_to_z(2, layer, front, other_y)

    def xta(layer):
        ensure((0, layer))
        c_to_x(layer, front, other_y, False)

    def poa(layer):
        ensure((1, layer))
        c_to_x(layer, front, yy, True)

    def pta(layer):
        ensure((2, layer))
        c_to_x(layer, front, other_y, True)

    def caa(layer):
        ensure((1, layer))
        ensure((2, layer))
        one_copy(4, layer, c_ref.at[layer, core, front, :, xx], sibling)

    def cba(layer):
        ensure((3, layer))
        one_copy(5, layer, c_ref.at[layer, core, front, :, 1 - xx], sibling)

    def zb(layer):
        c_to_z(12, layer, back, yy)

    def xb(layer):
        c_to_x(layer, back, yy, False)

    def pb(layer):
        ensure((12, layer))
        c_to_x(layer, back, yy, True)

    def yb1(layer):
        ensure((12, layer))
        one_copy(14, layer, c_ref.at[layer, core, back, :, xx, :, y_cols(yy)], y_peer)

    def yb2(layer):
        ensure((13, layer))
        one_copy(15, layer, c_ref.at[layer, core, back, :, 1 - xx, :, y_cols(yy)], y_peer)

    def kb1(layer):
        ensure((12, layer))
        ensure((13, layer))
        one_copy(16, layer, c_ref.at[layer, core, back, :, :, :, y_cols(yy)], sibling)

    def kb2(layer):
        ensure((14, layer))
        ensure((15, layer))
        one_copy(17, layer, c_ref.at[layer, core, back, :, :, :, y_cols(other_y)], sibling)

    def c_stage_5(layer):
        for name in (4, 5, 16, 17):
            finish((name, layer))

    def row_to_y(ref, layer):
        block = ref.at[layer, own_rows(my_dp), :]
        start((id(ref), 0, layer), remote(block, block, new_sems(1), y_peer))

    def row_to_sibling(ref, layer):
        block = ref.at[layer, own_rows(my_dp), :]
        start_all((id(ref), 1, layer), ref.at[layer, pl.ds(0, 2 * rows_dp), :], [(block, sibling)])

    def row_pass(ref, layer):
        finish((id(ref), 0, layer))
        block = ref.at[layer, own_rows(2 * (1 - yy) + core), :]
        start_all((id(ref), 1, layer), ref.at[layer, pl.ds(0, 2 * rows_dp), :], [(block, sibling)])

    def row_stage_end(ref, layer):
        finish((id(ref), 1, layer))

    def table_stage():
        every, own = S.tab_recv, S.tab_recv.at[0]
        rate, phase = I.rate[...], I.phase[...]
        decay = jnp.exp(-rate)
        twice = 2.0 * rate
        series = 1.0 - twice / 7.0
        for term in (6.0, 5.0, 4.0, 3.0, 2.0):
            series = 1.0 - series * (twice / term)
        loss = jnp.where(twice < 0.25, twice * series, 1.0 - jnp.exp(-twice))
        in_scale = jnp.sqrt(loss)
        every[0] = jnp.zeros((8, 128), F32)
        parts = (decay * jnp.cos(phase), decay * jnp.sin(phase), in_scale, jnp.exp(-twice) / in_scale)
        for row, value in enumerate(parts):
            for layer in range(layers):
                at = 4 * layer + row
                every[0, at : at + 1, 0:share] = value[layer : layer + 1]
        arrived = every.at[pl.ds(1, nseq - 1)]
        sem = new_sems(1)
        copies[8, 8] = remote(arrived, arrived, sem, x_peer)

        def one(k):
            remote(own, every.at[k], sem, {"seq": lax.rem(me + k, nseq)}).start()

        seq_loop(one)

    def table_end():
        finish((8, 8))
        lane = lax.broadcasted_iota(jnp.int32, (8, 128), 1)
        tiles = [jnp.zeros((8, 128), F32) for _ in range(p // 128)]
        for q in range(nseq):
            tile, first = (q * share) // 128, (q * share) % 128
            piece = S.tab_recv[from_rank(q)]
            if first:
                piece = pltpu.roll(piece, first, 1)
            here = (lane >= first) & (lane < first + share)
            tiles[tile] = jnp.where(here, piece, tiles[tile])
            if first + share > 128:
                tiles[tile + 1] = jnp.where(lane < first + share - 128, piece, tiles[tile + 1])
        for layer in range(layers):
            for tile in range(p // 128):
                tab_ref[layer, 0:4, tile * 128 : tile * 128 + 128] = tiles[tile][
                    4 * layer : 4 * layer + 4
                ]

    early = {}
    if inside:
        early = {
            (0, 10): [
                partial(cya, 0),
                partial(row_to_y, b_ref, 0),
                partial(zb, 0),
                table_stage,
                partial(xb, 0),
                partial(row_to_y, glu_ref, 0),
                partial(xoa, 0),
                partial(spoa, 0),
            ],
            (0, 12): [
                partial(pb, 0),
                partial(row_to_sibling, b_ref, 1),
                partial(xb, 1),
                partial(xta, 0),
                partial(cya, 1),
                partial(spta, 0),
                partial(yb1, 0),
                partial(row_to_sibling, b_ref, 0),
                partial(row_pass, b_ref, 0),
                partial(zb, 1),
                table_end,
                partial(poa, 0),
                partial(spoa, 1),
                partial(row_pass, glu_ref, 0),
                partial(yb2, 0),
                partial(pta, 0),
            ],
            (0, 14): [
                partial(row_to_y, b_ref, 1),
                partial(pb, 1),
                partial(kb1, 0),
                partial(spta, 1),
                partial(yb1, 1),
            ],
            (0, 15): [
                partial(xta, 1),
                partial(kb2, 0),
                partial(cba, 0),
                partial(xoa, 1),
                partial(yb2, 1),
                partial(caa, 0),
                partial(row_to_sibling, glu_ref, 0),
                partial(poa, 1),
                partial(row_to_sibling, glu_ref, 1),
            ],
            (0, 16): [
                partial(row_to_y, glu_ref, 1),
            ],
            (0, 18): [
                partial(row_pass, b_ref, 1),
            ],
            (0, 19): [
                partial(pta, 1),
            ],
            (0, 20): [
                partial(caa, 1),
            ],
            (1, 14): [
                partial(kb1, 1),
                partial(cba, 1),
                partial(kb2, 1),
            ],
            (1, 15): [
                partial(row_pass, glu_ref, 1),
            ],
        }

    def gather(layer, point):
        for stage in early.get((layer, point), []):
            stage()

    for fetch in reversed(fetches):
        fetch.wait()
    if inside:
        for layer in range(layers):
            cast_c(layer)
            cast_b(layer)
            cast_glu(layer)
    pl.semaphore_wait(barrier, greeted)
    gather(0, 10)

    for col in range(0, width, 128):
        perm[col // 128] = x_ref[:, col : col + 128].astype(F32)

        def place(j, carry, col=col):
            rows = pl.ds(pl.multiple_of(j * CHUNKS, CHUNKS), CHUNKS)
            stream[rows, col : col + 128] = perm[col // 128, pl.ds(j, CHUNKS, stride=steps), :]
            return carry

        lax.fori_loop(0, steps, place, 0, unroll=4)

    for layer in range(layers):
        gain = gain_ref[layer : layer + 1, :]
        bias = bias_ref[layer : layer + 1, :]
        skip = skip_ref[layer : layer + 1, :]

        def norm_rows(rows, first, carry, layer=layer, gain=gain, bias=bias):
            value = stream[rows, :]
            center = value - jnp.mean(value, axis=1, keepdims=True)
            spread = jnp.mean(center * center, axis=1, keepdims=True)
            inv = lax.rsqrt(spread + 1e-05)
            hat = center * inv
            xhat[layer, rows, :] = hat
            rstd[layer, rows, :] = inv
            nlow[layer, rows, :] = (hat * gain + bias).astype(BF16)
            return carry

        if layer == 0:
            gather(0, 11)
        row_loop(norm_rows, 0)
        gather(layer, 12)

        if inside:
            row_stage_end(b_ref, layer)
        in_scale = tab_ref[layer, 2:3, :]
        for col in range(0, 2 * p, 256):
            part = mm_nn(nlow[layer], b_ref[layer, :, col : col + 256])
            for half in range(col, col + 256, 128):
                scale_col = half % p
                drive[layer, :, half : half + 128] = (
                    part[:, half - col : half - col + 128].astype(BF16).astype(F32)
                    * in_scale[:, scale_col : scale_col + 128]
                )

        lam_re, lam_im, jumps = layer_powers(layer, False)
        ends = local_ends(drive.at[layer], 0, 0, lam_re, lam_im)
        prefix = local_prefix(ends, jumps)
        gather(layer, 13)
        send_totals(layer, prefix)
        gather(layer, 14)
        exchange_wait(layer)
        gather(layer, 15)
        carries = chunk_carries(layer, prefix, jumps)
        caus[layer, 0:CHUNKS, 0:p] = carries[0]
        caus[layer, 0:CHUNKS, p : 2 * p] = carries[1]
        anti[layer, tok : tok + CHUNKS, 0:p] = carries[2]
        anti[layer, tok : tok + CHUNKS, p : 2 * p] = carries[3]
        l_re = jnp.broadcast_to(lam_re, (CHUNKS, p))
        l_im = jnp.broadcast_to(lam_im, (CHUNKS, p))

        def state_pair(k, carry, layer=layer, l_re=l_re, l_im=l_im):
            s_re, s_im, r_re, r_im = carry
            first = pl.multiple_of(k * 2 * CHUNKS, 2 * CHUNKS)
            kept_re, kept_im = [], []
            for half in range(2):
                rows = pl.ds(first + half * CHUNKS, CHUNKS)
                s_re, s_im = cmul(l_re, l_im, s_re, s_im)
                s_re = s_re + drive[layer, rows, 0:p]
                s_im = s_im + drive[layer, rows, p : 2 * p]
                after = pl.ds(first + (half + 1) * CHUNKS, CHUNKS)
                caus[layer, after, 0:p] = s_re
                caus[layer, after, p : 2 * p] = s_im
                kept_re.append(s_re)
                kept_im.append(s_im)
            both = pl.ds(first, 2 * CHUNKS)
            feat[layer, both, 0:p] = jnp.concatenate(kept_re, axis=0).astype(BF16)
            feat[layer, both, p : 2 * p] = jnp.concatenate(kept_im, axis=0).astype(BF16)
            last = pl.multiple_of(tok - (k + 1) * 2 * CHUNKS, 2 * CHUNKS)
            kept_re, kept_im = [], []
            for half in (1, 0):
                rows = pl.ds(last + half * CHUNKS, CHUNKS)
                r_re, r_im = cmul(l_re, l_im, r_re, r_im)
                r_re = r_re + drive[layer, rows, 0:p]
                r_im = r_im + drive[layer, rows, p : 2 * p]
                anti[layer, rows, 0:p] = r_re
                anti[layer, rows, p : 2 * p] = r_im
                kept_re.insert(0, r_re)
                kept_im.insert(0, r_im)
            both = pl.ds(last, 2 * CHUNKS)
            feat[layer, both, 2 * p : 3 * p] = jnp.concatenate(kept_re, axis=0).astype(BF16)
            feat[layer, both, 3 * p : 4 * p] = jnp.concatenate(kept_im, axis=0).astype(BF16)
            return s_re, s_im, r_re, r_im

        lax.fori_loop(0, steps // 2, state_pair, carries, unroll=2)

        gather(layer, 16)
        for turn in range(2):
            half = (1 - own_half) if turn else own_half
            if inside and turn:
                c_stage_5(layer)
            part = mm_nn(feat[layer], c_ref[layer, half].reshape(4 * p, half_cols))
            for first, block in half_blocks(half):
                temp[:, block] = part[:, first : first + 128]
            gather(layer, 17 + turn)

        def act_rows(rows, first, carry, layer=layer, gain=gain, bias=bias, skip=skip):
            pre = temp[rows, :] + skip * (xhat[layer, rows, :] * gain + bias)
            square = pre * pre
            th = jnp.tanh(GELU_A * pre * (1.0 + GELU_B * square))
            cdf = 0.5 * (1.0 + th)
            out = pre * cdf
            gelu_out[layer, rows, :] = out
            gelu_low[layer, rows, :] = out.astype(BF16)
            gelu_der[layer, rows, :] = cdf + 0.5 * pre * (1.0 - th * th) * (
                GELU_A * (1.0 + 3.0 * GELU_B * square)
            )
            return carry

        row_loop(act_rows, 0)
        gather(layer, 19)
        if inside:
            row_stage_end(glu_ref, layer)
        for col in range(0, width, 256):
            temp[:, col : col + 256] = mm_nn(gelu_low[layer], glu_ref[layer, :, col : col + 256])
        gather(layer, 20)
        glu_bias = glub_ref[layer : layer + 1, :]
        last_layer = layer == layers - 1

        def gate_rows(rows, first, carry, layer=layer, glu_bias=glu_bias, last_layer=last_layer):
            gate = 1.0 / (1.0 + jnp.exp(-(temp[rows, :] + glu_bias)))
            sig[layer, rows, :] = gate
            new = stream[rows, :] + gelu_out[layer, rows, :] * gate
            if not last_layer:
                stream[rows, :] = new
                return carry
            return carry + fold8(new * row_mask(first))

        def row_mask(first):
            row = first + lax.broadcasted_iota(jnp.int32, (TILE, 1), 0)
            position = me * tok + (row & (CHUNKS - 1)) * steps + (row >> 3)
            return jnp.where(position < len_ref[0], 1.0, 0.0).astype(F32)

        pooled_part = row_loop(gate_rows, jnp.zeros((CHUNKS, width), F32) if last_layer else 0)
        gather(layer, 21)

    pool_slot = 2 * layers
    own_sum = jnp.sum(pooled_part, axis=0, keepdims=True)
    for part in range(2):
        for tile in range(width // 128):
            cols = slice(tile * 128, tile * 128 + 128)
            send_buf[pool_slot, part, tile : tile + 1, :] = own_sum[:, cols]
    exchange_start(pool_slot)
    exchange_wait(pool_slot)

    def add_pool(k, total):
        rows = [recv_buf[pool_slot, from_rank(k), r : r + 1, :] for r in range(width // 128)]
        return total + jnp.where(k == me, 0.0, jnp.concatenate(rows, axis=1))

    pooled_sum = lax.fori_loop(0, nseq, add_pool, own_sum)
    len_row = jnp.full((1, 1), len_ref[0], jnp.int32).astype(F32)
    pooled = pooled_sum / len_row
    logit = [
        jnp.sum(pooled * cw_ref[k : k + 1, :], axis=1, keepdims=True) + jnp.full((1, 1), cb_ref[k], F32)
        for k in range(classes)
    ]
    top = logit[0]
    for k in range(1, classes):
        top = jnp.maximum(top, logit[k])
    expo = [jnp.exp(v - top) for v in logit]
    norm = expo[0]
    for k in range(1, classes):
        norm = norm + expo[k]
    hot = [jnp.where(lab_ref[0] == k, 1.0, 0.0).astype(F32) for k in range(classes)]
    cross = top + jnp.log(norm)
    for k in range(classes):
        cross = cross - hot[k] * logit[k]
    lgrad = [len_row * (expo[k] / norm - hot[k]) for k in range(classes)]
    pooled_grad = lgrad[0] * cw_ref[0:1, :]
    for k in range(1, classes):
        pooled_grad = pooled_grad + lgrad[k] * cw_ref[k : k + 1, :]
    grad_row = pooled_grad / len_row
    once = jnp.where(me == 0, 1.0, 0.0).astype(F32)
    small_ref[...] = jnp.zeros(small_ref.shape, F32)
    head_row = 6 * layers
    lane = lax.broadcasted_iota(jnp.int32, (1, width), 1)
    bias_line = jnp.zeros((1, width), F32)
    for k in range(classes):
        put_line(head_row + k, pooled * lgrad[k] * once)
        bias_line = jnp.where(lane == k, lgrad[k] * once, bias_line)
    bias_line = jnp.where(lane == classes, cross * once, bias_line)
    put_line(head_row + classes, bias_line)

    groups = 4 * nz

    def loop(count, body):
        def one(k, carry):
            body(k)
            return carry

        lax.fori_loop(0, count, one, 0, unroll=4)

    def c_grad_start(layer, part):
        rows = feat[layer, :, part * 2 * p : (part + 1) * 2 * p]
        value = mm_tn(rows, mlow[1 - core]).reshape(groups, share, half_cols)
        CG.snd1[layer, part] = value.astype(BF16)
        copy = remote(CG.snd1.at[layer, part], CG.rcv1.at[layer, part], new_sems(1), sibling)
        start((6, layer, part), copy)
        CG.acc[layer, part] = mm_tn(rows, mlow[core]).reshape(groups, share, half_cols)

    def c_grad_first(layer, part):
        finish((6, layer, part))
        acc, rcv = CG.acc.at[layer, part], CG.rcv1.at[layer, part]
        if part == 0:

            def put(dst, cols):
                def one(g):
                    value = acc[g, :, cols] + rcv[g, :, cols].astype(F32)
                    dst[layer, g] = value.astype(dst.dtype)

                loop(groups, one)

            put(CG.snd2a, y_cols(1 - yy))
            copy = remote(CG.snd2a.at[layer], CG.rcv2a.at[layer], new_sems(1), y_peer)
            start((7, layer, part), copy)
            put(CG.acc2a, y_cols(yy))
        else:

            def put(dst, x):
                def one(h):
                    value = acc[2 * h + x] + rcv[2 * h + x].astype(F32)
                    dst[layer, h] = value.astype(dst.dtype)

                loop(groups // 2, one)

            put(CG.snd2b, 1 - xx)
            copy = remote(CG.snd2b.at[layer], CG.rcv2b.at[layer], new_sems(1), x_peer)
            start((7, layer, part), copy)
            put(CG.acc2b, xx)

    def c_grad_second(layer, part):
        finish((7, layer, part))
        if part == 0:

            def put(dst, x):
                def one(h):
                    value = CG.acc2a[layer, 2 * h + x] + CG.rcv2a[layer, 2 * h + x].astype(F32)
                    dst[layer, part, h] = value.astype(dst.dtype)

                loop(groups // 2, one)

            away, keep, peer = 1 - xx, xx, x_peer
        else:

            def put(dst, cols):
                def one(h):
                    value = CG.acc2b[layer, h, :, cols] + CG.rcv2b[layer, h, :, cols].astype(F32)
                    dst[layer, part, h] = value.astype(dst.dtype)

                loop(groups // 2, one)

            away, keep, peer = y_cols(1 - yy), y_cols(yy), y_peer
        put(CG.snd3, away)
        copy = remote(CG.snd3.at[layer, part], CG.rcv3.at[layer, part], new_sems(1), peer)
        start((8, layer, part), copy)
        put(CG.acc3, keep)

    def spread_z(name, src, dst):
        arrived = dst.at[pl.ds(1, nz - 1)]
        sem = new_sems(1)
        copies[name] = remote(arrived, arrived, sem, x_peer)
        for k in range(1, nz):
            peer = lax.rem(zz + k, nz)
            remote(src(peer), dst.at[k], sem, {"seq": 2 * peer + xx}).start()

    def c_grad_third(layer, part):
        finish((8, layer, part))

        def one(h):
            value = CG.acc3[layer, part, h] + CG.rcv3[layer, part, h].astype(F32)
            CG.acc3[layer, part, h] = value
            CG.snd4[layer, part, lax.rem(h, nz), h // nz] = value.astype(BF16)

        loop(groups // 2, one)
        snd = CG.snd4.at[layer, part]
        spread_z((9, layer, part), lambda peer: snd.at[peer], CG.rcv4.at[layer, part])

    def c_grad_end(layer, part):
        finish((9, layer, part))
        for plane in range(2):
            value = CG.acc3[layer, part, plane * nz + zz]
            for k in range(1, nz):
                value = value + CG.rcv4[layer, part, k, plane].astype(F32)
            O.c_out[layer, 2 * part + plane] = value

    def row_grad_start(G, layer):
        left, right = (gelu_low, ggrad) if G is GG else (nlow, dlow)
        for y in range(ny):
            block = left[layer, :, own_rows(2 * y + 1 - core)]
            G.snd1[layer, y] = mm_tn(block, right[...]).astype(BF16)
        copy = remote(G.snd1.at[layer], G.rcv1.at[layer], new_sems(1), sibling)
        start((id(G), 0, layer), copy)
        for y in range(ny):
            block = left[layer, :, own_rows(2 * y + core)]
            G.acc[layer, y] = mm_tn(block, right[...])

    def row_grad_y(G, layer):
        finish((id(G), 0, layer))
        acc, rcv = G.acc.at[layer], G.rcv1.at[layer]
        cast_rows(G.snd2.at[layer], acc.at[1 - yy], rows_dp, 32, rcv.at[1 - yy])
        copy = remote(G.snd2.at[layer], G.rcv2.at[layer], new_sems(1), y_peer)
        start((id(G), 1, layer), copy)
        cast_rows(G.acc2.at[layer], acc.at[yy], rows_dp, 32, rcv.at[yy])

    piece = rows_dp // nseq

    def row_grad_x(G, layer):
        finish((id(G), 1, layer))

        def put(dst, x):
            def one(z):
                rows = pl.ds(pl.multiple_of((2 * z + x) * piece, 16), piece)
                value = G.acc2[layer, rows, :] + G.rcv2[layer, rows, :].astype(F32)
                dst[layer, z] = value.astype(dst.dtype)

            loop(nz, one)

        put(G.snd3, 1 - xx)
        start((id(G), 2, layer), remote(G.snd3.at[layer], G.rcv3.at[layer], new_sems(1), x_peer))
        put(G.acc3, xx)

    def row_grad_z(G, layer):
        finish((id(G), 2, layer))

        def one(z):
            value = G.acc3[layer, z] + G.rcv3[layer, z].astype(F32)
            G.acc3[layer, z] = value
            G.snd4[layer, z] = value.astype(BF16)

        loop(nz, one)
        snd = G.snd4.at[layer]
        spread_z((id(G), 3, layer), lambda peer: snd.at[peer], G.rcv4.at[layer])

    def row_grad_back_z(G, layer):
        finish((id(G), 3, layer))
        value = G.acc3[layer, zz]
        for k in range(1, nz):
            value = value + G.rcv4[layer, k].astype(F32)
        G.full[layer, zz, xx] = value.astype(BF16)
        block = G.full.at[layer, zz, xx]
        total = G.full.at[layer, pl.ds(0, nz - 1), xx]
        start_all((id(G), 4, layer), total, [(block, peer) for peer in z_peers()])

    def row_grad_back_x(G, layer):
        finish((id(G), 4, layer))
        block = G.full.at[layer, :, xx]
        start((id(G), 5, layer), remote(block, block, new_sems(1), x_peer))

    def row_grad_end(G, layer):
        finish((id(G), 5, layer))
        out = O.b_out if G is BG else O.glu_out

        def one(z):
            for x in range(2):
                rows = pl.ds(pl.multiple_of((2 * z + x) * piece, 16), piece)
                out[layer, rows, :] = G.full[layer, z, x].astype(F32)

        loop(nz, one)

    small_rows = small_ref.shape[0]
    small_piece = small_rows // nseq

    def small_start():
        start((8, 0), remote(small_ref, S.small_core, new_sems(1), sibling))

    def small_y():
        finish((8, 0))
        S.small_sum[0] = small_ref[...] + S.small_core[...]
        start((8, 1), remote(S.small_sum.at[0], S.small_y, new_sems(1), y_peer))

    def small_part(q):
        return pl.ds(pl.multiple_of(q * small_piece, 8), small_piece)

    def small_spread(name, src, dst, wait_ref):
        sem = new_sems(1)
        copies[name] = remote(wait_ref, wait_ref, sem, x_peer)

        def one(k):
            peer = lax.rem(me + k, nseq)
            remote(src(peer), dst(k), sem, {"seq": peer}).start()

        seq_loop(one)

    def small_scatter():
        finish((8, 1))
        S.small_sum[1] = S.small_sum[0] + S.small_y[...]
        small_spread(
            (8, 2),
            lambda peer: S.small_sum.at[1, small_part(peer), :],
            lambda k: S.small_recv.at[k],
            S.small_recv.at[pl.ds(1, nseq - 1)],
        )

    def small_gather():
        finish((8, 2))
        value = S.small_sum[1, small_part(me), :]
        for k in range(1, nseq):
            value = value + S.small_recv[k]
        S.small_sum[2, small_part(me), :] = value
        block = S.small_sum.at[2, small_part(me), :]
        small_spread(
            (8, 3), lambda peer: block, lambda k: block, S.small_recv.at[pl.ds(1, nseq - 1)]
        )

    def small_end():
        finish((8, 3))
        O.small_out[...] = S.small_sum[2]

    order = {}
    if inside:
        order = {
            (1, 0): [
                partial(row_grad_start, GG, 1),
            ],
            (1, 2): [
                partial(row_grad_y, GG, 1),
            ],
            (1, 3): [
                partial(c_grad_start, 1, 0),
                partial(c_grad_start, 1, 1),
                partial(c_grad_first, 1, 0),
            ],
            (1, 4): [
                partial(c_grad_first, 1, 1),
            ],
            (1, 5): [
                partial(row_grad_start, BG, 1),
            ],
            (1, 6): [
                partial(row_grad_x, GG, 1),
            ],
            (0, 0): [
                partial(row_grad_y, BG, 1),
                partial(row_grad_start, GG, 0),
            ],
            (0, 3): [
                partial(c_grad_start, 0, 0),
                partial(row_grad_y, GG, 0),
                partial(c_grad_second, 1, 0),
                partial(c_grad_start, 0, 1),
            ],
            (0, 5): [
                partial(row_grad_z, GG, 1),
                partial(row_grad_start, BG, 0),
                partial(row_grad_x, BG, 1),
                partial(c_grad_third, 1, 0),
                partial(row_grad_y, BG, 0),
            ],
            (0, 6): [
                partial(row_grad_x, GG, 0),
                partial(row_grad_back_z, GG, 1),
                small_start,
            ],
            (0, 7): [
                partial(c_grad_first, 0, 1),
                partial(row_grad_z, BG, 1),
                small_y,
                partial(c_grad_end, 1, 0),
                partial(c_grad_first, 0, 0),
                partial(row_grad_z, GG, 0),
                partial(row_grad_x, BG, 0),
                small_scatter,
                partial(row_grad_back_z, BG, 1),
                partial(row_grad_back_x, GG, 1),
                partial(row_grad_back_z, GG, 0),
                partial(c_grad_second, 0, 1),
                partial(row_grad_z, BG, 0),
                small_gather,
                partial(c_grad_second, 1, 1),
                partial(c_grad_second, 0, 0),
                partial(c_grad_third, 0, 1),
                partial(row_grad_back_x, BG, 1),
                partial(row_grad_back_z, BG, 0),
                partial(c_grad_third, 1, 1),
                partial(row_grad_back_x, GG, 0),
                partial(row_grad_end, BG, 1),
                small_end,
                partial(row_grad_end, GG, 1),
                partial(row_grad_end, GG, 0),
                partial(c_grad_third, 0, 0),
                partial(row_grad_back_x, BG, 0),
                partial(c_grad_end, 0, 1),
                partial(c_grad_end, 1, 1),
                partial(c_grad_end, 0, 0),
                partial(row_grad_end, BG, 0),
            ],
        }

    def stages(layer, point):
        for stage in order.get((layer, point), []):
            stage()

    grad = stream

    def first_grad(rows, first, carry):
        grad[rows, :] = row_mask(first) * grad_row
        return carry

    row_loop(first_grad, 0)

    for layer in reversed(range(layers)):
        gain = gain_ref[layer : layer + 1, :]
        bias = bias_ref[layer : layer + 1, :]
        skip = skip_ref[layer : layer + 1, :]
        zero_sum = jnp.zeros((CHUNKS, width), F32)

        def gate_back(rows, first, total, layer=layer):
            gate = sig[layer, rows, :]
            low = (grad[rows, :] * gelu_out[layer, rows, :] * gate * (1.0 - gate)).astype(BF16)
            ggrad[rows, :] = low
            return total + fold8(low.astype(F32))

        total = row_loop(gate_back, zero_sum)
        stages(layer, 0)
        put_line(3 * layers + layer, jnp.sum(total, axis=0, keepdims=True))
        for col in range(0, width, 256):
            temp[:, col : col + 256] = mm_nt(ggrad[...], glu_ref[layer, col : col + 256, :])

        def mix_back(rows, first, total, layer=layer, gain=gain, bias=bias):
            act = grad[rows, :] * sig[layer, rows, :] + temp[rows, :]
            value = act * gelu_der[layer, rows, :]
            mix[rows, :] = value
            for h in range(2):
                for first, block in half_blocks(h):
                    at = block.start
                    mlow[h, rows, first : first + 128] = value[:, at : at + 128].astype(BF16)
            return total + fold8(value * (xhat[layer, rows, :] * gain + bias))

        total = row_loop(mix_back, zero_sum)
        put_line(2 * layers + layer, jnp.sum(total, axis=0, keepdims=True))
        stages(layer, 1)
        for plane in range(0, 4, 2):
            rows = [c_ref[layer, h, plane : plane + 2].reshape(2 * p, half_cols) for h in range(2)]
            wide[:, plane * p : (plane + 2) * p] = mm_nt(mlow[0], rows[0]) + mm_nt(mlow[1], rows[1])

        lam_re, lam_im, jumps = layer_powers(layer, True)
        ends = local_ends(wide, 2 * p, 0, lam_re, lam_im)
        prefix = local_prefix(ends, jumps)
        stages(layer, 2)
        slot = layers + layer
        send_totals(slot, prefix)
        stages(layer, 3)
        if not inside:
            for h in range(2):
                for col in range(0, 4 * p, 2 * p):
                    O.c_out[layer, col : col + 2 * p, h * half_cols : (h + 1) * half_cols] = mm_tn(
                        feat[layer, :, col : col + 2 * p], mlow[h]
                    ).astype(BF16)
            for col in range(0, width, 256):
                O.glu_out[layer, col : col + 256, :] = mm_tn(
                    gelu_low[layer, :, col : col + 256], ggrad[...]
                ).astype(BF16)
        exchange_wait(slot)
        stages(layer, 4)
        carries = chunk_carries(slot, prefix, jumps)
        l_re = jnp.broadcast_to(lam_re, (CHUNKS, p))
        l_im = jnp.broadcast_to(lam_im, (CHUNKS, p))
        zero = jnp.zeros((CHUNKS, p), F32)

        def anti_grad(j, carry, layer=layer, l_re=l_re, l_im=l_im):
            r_re, r_im, d_re, d_im = carry
            rows = pl.ds(pl.multiple_of(j * CHUNKS, CHUNKS), CHUNKS)
            after = pl.ds(pl.multiple_of((j + 1) * CHUNKS, CHUNKS), CHUNKS)
            r_re, r_im = cmul(l_re, l_im, r_re, r_im)
            r_re = r_re + wide[rows, 2 * p : 3 * p]
            r_im = r_im + wide[rows, 3 * p : 4 * p]
            wide[rows, 2 * p : 3 * p] = r_re
            wide[rows, 3 * p : 4 * p] = r_im
            q_re = anti[layer, after, 0:p]
            q_im = anti[layer, after, p : 2 * p]
            return r_re, r_im, d_re + (r_re * q_re + r_im * q_im), d_im + (r_im * q_re - r_re * q_im)

        _, _, d_re, d_im = lax.fori_loop(
            0, steps, anti_grad, (carries[0], carries[1], zero, zero), unroll=4
        )
        in_scale = jnp.broadcast_to(tab_ref[layer, 2:3, :], (CHUNKS, p))

        def caus_grad(k, carry, layer=layer, l_re=l_re, l_im=l_im, in_scale=in_scale):
            a_re, a_im, d_re, d_im, s_sum = carry
            last = pl.multiple_of(tok - (k + 1) * 2 * CHUNKS, 2 * CHUNKS)
            kept_re, kept_im = [], []
            for half in (1, 0):
                rows = pl.ds(last + half * CHUNKS, CHUNKS)
                a_re, a_im = cmul(l_re, l_im, a_re, a_im)
                a_re = a_re + wide[rows, 0:p]
                a_im = a_im + wide[rows, p : 2 * p]
                q_re = caus[layer, rows, 0:p]
                q_im = caus[layer, rows, p : 2 * p]
                d_re = d_re + (a_re * q_re + a_im * q_im)
                d_im = d_im + (a_im * q_re - a_re * q_im)
                t_re = a_re + wide[rows, 2 * p : 3 * p]
                t_im = a_im + wide[rows, 3 * p : 4 * p]
                s_sum = s_sum + (
                    t_re * drive[layer, rows, 0:p] + t_im * drive[layer, rows, p : 2 * p]
                )
                kept_re.insert(0, t_re * in_scale)
                kept_im.insert(0, t_im * in_scale)
            both = pl.ds(last, 2 * CHUNKS)
            dlow[both, 0:p] = jnp.concatenate(kept_re, axis=0).astype(BF16)
            dlow[both, p : 2 * p] = jnp.concatenate(kept_im, axis=0).astype(BF16)
            return a_re, a_im, d_re, d_im, s_sum

        _, _, d_re, d_im, s_sum = lax.fori_loop(
            0, steps // 2, caus_grad, (carries[2], carries[3], d_re, d_im, zero), unroll=2
        )
        d_re = jnp.sum(d_re, axis=0, keepdims=True)
        d_im = jnp.sum(d_im, axis=0, keepdims=True)
        s_sum = jnp.sum(s_sum, axis=0, keepdims=True) / tab_ref[layer, 2:3, :]
        true_re = tab_ref[layer, 0:1, :]
        true_im = tab_ref[layer, 1:2, :]
        pad = jnp.zeros((1, width - p), F32)
        rate_part = s_sum * tab_ref[layer, 3:4, :] - d_re * true_re - d_im * true_im
        put_line(4 * layers + layer, jnp.concatenate([rate_part, pad], axis=1))
        phase_part = d_im * true_re - d_re * true_im
        put_line(5 * layers + layer, jnp.concatenate([phase_part, pad], axis=1))

        stages(layer, 5)
        if not inside:
            for col in range(0, width, 256):
                O.b_out[layer, col : col + 256, :] = mm_tn(
                    nlow[layer, :, col : col + 256], dlow[...]
                ).astype(BF16)
        for col in range(0, width, 256):
            temp[:, col : col + 256] = mm_nt(dlow[...], b_ref[layer, col : col + 256, :])

        def norm_back(rows, first, carry, layer=layer, gain=gain, skip=skip):
            gain_sum, bias_sum = carry
            ngrad = mix[rows, :] * skip + temp[rows, :]
            hat = xhat[layer, rows, :]
            q = ngrad * gain
            mean_q = jnp.mean(q, axis=1, keepdims=True)
            mean_x = jnp.mean(q * hat, axis=1, keepdims=True)
            grad[rows, :] = grad[rows, :] + (q - mean_q - hat * mean_x) * rstd[layer, rows, :]
            return gain_sum + fold8(ngrad * hat), bias_sum + fold8(ngrad)

        gain_sum, bias_sum = row_loop(norm_back, (zero_sum, zero_sum))
        put_line(layer, jnp.sum(gain_sum, axis=0, keepdims=True))
        put_line(layers + layer, jnp.sum(bias_sum, axis=0, keepdims=True))
        stages(layer, 6)

    for col in range(0, width, 128):
        perm[col // 128] = grad[:, col : col + 128]

        def unplace(k, carry, col=col):
            first = k * CHUNKS
            chunk = first // steps
            rows = pl.ds((first - chunk * steps) * CHUNKS + chunk, CHUNKS, stride=CHUNKS)
            out = pl.ds(pl.multiple_of(first, CHUNKS), CHUNKS)
            gin_ref[out, col : col + 128] = perm[col // 128, rows, :]
            return carry

        lax.fori_loop(0, steps, unplace, 0, unroll=4)

    stages(0, 7)


def run_model(dims, inside, operands):
    layers, tok, width, states, classes, ndp, nseq = dims
    vmem = pl.BlockSpec(memory_space=pltpu.VMEM)
    smem = pl.BlockSpec(memory_space=pltpu.SMEM)
    hbm = pl.BlockSpec(memory_space=pltpu.HBM)
    lines = -(-(6 * layers + classes + 1) // 8) * 8
    small_shape = (lines * width // 128, 128)
    slots = 2 * layers + 1
    share, rows_dp = states // nseq, width // ndp
    per_layer = lambda cols, kind, rows=tok: pltpu.VMEM((layers, rows, cols), kind)
    if inside:
        b_shape, g_shape = (layers, rows_dp, 2 * states), (layers, rows_dp, width)
        c_shape, kind = (layers, 4, share, width // ndp), F32
    else:
        b_shape, g_shape = (layers, width, 2 * states), (layers, width, width)
        c_shape, kind = (layers, 4 * states, width), BF16
    scratch = [pltpu.VMEM(a.shape, a.dtype) for a in operands[3:]]
    scratch += [
        pltpu.SemaphoreType.DMA((len(operands) - 3,)),
        pltpu.VMEM((tok, width), F32),
        per_layer(width, F32),
        per_layer(1, F32),
        per_layer(width, BF16),
        per_layer(2 * states, F32),
        per_layer(2 * states, F32, tok + CHUNKS),
        per_layer(2 * states, F32, tok + CHUNKS),
        per_layer(4 * states, BF16),
        per_layer(width, F32),
        per_layer(width, BF16),
        per_layer(width, F32),
        per_layer(width, F32),
        pltpu.VMEM((tok, 4 * states), F32),
        pltpu.VMEM((tok, width), F32),
        pltpu.VMEM((tok, width), F32),
        pltpu.VMEM((2, tok, width // 2), BF16),
        pltpu.VMEM((tok, width), BF16),
        pltpu.VMEM((tok, 2 * states), BF16),
        pltpu.VMEM((width // 128, tok, 128), F32),
        pltpu.VMEM((slots, 2, 8, 128), F32),
        pltpu.VMEM((slots, nseq, 8, 128), F32),
        pltpu.SemaphoreType.DMA((slots,)),
        pltpu.SemaphoreType.DMA((slots,)),
    ]
    if inside:
        ny, nz, part, half = ndp // 2, nseq // 2, width // ndp, width // 2
        copies = 80
        scratch += [
            pltpu.VMEM((layers, 8, states), F32),
            pltpu.VMEM((nseq, 8, 128), F32),
            per_layer(2 * states, BF16, width),
            per_layer(width, BF16, width),
            pltpu.VMEM((layers, 2, 4, nz, 2, share, half), BF16),
            pltpu.SemaphoreType.DMA((copies,)),
            pltpu.SemaphoreType.DMA((copies,)),
            pltpu.VMEM(small_shape, F32),
            pltpu.VMEM(small_shape, F32),
            pltpu.VMEM(small_shape, F32),
            pltpu.VMEM((3,) + small_shape, F32),
            pltpu.VMEM((nseq, small_shape[0] // nseq, 128), F32),
        ]
        for cols in (2 * states, width):
            scratch += [
                pltpu.VMEM((layers, ny, rows_dp, cols), BF16),
                pltpu.VMEM((layers, ny, rows_dp, cols), BF16),
                pltpu.VMEM((layers, ny, rows_dp, cols), F32),
                per_layer(cols, BF16, rows_dp),
                per_layer(cols, BF16, rows_dp),
                per_layer(cols, F32, rows_dp),
                pltpu.VMEM((layers, nz, rows_dp // nseq, cols), BF16),
                pltpu.VMEM((layers, nz, rows_dp // nseq, cols), BF16),
                pltpu.VMEM((layers, nz, rows_dp // nseq, cols), F32),
                pltpu.VMEM((layers, nz, rows_dp // nseq, cols), BF16),
                pltpu.VMEM((layers, nz, rows_dp // nseq, cols), BF16),
                pltpu.VMEM((layers, nz, 2, rows_dp // nseq, cols), BF16),
            ]
        scratch += [
            pltpu.VMEM((layers, 2, 4 * nz, share, half), BF16),
            pltpu.VMEM((layers, 2, 4 * nz, share, half), BF16),
            pltpu.VMEM((layers, 2, 4 * nz, share, half), F32),
            pltpu.VMEM((layers, 4 * nz, share, part), BF16),
            pltpu.VMEM((layers, 4 * nz, share, part), BF16),
            pltpu.VMEM((layers, 4 * nz, share, part), F32),
            pltpu.VMEM((layers, 2 * nz, share, half), BF16),
            pltpu.VMEM((layers, 2 * nz, share, half), BF16),
            pltpu.VMEM((layers, 2 * nz, share, half), F32),
            pltpu.VMEM((layers, 2, 2 * nz, share, part), BF16),
            pltpu.VMEM((layers, 2, 2 * nz, share, part), BF16),
            pltpu.VMEM((layers, 2, 2 * nz, share, part), F32),
            pltpu.VMEM((layers, 2, nz, 2, share, part), BF16),
            pltpu.VMEM((layers, 2, nz, 2, share, part), BF16),
        ]
    return pl.pallas_call(
        partial(model_kernel, dims, inside),
        out_shape=(
            jax.ShapeDtypeStruct((tok, width), F32),
            jax.ShapeDtypeStruct(small_shape, F32),
            jax.ShapeDtypeStruct(b_shape, kind),
            jax.ShapeDtypeStruct(g_shape, kind),
            jax.ShapeDtypeStruct(c_shape, kind),
        ),
        in_specs=[smem] * 3 + [hbm] * (len(operands) - 3),
        out_specs=[vmem] * 5,
        scratch_shapes=scratch,
        compiler_params=pltpu.CompilerParams(
            collective_id=0, has_side_effects=True, vmem_limit_bytes=48 * 1024 * 1024
        ),
        cost_estimate=pl.CostEstimate(
            flops=6 * layers * tok * width * (6 * states + width),
            bytes_accessed=16 * 1024 * 1024,
            transcendentals=2 * layers * tok * width,
        ),
    )(*operands[:3], *[pltpu.with_memory_space_constraint(a, pltpu.HBM) for a in operands[3:]])


def finish_kernel(dims, *refs):
    layers, tok, width, states, classes, ndp, nseq = dims
    small = refs[4]
    loss, gain, bias, rate, phase, skip, glub, head_w, head_b = refs[9:18]
    held, sems = refs[18:22], refs[22]
    inward = [pltpu.make_async_copy(refs[k], held[k], sems.at[0, k]) for k in range(4)]
    outward = [pltpu.make_async_copy(held[k], refs[5 + k], sems.at[1, k]) for k in range(4)]
    for copy in inward:
        copy.start()
    for k in range(4):
        inward[k].wait()
        outward[k].start()
    tiles = width // 128

    def line(row, count=tiles):
        parts = [small[row * tiles + t : row * tiles + t + 1, :] for t in range(count)]
        return jnp.concatenate(parts, axis=1)

    for layer in range(layers):
        at = slice(layer, layer + 1)
        gain[at, :] = line(layer)
        bias[at, :] = line(layers + layer)
        skip[at, :] = line(2 * layers + layer)
        glub[at, :] = line(3 * layers + layer)
    share = states // nseq
    me = lax.axis_index("seq")
    for first, out in ((4 * layers, rate), (5 * layers, phase)):
        every = jnp.concatenate([line(first + layer) for layer in range(layers)], axis=0)
        mine = every[:, 0:share]
        for q in range(1, nseq):
            mine = jnp.where(me == q, every[:, q * share : (q + 1) * share], mine)
        out[...] = mine
    head = 6 * layers
    for k in range(classes):
        head_w[k : k + 1, :] = line(head + k)
    last = line(head + classes)
    head_b[...] = last[:, 0:classes]
    loss[...] = last[:, classes : classes + 1] / ndp
    for copy in outward:
        copy.wait()


def finish_outputs(dims, grad_inputs, small, b_grad, g_grad, c_grad):
    layers, tok, width, states, classes, ndp, nseq = dims
    vmem = pl.BlockSpec(memory_space=pltpu.VMEM)
    anywhere = pl.BlockSpec(memory_space=pl.ANY)
    large = (grad_inputs, b_grad, g_grad, c_grad)
    share = states // nseq
    rows = (layers, width)
    shapes = [(1, 1), rows, rows, (layers, share), (layers, share), rows, rows, (classes, width)]
    shapes.append((1, classes))
    results = pl.pallas_call(
        partial(finish_kernel, dims),
        out_shape=[jax.ShapeDtypeStruct(a.shape, F32) for a in large]
        + [jax.ShapeDtypeStruct(shape, F32) for shape in shapes],
        in_specs=[anywhere] * 4 + [vmem],
        out_specs=[anywhere] * 4 + [vmem] * 9,
        scratch_shapes=[pltpu.VMEM(a.shape, F32) for a in large]
        + [pltpu.SemaphoreType.DMA((2, 4))],
        compiler_params=pltpu.CompilerParams(vmem_limit_bytes=8 * 1024 * 1024),
    )(*large, small)
    gin, b_share, g_share, c_share, loss, gain, bias, rate, phase, skip, glub, head_w, head_b = results
    return (
        loss.reshape(()),
        gin[None],
        gain,
        bias,
        b_share,
        rate,
        phase,
        c_share,
        skip,
        g_share,
        glub,
        head_w.T,
        head_b.reshape(classes),
    )


def per_device(
    inputs,
    lengths,
    labels,
    norm_gain,
    norm_bias,
    b_proj,
    rate,
    phase,
    c_proj,
    skip,
    glu_weight,
    glu_bias,
    class_weight,
    class_bias,
):
    layers, width = norm_gain.shape
    tok = inputs.shape[1]
    ndp = lax.axis_size("dp")
    nseq = lax.axis_size("seq")
    states = c_proj.shape[2] * nseq
    classes = class_bias.shape[0]
    dims = (layers, tok, width, states, classes, ndp, nseq)
    share = states // nseq
    inside = (
        ndp == 4
        and nseq % 2 == 0
        and share % 16 == 0
        and (width // ndp) % 128 == 0
        and (width // ndp) % (16 * nseq) == 0
        and 4 * layers == 8
    )
    if inside:
        tables = (rate, phase)
        weights = (b_proj, glu_weight, c_proj)
    else:
        decay = jnp.exp(-rate)
        in_scale = jnp.sqrt(-jnp.expm1(-2.0 * rate))
        rows = [
            decay * jnp.cos(phase),
            decay * jnp.sin(phase),
            in_scale,
            jnp.exp(-2.0 * rate) / in_scale,
        ]
        table = lax.all_gather(jnp.stack(rows, axis=1), "seq", axis=2, tiled=True)
        tables = (table, phase)
        b_full = lax.all_gather(b_proj.astype(BF16), "dp", axis=1, tiled=True)
        g_full = lax.all_gather(glu_weight.astype(BF16), "dp", axis=1, tiled=True)
        c_half = lax.all_gather(c_proj.astype(BF16), "dp", axis=3, tiled=True)
        c_full = lax.all_gather(c_half, "seq", axis=2, tiled=True)
        c_full = c_full.reshape(layers, 4, states, 2, width // 2)
        c_full = jnp.moveaxis(c_full, 3, 1)
        weights = (b_full, g_full, c_full)
    grad_inputs, small, b_grad, g_grad, c_grad = run_model(
        dims,
        inside,
        (
            lengths,
            labels,
            class_bias,
            inputs[0],
            norm_gain,
            norm_bias,
            skip,
            glu_bias,
            *tables,
            class_weight.T,
            *weights,
        ),
    )
    if inside:
        return finish_outputs(dims, grad_inputs, small, b_grad, g_grad, c_grad)
    else:
        b_share = lax.psum_scatter(b_grad, "dp", scatter_dimension=1, tiled=True)
        g_share = lax.psum_scatter(g_grad, "dp", scatter_dimension=1, tiled=True)
        b_share = lax.psum(b_share, "seq").astype(F32)
        g_share = lax.psum(g_share, "seq").astype(F32)
        c_grad = c_grad.reshape(layers, 4, states, width)
        c_share = lax.psum_scatter(c_grad, "seq", scatter_dimension=2, tiled=True)
        c_share = lax.psum_scatter(c_share, "dp", scatter_dimension=3, tiled=True).astype(F32)
        small = lax.psum(small, ("dp", "seq"))
    small = small.reshape(-1, width)
    own = lax.axis_index("seq") * (states // nseq)

    def state_rows(first):
        return lax.dynamic_slice(small[first : first + layers], (0, own), (layers, states // nseq))

    head = 6 * layers
    return (
        small[head + classes, classes] / ndp,
        grad_inputs[None],
        small[0:layers],
        small[layers : 2 * layers],
        b_share,
        state_rows(4 * layers),
        state_rows(5 * layers),
        c_share,
        small[2 * layers : 3 * layers],
        g_share,
        small[3 * layers : 4 * layers],
        small[head : head + classes].T,
        small[head + classes, 0:classes],
    )


def solution(mesh):
    return jax.shard_map(
        per_device,
        mesh=mesh,
        in_specs=(
            P("dp", "seq", None),
            P("dp"),
            P("dp"),
            P(),
            P(),
            P(None, "dp", None),
            P(None, "seq"),
            P(None, "seq"),
            P(None, None, "seq", "dp"),
            P(),
            P(None, "dp", None),
            P(),
            P(),
            P(),
        ),
        out_specs=(
            P(),
            P("dp", "seq", None),
            P(),
            P(),
            P(None, "dp", None),
            P(None, "seq"),
            P(None, "seq"),
            P(None, None, "seq", "dp"),
            P(),
            P(None, "dp", None),
            P(),
            P(),
            P(),
        ),
        check_vma=False,
    )
```

```python
from functools import partial
from typing import Any, NamedTuple

import jax
import jax.numpy as jnp
from jax import lax
from jax.experimental import pallas as pl
from jax.experimental.pallas import tpu as pltpu
from jax.sharding import PartitionSpec as P

MESH = pl.DeviceIdType.MESH
F32 = jnp.float32
BF16 = jnp.bfloat16
CHUNKS = 8
TILE = 32
GELU_A = 0.7978845608028654
GELU_B = 0.044715


def mm_nn(left, right):
    return lax.dot_general(left, right, (((1,), (0,)), ((), ())), preferred_element_type=F32)


def mm_nt(left, right):
    return lax.dot_general(left, right, (((1,), (1,)), ((), ())), preferred_element_type=F32)


def mm_tn(left, right):
    return lax.dot_general(left, right, (((0,), (0,)), ((), ())), preferred_element_type=F32)


def cmul(a_re, a_im, b_re, b_im):
    return a_re * b_re - a_im * b_im, a_re * b_im + a_im * b_re


def fold8(value):
    total = value[0:8]
    for first in range(8, value.shape[0], 8):
        total = total + value[first : first + 8]
    return total


class Operands(NamedTuple):
    len: Any
    lab: Any
    cb: Any
    x: Any
    gain: Any
    bias: Any
    skip: Any
    glub: Any
    rate: Any
    phase: Any
    cw: Any
    b_in: Any
    glu_in: Any
    c_in: Any


class Results(NamedTuple):
    gin: Any
    small_out: Any
    b_out: Any
    glu_out: Any
    c_out: Any


class Local(NamedTuple):
    stream: Any
    xhat: Any
    rstd: Any
    nlow: Any
    drive: Any
    caus: Any
    anti: Any
    feat: Any
    gelu_out: Any
    gelu_low: Any
    gelu_der: Any
    sig: Any
    wide: Any
    temp: Any
    mix: Any
    mlow: Any
    ggrad: Any
    dlow: Any
    scale: Any
    perm: Any
    send_buf: Any
    recv_buf: Any
    send_sem: Any
    recv_sem: Any


class Shared(NamedTuple):
    tab: Any
    tab_recv: Any
    b_buf: Any
    glu_buf: Any
    c_buf: Any
    ssem: Any
    rsem: Any
    small: Any
    small_core: Any
    small_y: Any
    small_sum: Any
    small_recv: Any


class RowGrad(NamedTuple):
    snd1: Any
    rcv1: Any
    acc: Any
    snd2: Any
    rcv2: Any
    acc2: Any
    snd3: Any
    rcv3: Any
    acc3: Any
    snd4: Any
    rcv4: Any
    full: Any


class ColGrad(NamedTuple):
    snd1: Any
    rcv1: Any
    acc: Any
    snd2a: Any
    rcv2a: Any
    acc2a: Any
    snd2b: Any
    rcv2b: Any
    acc2b: Any
    snd3: Any
    rcv3: Any
    acc3: Any
    snd4: Any
    rcv4: Any


def take(refs, kind):
    count = len(kind._fields)
    return kind(*refs[:count]), refs[count:]


def model_kernel(dims, inside, *refs):
    layers, tok, width, states, classes, ndp, nseq = dims
    given, refs = take(refs, Operands)
    O, refs = take(refs, Results)
    fetched, refs = refs[: len(given) - 3], refs[len(given) - 3 :]
    fetch_sem, refs = refs[0], refs[1:]
    I = Operands(*given[:3], *fetched)
    L, refs = take(refs, Local)
    if inside:
        S, refs = take(refs, Shared)
        BA, refs = take(refs, RowGrad)
        BB, refs = take(refs, RowGrad)
        GG, refs = take(refs, RowGrad)
        CG, refs = take(refs, ColGrad)
        tab_ref, b_ref, glu_ref, c_ref, small_ref = S.tab, S.b_buf, S.glu_buf, S.c_buf, S.small
    else:
        tab_ref, b_ref, glu_ref, c_ref, small_ref = I.rate, I.b_in, I.glu_in, I.c_in, O.small_out
    len_ref, lab_ref, x_ref = I.len, I.lab, I.x
    gain_ref, bias_ref, skip_ref, glub_ref = I.gain, I.bias, I.skip, I.glub
    cw_ref, cb_ref, gin_ref = I.cw, I.cb, O.gin
    stream, xhat, rstd, nlow, drive = L.stream, L.xhat, L.rstd, L.nlow, L.drive
    caus, anti, feat, gelu_out, gelu_low = L.caus, L.anti, L.feat, L.gelu_out, L.gelu_low
    gelu_der, sig, wide, temp, mix = L.gelu_der, L.sig, L.wide, L.temp, L.mix
    mlow, ggrad, dlow, perm = L.mlow, L.ggrad, L.dlow, L.perm
    send_buf, recv_buf = L.send_buf, L.recv_buf
    send_sem, recv_sem = L.send_sem, L.recv_sem
    steps = tok // CHUNKS
    half_cols = width // 2
    me = lax.axis_index("seq")
    my_dp = lax.axis_index("dp")
    p = states
    core, yy = lax.rem(my_dp, 2), my_dp // 2
    xx, zz = lax.rem(me, 2), me // 2
    ny, nz = ndp // 2, nseq // 2
    own_half = core if inside else 0

    barrier = pltpu.get_barrier_semaphore()

    def greet(k, carry):
        peer = lax.rem(me + k, nseq)
        pl.semaphore_signal(barrier, inc=1, device_id={"seq": peer}, device_id_type=MESH)
        return carry

    lax.fori_loop(1, nseq, greet, 0, unroll=True)
    greeted = nseq - 1
    sibling = {"dp": 2 * yy + 1 - core}
    y_peer = {"dp": 2 * (1 - yy) + core}
    x_peer = {"seq": 2 * zz + 1 - xx}
    if inside:
        for peer in (sibling, y_peer):
            pl.semaphore_signal(barrier, inc=1, device_id=peer, device_id_type=MESH)
        greeted += 2

    fetches = [
        pltpu.make_async_copy(src, dst, fetch_sem.at[k])
        for k, (src, dst) in enumerate(zip(given[3:], fetched))
    ]
    for fetch in reversed(fetches):
        fetch.start()

    used = [0]

    def new_sems(count):
        first = used[0]
        used[0] += count
        return first

    def remote(src, dst, sem, peer):
        return pltpu.make_async_remote_copy(
            src_ref=src,
            dst_ref=dst,
            send_sem=S.ssem.at[sem],
            recv_sem=S.rsem.at[sem],
            device_id=peer,
            device_id_type=MESH,
        )

    def seq_loop(body):
        def one(k, carry):
            body(k)
            return carry

        lax.fori_loop(1, nseq, one, 0, unroll=True)

    def cast_rows(dst, src, rows, step, extra=None):
        def one(k, carry):
            part = pl.ds(pl.multiple_of(k * step, step), step)
            value = src[part, :].astype(F32)
            if extra is not None:
                value = value + extra[part, :].astype(F32)
            dst[part, :] = value.astype(dst.dtype)
            return carry

        lax.fori_loop(0, rows // step, one, 0, unroll=4)

    def row_loop(body, init, unroll=4):
        def step(k, carry):
            rows = pl.ds(pl.multiple_of(k * TILE, TILE), TILE)
            return body(rows, k * TILE, carry)

        return lax.fori_loop(0, tok // TILE, step, init, unroll=unroll)

    def exchange_start(slot):
        def one(k, carry):
            peer = lax.rem(me + k, nseq)
            pltpu.make_async_remote_copy(
                src_ref=send_buf.at[slot, (peer - me + nseq) // nseq],
                dst_ref=recv_buf.at[slot, k],
                send_sem=send_sem.at[slot],
                recv_sem=recv_sem.at[slot],
                device_id={"seq": peer},
                device_id_type=MESH,
            ).start()
            return carry

        lax.fori_loop(1, nseq, one, 0, unroll=True)

    def exchange_wait(slot):
        arrived = recv_buf.at[slot, pl.ds(1, nseq - 1)]
        pltpu.make_async_remote_copy(
            src_ref=arrived,
            dst_ref=arrived,
            send_sem=send_sem.at[slot],
            recv_sem=recv_sem.at[slot],
            device_id={"seq": lax.rem(me + 1, nseq)},
            device_id_type=MESH,
        ).wait()

    def from_rank(q):
        return lax.rem(me - q + nseq, nseq)

    sub = lax.broadcasted_iota(jnp.int32, (CHUNKS, p), 0)

    def layer_powers(layer, conj):
        lam_re = tab_ref[layer, 0:1, :]
        lam_im = tab_ref[layer, 1:2, :]
        if conj:
            lam_im = -lam_im
        pw_re, pw_im = lam_re, lam_im
        count = 1
        while count < steps:
            pw_re, pw_im = cmul(pw_re, pw_im, pw_re, pw_im)
            count *= 2
        jumps = [(pw_re, pw_im)]
        for _ in range(3):
            pw_re, pw_im = cmul(pw_re, pw_im, pw_re, pw_im)
            jumps.append((pw_re, pw_im))
        return lam_re, lam_im, jumps

    def jump_table(jumps, index):
        re = jnp.ones((CHUNKS, p), F32)
        im = jnp.zeros((CHUNKS, p), F32)
        for bit in range(3):
            new_re, new_im = cmul(re, im, jumps[bit][0], jumps[bit][1])
            has = (index & (1 << bit)) != 0
            re = jnp.where(has, new_re, re)
            im = jnp.where(has, new_im, im)
        return re, im

    def local_ends(src, first_c, first_a, lam_re, lam_im):
        zero = jnp.zeros((CHUNKS, p), F32)
        l_re = jnp.broadcast_to(lam_re, (CHUNKS, p))
        l_im = jnp.broadcast_to(lam_im, (CHUNKS, p))

        def step(j, carry):
            e_re, e_im, f_re, f_im = carry
            up = pl.ds(pl.multiple_of(j * CHUNKS, CHUNKS), CHUNKS)
            down = pl.ds(pl.multiple_of((steps - 1 - j) * CHUNKS, CHUNKS), CHUNKS)
            e_re, e_im = cmul(l_re, l_im, e_re, e_im)
            f_re, f_im = cmul(l_re, l_im, f_re, f_im)
            return (
                e_re + src[up, first_c : first_c + p],
                e_im + src[up, first_c + p : first_c + 2 * p],
                f_re + src[down, first_a : first_a + p],
                f_im + src[down, first_a + p : first_a + 2 * p],
            )

        return lax.fori_loop(0, steps, step, (zero,) * 4, unroll=8)

    def local_prefix(ends, jumps):
        e_re, e_im, f_re, f_im = ends
        for bit in range(3):
            shift = 1 << bit
            j_re, j_im = jumps[bit]
            s_re = jnp.where(sub >= shift, pltpu.roll(e_re, shift, 0), 0.0)
            s_im = jnp.where(sub >= shift, pltpu.roll(e_im, shift, 0), 0.0)
            a_re, a_im = cmul(j_re, j_im, s_re, s_im)
            e_re, e_im = e_re + a_re, e_im + a_im
            s_re = jnp.where(sub < CHUNKS - shift, pltpu.roll(f_re, CHUNKS - shift, 0), 0.0)
            s_im = jnp.where(sub < CHUNKS - shift, pltpu.roll(f_im, CHUNKS - shift, 0), 0.0)
            a_re, a_im = cmul(j_re, j_im, s_re, s_im)
            f_re, f_im = f_re + a_re, f_im + a_im
        return e_re, e_im, f_re, f_im

    def send_totals(slot, prefix):
        e_re, e_im, f_re, f_im = prefix
        last, first = slice(CHUNKS - 1, CHUNKS), slice(0, 1)
        for tile in range(p // 128):
            cols = slice(tile * 128, tile * 128 + 128)
            for row, value, part, at in (
                (tile, e_re, 1, last),
                (p // 128 + tile, e_im, 1, last),
                (tile, f_re, 0, first),
                (p // 128 + tile, f_im, 0, first),
            ):
                send_buf[slot, part, row : row + 1, :] = value[at, cols]
        exchange_start(slot)

    def chunk_carries(slot, prefix, jumps, tables):
        e_re, e_im, f_re, f_im = prefix
        d_re, d_im = jumps[3]
        zero = jnp.zeros((1, p), F32)

        def arrived(q, first):
            rows = range(first, first + p // 128)
            return jnp.concatenate([recv_buf[slot, from_rank(q), r : r + 1, :] for r in rows], axis=1)

        def step(k, carry):
            c_re, c_im, a_re, a_im = carry
            n_re, n_im = cmul(d_re, d_im, c_re, c_im)
            use = k < me
            c_re = jnp.where(use, n_re + arrived(k, 0), c_re)
            c_im = jnp.where(use, n_im + arrived(k, p // 128), c_im)
            back = nseq - 1 - k
            n_re, n_im = cmul(d_re, d_im, a_re, a_im)
            use = back > me
            a_re = jnp.where(use, n_re + arrived(back, 0), a_re)
            a_im = jnp.where(use, n_im + arrived(back, p // 128), a_im)
            return c_re, c_im, a_re, a_im

        c_re, c_im, a_re, a_im = lax.fori_loop(0, nseq, step, (zero,) * 4, unroll=True)
        t_re, t_im = tables[0]
        g_re, g_im = cmul(t_re, t_im, c_re, c_im)
        in_c_re = g_re + jnp.where(sub >= 1, pltpu.roll(e_re, 1, 0), 0.0)
        in_c_im = g_im + jnp.where(sub >= 1, pltpu.roll(e_im, 1, 0), 0.0)
        t_re, t_im = tables[1]
        g_re, g_im = cmul(t_re, t_im, a_re, a_im)
        in_a_re = g_re + jnp.where(sub < CHUNKS - 1, pltpu.roll(f_re, CHUNKS - 1, 0), 0.0)
        in_a_im = g_im + jnp.where(sub < CHUNKS - 1, pltpu.roll(f_im, CHUNKS - 1, 0), 0.0)
        return in_c_re, in_c_im, in_a_re, in_a_im

    def half_blocks(half):
        blocks = []
        for first in range(0, half_cols, 128):
            if inside:
                at = (2 * (first // part_cols) + half) * part_cols + first % part_cols
            else:
                at = half * half_cols + first
            if not isinstance(at, int):
                at = pl.multiple_of(at, 128)
            blocks.append((first, pl.ds(at, 128)))
        return blocks

    def put_line(line, row):
        for col in range(0, width, 128):
            at = line * (width // 128) + col // 128
            small_ref[at : at + 1, :] = row[:, col : col + 128]

    part_cols = width // ndp
    rows_dp = width // ndp
    share = p // nseq

    def own_rows(index):
        return pl.ds(pl.multiple_of(index * rows_dp, 16), rows_dp)

    def cast_c(layer):
        cols = pl.ds(pl.multiple_of(yy * part_cols, 128), part_cols)
        c_ref[layer, core, :, zz, xx, :, cols] = I.c_in[layer].astype(BF16)

    def cast_b(layer):
        b_ref[layer, own_rows(my_dp), :] = I.b_in[layer].astype(BF16)

    def cast_glu(layer):
        glu_ref[layer, own_rows(my_dp), :] = I.glu_in[layer].astype(BF16)

    copies, sem_of = {}, {}

    def start(name, copy):
        copies[name] = copy
        copy.start()

    def finish(name):
        copies.pop(name).wait()

    def ensure(name):
        if name in copies:
            finish(name)

    def y_cols(y):
        return pl.ds(pl.multiple_of(y * part_cols, 128), part_cols)

    def start_all(name, total, pairs):
        if name not in copies:
            sem_of[name] = new_sems(1)
            copies[name] = remote(total, total, sem_of[name], x_peer)
        for block, peer in pairs:
            remote(block, block, sem_of[name], peer).start()

    def z_peers():
        return [{"seq": 2 * lax.rem(zz + k, nz) + xx} for k in range(1, nz)]

    front, back = pl.ds(0, 2), pl.ds(2, 2)
    other_y = 1 - yy

    def c_piece(layer, planes, z, x, y):
        return c_ref.at[layer, core, planes, z, x, :, y_cols(y)]

    def c_to_z(name, layer, planes, y):
        total = c_ref.at[layer, core, planes, pl.ds(0, nz - 1), xx, :, y_cols(y)]
        block = c_piece(layer, planes, zz, xx, y)
        start_all((name, layer), total, [(block, peer) for peer in z_peers()])

    def c_to_x(layer, planes, y, others):
        if planes is front:
            name, total = 3, c_ref.at[layer, core, planes, :, xx]
        else:
            name, total = 13, c_ref.at[layer, core, planes, :, xx, :, y_cols(yy)]
        ranks = [lax.rem(zz + k, nz) for k in range(1, nz)] if others else [zz]
        pairs = [(c_piece(layer, planes, z, xx, y), x_peer) for z in ranks]
        start_all((name, layer), total, pairs)

    def one_copy(name, layer, block, peer):
        start((name, layer), remote(block, block, new_sems(1), peer))

    def cya(layer):
        one_copy(0, layer, c_piece(layer, front, zz, xx, yy), y_peer)

    def spoa(layer):
        c_to_z(1, layer, front, yy)

    def xoa(layer):
        c_to_x(layer, front, yy, False)

    def spta(layer):
        ensure((0, layer))
        c_to_z(2, layer, front, other_y)

    def xta(layer):
        ensure((0, layer))
        c_to_x(layer, front, other_y, False)

    def poa(layer):
        ensure((1, layer))
        c_to_x(layer, front, yy, True)

    def pta(layer):
        ensure((2, layer))
        c_to_x(layer, front, other_y, True)

    def caa(layer):
        ensure((1, layer))
        ensure((2, layer))
        one_copy(4, layer, c_ref.at[layer, core, front, :, xx], sibling)

    def cba(layer):
        ensure((3, layer))
        one_copy(5, layer, c_ref.at[layer, core, front, :, 1 - xx], sibling)

    def zb(layer):
        c_to_z(12, layer, back, yy)

    def xb(layer):
        c_to_x(layer, back, yy, False)

    def pb(layer):
        ensure((12, layer))
        c_to_x(layer, back, yy, True)

    def yb1(layer):
        ensure((12, layer))
        one_copy(14, layer, c_ref.at[layer, core, back, :, xx, :, y_cols(yy)], y_peer)

    def yb2(layer):
        ensure((13, layer))
        one_copy(15, layer, c_ref.at[layer, core, back, :, 1 - xx, :, y_cols(yy)], y_peer)

    def kb1(layer):
        ensure((12, layer))
        ensure((13, layer))
        one_copy(16, layer, c_ref.at[layer, core, back, :, :, :, y_cols(yy)], sibling)

    def kb2(layer):
        ensure((14, layer))
        ensure((15, layer))
        one_copy(17, layer, c_ref.at[layer, core, back, :, :, :, y_cols(other_y)], sibling)

    def c_stage_5(layer):
        for name in (4, 5, 16, 17):
            finish((name, layer))

    def row_to_y(ref, layer):
        block = ref.at[layer, own_rows(my_dp), :]
        start((id(ref), 0, layer), remote(block, block, new_sems(1), y_peer))

    def row_to_sibling(ref, layer):
        block = ref.at[layer, own_rows(my_dp), :]
        start_all((id(ref), 1, layer), ref.at[layer, pl.ds(0, 2 * rows_dp), :], [(block, sibling)])

    def row_pass(ref, layer):
        finish((id(ref), 0, layer))
        block = ref.at[layer, own_rows(2 * (1 - yy) + core), :]
        start_all((id(ref), 1, layer), ref.at[layer, pl.ds(0, 2 * rows_dp), :], [(block, sibling)])

    def row_stage_end(ref, layer):
        finish((id(ref), 1, layer))

    def table_stage():
        every, own = S.tab_recv, S.tab_recv.at[0]
        rate, phase = I.rate[...], I.phase[...]
        decay = jnp.exp(-rate)
        twice = 2.0 * rate
        series = 1.0 - twice / 7.0
        for term in (6.0, 5.0, 4.0, 3.0, 2.0):
            series = 1.0 - series * (twice / term)
        loss = jnp.where(twice < 0.25, twice * series, 1.0 - jnp.exp(-twice))
        in_scale = jnp.sqrt(loss)
        every[0] = jnp.zeros((8, 128), F32)
        parts = (decay * jnp.cos(phase), decay * jnp.sin(phase), in_scale, jnp.exp(-twice) / in_scale)
        for row, value in enumerate(parts):
            for layer in range(layers):
                at = 4 * layer + row
                every[0, at : at + 1, 0:share] = value[layer : layer + 1]
        arrived = every.at[pl.ds(1, nseq - 1)]
        sem = new_sems(1)
        copies[8, 8] = remote(arrived, arrived, sem, x_peer)

        def one(k):
            remote(own, every.at[k], sem, {"seq": lax.rem(me + k, nseq)}).start()

        seq_loop(one)

    def table_end():
        finish((8, 8))
        lane = lax.broadcasted_iota(jnp.int32, (8, 128), 1)
        tiles = [jnp.zeros((8, 128), F32) for _ in range(p // 128)]
        for q in range(nseq):
            tile, first = (q * share) // 128, (q * share) % 128
            piece = S.tab_recv[from_rank(q)]
            if first:
                piece = pltpu.roll(piece, first, 1)
            here = (lane >= first) & (lane < first + share)
            tiles[tile] = jnp.where(here, piece, tiles[tile])
            if first + share > 128:
                tiles[tile + 1] = jnp.where(lane < first + share - 128, piece, tiles[tile + 1])
        for layer in range(layers):
            for tile in range(p // 128):
                tab_ref[layer, 0:4, tile * 128 : tile * 128 + 128] = tiles[tile][
                    4 * layer : 4 * layer + 4
                ]

    early = {}
    if inside:
        early = {
            (0, 10): [
                partial(cya, 0),
                partial(row_to_y, b_ref, 0),
                partial(zb, 0),
                table_stage,
                partial(xb, 0),
                partial(row_to_y, glu_ref, 0),
                partial(xoa, 0),
                partial(spoa, 0),
            ],
            (0, 12): [
                partial(pb, 0),
                partial(row_to_sibling, b_ref, 1),
                partial(xb, 1),
                partial(xta, 0),
                partial(cya, 1),
                partial(spta, 0),
                partial(yb1, 0),
                partial(row_to_sibling, b_ref, 0),
                partial(row_pass, b_ref, 0),
                partial(zb, 1),
                table_end,
                partial(poa, 0),
                partial(spoa, 1),
                partial(row_pass, glu_ref, 0),
                partial(yb2, 0),
                partial(pta, 0),
            ],
            (0, 14): [
                partial(row_to_y, b_ref, 1),
                partial(pb, 1),
                partial(kb1, 0),
                partial(spta, 1),
                partial(yb1, 1),
            ],
            (0, 15): [
                partial(xta, 1),
                partial(kb2, 0),
                partial(cba, 0),
                partial(xoa, 1),
                partial(yb2, 1),
                partial(caa, 0),
                partial(row_to_sibling, glu_ref, 0),
                partial(poa, 1),
                partial(row_to_sibling, glu_ref, 1),
            ],
            (0, 16): [
                partial(row_to_y, glu_ref, 1),
            ],
            (0, 18): [
                partial(row_pass, b_ref, 1),
            ],
            (0, 19): [
                partial(pta, 1),
            ],
            (0, 20): [
                partial(caa, 1),
            ],
            (1, 14): [
                partial(kb1, 1),
                partial(cba, 1),
                partial(kb2, 1),
            ],
            (1, 15): [
                partial(row_pass, glu_ref, 1),
            ],
        }

    def gather(layer, point):
        for stage in early.get((layer, point), []):
            stage()

    for fetch in reversed(fetches):
        fetch.wait()
    if inside:
        for layer in range(layers):
            cast_c(layer)
            cast_b(layer)
            cast_glu(layer)
    for col in range(0, width, 128):
        perm[col // 128] = x_ref[:, col : col + 128].astype(F32)

        def place(j, carry, col=col):
            rows = pl.ds(pl.multiple_of(j * CHUNKS, CHUNKS), CHUNKS)
            stream[rows, col : col + 128] = perm[col // 128, pl.ds(j, CHUNKS, stride=steps), :]
            return carry

        lax.fori_loop(0, steps, place, 0, unroll=4)

    for layer in range(layers):
        gain = gain_ref[layer : layer + 1, :]
        bias = bias_ref[layer : layer + 1, :]
        skip = skip_ref[layer : layer + 1, :]

        def norm_rows(rows, first, carry, layer=layer, gain=gain, bias=bias):
            value = stream[rows, :]
            center = value - jnp.mean(value, axis=1, keepdims=True)
            spread = jnp.mean(center * center, axis=1, keepdims=True)
            inv = lax.rsqrt(spread + 1e-05)
            hat = center * inv
            xhat[layer, rows, :] = hat
            rstd[layer, rows, :] = inv
            nlow[layer, rows, :] = (hat * gain + bias).astype(BF16)
            return carry

        row_loop(norm_rows, 0)
        if layer == 0:
            pl.semaphore_wait(barrier, greeted)
            gather(0, 10)
            gather(0, 11)
        gather(layer, 12)

        if inside:
            row_stage_end(b_ref, layer)
        in_scale = tab_ref[layer, 2:3, :]
        for col in range(0, 2 * p, 256):
            part = mm_nn(nlow[layer], b_ref[layer, :, col : col + 256])
            for half in range(col, col + 256, 128):
                scale_col = half % p
                drive[layer, :, half : half + 128] = (
                    part[:, half - col : half - col + 128].astype(BF16).astype(F32)
                    * in_scale[:, scale_col : scale_col + 128]
                )

        lam_re, lam_im, jumps = layer_powers(layer, False)
        ends = local_ends(drive.at[layer], 0, 0, lam_re, lam_im)
        prefix = local_prefix(ends, jumps)
        gather(layer, 13)
        send_totals(layer, prefix)
        gather(layer, 14)
        tables = (jump_table(jumps, sub), jump_table(jumps, CHUNKS - 1 - sub))
        exchange_wait(layer)
        gather(layer, 15)
        carries = chunk_carries(layer, prefix, jumps, tables)
        caus[layer, 0:CHUNKS, 0:p] = carries[0]
        caus[layer, 0:CHUNKS, p : 2 * p] = carries[1]
        anti[layer, tok : tok + CHUNKS, 0:p] = carries[2]
        anti[layer, tok : tok + CHUNKS, p : 2 * p] = carries[3]
        l_re = jnp.broadcast_to(lam_re, (CHUNKS, p))
        l_im = jnp.broadcast_to(lam_im, (CHUNKS, p))

        def state_pair(k, carry, layer=layer, l_re=l_re, l_im=l_im):
            s_re, s_im, r_re, r_im = carry
            first = pl.multiple_of(k * 2 * CHUNKS, 2 * CHUNKS)
            kept_re, kept_im = [], []
            for half in range(2):
                rows = pl.ds(first + half * CHUNKS, CHUNKS)
                s_re, s_im = cmul(l_re, l_im, s_re, s_im)
                s_re = s_re + drive[layer, rows, 0:p]
                s_im = s_im + drive[layer, rows, p : 2 * p]
                after = pl.ds(first + (half + 1) * CHUNKS, CHUNKS)
                caus[layer, after, 0:p] = s_re
                caus[layer, after, p : 2 * p] = s_im
                kept_re.append(s_re)
                kept_im.append(s_im)
            both = pl.ds(first, 2 * CHUNKS)
            feat[layer, both, 0:p] = jnp.concatenate(kept_re, axis=0).astype(BF16)
            feat[layer, both, p : 2 * p] = jnp.concatenate(kept_im, axis=0).astype(BF16)
            last = pl.multiple_of(tok - (k + 1) * 2 * CHUNKS, 2 * CHUNKS)
            kept_re, kept_im = [], []
            for half in (1, 0):
                rows = pl.ds(last + half * CHUNKS, CHUNKS)
                r_re, r_im = cmul(l_re, l_im, r_re, r_im)
                r_re = r_re + drive[layer, rows, 0:p]
                r_im = r_im + drive[layer, rows, p : 2 * p]
                anti[layer, rows, 0:p] = r_re
                anti[layer, rows, p : 2 * p] = r_im
                kept_re.insert(0, r_re)
                kept_im.insert(0, r_im)
            both = pl.ds(last, 2 * CHUNKS)
            feat[layer, both, 2 * p : 3 * p] = jnp.concatenate(kept_re, axis=0).astype(BF16)
            feat[layer, both, 3 * p : 4 * p] = jnp.concatenate(kept_im, axis=0).astype(BF16)
            return s_re, s_im, r_re, r_im

        lax.fori_loop(0, steps // 2, state_pair, carries, unroll=4)

        gather(layer, 16)
        for turn in range(2):
            half = (1 - own_half) if turn else own_half
            if inside and turn:
                c_stage_5(layer)
            part = mm_nn(feat[layer], c_ref[layer, half].reshape(4 * p, half_cols))
            for first, block in half_blocks(half):
                temp[:, block] = part[:, first : first + 128]
            gather(layer, 17 + turn)

        def act_rows(rows, first, carry, layer=layer, gain=gain, bias=bias, skip=skip):
            pre = temp[rows, :] + skip * (xhat[layer, rows, :] * gain + bias)
            square = pre * pre
            th = jnp.tanh(GELU_A * pre * (1.0 + GELU_B * square))
            cdf = 0.5 * (1.0 + th)
            out = pre * cdf
            gelu_out[layer, rows, :] = out
            gelu_low[layer, rows, :] = out.astype(BF16)
            gelu_der[layer, rows, :] = cdf + 0.5 * pre * (1.0 - th * th) * (
                GELU_A * (1.0 + 3.0 * GELU_B * square)
            )
            return carry

        row_loop(act_rows, 0)
        gather(layer, 19)
        if inside:
            row_stage_end(glu_ref, layer)
        for col in range(0, width, 256):
            temp[:, col : col + 256] = mm_nn(gelu_low[layer], glu_ref[layer, :, col : col + 256])
        gather(layer, 20)
        glu_bias = glub_ref[layer : layer + 1, :]
        last_layer = layer == layers - 1

        def gate_rows(rows, first, carry, layer=layer, glu_bias=glu_bias, last_layer=last_layer):
            gate = 1.0 / (1.0 + jnp.exp(-(temp[rows, :] + glu_bias)))
            sig[layer, rows, :] = gate
            new = stream[rows, :] + gelu_out[layer, rows, :] * gate
            if not last_layer:
                stream[rows, :] = new
                return carry
            return carry + fold8(new * row_mask(first))

        def row_mask(first):
            row = first + lax.broadcasted_iota(jnp.int32, (TILE, 1), 0)
            position = me * tok + (row & (CHUNKS - 1)) * steps + (row >> 3)
            return jnp.where(position < len_ref[0], 1.0, 0.0).astype(F32)

        pooled_part = row_loop(gate_rows, jnp.zeros((CHUNKS, width), F32) if last_layer else 0)
        gather(layer, 21)

    pool_slot = 2 * layers
    own_sum = jnp.sum(pooled_part, axis=0, keepdims=True)
    for part in range(2):
        for tile in range(width // 128):
            cols = slice(tile * 128, tile * 128 + 128)
            send_buf[pool_slot, part, tile : tile + 1, :] = own_sum[:, cols]
    exchange_start(pool_slot)

    small_ref[...] = jnp.zeros(small_ref.shape, F32)
    head_row = 6 * layers
    heads = []

    def head():
        if heads:
            return
        exchange_wait(pool_slot)

        def add_pool(k, total):
            rows = [recv_buf[pool_slot, from_rank(k), r : r + 1, :] for r in range(width // 128)]
            return total + jnp.where(k == me, 0.0, jnp.concatenate(rows, axis=1))

        pooled_sum = lax.fori_loop(0, nseq, add_pool, own_sum, unroll=True)
        len_row = jnp.full((1, 1), len_ref[0], jnp.int32).astype(F32)
        pooled = pooled_sum / len_row
        logit = [
            jnp.sum(pooled * cw_ref[k : k + 1, :], axis=1, keepdims=True)
            + jnp.full((1, 1), cb_ref[k], F32)
            for k in range(classes)
        ]
        top = logit[0]
        for k in range(1, classes):
            top = jnp.maximum(top, logit[k])
        expo = [jnp.exp(v - top) for v in logit]
        norm = expo[0]
        for k in range(1, classes):
            norm = norm + expo[k]
        hot = [jnp.where(lab_ref[0] == k, 1.0, 0.0).astype(F32) for k in range(classes)]
        cross = top + jnp.log(norm)
        for k in range(classes):
            cross = cross - hot[k] * logit[k]
        excess = [expo[k] / norm - hot[k] for k in range(classes)]
        once = jnp.where(me == 0, 1.0, 0.0).astype(F32)
        lane = lax.broadcasted_iota(jnp.int32, (1, width), 1)
        bias_line = jnp.zeros((1, width), F32)
        for k in range(classes):
            lgrad = len_row * excess[k] * once
            put_line(head_row + k, pooled * lgrad)
            bias_line = jnp.where(lane == k, lgrad, bias_line)
        bias_line = jnp.where(lane == classes, cross * once, bias_line)
        put_line(head_row + classes, bias_line)
        factors = jnp.ones((1, 1), F32)
        row = excess[0] * cw_ref[0:1, :]
        if classes == 2:
            factors, row = excess[0], cw_ref[0:1, :] - cw_ref[1:2, :]
        else:
            for k in range(1, classes):
                row = row + excess[k] * cw_ref[k : k + 1, :]
        L.scale[...] = jnp.broadcast_to(factors, (8, 128))
        heads.append(row)

    def factor():
        return L.scale[0:1, 0:1]

    if classes == 2:
        grad_row = cw_ref[0:1, :] - cw_ref[1:2, :]
    else:
        head()
        grad_row = heads[0]

    def scale_small():
        rows = head_row * (width // 128)
        small_ref[0:rows, :] = small_ref[0:rows, :] * factor()

    groups = 4 * nz

    def loop(count, body):
        def one(k, carry):
            body(k)
            return carry

        lax.fori_loop(0, count, one, 0, unroll=4)

    def c_grad_start(layer, part):
        rows = feat[layer, :, part * 2 * p : (part + 1) * 2 * p]
        value = (mm_tn(rows, mlow[layer, 1 - core]) * factor()).reshape(groups, share, half_cols)
        CG.snd1[layer, part] = value.astype(BF16)
        copy = remote(CG.snd1.at[layer, part], CG.rcv1.at[layer, part], new_sems(1), sibling)
        start((6, layer, part), copy)
        value = mm_tn(rows, mlow[layer, core]) * factor()
        CG.acc[layer, part] = value.reshape(groups, share, half_cols)

    def c_grad_first(layer, part):
        finish((6, layer, part))
        acc, rcv = CG.acc.at[layer, part], CG.rcv1.at[layer, part]
        if part == 0:

            def put(dst, cols):
                def one(g):
                    value = acc[g, :, cols] + rcv[g, :, cols].astype(F32)
                    dst[layer, g] = value.astype(dst.dtype)

                loop(groups, one)

            put(CG.snd2a, y_cols(1 - yy))
            copy = remote(CG.snd2a.at[layer], CG.rcv2a.at[layer], new_sems(1), y_peer)
            start((7, layer, part), copy)
            put(CG.acc2a, y_cols(yy))
        else:

            def put(dst, x):
                def one(h):
                    value = acc[2 * h + x] + rcv[2 * h + x].astype(F32)
                    dst[layer, h] = value.astype(dst.dtype)

                loop(groups // 2, one)

            put(CG.snd2b, 1 - xx)
            copy = remote(CG.snd2b.at[layer], CG.rcv2b.at[layer], new_sems(1), x_peer)
            start((7, layer, part), copy)
            put(CG.acc2b, xx)

    def c_grad_second(layer, part):
        finish((7, layer, part))
        if part == 0:

            def put(dst, x):
                def one(h):
                    value = CG.acc2a[layer, 2 * h + x] + CG.rcv2a[layer, 2 * h + x].astype(F32)
                    dst[layer, part, h] = value.astype(dst.dtype)

                loop(groups // 2, one)

            away, keep, peer = 1 - xx, xx, x_peer
        else:

            def put(dst, cols):
                def one(h):
                    value = CG.acc2b[layer, h, :, cols] + CG.rcv2b[layer, h, :, cols].astype(F32)
                    dst[layer, part, h] = value.astype(dst.dtype)

                loop(groups // 2, one)

            away, keep, peer = y_cols(1 - yy), y_cols(yy), y_peer
        put(CG.snd3, away)
        copy = remote(CG.snd3.at[layer, part], CG.rcv3.at[layer, part], new_sems(1), peer)
        start((8, layer, part), copy)
        put(CG.acc3, keep)

    def spread_z(name, src, dst):
        arrived = dst.at[pl.ds(1, nz - 1)]
        sem = new_sems(1)
        copies[name] = remote(arrived, arrived, sem, x_peer)
        for k in range(1, nz):
            peer = lax.rem(zz + k, nz)
            remote(src(peer), dst.at[k], sem, {"seq": 2 * peer + xx}).start()

    def c_grad_third(layer, part):
        finish((8, layer, part))

        def one(h):
            value = CG.acc3[layer, part, h] + CG.rcv3[layer, part, h].astype(F32)
            CG.acc3[layer, part, h] = value
            CG.snd4[layer, part, lax.rem(h, nz), h // nz] = value.astype(BF16)

        loop(groups // 2, one)
        snd = CG.snd4.at[layer, part]
        spread_z((9, layer, part), lambda peer: snd.at[peer], CG.rcv4.at[layer, part])

    def c_grad_end(layer, part):
        finish((9, layer, part))
        for plane in range(2):
            value = CG.acc3[layer, part, plane * nz + zz]
            for k in range(1, nz):
                value = value + CG.rcv4[layer, part, k, plane].astype(F32)
            O.c_out[layer, 2 * part + plane] = value

    def row_grad_start(G, layer):
        if G is GG:
            left, right = gelu_low, ggrad[layer]
        elif G is BA:
            left, right = nlow, dlow[layer, :, 0:p]
        else:
            left, right = nlow, dlow[layer, :, p : 2 * p]
        for y in range(ny):
            block = left[layer, :, own_rows(2 * y + 1 - core)]
            G.snd1[layer, y] = (mm_tn(block, right) * factor()).astype(BF16)
        copy = remote(G.snd1.at[layer], G.rcv1.at[layer], new_sems(1), sibling)
        start((id(G), 0, layer), copy)
        for y in range(ny):
            block = left[layer, :, own_rows(2 * y + core)]
            G.acc[layer, y] = mm_tn(block, right) * factor()

    def row_grad_y(G, layer):
        finish((id(G), 0, layer))
        acc, rcv = G.acc.at[layer], G.rcv1.at[layer]
        cast_rows(G.snd2.at[layer], acc.at[1 - yy], rows_dp, 32, rcv.at[1 - yy])
        copy = remote(G.snd2.at[layer], G.rcv2.at[layer], new_sems(1), y_peer)
        start((id(G), 1, layer), copy)
        cast_rows(G.acc2.at[layer], acc.at[yy], rows_dp, 32, rcv.at[yy])

    piece = rows_dp // nseq

    def row_grad_x(G, layer):
        finish((id(G), 1, layer))

        def put(dst, x):
            def one(z):
                rows = pl.ds(pl.multiple_of((2 * z + x) * piece, 16), piece)
                value = G.acc2[layer, rows, :] + G.rcv2[layer, rows, :].astype(F32)
                dst[layer, z] = value.astype(dst.dtype)

            loop(nz, one)

        put(G.snd3, 1 - xx)
        start((id(G), 2, layer), remote(G.snd3.at[layer], G.rcv3.at[layer], new_sems(1), x_peer))
        put(G.acc3, xx)

    def row_grad_z(G, layer):
        finish((id(G), 2, layer))

        def one(z):
            value = G.acc3[layer, z] + G.rcv3[layer, z].astype(F32)
            G.acc3[layer, z] = value
            G.snd4[layer, z] = value.astype(BF16)

        loop(nz, one)
        snd = G.snd4.at[layer]
        spread_z((id(G), 3, layer), lambda peer: snd.at[peer], G.rcv4.at[layer])

    def row_grad_back_z(G, layer):
        finish((id(G), 3, layer))
        value = G.acc3[layer, zz]
        for k in range(1, nz):
            value = value + G.rcv4[layer, k].astype(F32)
        G.full[layer, zz, xx] = value.astype(BF16)
        block = G.full.at[layer, zz, xx]
        total = G.full.at[layer, pl.ds(0, nz - 1), xx]
        start_all((id(G), 4, layer), total, [(block, peer) for peer in z_peers()])

    def row_grad_back_x(G, layer):
        finish((id(G), 4, layer))
        block = G.full.at[layer, :, xx]
        start((id(G), 5, layer), remote(block, block, new_sems(1), x_peer))

    def row_grad_end(G, layer):
        finish((id(G), 5, layer))
        out = O.glu_out if G is GG else O.b_out
        cols = pl.ds(p if G is BB else 0, G.full.shape[-1])

        def one(z):
            for x in range(2):
                rows = pl.ds(pl.multiple_of((2 * z + x) * piece, 16), piece)
                out[layer, rows, cols] = G.full[layer, z, x].astype(F32)

        loop(nz, one)

    small_rows = small_ref.shape[0]
    small_piece = small_rows // nseq

    def small_start():
        scale_small()
        start((8, 0), remote(small_ref, S.small_core, new_sems(1), sibling))

    def small_y():
        finish((8, 0))
        S.small_sum[0] = small_ref[...] + S.small_core[...]
        start((8, 1), remote(S.small_sum.at[0], S.small_y, new_sems(1), y_peer))

    def small_part(q):
        return pl.ds(pl.multiple_of(q * small_piece, 8), small_piece)

    def small_spread(name, src, dst, wait_ref):
        sem = new_sems(1)
        copies[name] = remote(wait_ref, wait_ref, sem, x_peer)

        def one(k):
            peer = lax.rem(me + k, nseq)
            remote(src(peer), dst(k), sem, {"seq": peer}).start()

        seq_loop(one)

    def small_scatter():
        finish((8, 1))
        S.small_sum[1] = S.small_sum[0] + S.small_y[...]
        small_spread(
            (8, 2),
            lambda peer: S.small_sum.at[1, small_part(peer), :],
            lambda k: S.small_recv.at[k],
            S.small_recv.at[pl.ds(1, nseq - 1)],
        )

    def small_gather():
        finish((8, 2))
        value = S.small_sum[1, small_part(me), :]
        for k in range(1, nseq):
            value = value + S.small_recv[k]
        S.small_sum[2, small_part(me), :] = value
        block = S.small_sum.at[2, small_part(me), :]
        small_spread(
            (8, 3), lambda peer: block, lambda k: block, S.small_recv.at[pl.ds(1, nseq - 1)]
        )

    def small_end():
        finish((8, 3))
        O.small_out[...] = S.small_sum[2]

    order = {(layers - 1, 3): [head]}
    if inside:
        order = {
            (1, 3): [
                head,
                partial(row_grad_start, GG, 1),
                partial(c_grad_start, 1, 1),
            ],
            (1, 5): [
                partial(row_grad_y, GG, 1),
            ],
            (1, 6): [
                partial(row_grad_start, BB, 1),
                partial(c_grad_first, 1, 1),
            ],
            (0, 0): [
                partial(row_grad_start, BA, 1),
                partial(row_grad_y, BB, 1),
            ],
            (0, 1): [
                partial(row_grad_start, GG, 0),
            ],
            (0, 2): [
                partial(row_grad_y, BA, 1),
            ],
            (0, 3): [
                partial(row_grad_x, GG, 1),
                partial(row_grad_y, GG, 0),
                partial(c_grad_start, 0, 1),
                partial(c_grad_start, 1, 0),
                partial(row_grad_x, BB, 1),
            ],
            (0, 5): [
                partial(row_grad_start, BB, 0),
                partial(row_grad_x, BA, 1),
                partial(c_grad_second, 1, 1),
                partial(c_grad_first, 0, 1),
                partial(row_grad_z, BB, 1),
                partial(row_grad_z, GG, 1),
                partial(c_grad_start, 0, 0),
                partial(row_grad_start, BA, 0),
                partial(row_grad_y, BB, 0),
                partial(row_grad_x, GG, 0),
                partial(row_grad_z, BA, 1),
            ],
            (0, 6): [
                partial(row_grad_y, BA, 0),
                partial(c_grad_third, 1, 1),
                small_start,
                partial(row_grad_back_z, GG, 1),
                partial(c_grad_first, 1, 0),
            ],
            (0, 7): [
                partial(row_grad_back_z, BB, 1),
                small_y,
                partial(row_grad_back_z, BA, 1),
                partial(c_grad_first, 0, 0),
                partial(c_grad_second, 0, 1),
                partial(row_grad_x, BB, 0),
                partial(row_grad_x, BA, 0),
                partial(row_grad_z, GG, 0),
                partial(row_grad_z, BB, 0),
                partial(row_grad_back_x, GG, 1),
                partial(row_grad_z, BA, 0),
                partial(c_grad_second, 1, 0),
                small_scatter,
                partial(row_grad_back_x, BB, 1),
                partial(row_grad_back_x, BA, 1),
                partial(row_grad_back_z, GG, 0),
                partial(row_grad_back_z, BB, 0),
                partial(row_grad_back_z, BA, 0),
                partial(c_grad_third, 1, 0),
                small_gather,
                partial(c_grad_second, 0, 0),
                partial(row_grad_end, BB, 1),
                partial(row_grad_back_x, BA, 0),
                partial(row_grad_end, GG, 1),
                partial(c_grad_third, 0, 1),
                partial(c_grad_end, 1, 1),
                partial(row_grad_back_x, GG, 0),
                partial(c_grad_third, 0, 0),
                partial(row_grad_end, BA, 1),
                partial(row_grad_back_x, BB, 0),
                partial(c_grad_end, 0, 1),
                partial(row_grad_end, BB, 0),
                small_end,
                partial(row_grad_end, GG, 0),
                partial(row_grad_end, BA, 0),
                partial(c_grad_end, 1, 0),
                partial(c_grad_end, 0, 0),
            ],
        }

    def stages(layer, point):
        for stage in order.get((layer, point), []):
            stage()

    grad = stream

    def first_grad(rows, first, carry):
        grad[rows, :] = row_mask(first) * grad_row
        return carry

    row_loop(first_grad, 0)

    for layer in reversed(range(layers)):
        gain = gain_ref[layer : layer + 1, :]
        bias = bias_ref[layer : layer + 1, :]
        skip = skip_ref[layer : layer + 1, :]
        zero_sum = jnp.zeros((CHUNKS, width), F32)

        def gate_back(rows, first, total, layer=layer):
            gate = sig[layer, rows, :]
            low = (grad[rows, :] * gelu_out[layer, rows, :] * gate * (1.0 - gate)).astype(BF16)
            ggrad[layer, rows, :] = low
            return total + fold8(low.astype(F32))

        total = row_loop(gate_back, zero_sum)
        stages(layer, 0)
        put_line(3 * layers + layer, jnp.sum(total, axis=0, keepdims=True))
        for col in range(0, width, 256):
            temp[:, col : col + 256] = mm_nt(ggrad[layer], glu_ref[layer, col : col + 256, :])

        def mix_back(rows, first, total, layer=layer, gain=gain, bias=bias):
            act = grad[rows, :] * sig[layer, rows, :] + temp[rows, :]
            value = act * gelu_der[layer, rows, :]
            mix[rows, :] = value
            for h in range(2):
                for first, block in half_blocks(h):
                    at = block.start
                    mlow[layer, h, rows, first : first + 128] = value[:, at : at + 128].astype(BF16)
            return total + fold8(value * (xhat[layer, rows, :] * gain + bias))

        total = row_loop(mix_back, zero_sum)
        put_line(2 * layers + layer, jnp.sum(total, axis=0, keepdims=True))
        stages(layer, 1)
        for plane in range(0, 4, 2):
            rows = [c_ref[layer, h, plane : plane + 2].reshape(2 * p, half_cols) for h in range(2)]
            wide[:, plane * p : (plane + 2) * p] = mm_nt(mlow[layer, 0], rows[0]) + mm_nt(
                mlow[layer, 1], rows[1]
            )

        lam_re, lam_im, jumps = layer_powers(layer, True)
        ends = local_ends(wide, 2 * p, 0, lam_re, lam_im)
        prefix = local_prefix(ends, jumps)
        stages(layer, 2)
        slot = layers + layer
        send_totals(slot, prefix)
        stages(layer, 3)
        if not inside:
            for h in range(2):
                for col in range(0, 4 * p, 2 * p):
                    value = mm_tn(feat[layer, :, col : col + 2 * p], mlow[layer, h]) * factor()
                    cols = slice(h * half_cols, (h + 1) * half_cols)
                    O.c_out[layer, col : col + 2 * p, cols] = value.astype(BF16)
            for col in range(0, width, 256):
                value = mm_tn(gelu_low[layer, :, col : col + 256], ggrad[layer]) * factor()
                O.glu_out[layer, col : col + 256, :] = value.astype(BF16)
        tables = (jump_table(jumps, sub), jump_table(jumps, CHUNKS - 1 - sub))
        exchange_wait(slot)
        stages(layer, 4)
        carries = chunk_carries(slot, prefix, jumps, tables)
        l_re = jnp.broadcast_to(lam_re, (CHUNKS, p))
        l_im = jnp.broadcast_to(lam_im, (CHUNKS, p))
        zero = jnp.zeros((CHUNKS, p), F32)

        def anti_grad(j, carry, layer=layer, l_re=l_re, l_im=l_im):
            r_re, r_im, d_re, d_im = carry
            rows = pl.ds(pl.multiple_of(j * CHUNKS, CHUNKS), CHUNKS)
            after = pl.ds(pl.multiple_of((j + 1) * CHUNKS, CHUNKS), CHUNKS)
            r_re, r_im = cmul(l_re, l_im, r_re, r_im)
            r_re = r_re + wide[rows, 2 * p : 3 * p]
            r_im = r_im + wide[rows, 3 * p : 4 * p]
            wide[rows, 2 * p : 3 * p] = r_re
            wide[rows, 3 * p : 4 * p] = r_im
            q_re = anti[layer, after, 0:p]
            q_im = anti[layer, after, p : 2 * p]
            return r_re, r_im, d_re + (r_re * q_re + r_im * q_im), d_im + (r_im * q_re - r_re * q_im)

        _, _, d_re, d_im = lax.fori_loop(
            0, steps, anti_grad, (carries[0], carries[1], zero, zero), unroll=4
        )
        in_scale = jnp.broadcast_to(tab_ref[layer, 2:3, :], (CHUNKS, p))

        def caus_grad(k, carry, layer=layer, l_re=l_re, l_im=l_im, in_scale=in_scale):
            a_re, a_im, d_re, d_im, s_sum = carry
            last = pl.multiple_of(tok - (k + 1) * 2 * CHUNKS, 2 * CHUNKS)
            kept_re, kept_im = [], []
            for half in (1, 0):
                rows = pl.ds(last + half * CHUNKS, CHUNKS)
                a_re, a_im = cmul(l_re, l_im, a_re, a_im)
                a_re = a_re + wide[rows, 0:p]
                a_im = a_im + wide[rows, p : 2 * p]
                q_re = caus[layer, rows, 0:p]
                q_im = caus[layer, rows, p : 2 * p]
                d_re = d_re + (a_re * q_re + a_im * q_im)
                d_im = d_im + (a_im * q_re - a_re * q_im)
                t_re = a_re + wide[rows, 2 * p : 3 * p]
                t_im = a_im + wide[rows, 3 * p : 4 * p]
                s_sum = s_sum + (
                    t_re * drive[layer, rows, 0:p] + t_im * drive[layer, rows, p : 2 * p]
                )
                kept_re.insert(0, t_re * in_scale)
                kept_im.insert(0, t_im * in_scale)
            both = pl.ds(last, 2 * CHUNKS)
            dlow[layer, both, 0:p] = jnp.concatenate(kept_re, axis=0).astype(BF16)
            dlow[layer, both, p : 2 * p] = jnp.concatenate(kept_im, axis=0).astype(BF16)
            return a_re, a_im, d_re, d_im, s_sum

        _, _, d_re, d_im, s_sum = lax.fori_loop(
            0, steps // 2, caus_grad, (carries[2], carries[3], d_re, d_im, zero), unroll=2
        )
        d_re = jnp.sum(d_re, axis=0, keepdims=True)
        d_im = jnp.sum(d_im, axis=0, keepdims=True)
        s_sum = jnp.sum(s_sum, axis=0, keepdims=True) / tab_ref[layer, 2:3, :]
        true_re = tab_ref[layer, 0:1, :]
        true_im = tab_ref[layer, 1:2, :]
        pad = jnp.zeros((1, width - p), F32)
        rate_part = s_sum * tab_ref[layer, 3:4, :] - d_re * true_re - d_im * true_im
        put_line(4 * layers + layer, jnp.concatenate([rate_part, pad], axis=1))
        phase_part = d_im * true_re - d_re * true_im
        put_line(5 * layers + layer, jnp.concatenate([phase_part, pad], axis=1))

        stages(layer, 5)
        if not inside:
            for col in range(0, width, 256):
                value = mm_tn(nlow[layer, :, col : col + 256], dlow[layer]) * factor()
                O.b_out[layer, col : col + 256, :] = value.astype(BF16)
        for col in range(0, width, 256):
            temp[:, col : col + 256] = mm_nt(dlow[layer], b_ref[layer, col : col + 256, :])

        def norm_back(rows, first, carry, layer=layer, gain=gain, skip=skip):
            gain_sum, bias_sum = carry
            ngrad = mix[rows, :] * skip + temp[rows, :]
            hat = xhat[layer, rows, :]
            q = ngrad * gain
            mean_q = jnp.mean(q, axis=1, keepdims=True)
            mean_x = jnp.mean(q * hat, axis=1, keepdims=True)
            grad[rows, :] = grad[rows, :] + (q - mean_q - hat * mean_x) * rstd[layer, rows, :]
            return gain_sum + fold8(ngrad * hat), bias_sum + fold8(ngrad)

        gain_sum, bias_sum = row_loop(norm_back, (zero_sum, zero_sum))
        put_line(layer, jnp.sum(gain_sum, axis=0, keepdims=True))
        put_line(layers + layer, jnp.sum(bias_sum, axis=0, keepdims=True))
        stages(layer, 6)

    if not inside:
        scale_small()
    for col in range(0, width, 128):
        perm[col // 128] = grad[:, col : col + 128] * factor()

        def unplace(k, carry, col=col):
            first = k * CHUNKS
            chunk = first // steps
            rows = pl.ds((first - chunk * steps) * CHUNKS + chunk, CHUNKS, stride=CHUNKS)
            out = pl.ds(pl.multiple_of(first, CHUNKS), CHUNKS)
            gin_ref[out, col : col + 128] = perm[col // 128, rows, :]
            return carry

        lax.fori_loop(0, steps, unplace, 0, unroll=4)

    stages(0, 7)


def run_model(dims, inside, operands):
    layers, tok, width, states, classes, ndp, nseq = dims
    vmem = pl.BlockSpec(memory_space=pltpu.VMEM)
    smem = pl.BlockSpec(memory_space=pltpu.SMEM)
    hbm = pl.BlockSpec(memory_space=pltpu.HBM)
    lines = -(-(6 * layers + classes + 1) // 8) * 8
    small_shape = (lines * width // 128, 128)
    slots = 2 * layers + 1
    share, rows_dp = states // nseq, width // ndp
    per_layer = lambda cols, kind, rows=tok: pltpu.VMEM((layers, rows, cols), kind)
    if inside:
        b_shape, g_shape = (layers, rows_dp, 2 * states), (layers, rows_dp, width)
        c_shape, kind = (layers, 4, share, width // ndp), F32
    else:
        b_shape, g_shape = (layers, width, 2 * states), (layers, width, width)
        c_shape, kind = (layers, 4 * states, width), BF16
    scratch = [pltpu.VMEM(a.shape, a.dtype) for a in operands[3:]]
    scratch += [
        pltpu.SemaphoreType.DMA((len(operands) - 3,)),
        pltpu.VMEM((tok, width), F32),
        per_layer(width, F32),
        per_layer(1, F32),
        per_layer(width, BF16),
        per_layer(2 * states, F32),
        per_layer(2 * states, F32, tok + CHUNKS),
        per_layer(2 * states, F32, tok + CHUNKS),
        per_layer(4 * states, BF16),
        per_layer(width, F32),
        per_layer(width, BF16),
        per_layer(width, F32),
        per_layer(width, F32),
        pltpu.VMEM((tok, 4 * states), F32),
        pltpu.VMEM((tok, width), F32),
        pltpu.VMEM((tok, width), F32),
        pltpu.VMEM((layers, 2, tok, width // 2), BF16),
        per_layer(width, BF16),
        per_layer(2 * states, BF16),
        pltpu.VMEM((8, 128), F32),
        pltpu.VMEM((width // 128, tok, 128), F32),
        pltpu.VMEM((slots, 2, 8, 128), F32),
        pltpu.VMEM((slots, nseq, 8, 128), F32),
        pltpu.SemaphoreType.DMA((slots,)),
        pltpu.SemaphoreType.DMA((slots,)),
    ]
    if inside:
        ny, nz, part, half = ndp // 2, nseq // 2, width // ndp, width // 2
        copies = 92
        scratch += [
            pltpu.VMEM((layers, 8, states), F32),
            pltpu.VMEM((nseq, 8, 128), F32),
            per_layer(2 * states, BF16, width),
            per_layer(width, BF16, width),
            pltpu.VMEM((layers, 2, 4, nz, 2, share, half), BF16),
            pltpu.SemaphoreType.DMA((copies,)),
            pltpu.SemaphoreType.DMA((copies,)),
            pltpu.VMEM(small_shape, F32),
            pltpu.VMEM(small_shape, F32),
            pltpu.VMEM(small_shape, F32),
            pltpu.VMEM((3,) + small_shape, F32),
            pltpu.VMEM((nseq, small_shape[0] // nseq, 128), F32),
        ]
        for cols in (states, states, width):
            scratch += [
                pltpu.VMEM((layers, ny, rows_dp, cols), BF16),
                pltpu.VMEM((layers, ny, rows_dp, cols), BF16),
                pltpu.VMEM((layers, ny, rows_dp, cols), F32),
                per_layer(cols, BF16, rows_dp),
                per_layer(cols, BF16, rows_dp),
                per_layer(cols, F32, rows_dp),
                pltpu.VMEM((layers, nz, rows_dp // nseq, cols), BF16),
                pltpu.VMEM((layers, nz, rows_dp // nseq, cols), BF16),
                pltpu.VMEM((layers, nz, rows_dp // nseq, cols), F32),
                pltpu.VMEM((layers, nz, rows_dp // nseq, cols), BF16),
                pltpu.VMEM((layers, nz, rows_dp // nseq, cols), BF16),
                pltpu.VMEM((layers, nz, 2, rows_dp // nseq, cols), BF16),
            ]
        scratch += [
            pltpu.VMEM((layers, 2, 4 * nz, share, half), BF16),
            pltpu.VMEM((layers, 2, 4 * nz, share, half), BF16),
            pltpu.VMEM((layers, 2, 4 * nz, share, half), F32),
            pltpu.VMEM((layers, 4 * nz, share, part), BF16),
            pltpu.VMEM((layers, 4 * nz, share, part), BF16),
            pltpu.VMEM((layers, 4 * nz, share, part), F32),
            pltpu.VMEM((layers, 2 * nz, share, half), BF16),
            pltpu.VMEM((layers, 2 * nz, share, half), BF16),
            pltpu.VMEM((layers, 2 * nz, share, half), F32),
            pltpu.VMEM((layers, 2, 2 * nz, share, part), BF16),
            pltpu.VMEM((layers, 2, 2 * nz, share, part), BF16),
            pltpu.VMEM((layers, 2, 2 * nz, share, part), F32),
            pltpu.VMEM((layers, 2, nz, 2, share, part), BF16),
            pltpu.VMEM((layers, 2, nz, 2, share, part), BF16),
        ]
    return pl.pallas_call(
        partial(model_kernel, dims, inside),
        out_shape=(
            jax.ShapeDtypeStruct((tok, width), F32),
            jax.ShapeDtypeStruct(small_shape, F32),
            jax.ShapeDtypeStruct(b_shape, kind),
            jax.ShapeDtypeStruct(g_shape, kind),
            jax.ShapeDtypeStruct(c_shape, kind),
        ),
        in_specs=[smem] * 3 + [hbm] * (len(operands) - 3),
        out_specs=[vmem] * 5,
        scratch_shapes=scratch,
        compiler_params=pltpu.CompilerParams(
            collective_id=0, has_side_effects=True, vmem_limit_bytes=48 * 1024 * 1024
        ),
        cost_estimate=pl.CostEstimate(
            flops=6 * layers * tok * width * (6 * states + width),
            bytes_accessed=16 * 1024 * 1024,
            transcendentals=2 * layers * tok * width,
        ),
    )(*operands[:3], *[pltpu.with_memory_space_constraint(a, pltpu.HBM) for a in operands[3:]])


def finish_kernel(dims, *refs):
    layers, tok, width, states, classes, ndp, nseq = dims
    small = refs[4]
    loss, gain, bias, rate, phase, skip, glub, head_w, head_b = refs[9:18]
    sems = refs[18]
    outward = [pltpu.make_async_copy(refs[k], refs[5 + k], sems.at[k]) for k in range(4)]
    for copy in outward:
        copy.start()
    tiles = width // 128

    def line(row, count=tiles):
        parts = [small[row * tiles + t : row * tiles + t + 1, :] for t in range(count)]
        return jnp.concatenate(parts, axis=1)

    for layer in range(layers):
        at = slice(layer, layer + 1)
        gain[at, :] = line(layer)
        bias[at, :] = line(layers + layer)
        skip[at, :] = line(2 * layers + layer)
        glub[at, :] = line(3 * layers + layer)
    share = states // nseq
    me = lax.axis_index("seq")
    for first, out in ((4 * layers, rate), (5 * layers, phase)):
        every = jnp.concatenate([line(first + layer) for layer in range(layers)], axis=0)
        mine = every[:, 0:share]
        for q in range(1, nseq):
            mine = jnp.where(me == q, every[:, q * share : (q + 1) * share], mine)
        out[...] = mine
    head = 6 * layers
    for k in range(classes):
        head_w[k : k + 1, :] = line(head + k)
    last = line(head + classes)
    head_b[...] = last[:, 0:classes]
    loss[...] = last[:, classes : classes + 1] / ndp
    for copy in outward:
        copy.wait()


def finish_outputs(dims, grad_inputs, small, b_grad, g_grad, c_grad):
    layers, tok, width, states, classes, ndp, nseq = dims
    vmem = pl.BlockSpec(memory_space=pltpu.VMEM)
    anywhere = pl.BlockSpec(memory_space=pl.ANY)
    large = (grad_inputs, b_grad, g_grad, c_grad)
    share = states // nseq
    rows = (layers, width)
    shapes = [(1, 1), rows, rows, (layers, share), (layers, share), rows, rows, (classes, width)]
    shapes.append((1, classes))
    results = pl.pallas_call(
        partial(finish_kernel, dims),
        out_shape=[jax.ShapeDtypeStruct(a.shape, F32) for a in large]
        + [jax.ShapeDtypeStruct(shape, F32) for shape in shapes],
        in_specs=[vmem] * 5,
        out_specs=[anywhere] * 4 + [vmem] * 9,
        scratch_shapes=[pltpu.SemaphoreType.DMA((4,))],
        compiler_params=pltpu.CompilerParams(vmem_limit_bytes=8 * 1024 * 1024),
    )(*large, small)
    gin, b_share, g_share, c_share, loss, gain, bias, rate, phase, skip, glub, head_w, head_b = results
    return (
        loss.reshape(()),
        gin[None],
        gain,
        bias,
        b_share,
        rate,
        phase,
        c_share,
        skip,
        g_share,
        glub,
        head_w.T,
        head_b.reshape(classes),
    )


def per_device(
    inputs,
    lengths,
    labels,
    norm_gain,
    norm_bias,
    b_proj,
    rate,
    phase,
    c_proj,
    skip,
    glu_weight,
    glu_bias,
    class_weight,
    class_bias,
):
    layers, width = norm_gain.shape
    tok = inputs.shape[1]
    ndp = lax.axis_size("dp")
    nseq = lax.axis_size("seq")
    states = c_proj.shape[2] * nseq
    classes = class_bias.shape[0]
    dims = (layers, tok, width, states, classes, ndp, nseq)
    share = states // nseq
    inside = (
        ndp == 4
        and nseq % 2 == 0
        and share % 16 == 0
        and (width // ndp) % 128 == 0
        and (width // ndp) % (16 * nseq) == 0
        and 4 * layers == 8
    )
    if inside:
        tables = (rate, phase)
        weights = (b_proj, glu_weight, c_proj)
    else:
        decay = jnp.exp(-rate)
        in_scale = jnp.sqrt(-jnp.expm1(-2.0 * rate))
        rows = [
            decay * jnp.cos(phase),
            decay * jnp.sin(phase),
            in_scale,
            jnp.exp(-2.0 * rate) / in_scale,
        ]
        table = lax.all_gather(jnp.stack(rows, axis=1), "seq", axis=2, tiled=True)
        tables = (table, phase)
        b_full = lax.all_gather(b_proj.astype(BF16), "dp", axis=1, tiled=True)
        g_full = lax.all_gather(glu_weight.astype(BF16), "dp", axis=1, tiled=True)
        c_half = lax.all_gather(c_proj.astype(BF16), "dp", axis=3, tiled=True)
        c_full = lax.all_gather(c_half, "seq", axis=2, tiled=True)
        c_full = c_full.reshape(layers, 4, states, 2, width // 2)
        c_full = jnp.moveaxis(c_full, 3, 1)
        weights = (b_full, g_full, c_full)
    grad_inputs, small, b_grad, g_grad, c_grad = run_model(
        dims,
        inside,
        (
            lengths,
            labels,
            class_bias,
            inputs[0],
            norm_gain,
            norm_bias,
            skip,
            glu_bias,
            *tables,
            class_weight.T,
            *weights,
        ),
    )
    if inside:
        return finish_outputs(dims, grad_inputs, small, b_grad, g_grad, c_grad)
    else:
        b_share = lax.psum_scatter(b_grad, "dp", scatter_dimension=1, tiled=True)
        g_share = lax.psum_scatter(g_grad, "dp", scatter_dimension=1, tiled=True)
        b_share = lax.psum(b_share, "seq").astype(F32)
        g_share = lax.psum(g_share, "seq").astype(F32)
        c_grad = c_grad.reshape(layers, 4, states, width)
        c_share = lax.psum_scatter(c_grad, "seq", scatter_dimension=2, tiled=True)
        c_share = lax.psum_scatter(c_share, "dp", scatter_dimension=3, tiled=True).astype(F32)
        small = lax.psum(small, ("dp", "seq"))
    small = small.reshape(-1, width)
    own = lax.axis_index("seq") * (states // nseq)

    def state_rows(first):
        return lax.dynamic_slice(small[first : first + layers], (0, own), (layers, states // nseq))

    head = 6 * layers
    return (
        small[head + classes, classes] / ndp,
        grad_inputs[None],
        small[0:layers],
        small[layers : 2 * layers],
        b_share,
        state_rows(4 * layers),
        state_rows(5 * layers),
        c_share,
        small[2 * layers : 3 * layers],
        g_share,
        small[3 * layers : 4 * layers],
        small[head : head + classes].T,
        small[head + classes, 0:classes],
    )


def solution(mesh):
    return jax.shard_map(
        per_device,
        mesh=mesh,
        in_specs=(
            P("dp", "seq", None),
            P("dp"),
            P("dp"),
            P(),
            P(),
            P(None, "dp", None),
            P(None, "seq"),
            P(None, "seq"),
            P(None, None, "seq", "dp"),
            P(),
            P(None, "dp", None),
            P(),
            P(),
            P(),
        ),
        out_specs=(
            P(),
            P("dp", "seq", None),
            P(),
            P(),
            P(None, "dp", None),
            P(None, "seq"),
            P(None, "seq"),
            P(None, None, "seq", "dp"),
            P(),
            P(None, "dp", None),
            P(),
            P(),
            P(),
        ),
        check_vma=False,
    )
```

```python
from functools import partial
from typing import Any, NamedTuple

import jax
import jax.numpy as jnp
from jax import lax
from jax.experimental import pallas as pl
from jax.experimental.pallas import tpu as pltpu
from jax.sharding import PartitionSpec as P

MESH = pl.DeviceIdType.MESH
F32 = jnp.float32
BF16 = jnp.bfloat16
CHUNKS = 8
TILE = 32
GELU_A = 0.7978845608028654
GELU_B = 0.044715


def mm_nn(left, right):
    return lax.dot_general(left, right, (((1,), (0,)), ((), ())), preferred_element_type=F32)


def mm_nt(left, right):
    return lax.dot_general(left, right, (((1,), (1,)), ((), ())), preferred_element_type=F32)


def mm_tn(left, right):
    return lax.dot_general(left, right, (((0,), (0,)), ((), ())), preferred_element_type=F32)


def cmul(a_re, a_im, b_re, b_im):
    return a_re * b_re - a_im * b_im, a_re * b_im + a_im * b_re


def fold8(value):
    total = value[0:8]
    for first in range(8, value.shape[0], 8):
        total = total + value[first : first + 8]
    return total


class Operands(NamedTuple):
    len: Any
    lab: Any
    cb: Any
    x: Any
    gain: Any
    bias: Any
    skip: Any
    glub: Any
    rate: Any
    phase: Any
    cw: Any
    b_in: Any
    glu_in: Any
    c_in: Any


class Results(NamedTuple):
    gin: Any
    small_out: Any
    b_out: Any
    glu_out: Any
    c_out: Any


class Local(NamedTuple):
    stream: Any
    xhat: Any
    rstd: Any
    nlow: Any
    drive: Any
    caus: Any
    anti: Any
    feat: Any
    gelu_out: Any
    gelu_low: Any
    gelu_der: Any
    sig: Any
    wide: Any
    temp: Any
    mix: Any
    mlow: Any
    ggrad: Any
    dlow: Any
    scale: Any
    perm: Any
    send_buf: Any
    recv_buf: Any
    send_sem: Any
    recv_sem: Any


class Shared(NamedTuple):
    tab: Any
    tab_recv: Any
    b_buf: Any
    glu_buf: Any
    c_buf: Any
    ssem: Any
    rsem: Any
    small: Any
    small_core: Any
    small_y: Any
    small_sum: Any
    small_recv: Any


class RowGrad(NamedTuple):
    snd1: Any
    rcv1: Any
    acc: Any
    snd2: Any
    rcv2: Any
    acc2: Any
    snd3: Any
    rcv3: Any
    acc3: Any
    snd4: Any
    rcv4: Any
    full: Any


class ColGrad(NamedTuple):
    snd1: Any
    rcv1: Any
    acc: Any
    snd2a: Any
    rcv2a: Any
    acc2a: Any
    snd2b: Any
    rcv2b: Any
    acc2b: Any
    snd3: Any
    rcv3: Any
    acc3: Any
    snd4: Any
    rcv4: Any


def take(refs, kind):
    count = len(kind._fields)
    return kind(*refs[:count]), refs[count:]


def model_kernel(dims, inside, *refs):
    layers, tok, width, states, classes, ndp, nseq = dims
    given, refs = take(refs, Operands)
    O, refs = take(refs, Results)
    fetched, refs = refs[: len(given) - 3], refs[len(given) - 3 :]
    fetch_sem, refs = refs[0], refs[1:]
    I = Operands(*given[:3], *fetched)
    L, refs = take(refs, Local)
    if inside:
        S, refs = take(refs, Shared)
        BA, refs = take(refs, RowGrad)
        BB, refs = take(refs, RowGrad)
        GG, refs = take(refs, RowGrad)
        CG, refs = take(refs, ColGrad)
        tab_ref, b_ref, glu_ref, c_ref, small_ref = S.tab, S.b_buf, S.glu_buf, S.c_buf, S.small
    else:
        tab_ref, b_ref, glu_ref, c_ref, small_ref = I.rate, I.b_in, I.glu_in, I.c_in, O.small_out
    len_ref, lab_ref, x_ref = I.len, I.lab, I.x
    gain_ref, bias_ref, skip_ref, glub_ref = I.gain, I.bias, I.skip, I.glub
    cw_ref, cb_ref, gin_ref = I.cw, I.cb, O.gin
    stream, xhat, rstd, nlow, drive = L.stream, L.xhat, L.rstd, L.nlow, L.drive
    caus, anti, feat, gelu_out, gelu_low = L.caus, L.anti, L.feat, L.gelu_out, L.gelu_low
    gelu_der, sig, wide, temp, mix = L.gelu_der, L.sig, L.wide, L.temp, L.mix
    mlow, ggrad, dlow, perm = L.mlow, L.ggrad, L.dlow, L.perm
    send_buf, recv_buf = L.send_buf, L.recv_buf
    send_sem, recv_sem = L.send_sem, L.recv_sem
    steps = tok // CHUNKS
    half_cols = width // 2
    me = lax.axis_index("seq")
    my_dp = lax.axis_index("dp")
    p = states
    core, yy = lax.rem(my_dp, 2), my_dp // 2
    xx, zz = lax.rem(me, 2), me // 2
    ny, nz = ndp // 2, nseq // 2
    own_half = core if inside else 0

    barrier = pltpu.get_barrier_semaphore()

    def greet(k, carry):
        peer = lax.rem(me + k, nseq)
        pl.semaphore_signal(barrier, inc=1, device_id={"seq": peer}, device_id_type=MESH)
        return carry

    lax.fori_loop(1, nseq, greet, 0, unroll=True)
    greeted = nseq - 1
    sibling = {"dp": 2 * yy + 1 - core}
    y_peer = {"dp": 2 * (1 - yy) + core}
    x_peer = {"seq": 2 * zz + 1 - xx}
    if inside:
        for peer in (sibling, y_peer):
            pl.semaphore_signal(barrier, inc=1, device_id=peer, device_id_type=MESH)
        greeted += 2

    fetches = [
        pltpu.make_async_copy(src, dst, fetch_sem.at[k])
        for k, (src, dst) in enumerate(zip(given[3:], fetched))
    ]
    for fetch in reversed(fetches):
        fetch.start()

    used = [0]

    def new_sems(count):
        first = used[0]
        used[0] += count
        return first

    def remote(src, dst, sem, peer):
        return pltpu.make_async_remote_copy(
            src_ref=src,
            dst_ref=dst,
            send_sem=S.ssem.at[sem],
            recv_sem=S.rsem.at[sem],
            device_id=peer,
            device_id_type=MESH,
        )

    def seq_loop(body):
        def one(k, carry):
            body(k)
            return carry

        lax.fori_loop(1, nseq, one, 0, unroll=True)

    def cast_rows(dst, src, rows, step, extra=None):
        def one(k, carry):
            part = pl.ds(pl.multiple_of(k * step, step), step)
            value = src[part, :].astype(F32)
            if extra is not None:
                value = value + extra[part, :].astype(F32)
            dst[part, :] = value.astype(dst.dtype)
            return carry

        lax.fori_loop(0, rows // step, one, 0, unroll=4)

    def row_loop(body, init, unroll=4):
        def step(k, carry):
            rows = pl.ds(pl.multiple_of(k * TILE, TILE), TILE)
            return body(rows, k * TILE, carry)

        return lax.fori_loop(0, tok // TILE, step, init, unroll=unroll)

    def exchange_start(slot):
        def one(k, carry):
            peer = lax.rem(me + k, nseq)
            pltpu.make_async_remote_copy(
                src_ref=send_buf.at[slot, (peer - me + nseq) // nseq],
                dst_ref=recv_buf.at[slot, k],
                send_sem=send_sem.at[slot],
                recv_sem=recv_sem.at[slot],
                device_id={"seq": peer},
                device_id_type=MESH,
            ).start()
            return carry

        lax.fori_loop(1, nseq, one, 0, unroll=True)

    def exchange_wait(slot):
        arrived = recv_buf.at[slot, pl.ds(1, nseq - 1)]
        pltpu.make_async_remote_copy(
            src_ref=arrived,
            dst_ref=arrived,
            send_sem=send_sem.at[slot],
            recv_sem=recv_sem.at[slot],
            device_id={"seq": lax.rem(me + 1, nseq)},
            device_id_type=MESH,
        ).wait()

    def from_rank(q):
        return lax.rem(me - q + nseq, nseq)

    sub = lax.broadcasted_iota(jnp.int32, (CHUNKS, p), 0)

    def layer_powers(layer, conj):
        lam_re = tab_ref[layer, 0:1, :]
        lam_im = tab_ref[layer, 1:2, :]
        if conj:
            lam_im = -lam_im
        pw_re, pw_im = lam_re, lam_im
        count = 1
        while count < steps:
            pw_re, pw_im = cmul(pw_re, pw_im, pw_re, pw_im)
            count *= 2
        jumps = [(pw_re, pw_im)]
        for _ in range(3):
            pw_re, pw_im = cmul(pw_re, pw_im, pw_re, pw_im)
            jumps.append((pw_re, pw_im))
        return lam_re, lam_im, jumps

    def jump_table(jumps, index):
        re = jnp.ones((CHUNKS, p), F32)
        im = jnp.zeros((CHUNKS, p), F32)
        for bit in range(3):
            new_re, new_im = cmul(re, im, jumps[bit][0], jumps[bit][1])
            has = (index & (1 << bit)) != 0
            re = jnp.where(has, new_re, re)
            im = jnp.where(has, new_im, im)
        return re, im

    def local_ends(src, first_c, first_a, lam_re, lam_im):
        zero = jnp.zeros((CHUNKS, p), F32)
        l_re = jnp.broadcast_to(lam_re, (CHUNKS, p))
        l_im = jnp.broadcast_to(lam_im, (CHUNKS, p))

        def step(j, carry):
            e_re, e_im, f_re, f_im = carry
            up = pl.ds(pl.multiple_of(j * CHUNKS, CHUNKS), CHUNKS)
            down = pl.ds(pl.multiple_of((steps - 1 - j) * CHUNKS, CHUNKS), CHUNKS)
            e_re, e_im = cmul(l_re, l_im, e_re, e_im)
            f_re, f_im = cmul(l_re, l_im, f_re, f_im)
            return (
                e_re + src[up, first_c : first_c + p],
                e_im + src[up, first_c + p : first_c + 2 * p],
                f_re + src[down, first_a : first_a + p],
                f_im + src[down, first_a + p : first_a + 2 * p],
            )

        return lax.fori_loop(0, steps, step, (zero,) * 4, unroll=8)

    def local_prefix(ends, jumps):
        e_re, e_im, f_re, f_im = ends
        for bit in range(3):
            shift = 1 << bit
            j_re, j_im = jumps[bit]
            s_re = jnp.where(sub >= shift, pltpu.roll(e_re, shift, 0), 0.0)
            s_im = jnp.where(sub >= shift, pltpu.roll(e_im, shift, 0), 0.0)
            a_re, a_im = cmul(j_re, j_im, s_re, s_im)
            e_re, e_im = e_re + a_re, e_im + a_im
            s_re = jnp.where(sub < CHUNKS - shift, pltpu.roll(f_re, CHUNKS - shift, 0), 0.0)
            s_im = jnp.where(sub < CHUNKS - shift, pltpu.roll(f_im, CHUNKS - shift, 0), 0.0)
            a_re, a_im = cmul(j_re, j_im, s_re, s_im)
            f_re, f_im = f_re + a_re, f_im + a_im
        return e_re, e_im, f_re, f_im

    def send_totals(slot, prefix):
        e_re, e_im, f_re, f_im = prefix
        last, first = slice(CHUNKS - 1, CHUNKS), slice(0, 1)
        for tile in range(p // 128):
            cols = slice(tile * 128, tile * 128 + 128)
            for row, value, part, at in (
                (tile, e_re, 1, last),
                (p // 128 + tile, e_im, 1, last),
                (tile, f_re, 0, first),
                (p // 128 + tile, f_im, 0, first),
            ):
                send_buf[slot, part, row : row + 1, :] = value[at, cols]
        exchange_start(slot)

    def chunk_carries(slot, prefix, jumps, tables):
        e_re, e_im, f_re, f_im = prefix
        d_re, d_im = jumps[3]
        zero = jnp.zeros((1, p), F32)

        def arrived(q, first):
            rows = range(first, first + p // 128)
            return jnp.concatenate([recv_buf[slot, from_rank(q), r : r + 1, :] for r in rows], axis=1)

        def step(k, carry):
            c_re, c_im, a_re, a_im = carry
            n_re, n_im = cmul(d_re, d_im, c_re, c_im)
            use = k < me
            c_re = jnp.where(use, n_re + arrived(k, 0), c_re)
            c_im = jnp.where(use, n_im + arrived(k, p // 128), c_im)
            back = nseq - 1 - k
            n_re, n_im = cmul(d_re, d_im, a_re, a_im)
            use = back > me
            a_re = jnp.where(use, n_re + arrived(back, 0), a_re)
            a_im = jnp.where(use, n_im + arrived(back, p // 128), a_im)
            return c_re, c_im, a_re, a_im

        c_re, c_im, a_re, a_im = lax.fori_loop(0, nseq, step, (zero,) * 4, unroll=True)
        t_re, t_im = tables[0]
        g_re, g_im = cmul(t_re, t_im, c_re, c_im)
        in_c_re = g_re + jnp.where(sub >= 1, pltpu.roll(e_re, 1, 0), 0.0)
        in_c_im = g_im + jnp.where(sub >= 1, pltpu.roll(e_im, 1, 0), 0.0)
        t_re, t_im = tables[1]
        g_re, g_im = cmul(t_re, t_im, a_re, a_im)
        in_a_re = g_re + jnp.where(sub < CHUNKS - 1, pltpu.roll(f_re, CHUNKS - 1, 0), 0.0)
        in_a_im = g_im + jnp.where(sub < CHUNKS - 1, pltpu.roll(f_im, CHUNKS - 1, 0), 0.0)
        return in_c_re, in_c_im, in_a_re, in_a_im

    def half_blocks(half):
        blocks = []
        for first in range(0, half_cols, 128):
            if inside:
                at = (2 * (first // part_cols) + half) * part_cols + first % part_cols
            else:
                at = half * half_cols + first
            if not isinstance(at, int):
                at = pl.multiple_of(at, 128)
            blocks.append((first, pl.ds(at, 128)))
        return blocks

    def put_line(line, row):
        for col in range(0, width, 128):
            at = line * (width // 128) + col // 128
            small_ref[at : at + 1, :] = row[:, col : col + 128]

    part_cols = width // ndp
    rows_dp = width // ndp
    share = p // nseq

    def own_rows(index):
        return pl.ds(pl.multiple_of(index * rows_dp, 16), rows_dp)

    def cast_c(layer):
        cols = pl.ds(pl.multiple_of(yy * part_cols, 128), part_cols)
        c_ref[layer, core, :, zz, xx, :, cols] = I.c_in[layer].astype(BF16)

    def cast_b(layer):
        b_ref[layer, own_rows(my_dp), :] = I.b_in[layer].astype(BF16)

    def cast_glu(layer):
        glu_ref[layer, own_rows(my_dp), :] = I.glu_in[layer].astype(BF16)

    copies, sem_of = {}, {}

    def start(name, copy):
        copies[name] = copy
        copy.start()

    def finish(name):
        copies.pop(name).wait()

    def ensure(name):
        if name in copies:
            finish(name)

    def y_cols(y):
        return pl.ds(pl.multiple_of(y * part_cols, 128), part_cols)

    def start_all(name, total, pairs):
        if name not in copies:
            sem_of[name] = new_sems(1)
            copies[name] = remote(total, total, sem_of[name], x_peer)
        for block, peer in pairs:
            remote(block, block, sem_of[name], peer).start()

    def z_peers():
        return [{"seq": 2 * lax.rem(zz + k, nz) + xx} for k in range(1, nz)]

    front, back = pl.ds(0, 2), pl.ds(2, 2)
    other_y = 1 - yy

    def c_piece(layer, planes, z, x, y):
        return c_ref.at[layer, core, planes, z, x, :, y_cols(y)]

    def c_to_z(name, layer, planes, y):
        total = c_ref.at[layer, core, planes, pl.ds(0, nz - 1), xx, :, y_cols(y)]
        block = c_piece(layer, planes, zz, xx, y)
        start_all((name, layer), total, [(block, peer) for peer in z_peers()])

    def c_to_x(layer, planes, y, others):
        if planes is front:
            name, total = 3, c_ref.at[layer, core, planes, :, xx]
        else:
            name, total = 13, c_ref.at[layer, core, planes, :, xx, :, y_cols(yy)]
        ranks = [lax.rem(zz + k, nz) for k in range(1, nz)] if others else [zz]
        pairs = [(c_piece(layer, planes, z, xx, y), x_peer) for z in ranks]
        start_all((name, layer), total, pairs)

    def one_copy(name, layer, block, peer):
        start((name, layer), remote(block, block, new_sems(1), peer))

    def to_sibling(layer, block):
        start_all((4, layer), c_ref.at[layer, core], [(block, sibling)])

    def back_to_y(layer, x):
        total = c_ref.at[layer, core, back, :, :, :, y_cols(yy)]
        block = c_ref.at[layer, core, back, :, x, :, y_cols(yy)]
        start_all((14, layer), total, [(block, y_peer)])

    def cya(layer):
        one_copy(0, layer, c_piece(layer, front, zz, xx, yy), y_peer)

    def spoa(layer):
        c_to_z(1, layer, front, yy)

    def xoa(layer):
        c_to_x(layer, front, yy, False)

    def spta(layer):
        ensure((0, layer))
        c_to_z(2, layer, front, other_y)

    def xta(layer):
        ensure((0, layer))
        c_to_x(layer, front, other_y, False)

    def poa(layer):
        ensure((1, layer))
        c_to_x(layer, front, yy, True)

    def pta(layer):
        ensure((2, layer))
        c_to_x(layer, front, other_y, True)

    def caa(layer):
        ensure((1, layer))
        ensure((2, layer))
        to_sibling(layer, c_ref.at[layer, core, front, :, xx])

    def cba(layer):
        ensure((3, layer))
        to_sibling(layer, c_ref.at[layer, core, front, :, 1 - xx])

    def zb(layer):
        c_to_z(12, layer, back, yy)

    def xb(layer):
        c_to_x(layer, back, yy, False)

    def pb(layer):
        ensure((12, layer))
        c_to_x(layer, back, yy, True)

    def yb1(layer):
        ensure((12, layer))
        back_to_y(layer, xx)

    def yb2(layer):
        ensure((13, layer))
        back_to_y(layer, 1 - xx)

    def kb1(layer):
        ensure((12, layer))
        ensure((13, layer))
        to_sibling(layer, c_ref.at[layer, core, back, :, :, :, y_cols(yy)])

    def kb2(layer):
        ensure((14, layer))
        to_sibling(layer, c_ref.at[layer, core, back, :, :, :, y_cols(other_y)])

    def c_stage_5(layer):
        finish((4, layer))

    def row_to_y(ref, layer):
        block = ref.at[layer, own_rows(my_dp), :]
        start((id(ref), 0, layer), remote(block, block, new_sems(1), y_peer))

    def row_to_sibling(ref, layer):
        block = ref.at[layer, own_rows(my_dp), :]
        start_all((id(ref), 1, layer), ref.at[layer, pl.ds(0, 2 * rows_dp), :], [(block, sibling)])

    def row_pass(ref, layer):
        finish((id(ref), 0, layer))
        block = ref.at[layer, own_rows(2 * (1 - yy) + core), :]
        start_all((id(ref), 1, layer), ref.at[layer, pl.ds(0, 2 * rows_dp), :], [(block, sibling)])

    def row_stage_end(ref, layer):
        finish((id(ref), 1, layer))

    def table_stage():
        every, own = S.tab_recv, S.tab_recv.at[0]
        rate, phase = I.rate[...], I.phase[...]
        decay = jnp.exp(-rate)
        twice = 2.0 * rate
        series = 1.0 - twice / 7.0
        for term in (6.0, 5.0, 4.0, 3.0, 2.0):
            series = 1.0 - series * (twice / term)
        loss = jnp.where(twice < 0.25, twice * series, 1.0 - jnp.exp(-twice))
        in_scale = jnp.sqrt(loss)
        every[0] = jnp.zeros((8, 128), F32)
        parts = (decay * jnp.cos(phase), decay * jnp.sin(phase), in_scale, jnp.exp(-twice) / in_scale)
        for row, value in enumerate(parts):
            for layer in range(layers):
                at = 4 * layer + row
                every[0, at : at + 1, 0:share] = value[layer : layer + 1]
        arrived = every.at[pl.ds(1, nseq - 1)]
        sem = new_sems(1)
        copies[8, 8] = remote(arrived, arrived, sem, x_peer)

        def one(k):
            remote(own, every.at[k], sem, {"seq": lax.rem(me + k, nseq)}).start()

        seq_loop(one)

    def table_end():
        finish((8, 8))
        lane = lax.broadcasted_iota(jnp.int32, (8, 128), 1)
        tiles = [jnp.zeros((8, 128), F32) for _ in range(p // 128)]
        for q in range(nseq):
            tile, first = (q * share) // 128, (q * share) % 128
            piece = S.tab_recv[from_rank(q)]
            if first:
                piece = pltpu.roll(piece, first, 1)
            here = (lane >= first) & (lane < first + share)
            tiles[tile] = jnp.where(here, piece, tiles[tile])
            if first + share > 128:
                tiles[tile + 1] = jnp.where(lane < first + share - 128, piece, tiles[tile + 1])
        for layer in range(layers):
            for tile in range(p // 128):
                tab_ref[layer, 0:4, tile * 128 : tile * 128 + 128] = tiles[tile][
                    4 * layer : 4 * layer + 4
                ]

    early = {}
    if inside:
        early = {
            (0, 10): [
                partial(cya, 0),
                partial(row_to_y, b_ref, 0),
                partial(zb, 0),
                table_stage,
                partial(xb, 0),
                partial(row_to_y, glu_ref, 0),
                partial(xoa, 0),
                partial(spoa, 0),
            ],
            (0, 12): [
                partial(pb, 0),
                partial(row_to_sibling, b_ref, 1),
                partial(xb, 1),
                partial(xta, 0),
                partial(cya, 1),
                partial(spta, 0),
                partial(yb1, 0),
                partial(row_to_sibling, b_ref, 0),
                partial(row_pass, b_ref, 0),
                partial(zb, 1),
                partial(spoa, 1),
                table_end,
                partial(poa, 0),
                partial(row_pass, glu_ref, 0),
                partial(yb2, 0),
                partial(pta, 0),
            ],
            (0, 14): [
                partial(row_to_y, b_ref, 1),
                partial(pb, 1),
                partial(kb1, 0),
                partial(spta, 1),
                partial(yb1, 1),
            ],
            (0, 15): [
                partial(xta, 1),
                partial(kb2, 0),
                partial(cba, 0),
                partial(xoa, 1),
                partial(yb2, 1),
                partial(caa, 0),
                partial(row_to_sibling, glu_ref, 0),
                partial(poa, 1),
                partial(row_to_sibling, glu_ref, 1),
            ],
            (0, 16): [
                partial(row_to_y, glu_ref, 1),
            ],
            (0, 19): [
                partial(row_pass, b_ref, 1),
                partial(pta, 1),
            ],
            (0, 20): [
                partial(caa, 1),
            ],
            (1, 14): [
                partial(kb1, 1),
                partial(cba, 1),
                partial(kb2, 1),
            ],
            (1, 15): [
                partial(row_pass, glu_ref, 1),
            ],
        }

    def gather(layer, point):
        for stage in early.get((layer, point), []):
            stage()

    for fetch in reversed(fetches):
        fetch.wait()
    if inside:
        for layer in range(layers):
            cast_c(layer)
            cast_b(layer)
            cast_glu(layer)
    pl.semaphore_wait(barrier, greeted)
    gather(0, 10)
    for col in range(0, width, 128):
        perm[col // 128] = x_ref[:, col : col + 128].astype(F32)

        def place(j, carry, col=col):
            rows = pl.ds(pl.multiple_of(j * CHUNKS, CHUNKS), CHUNKS)
            stream[rows, col : col + 128] = perm[col // 128, pl.ds(j, CHUNKS, stride=steps), :]
            return carry

        lax.fori_loop(0, steps, place, 0, unroll=4)

    for layer in range(layers):
        gain = gain_ref[layer : layer + 1, :]
        bias = bias_ref[layer : layer + 1, :]
        skip = skip_ref[layer : layer + 1, :]

        def norm_rows(rows, first, carry, layer=layer, gain=gain, bias=bias):
            value = stream[rows, :]
            center = value - jnp.mean(value, axis=1, keepdims=True)
            spread = jnp.mean(center * center, axis=1, keepdims=True)
            inv = lax.rsqrt(spread + 1e-05)
            hat = center * inv
            xhat[layer, rows, :] = hat
            rstd[layer, rows, :] = inv
            nlow[layer, rows, :] = (hat * gain + bias).astype(BF16)
            return carry

        row_loop(norm_rows, 0)
        if layer == 0:
            gather(0, 11)
        gather(layer, 12)

        if inside:
            row_stage_end(b_ref, layer)
        in_scale = tab_ref[layer, 2:3, :]
        for col in range(0, 2 * p, 256):
            part = mm_nn(nlow[layer], b_ref[layer, :, col : col + 256])
            for half in range(col, col + 256, 128):
                scale_col = half % p
                drive[layer, :, half : half + 128] = (
                    part[:, half - col : half - col + 128].astype(BF16).astype(F32)
                    * in_scale[:, scale_col : scale_col + 128]
                )

        lam_re, lam_im, jumps = layer_powers(layer, False)
        ends = local_ends(drive.at[layer], 0, 0, lam_re, lam_im)
        prefix = local_prefix(ends, jumps)
        gather(layer, 13)
        send_totals(layer, prefix)
        gather(layer, 14)
        tables = (jump_table(jumps, sub), jump_table(jumps, CHUNKS - 1 - sub))
        exchange_wait(layer)
        gather(layer, 15)
        carries = chunk_carries(layer, prefix, jumps, tables)
        caus[layer, 0:CHUNKS, 0:p] = carries[0]
        caus[layer, 0:CHUNKS, p : 2 * p] = carries[1]
        anti[layer, tok : tok + CHUNKS, 0:p] = carries[2]
        anti[layer, tok : tok + CHUNKS, p : 2 * p] = carries[3]
        l_re = jnp.broadcast_to(lam_re, (CHUNKS, p))
        l_im = jnp.broadcast_to(lam_im, (CHUNKS, p))

        def state_pair(k, carry, layer=layer, l_re=l_re, l_im=l_im):
            s_re, s_im, r_re, r_im = carry
            first = pl.multiple_of(k * 2 * CHUNKS, 2 * CHUNKS)
            kept_re, kept_im = [], []
            for half in range(2):
                rows = pl.ds(first + half * CHUNKS, CHUNKS)
                s_re, s_im = cmul(l_re, l_im, s_re, s_im)
                s_re = s_re + drive[layer, rows, 0:p]
                s_im = s_im + drive[layer, rows, p : 2 * p]
                after = pl.ds(first + (half + 1) * CHUNKS, CHUNKS)
                caus[layer, after, 0:p] = s_re
                caus[layer, after, p : 2 * p] = s_im
                kept_re.append(s_re)
                kept_im.append(s_im)
            both = pl.ds(first, 2 * CHUNKS)
            feat[layer, both, 0:p] = jnp.concatenate(kept_re, axis=0).astype(BF16)
            feat[layer, both, p : 2 * p] = jnp.concatenate(kept_im, axis=0).astype(BF16)
            last = pl.multiple_of(tok - (k + 1) * 2 * CHUNKS, 2 * CHUNKS)
            kept_re, kept_im = [], []
            for half in (1, 0):
                rows = pl.ds(last + half * CHUNKS, CHUNKS)
                r_re, r_im = cmul(l_re, l_im, r_re, r_im)
                r_re = r_re + drive[layer, rows, 0:p]
                r_im = r_im + drive[layer, rows, p : 2 * p]
                anti[layer, rows, 0:p] = r_re
                anti[layer, rows, p : 2 * p] = r_im
                kept_re.insert(0, r_re)
                kept_im.insert(0, r_im)
            both = pl.ds(last, 2 * CHUNKS)
            feat[layer, both, 2 * p : 3 * p] = jnp.concatenate(kept_re, axis=0).astype(BF16)
            feat[layer, both, 3 * p : 4 * p] = jnp.concatenate(kept_im, axis=0).astype(BF16)
            return s_re, s_im, r_re, r_im

        lax.fori_loop(0, steps // 2, state_pair, carries, unroll=4)

        gather(layer, 16)
        for turn in range(2):
            half = (1 - own_half) if turn else own_half
            if inside and turn:
                c_stage_5(layer)
            part = mm_nn(feat[layer], c_ref[layer, half].reshape(4 * p, half_cols))
            for first, block in half_blocks(half):
                temp[:, block] = part[:, first : first + 128]
            gather(layer, 17 + turn)

        def act_rows(rows, first, carry, layer=layer, gain=gain, bias=bias, skip=skip):
            pre = temp[rows, :] + skip * (xhat[layer, rows, :] * gain + bias)
            square = pre * pre
            th = jnp.tanh(GELU_A * pre * (1.0 + GELU_B * square))
            cdf = 0.5 * (1.0 + th)
            out = pre * cdf
            gelu_out[layer, rows, :] = out
            gelu_low[layer, rows, :] = out.astype(BF16)
            gelu_der[layer, rows, :] = cdf + 0.5 * pre * (1.0 - th * th) * (
                GELU_A * (1.0 + 3.0 * GELU_B * square)
            )
            return carry

        row_loop(act_rows, 0)
        gather(layer, 19)
        if inside:
            row_stage_end(glu_ref, layer)
        for col in range(0, width, 256):
            temp[:, col : col + 256] = mm_nn(gelu_low[layer], glu_ref[layer, :, col : col + 256])
        gather(layer, 20)
        glu_bias = glub_ref[layer : layer + 1, :]
        last_layer = layer == layers - 1

        def gate_rows(rows, first, carry, layer=layer, glu_bias=glu_bias, last_layer=last_layer):
            gate = 1.0 / (1.0 + jnp.exp(-(temp[rows, :] + glu_bias)))
            sig[layer, rows, :] = gate
            new = stream[rows, :] + gelu_out[layer, rows, :] * gate
            if not last_layer:
                stream[rows, :] = new
                return carry
            return carry + fold8(new * row_mask(first))

        def row_mask(first):
            row = first + lax.broadcasted_iota(jnp.int32, (TILE, 1), 0)
            position = me * tok + (row & (CHUNKS - 1)) * steps + (row >> 3)
            return jnp.where(position < len_ref[0], 1.0, 0.0).astype(F32)

        pooled_part = row_loop(gate_rows, jnp.zeros((CHUNKS, width), F32) if last_layer else 0)
        gather(layer, 21)

    pool_slot = 2 * layers
    own_sum = jnp.sum(pooled_part, axis=0, keepdims=True)
    for part in range(2):
        for tile in range(width // 128):
            cols = slice(tile * 128, tile * 128 + 128)
            send_buf[pool_slot, part, tile : tile + 1, :] = own_sum[:, cols]
    exchange_start(pool_slot)

    small_ref[...] = jnp.zeros(small_ref.shape, F32)
    head_row = 6 * layers
    heads = []

    def head():
        if heads:
            return
        exchange_wait(pool_slot)

        def add_pool(k, total):
            rows = [recv_buf[pool_slot, from_rank(k), r : r + 1, :] for r in range(width // 128)]
            return total + jnp.where(k == me, 0.0, jnp.concatenate(rows, axis=1))

        pooled_sum = lax.fori_loop(0, nseq, add_pool, own_sum, unroll=True)
        len_row = jnp.full((1, 1), len_ref[0], jnp.int32).astype(F32)
        pooled = pooled_sum / len_row
        logit = [
            jnp.sum(pooled * cw_ref[k : k + 1, :], axis=1, keepdims=True)
            + jnp.full((1, 1), cb_ref[k], F32)
            for k in range(classes)
        ]
        top = logit[0]
        for k in range(1, classes):
            top = jnp.maximum(top, logit[k])
        expo = [jnp.exp(v - top) for v in logit]
        norm = expo[0]
        for k in range(1, classes):
            norm = norm + expo[k]
        hot = [jnp.where(lab_ref[0] == k, 1.0, 0.0).astype(F32) for k in range(classes)]
        cross = top + jnp.log(norm)
        for k in range(classes):
            cross = cross - hot[k] * logit[k]
        excess = [expo[k] / norm - hot[k] for k in range(classes)]
        once = jnp.where(me == 0, 1.0, 0.0).astype(F32)
        lane = lax.broadcasted_iota(jnp.int32, (1, width), 1)
        bias_line = jnp.zeros((1, width), F32)
        for k in range(classes):
            lgrad = len_row * excess[k] * once
            put_line(head_row + k, pooled * lgrad)
            bias_line = jnp.where(lane == k, lgrad, bias_line)
        bias_line = jnp.where(lane == classes, cross * once, bias_line)
        put_line(head_row + classes, bias_line)
        factors = jnp.ones((1, 1), F32)
        row = excess[0] * cw_ref[0:1, :]
        if classes == 2:
            first = expo[0] / norm
            factors = hot[0] * (-expo[1] / norm) + (1.0 - hot[0]) * first
            row = cw_ref[0:1, :] - cw_ref[1:2, :]
        else:
            for k in range(1, classes):
                row = row + excess[k] * cw_ref[k : k + 1, :]
        L.scale[...] = jnp.broadcast_to(factors, (8, 128))
        heads.append(row)

    def factor():
        return L.scale[0:1, 0:1]

    if classes == 2:
        grad_row = cw_ref[0:1, :] - cw_ref[1:2, :]
    else:
        head()
        grad_row = heads[0]

    def scale_small():
        rows = head_row * (width // 128)
        small_ref[0:rows, :] = small_ref[0:rows, :] * factor()

    groups = 4 * nz

    def loop(count, body):
        def one(k, carry):
            body(k)
            return carry

        lax.fori_loop(0, count, one, 0, unroll=4)

    def c_grad_start(layer, part):
        rows = feat[layer, :, part * 2 * p : (part + 1) * 2 * p]
        value = (mm_tn(rows, mlow[layer, 1 - core]) * factor()).reshape(groups, share, half_cols)
        CG.snd1[layer, part] = value.astype(BF16)
        copy = remote(CG.snd1.at[layer, part], CG.rcv1.at[layer, part], new_sems(1), sibling)
        start((6, layer, part), copy)
        value = mm_tn(rows, mlow[layer, core]) * factor()
        CG.acc[layer, part] = value.reshape(groups, share, half_cols)

    def c_grad_first(layer, part):
        finish((6, layer, part))
        acc, rcv = CG.acc.at[layer, part], CG.rcv1.at[layer, part]
        if part == 0:

            def put(dst, cols):
                def one(g):
                    value = acc[g, :, cols] + rcv[g, :, cols].astype(F32)
                    dst[layer, g] = value.astype(dst.dtype)

                loop(groups, one)

            put(CG.snd2a, y_cols(1 - yy))
            copy = remote(CG.snd2a.at[layer], CG.rcv2a.at[layer], new_sems(1), y_peer)
            start((7, layer, part), copy)
            put(CG.acc2a, y_cols(yy))
        else:

            def put(dst, x):
                def one(h):
                    value = acc[2 * h + x] + rcv[2 * h + x].astype(F32)
                    dst[layer, h] = value.astype(dst.dtype)

                loop(groups // 2, one)

            put(CG.snd2b, 1 - xx)
            copy = remote(CG.snd2b.at[layer], CG.rcv2b.at[layer], new_sems(1), x_peer)
            start((7, layer, part), copy)
            put(CG.acc2b, xx)

    def c_grad_second(layer, part):
        finish((7, layer, part))
        if part == 0:

            def put(dst, x):
                def one(h):
                    value = CG.acc2a[layer, 2 * h + x] + CG.rcv2a[layer, 2 * h + x].astype(F32)
                    dst[layer, part, h] = value.astype(dst.dtype)

                loop(groups // 2, one)

            away, keep, peer = 1 - xx, xx, x_peer
        else:

            def put(dst, cols):
                def one(h):
                    value = CG.acc2b[layer, h, :, cols] + CG.rcv2b[layer, h, :, cols].astype(F32)
                    dst[layer, part, h] = value.astype(dst.dtype)

                loop(groups // 2, one)

            away, keep, peer = y_cols(1 - yy), y_cols(yy), y_peer
        put(CG.snd3, away)
        copy = remote(CG.snd3.at[layer, part], CG.rcv3.at[layer, part], new_sems(1), peer)
        start((8, layer, part), copy)
        put(CG.acc3, keep)

    def spread_z(name, src, dst):
        arrived = dst.at[pl.ds(1, nz - 1)]
        sem = new_sems(1)
        copies[name] = remote(arrived, arrived, sem, x_peer)
        for k in range(1, nz):
            peer = lax.rem(zz + k, nz)
            remote(src(peer), dst.at[k], sem, {"seq": 2 * peer + xx}).start()

    def c_grad_third(layer, part):
        finish((8, layer, part))

        def one(h):
            value = CG.acc3[layer, part, h] + CG.rcv3[layer, part, h].astype(F32)
            CG.acc3[layer, part, h] = value
            CG.snd4[layer, part, lax.rem(h, nz), h // nz] = value.astype(BF16)

        loop(groups // 2, one)
        snd = CG.snd4.at[layer, part]
        spread_z((9, layer, part), lambda peer: snd.at[peer], CG.rcv4.at[layer, part])

    def c_grad_end(layer, part):
        finish((9, layer, part))
        for plane in range(2):
            value = CG.acc3[layer, part, plane * nz + zz]
            for k in range(1, nz):
                value = value + CG.rcv4[layer, part, k, plane].astype(F32)
            O.c_out[layer, 2 * part + plane] = value

    def row_grad_start(G, layer):
        if G is GG:
            left, right = gelu_low, ggrad[layer]
        elif G is BA:
            left, right = nlow, dlow[layer, :, 0:p]
        else:
            left, right = nlow, dlow[layer, :, p : 2 * p]
        for y in range(ny):
            block = left[layer, :, own_rows(2 * y + 1 - core)]
            G.snd1[layer, y] = (mm_tn(block, right) * factor()).astype(BF16)
        copy = remote(G.snd1.at[layer], G.rcv1.at[layer], new_sems(1), sibling)
        start((id(G), 0, layer), copy)
        for y in range(ny):
            block = left[layer, :, own_rows(2 * y + core)]
            G.acc[layer, y] = mm_tn(block, right) * factor()

    def row_grad_y(G, layer):
        finish((id(G), 0, layer))
        acc, rcv = G.acc.at[layer], G.rcv1.at[layer]
        cast_rows(G.snd2.at[layer], acc.at[1 - yy], rows_dp, 32, rcv.at[1 - yy])
        copy = remote(G.snd2.at[layer], G.rcv2.at[layer], new_sems(1), y_peer)
        start((id(G), 1, layer), copy)
        cast_rows(G.acc2.at[layer], acc.at[yy], rows_dp, 32, rcv.at[yy])

    piece = rows_dp // nseq

    def row_grad_x(G, layer):
        finish((id(G), 1, layer))

        def put(dst, x):
            def one(z):
                rows = pl.ds(pl.multiple_of((2 * z + x) * piece, 16), piece)
                value = G.acc2[layer, rows, :] + G.rcv2[layer, rows, :].astype(F32)
                dst[layer, z] = value.astype(dst.dtype)

            loop(nz, one)

        put(G.snd3, 1 - xx)
        start((id(G), 2, layer), remote(G.snd3.at[layer], G.rcv3.at[layer], new_sems(1), x_peer))
        put(G.acc3, xx)

    def row_grad_z(G, layer):
        finish((id(G), 2, layer))

        def one(z):
            value = G.acc3[layer, z] + G.rcv3[layer, z].astype(F32)
            G.acc3[layer, z] = value
            G.snd4[layer, z] = value.astype(BF16)

        loop(nz, one)
        snd = G.snd4.at[layer]
        spread_z((id(G), 3, layer), lambda peer: snd.at[peer], G.rcv4.at[layer])

    def row_grad_back_z(G, layer):
        finish((id(G), 3, layer))
        value = G.acc3[layer, zz]
        for k in range(1, nz):
            value = value + G.rcv4[layer, k].astype(F32)
        G.full[layer, zz, xx] = value.astype(BF16)
        block = G.full.at[layer, zz, xx]
        total = G.full.at[layer, pl.ds(0, nz - 1), xx]
        start_all((id(G), 4, layer), total, [(block, peer) for peer in z_peers()])

    def row_grad_back_all(G, layer):
        finish((id(G), 3, layer))
        value = G.acc3[layer, zz]
        for k in range(1, nz):
            value = value + G.rcv4[layer, k].astype(F32)
        G.full[layer, zz, xx] = value.astype(BF16)
        block = G.full.at[layer, zz, xx]
        same = [(block, peer) for peer in z_peers()]
        start_all((id(G), 4, layer), G.full.at[layer, pl.ds(0, nz - 1), xx], same)
        cross = [(block, {"seq": 2 * lax.rem(zz + k, nz) + 1 - xx}) for k in range(nz)]
        start_all((id(G), 5, layer), G.full.at[layer, :, xx], cross)

    def row_grad_back_x(G, layer):
        finish((id(G), 4, layer))
        block = G.full.at[layer, :, xx]
        start((id(G), 5, layer), remote(block, block, new_sems(1), x_peer))

    def row_grad_end(G, layer):
        ensure((id(G), 4, layer))
        finish((id(G), 5, layer))
        out = O.glu_out if G is GG else O.b_out
        cols = pl.ds(p if G is BB else 0, G.full.shape[-1])

        def one(z):
            for x in range(2):
                rows = pl.ds(pl.multiple_of((2 * z + x) * piece, 16), piece)
                out[layer, rows, cols] = G.full[layer, z, x].astype(F32)

        loop(nz, one)

    small_rows = small_ref.shape[0]
    small_piece = small_rows // nseq

    def small_start():
        scale_small()
        start((8, 0), remote(small_ref, S.small_core, new_sems(1), sibling))

    def small_y():
        finish((8, 0))
        S.small_sum[0] = small_ref[...] + S.small_core[...]
        start((8, 1), remote(S.small_sum.at[0], S.small_y, new_sems(1), y_peer))

    def small_part(q):
        return pl.ds(pl.multiple_of(q * small_piece, 8), small_piece)

    def small_spread(name, src, dst, wait_ref):
        sem = new_sems(1)
        copies[name] = remote(wait_ref, wait_ref, sem, x_peer)

        def one(k):
            peer = lax.rem(me + k, nseq)
            remote(src(peer), dst(k), sem, {"seq": peer}).start()

        seq_loop(one)

    def small_scatter():
        finish((8, 1))
        S.small_sum[1] = S.small_sum[0] + S.small_y[...]
        small_spread(
            (8, 2),
            lambda peer: S.small_sum.at[1, small_part(peer), :],
            lambda k: S.small_recv.at[k],
            S.small_recv.at[pl.ds(1, nseq - 1)],
        )

    def small_gather():
        finish((8, 2))
        value = S.small_sum[1, small_part(me), :]
        for k in range(1, nseq):
            value = value + S.small_recv[k]
        S.small_sum[2, small_part(me), :] = value
        block = S.small_sum.at[2, small_part(me), :]
        small_spread(
            (8, 3), lambda peer: block, lambda k: block, S.small_recv.at[pl.ds(1, nseq - 1)]
        )

    def small_end():
        finish((8, 3))
        O.small_out[...] = S.small_sum[2]

    order = {(layers - 1, 3): [head]}
    if inside:
        order = {
            (1, 3): [
                head,
                partial(row_grad_start, GG, 1),
                partial(c_grad_start, 1, 1),
                partial(row_grad_y, GG, 1),
            ],
            (1, 5): [
                partial(row_grad_start, BA, 1),
                partial(c_grad_first, 1, 1),
                partial(row_grad_start, BB, 1),
            ],
            (1, 6): [
                partial(row_grad_y, BA, 1),
            ],
            (0, 1): [
                partial(row_grad_start, GG, 0),
                partial(row_grad_y, BB, 1),
            ],
            (0, 3): [
                partial(row_grad_y, GG, 0),
                partial(c_grad_start, 1, 0),
                partial(row_grad_x, BA, 1),
                partial(c_grad_start, 0, 1),
                partial(c_grad_second, 1, 1),
                partial(row_grad_x, GG, 1),
                partial(c_grad_start, 0, 0),
                partial(row_grad_x, BB, 1),
            ],
            (0, 5): [
                partial(row_grad_start, BB, 0),
                partial(c_grad_first, 0, 1),
                partial(row_grad_z, BA, 1),
                partial(row_grad_start, BA, 0),
                partial(row_grad_y, BB, 0),
                partial(row_grad_z, GG, 1),
                partial(row_grad_x, GG, 0),
                partial(row_grad_y, BA, 0),
                partial(c_grad_first, 0, 0),
                partial(row_grad_z, BB, 1),
            ],
            (0, 6): [
                small_start,
                partial(c_grad_third, 1, 1),
                small_y,
                partial(row_grad_x, BB, 0),
                partial(row_grad_back_z, BA, 1),
            ],
            (0, 7): [
                partial(row_grad_back_z, GG, 1),
                partial(row_grad_x, BA, 0),
                partial(row_grad_z, GG, 0),
                partial(c_grad_first, 1, 0),
                partial(row_grad_z, BB, 0),
                partial(c_grad_second, 0, 1),
                partial(row_grad_back_x, BA, 1),
                partial(row_grad_z, BA, 0),
                partial(row_grad_back_z, BB, 1),
                partial(c_grad_second, 0, 0),
                small_scatter,
                partial(row_grad_back_z, GG, 0),
                partial(row_grad_back_z, BB, 0),
                partial(row_grad_back_x, GG, 1),
                partial(row_grad_end, BA, 1),
                partial(row_grad_back_z, BA, 0),
                partial(c_grad_third, 0, 0),
                partial(c_grad_second, 1, 0),
                small_gather,
                partial(c_grad_third, 0, 1),
                partial(row_grad_back_x, BB, 1),
                partial(row_grad_back_x, GG, 0),
                partial(c_grad_third, 1, 0),
                partial(row_grad_back_x, BB, 0),
                partial(row_grad_back_x, BA, 0),
                partial(c_grad_end, 0, 0),
                partial(row_grad_end, GG, 1),
                partial(c_grad_end, 1, 1),
                partial(row_grad_end, GG, 0),
                small_end,
                partial(row_grad_end, BB, 1),
                partial(c_grad_end, 0, 1),
                partial(row_grad_end, BB, 0),
                partial(row_grad_end, BA, 0),
                partial(c_grad_end, 1, 0),
            ],
        }

    def stages(layer, point):
        for stage in order.get((layer, point), []):
            stage()

    grad = stream

    def first_grad(rows, first, carry):
        grad[rows, :] = row_mask(first) * grad_row
        return carry

    row_loop(first_grad, 0)

    for layer in reversed(range(layers)):
        gain = gain_ref[layer : layer + 1, :]
        bias = bias_ref[layer : layer + 1, :]
        skip = skip_ref[layer : layer + 1, :]
        zero_sum = jnp.zeros((CHUNKS, width), F32)

        def gate_back(rows, first, total, layer=layer):
            gate = sig[layer, rows, :]
            low = (grad[rows, :] * gelu_out[layer, rows, :] * gate * (1.0 - gate)).astype(BF16)
            ggrad[layer, rows, :] = low
            return total + fold8(low.astype(F32))

        total = row_loop(gate_back, zero_sum)
        stages(layer, 0)
        put_line(3 * layers + layer, jnp.sum(total, axis=0, keepdims=True))
        for col in range(0, width, 256):
            temp[:, col : col + 256] = mm_nt(ggrad[layer], glu_ref[layer, col : col + 256, :])

        def mix_back(rows, first, total, layer=layer, gain=gain, bias=bias):
            act = grad[rows, :] * sig[layer, rows, :] + temp[rows, :]
            value = act * gelu_der[layer, rows, :]
            mix[rows, :] = value
            for h in range(2):
                for first, block in half_blocks(h):
                    at = block.start
                    mlow[layer, h, rows, first : first + 128] = value[:, at : at + 128].astype(BF16)
            return total + fold8(value * (xhat[layer, rows, :] * gain + bias))

        total = row_loop(mix_back, zero_sum)
        put_line(2 * layers + layer, jnp.sum(total, axis=0, keepdims=True))
        stages(layer, 1)
        for plane in range(0, 4, 2):
            rows = [c_ref[layer, h, plane : plane + 2].reshape(2 * p, half_cols) for h in range(2)]
            wide[:, plane * p : (plane + 2) * p] = mm_nt(mlow[layer, 0], rows[0]) + mm_nt(
                mlow[layer, 1], rows[1]
            )

        lam_re, lam_im, jumps = layer_powers(layer, True)
        ends = local_ends(wide, 2 * p, 0, lam_re, lam_im)
        prefix = local_prefix(ends, jumps)
        stages(layer, 2)
        slot = layers + layer
        send_totals(slot, prefix)
        stages(layer, 3)
        if not inside:
            for h in range(2):
                for col in range(0, 4 * p, 2 * p):
                    value = mm_tn(feat[layer, :, col : col + 2 * p], mlow[layer, h]) * factor()
                    cols = slice(h * half_cols, (h + 1) * half_cols)
                    O.c_out[layer, col : col + 2 * p, cols] = value.astype(BF16)
            for col in range(0, width, 256):
                value = mm_tn(gelu_low[layer, :, col : col + 256], ggrad[layer]) * factor()
                O.glu_out[layer, col : col + 256, :] = value.astype(BF16)
        tables = (jump_table(jumps, sub), jump_table(jumps, CHUNKS - 1 - sub))
        exchange_wait(slot)
        stages(layer, 4)
        carries = chunk_carries(slot, prefix, jumps, tables)
        l_re = jnp.broadcast_to(lam_re, (CHUNKS, p))
        l_im = jnp.broadcast_to(lam_im, (CHUNKS, p))
        zero = jnp.zeros((CHUNKS, p), F32)

        def anti_grad(j, carry, layer=layer, l_re=l_re, l_im=l_im):
            r_re, r_im, d_re, d_im = carry
            rows = pl.ds(pl.multiple_of(j * CHUNKS, CHUNKS), CHUNKS)
            after = pl.ds(pl.multiple_of((j + 1) * CHUNKS, CHUNKS), CHUNKS)
            r_re, r_im = cmul(l_re, l_im, r_re, r_im)
            r_re = r_re + wide[rows, 2 * p : 3 * p]
            r_im = r_im + wide[rows, 3 * p : 4 * p]
            wide[rows, 2 * p : 3 * p] = r_re
            wide[rows, 3 * p : 4 * p] = r_im
            q_re = anti[layer, after, 0:p]
            q_im = anti[layer, after, p : 2 * p]
            return r_re, r_im, d_re + (r_re * q_re + r_im * q_im), d_im + (r_im * q_re - r_re * q_im)

        _, _, d_re, d_im = lax.fori_loop(
            0, steps, anti_grad, (carries[0], carries[1], zero, zero), unroll=4
        )
        in_scale = jnp.broadcast_to(tab_ref[layer, 2:3, :], (CHUNKS, p))

        def caus_grad(k, carry, layer=layer, l_re=l_re, l_im=l_im, in_scale=in_scale):
            a_re, a_im, d_re, d_im, s_sum = carry
            last = pl.multiple_of(tok - (k + 1) * 2 * CHUNKS, 2 * CHUNKS)
            kept_re, kept_im = [], []
            for half in (1, 0):
                rows = pl.ds(last + half * CHUNKS, CHUNKS)
                a_re, a_im = cmul(l_re, l_im, a_re, a_im)
                a_re = a_re + wide[rows, 0:p]
                a_im = a_im + wide[rows, p : 2 * p]
                q_re = caus[layer, rows, 0:p]
                q_im = caus[layer, rows, p : 2 * p]
                d_re = d_re + (a_re * q_re + a_im * q_im)
                d_im = d_im + (a_im * q_re - a_re * q_im)
                t_re = a_re + wide[rows, 2 * p : 3 * p]
                t_im = a_im + wide[rows, 3 * p : 4 * p]
                s_sum = s_sum + (
                    t_re * drive[layer, rows, 0:p] + t_im * drive[layer, rows, p : 2 * p]
                )
                kept_re.insert(0, t_re * in_scale)
                kept_im.insert(0, t_im * in_scale)
            both = pl.ds(last, 2 * CHUNKS)
            dlow[layer, both, 0:p] = jnp.concatenate(kept_re, axis=0).astype(BF16)
            dlow[layer, both, p : 2 * p] = jnp.concatenate(kept_im, axis=0).astype(BF16)
            return a_re, a_im, d_re, d_im, s_sum

        _, _, d_re, d_im, s_sum = lax.fori_loop(
            0, steps // 2, caus_grad, (carries[2], carries[3], d_re, d_im, zero), unroll=2
        )
        d_re = jnp.sum(d_re, axis=0, keepdims=True)
        d_im = jnp.sum(d_im, axis=0, keepdims=True)
        s_sum = jnp.sum(s_sum, axis=0, keepdims=True) / tab_ref[layer, 2:3, :]
        true_re = tab_ref[layer, 0:1, :]
        true_im = tab_ref[layer, 1:2, :]
        pad = jnp.zeros((1, width - p), F32)
        rate_part = s_sum * tab_ref[layer, 3:4, :] - d_re * true_re - d_im * true_im
        put_line(4 * layers + layer, jnp.concatenate([rate_part, pad], axis=1))
        phase_part = d_im * true_re - d_re * true_im
        put_line(5 * layers + layer, jnp.concatenate([phase_part, pad], axis=1))

        stages(layer, 5)
        if not inside:
            for col in range(0, width, 256):
                value = mm_tn(nlow[layer, :, col : col + 256], dlow[layer]) * factor()
                O.b_out[layer, col : col + 256, :] = value.astype(BF16)
        for col in range(0, width, 256):
            temp[:, col : col + 256] = mm_nt(dlow[layer], b_ref[layer, col : col + 256, :])

        def norm_back(rows, first, carry, layer=layer, gain=gain, skip=skip):
            gain_sum, bias_sum = carry
            ngrad = mix[rows, :] * skip + temp[rows, :]
            hat = xhat[layer, rows, :]
            q = ngrad * gain
            mean_q = jnp.mean(q, axis=1, keepdims=True)
            mean_x = jnp.mean(q * hat, axis=1, keepdims=True)
            grad[rows, :] = grad[rows, :] + (q - mean_q - hat * mean_x) * rstd[layer, rows, :]
            return gain_sum + fold8(ngrad * hat), bias_sum + fold8(ngrad)

        gain_sum, bias_sum = row_loop(norm_back, (zero_sum, zero_sum))
        put_line(layer, jnp.sum(gain_sum, axis=0, keepdims=True))
        put_line(layers + layer, jnp.sum(bias_sum, axis=0, keepdims=True))
        stages(layer, 6)

    if not inside:
        scale_small()
    for col in range(0, width, 128):
        perm[col // 128] = grad[:, col : col + 128] * factor()

        def unplace(k, carry, col=col):
            first = k * CHUNKS
            chunk = first // steps
            rows = pl.ds((first - chunk * steps) * CHUNKS + chunk, CHUNKS, stride=CHUNKS)
            out = pl.ds(pl.multiple_of(first, CHUNKS), CHUNKS)
            gin_ref[out, col : col + 128] = perm[col // 128, rows, :]
            return carry

        lax.fori_loop(0, steps, unplace, 0, unroll=4)

    stages(0, 7)


def run_model(dims, inside, operands):
    layers, tok, width, states, classes, ndp, nseq = dims
    vmem = pl.BlockSpec(memory_space=pltpu.VMEM)
    smem = pl.BlockSpec(memory_space=pltpu.SMEM)
    hbm = pl.BlockSpec(memory_space=pltpu.HBM)
    lines = -(-(6 * layers + classes + 1) // 8) * 8
    small_shape = (lines * width // 128, 128)
    slots = 2 * layers + 1
    share, rows_dp = states // nseq, width // ndp
    per_layer = lambda cols, kind, rows=tok: pltpu.VMEM((layers, rows, cols), kind)
    if inside:
        b_shape, g_shape = (layers, rows_dp, 2 * states), (layers, rows_dp, width)
        c_shape, kind = (layers, 4, share, width // ndp), F32
    else:
        b_shape, g_shape = (layers, width, 2 * states), (layers, width, width)
        c_shape, kind = (layers, 4 * states, width), BF16
    scratch = [pltpu.VMEM(a.shape, a.dtype) for a in operands[3:]]
    scratch += [
        pltpu.SemaphoreType.DMA((len(operands) - 3,)),
        pltpu.VMEM((tok, width), F32),
        per_layer(width, F32),
        per_layer(1, F32),
        per_layer(width, BF16),
        per_layer(2 * states, F32),
        per_layer(2 * states, F32, tok + CHUNKS),
        per_layer(2 * states, F32, tok + CHUNKS),
        per_layer(4 * states, BF16),
        per_layer(width, F32),
        per_layer(width, BF16),
        per_layer(width, F32),
        per_layer(width, F32),
        pltpu.VMEM((tok, 4 * states), F32),
        pltpu.VMEM((tok, width), F32),
        pltpu.VMEM((tok, width), F32),
        pltpu.VMEM((layers, 2, tok, width // 2), BF16),
        per_layer(width, BF16),
        per_layer(2 * states, BF16),
        pltpu.VMEM((8, 128), F32),
        pltpu.VMEM((width // 128, tok, 128), F32),
        pltpu.VMEM((slots, 2, 8, 128), F32),
        pltpu.VMEM((slots, nseq, 8, 128), F32),
        pltpu.SemaphoreType.DMA((slots,)),
        pltpu.SemaphoreType.DMA((slots,)),
    ]
    if inside:
        ny, nz, part, half = ndp // 2, nseq // 2, width // ndp, width // 2
        copies = 81
        scratch += [
            pltpu.VMEM((layers, 8, states), F32),
            pltpu.VMEM((nseq, 8, 128), F32),
            per_layer(2 * states, BF16, width),
            per_layer(width, BF16, width),
            pltpu.VMEM((layers, 2, 4, nz, 2, share, half), BF16),
            pltpu.SemaphoreType.DMA((copies,)),
            pltpu.SemaphoreType.DMA((copies,)),
            pltpu.VMEM(small_shape, F32),
            pltpu.VMEM(small_shape, F32),
            pltpu.VMEM(small_shape, F32),
            pltpu.VMEM((3,) + small_shape, F32),
            pltpu.VMEM((nseq, small_shape[0] // nseq, 128), F32),
        ]
        for cols in (states, states, width):
            scratch += [
                pltpu.VMEM((layers, ny, rows_dp, cols), BF16),
                pltpu.VMEM((layers, ny, rows_dp, cols), BF16),
                pltpu.VMEM((layers, ny, rows_dp, cols), F32),
                per_layer(cols, BF16, rows_dp),
                per_layer(cols, BF16, rows_dp),
                per_layer(cols, F32, rows_dp),
                pltpu.VMEM((layers, nz, rows_dp // nseq, cols), BF16),
                pltpu.VMEM((layers, nz, rows_dp // nseq, cols), BF16),
                pltpu.VMEM((layers, nz, rows_dp // nseq, cols), F32),
                pltpu.VMEM((layers, nz, rows_dp // nseq, cols), BF16),
                pltpu.VMEM((layers, nz, rows_dp // nseq, cols), BF16),
                pltpu.VMEM((layers, nz, 2, rows_dp // nseq, cols), BF16),
            ]
        scratch += [
            pltpu.VMEM((layers, 2, 4 * nz, share, half), BF16),
            pltpu.VMEM((layers, 2, 4 * nz, share, half), BF16),
            pltpu.VMEM((layers, 2, 4 * nz, share, half), F32),
            pltpu.VMEM((layers, 4 * nz, share, part), BF16),
            pltpu.VMEM((layers, 4 * nz, share, part), BF16),
            pltpu.VMEM((layers, 4 * nz, share, part), F32),
            pltpu.VMEM((layers, 2 * nz, share, half), BF16),
            pltpu.VMEM((layers, 2 * nz, share, half), BF16),
            pltpu.VMEM((layers, 2 * nz, share, half), F32),
            pltpu.VMEM((layers, 2, 2 * nz, share, part), BF16),
            pltpu.VMEM((layers, 2, 2 * nz, share, part), BF16),
            pltpu.VMEM((layers, 2, 2 * nz, share, part), F32),
            pltpu.VMEM((layers, 2, nz, 2, share, part), BF16),
            pltpu.VMEM((layers, 2, nz, 2, share, part), BF16),
        ]
    return pl.pallas_call(
        partial(model_kernel, dims, inside),
        out_shape=(
            jax.ShapeDtypeStruct((tok, width), F32),
            jax.ShapeDtypeStruct(small_shape, F32),
            jax.ShapeDtypeStruct(b_shape, kind),
            jax.ShapeDtypeStruct(g_shape, kind),
            jax.ShapeDtypeStruct(c_shape, kind),
        ),
        in_specs=[smem] * 3 + [hbm] * (len(operands) - 3),
        out_specs=[vmem] * 5,
        scratch_shapes=scratch,
        compiler_params=pltpu.CompilerParams(
            collective_id=0, has_side_effects=True, vmem_limit_bytes=48 * 1024 * 1024
        ),
        cost_estimate=pl.CostEstimate(
            flops=6 * layers * tok * width * (6 * states + width),
            bytes_accessed=16 * 1024 * 1024,
            transcendentals=2 * layers * tok * width,
        ),
    )(*operands[:3], *[pltpu.with_memory_space_constraint(a, pltpu.HBM) for a in operands[3:]])


def finish_kernel(dims, *refs):
    layers, tok, width, states, classes, ndp, nseq = dims
    small = refs[4]
    loss, gain, bias, rate, phase, skip, glub, head_w, head_b = refs[9:18]
    sems = refs[18]
    outward = [pltpu.make_async_copy(refs[k], refs[5 + k], sems.at[k]) for k in range(4)]
    for copy in outward:
        copy.start()
    tiles = width // 128

    def line(row, count=tiles):
        parts = [small[row * tiles + t : row * tiles + t + 1, :] for t in range(count)]
        return jnp.concatenate(parts, axis=1)

    for layer in range(layers):
        at = slice(layer, layer + 1)
        gain[at, :] = line(layer)
        bias[at, :] = line(layers + layer)
        skip[at, :] = line(2 * layers + layer)
        glub[at, :] = line(3 * layers + layer)
    share = states // nseq
    me = lax.axis_index("seq")
    for first, out in ((4 * layers, rate), (5 * layers, phase)):
        every = jnp.concatenate([line(first + layer) for layer in range(layers)], axis=0)
        mine = every[:, 0:share]
        for q in range(1, nseq):
            mine = jnp.where(me == q, every[:, q * share : (q + 1) * share], mine)
        out[...] = mine
    head = 6 * layers
    for k in range(classes):
        head_w[k : k + 1, :] = line(head + k)
    last = line(head + classes)
    head_b[...] = last[:, 0:classes]
    loss[...] = last[:, classes : classes + 1] / ndp
    for copy in outward:
        copy.wait()


def finish_outputs(dims, grad_inputs, small, b_grad, g_grad, c_grad):
    layers, tok, width, states, classes, ndp, nseq = dims
    vmem = pl.BlockSpec(memory_space=pltpu.VMEM)
    anywhere = pl.BlockSpec(memory_space=pl.ANY)
    large = (grad_inputs, b_grad, g_grad, c_grad)
    share = states // nseq
    rows = (layers, width)
    shapes = [(1, 1), rows, rows, (layers, share), (layers, share), rows, rows, (classes, width)]
    shapes.append((1, classes))
    results = pl.pallas_call(
        partial(finish_kernel, dims),
        out_shape=[jax.ShapeDtypeStruct(a.shape, F32) for a in large]
        + [jax.ShapeDtypeStruct(shape, F32) for shape in shapes],
        in_specs=[vmem] * 5,
        out_specs=[anywhere] * 4 + [vmem] * 9,
        scratch_shapes=[pltpu.SemaphoreType.DMA((4,))],
        compiler_params=pltpu.CompilerParams(vmem_limit_bytes=8 * 1024 * 1024),
    )(*large, small)
    gin, b_share, g_share, c_share, loss, gain, bias, rate, phase, skip, glub, head_w, head_b = results
    return (
        loss.reshape(()),
        gin[None],
        gain,
        bias,
        b_share,
        rate,
        phase,
        c_share,
        skip,
        g_share,
        glub,
        head_w.T,
        head_b.reshape(classes),
    )


def per_device(
    inputs,
    lengths,
    labels,
    norm_gain,
    norm_bias,
    b_proj,
    rate,
    phase,
    c_proj,
    skip,
    glu_weight,
    glu_bias,
    class_weight,
    class_bias,
):
    layers, width = norm_gain.shape
    tok = inputs.shape[1]
    ndp = lax.axis_size("dp")
    nseq = lax.axis_size("seq")
    states = c_proj.shape[2] * nseq
    classes = class_bias.shape[0]
    dims = (layers, tok, width, states, classes, ndp, nseq)
    share = states // nseq
    inside = (
        ndp == 4
        and nseq % 2 == 0
        and share % 16 == 0
        and (width // ndp) % 128 == 0
        and (width // ndp) % (16 * nseq) == 0
        and 4 * layers == 8
    )
    if inside:
        tables = (rate, phase)
        weights = (b_proj, glu_weight, c_proj)
    else:
        decay = jnp.exp(-rate)
        in_scale = jnp.sqrt(-jnp.expm1(-2.0 * rate))
        rows = [
            decay * jnp.cos(phase),
            decay * jnp.sin(phase),
            in_scale,
            jnp.exp(-2.0 * rate) / in_scale,
        ]
        table = lax.all_gather(jnp.stack(rows, axis=1), "seq", axis=2, tiled=True)
        tables = (table, phase)
        b_full = lax.all_gather(b_proj.astype(BF16), "dp", axis=1, tiled=True)
        g_full = lax.all_gather(glu_weight.astype(BF16), "dp", axis=1, tiled=True)
        c_half = lax.all_gather(c_proj.astype(BF16), "dp", axis=3, tiled=True)
        c_full = lax.all_gather(c_half, "seq", axis=2, tiled=True)
        c_full = c_full.reshape(layers, 4, states, 2, width // 2)
        c_full = jnp.moveaxis(c_full, 3, 1)
        weights = (b_full, g_full, c_full)
    grad_inputs, small, b_grad, g_grad, c_grad = run_model(
        dims,
        inside,
        (
            lengths,
            labels,
            class_bias,
            inputs[0],
            norm_gain,
            norm_bias,
            skip,
            glu_bias,
            *tables,
            class_weight.T,
            *weights,
        ),
    )
    if inside:
        return finish_outputs(dims, grad_inputs, small, b_grad, g_grad, c_grad)
    else:
        b_share = lax.psum_scatter(b_grad, "dp", scatter_dimension=1, tiled=True)
        g_share = lax.psum_scatter(g_grad, "dp", scatter_dimension=1, tiled=True)
        b_share = lax.psum(b_share, "seq").astype(F32)
        g_share = lax.psum(g_share, "seq").astype(F32)
        c_grad = c_grad.reshape(layers, 4, states, width)
        c_share = lax.psum_scatter(c_grad, "seq", scatter_dimension=2, tiled=True)
        c_share = lax.psum_scatter(c_share, "dp", scatter_dimension=3, tiled=True).astype(F32)
        small = lax.psum(small, ("dp", "seq"))
    small = small.reshape(-1, width)
    own = lax.axis_index("seq") * (states // nseq)

    def state_rows(first):
        return lax.dynamic_slice(small[first : first + layers], (0, own), (layers, states // nseq))

    head = 6 * layers
    return (
        small[head + classes, classes] / ndp,
        grad_inputs[None],
        small[0:layers],
        small[layers : 2 * layers],
        b_share,
        state_rows(4 * layers),
        state_rows(5 * layers),
        c_share,
        small[2 * layers : 3 * layers],
        g_share,
        small[3 * layers : 4 * layers],
        small[head : head + classes].T,
        small[head + classes, 0:classes],
    )


def solution(mesh):
    return jax.shard_map(
        per_device,
        mesh=mesh,
        in_specs=(
            P("dp", "seq", None),
            P("dp"),
            P("dp"),
            P(),
            P(),
            P(None, "dp", None),
            P(None, "seq"),
            P(None, "seq"),
            P(None, None, "seq", "dp"),
            P(),
            P(None, "dp", None),
            P(),
            P(),
            P(),
        ),
        out_specs=(
            P(),
            P("dp", "seq", None),
            P(),
            P(),
            P(None, "dp", None),
            P(None, "seq"),
            P(None, "seq"),
            P(None, None, "seq", "dp"),
            P(),
            P(None, "dp", None),
            P(),
            P(),
            P(),
        ),
        check_vma=False,
    )
```

```python
from functools import partial
from typing import Any, NamedTuple

import jax
import jax.numpy as jnp
from jax import lax
from jax.experimental import pallas as pl
from jax.experimental.pallas import tpu as pltpu
from jax.sharding import PartitionSpec as P

MESH = pl.DeviceIdType.MESH
F32 = jnp.float32
BF16 = jnp.bfloat16
CHUNKS = 8
TILE = 32
GELU_A = 0.7978845608028654
GELU_B = 0.044715


def mm_nn(left, right):
    return lax.dot_general(left, right, (((1,), (0,)), ((), ())), preferred_element_type=F32)


def mm_nt(left, right):
    return lax.dot_general(left, right, (((1,), (1,)), ((), ())), preferred_element_type=F32)


def mm_tn(left, right):
    return lax.dot_general(left, right, (((0,), (0,)), ((), ())), preferred_element_type=F32)


def cmul(a_re, a_im, b_re, b_im):
    return a_re * b_re - a_im * b_im, a_re * b_im + a_im * b_re


def fold8(value):
    total = value[0:8]
    for first in range(8, value.shape[0], 8):
        total = total + value[first : first + 8]
    return total


class Operands(NamedTuple):
    len: Any
    lab: Any
    cb: Any
    x: Any
    gain: Any
    bias: Any
    skip: Any
    glub: Any
    rate: Any
    phase: Any
    cw: Any
    b_in: Any
    glu_in: Any
    c_in: Any


class Results(NamedTuple):
    gin: Any
    small_out: Any
    b_out: Any
    glu_out: Any
    c_out: Any


class Local(NamedTuple):
    stream: Any
    xhat: Any
    rstd: Any
    nlow: Any
    drive: Any
    caus: Any
    anti: Any
    feat: Any
    gelu_out: Any
    gelu_low: Any
    gelu_der: Any
    sig: Any
    wide: Any
    temp: Any
    mix: Any
    mlow: Any
    ggrad: Any
    dlow: Any
    scale: Any
    perm: Any
    send_buf: Any
    recv_buf: Any
    send_sem: Any
    recv_sem: Any


class Shared(NamedTuple):
    tab: Any
    tab_recv: Any
    b_buf: Any
    glu_buf: Any
    c_buf: Any
    ssem: Any
    rsem: Any
    small: Any
    small_core: Any
    small_y: Any
    small_sum: Any
    small_recv: Any


class RowGrad(NamedTuple):
    snd1: Any
    rcv1: Any
    acc: Any
    snd2: Any
    rcv2: Any
    acc2: Any
    snd3: Any
    rcv3: Any
    acc3: Any
    snd4: Any
    rcv4: Any
    full: Any


class ColGrad(NamedTuple):
    snd1: Any
    rcv1: Any
    acc: Any
    snd2a: Any
    rcv2a: Any
    acc2a: Any
    snd2b: Any
    rcv2b: Any
    acc2b: Any
    snd3: Any
    rcv3: Any
    acc3: Any
    snd4: Any
    rcv4: Any


def take(refs, kind):
    count = len(kind._fields)
    return kind(*refs[:count]), refs[count:]


def model_kernel(dims, inside, *refs):
    layers, tok, width, states, classes, ndp, nseq = dims
    given, refs = take(refs, Operands)
    O, refs = take(refs, Results)
    fetched, refs = refs[: len(given) - 3], refs[len(given) - 3 :]
    fetch_sem, refs = refs[0], refs[1:]
    I = Operands(*given[:3], *fetched)
    L, refs = take(refs, Local)
    if inside:
        S, refs = take(refs, Shared)
        BA, refs = take(refs, RowGrad)
        BB, refs = take(refs, RowGrad)
        GG, refs = take(refs, RowGrad)
        CG, refs = take(refs, ColGrad)
        tab_ref, b_ref, glu_ref, c_ref, small_ref = S.tab, S.b_buf, S.glu_buf, S.c_buf, S.small
    else:
        tab_ref, b_ref, glu_ref, c_ref, small_ref = I.rate, I.b_in, I.glu_in, I.c_in, O.small_out
    len_ref, lab_ref, x_ref = I.len, I.lab, I.x
    gain_ref, bias_ref, skip_ref, glub_ref = I.gain, I.bias, I.skip, I.glub
    cw_ref, cb_ref, gin_ref = I.cw, I.cb, O.gin
    stream, xhat, rstd, nlow, drive = L.stream, L.xhat, L.rstd, L.nlow, L.drive
    caus, anti, feat, gelu_out, gelu_low = L.caus, L.anti, L.feat, L.gelu_out, L.gelu_low
    gelu_der, sig, wide, temp, mix = L.gelu_der, L.sig, L.wide, L.temp, L.mix
    mlow, ggrad, dlow, perm = L.mlow, L.ggrad, L.dlow, L.perm
    send_buf, recv_buf = L.send_buf, L.recv_buf
    send_sem, recv_sem = L.send_sem, L.recv_sem
    steps = tok // CHUNKS
    half_cols = width // 2
    me = lax.axis_index("seq")
    my_dp = lax.axis_index("dp")
    p = states
    core, yy = lax.rem(my_dp, 2), my_dp // 2
    xx, zz = lax.rem(me, 2), me // 2
    ny, nz = ndp // 2, nseq // 2
    own_half = core if inside else 0

    barrier = pltpu.get_barrier_semaphore()

    def greet(k, carry):
        peer = lax.rem(me + k, nseq)
        pl.semaphore_signal(barrier, inc=1, device_id={"seq": peer}, device_id_type=MESH)
        return carry

    lax.fori_loop(1, nseq, greet, 0, unroll=True)
    greeted = nseq - 1
    sibling = {"dp": 2 * yy + 1 - core}
    y_peer = {"dp": 2 * (1 - yy) + core}
    x_peer = {"seq": 2 * zz + 1 - xx}
    if inside:
        for peer in (sibling, y_peer):
            pl.semaphore_signal(barrier, inc=1, device_id=peer, device_id_type=MESH)
        greeted += 2

    fetches = [
        pltpu.make_async_copy(src, dst, fetch_sem.at[k])
        for k, (src, dst) in enumerate(zip(given[3:], fetched))
    ]
    for fetch in reversed(fetches):
        fetch.start()

    used = [0]

    def new_sems(count):
        first = used[0]
        used[0] += count
        return first

    def remote(src, dst, sem, peer):
        return pltpu.make_async_remote_copy(
            src_ref=src,
            dst_ref=dst,
            send_sem=S.ssem.at[sem],
            recv_sem=S.rsem.at[sem],
            device_id=peer,
            device_id_type=MESH,
        )

    def seq_loop(body):
        def one(k, carry):
            body(k)
            return carry

        lax.fori_loop(1, nseq, one, 0, unroll=True)

    def cast_rows(dst, src, rows, step, extra=None):
        def one(k, carry):
            part = pl.ds(pl.multiple_of(k * step, step), step)
            value = src[part, :].astype(F32)
            if extra is not None:
                value = value + extra[part, :].astype(F32)
            dst[part, :] = value.astype(dst.dtype)
            return carry

        lax.fori_loop(0, rows // step, one, 0, unroll=4)

    def row_loop(body, init, unroll=8):
        def step(k, carry):
            rows = pl.ds(pl.multiple_of(k * TILE, TILE), TILE)
            return body(rows, k * TILE, carry)

        return lax.fori_loop(0, tok // TILE, step, init, unroll=unroll)

    def exchange_start(slot):
        def one(k, carry):
            peer = lax.rem(me + k, nseq)
            pltpu.make_async_remote_copy(
                src_ref=send_buf.at[slot, (peer - me + nseq) // nseq],
                dst_ref=recv_buf.at[slot, k],
                send_sem=send_sem.at[slot],
                recv_sem=recv_sem.at[slot],
                device_id={"seq": peer},
                device_id_type=MESH,
            ).start()
            return carry

        lax.fori_loop(1, nseq, one, 0, unroll=True)

    def exchange_wait(slot):
        arrived = recv_buf.at[slot, pl.ds(1, nseq - 1)]
        pltpu.make_async_remote_copy(
            src_ref=arrived,
            dst_ref=arrived,
            send_sem=send_sem.at[slot],
            recv_sem=recv_sem.at[slot],
            device_id={"seq": lax.rem(me + 1, nseq)},
            device_id_type=MESH,
        ).wait()

    def from_rank(q):
        return lax.rem(me - q + nseq, nseq)

    sub = lax.broadcasted_iota(jnp.int32, (CHUNKS, p), 0)

    def layer_powers(layer, conj):
        lam_re = tab_ref[layer, 0:1, :]
        lam_im = tab_ref[layer, 1:2, :]
        if conj:
            lam_im = -lam_im
        pw_re, pw_im = lam_re, lam_im
        count = 1
        while count < steps:
            pw_re, pw_im = cmul(pw_re, pw_im, pw_re, pw_im)
            count *= 2
        jumps = [(pw_re, pw_im)]
        for _ in range(3):
            pw_re, pw_im = cmul(pw_re, pw_im, pw_re, pw_im)
            jumps.append((pw_re, pw_im))
        return lam_re, lam_im, jumps

    def jump_table(jumps, index):
        re = jnp.ones((CHUNKS, p), F32)
        im = jnp.zeros((CHUNKS, p), F32)
        for bit in range(3):
            new_re, new_im = cmul(re, im, jumps[bit][0], jumps[bit][1])
            has = (index & (1 << bit)) != 0
            re = jnp.where(has, new_re, re)
            im = jnp.where(has, new_im, im)
        return re, im

    def local_ends(src, first_c, first_a, lam_re, lam_im):
        zero = jnp.zeros((CHUNKS, p), F32)
        l_re = jnp.broadcast_to(lam_re, (CHUNKS, p))
        l_im = jnp.broadcast_to(lam_im, (CHUNKS, p))

        def step(j, carry):
            e_re, e_im, f_re, f_im = carry
            up = pl.ds(pl.multiple_of(j * CHUNKS, CHUNKS), CHUNKS)
            down = pl.ds(pl.multiple_of((steps - 1 - j) * CHUNKS, CHUNKS), CHUNKS)
            e_re, e_im = cmul(l_re, l_im, e_re, e_im)
            f_re, f_im = cmul(l_re, l_im, f_re, f_im)
            return (
                e_re + src[up, first_c : first_c + p],
                e_im + src[up, first_c + p : first_c + 2 * p],
                f_re + src[down, first_a : first_a + p],
                f_im + src[down, first_a + p : first_a + 2 * p],
            )

        return lax.fori_loop(0, steps, step, (zero,) * 4, unroll=8)

    def local_prefix(ends, jumps):
        e_re, e_im, f_re, f_im = ends
        for bit in range(3):
            shift = 1 << bit
            j_re, j_im = jumps[bit]
            s_re = jnp.where(sub >= shift, pltpu.roll(e_re, shift, 0), 0.0)
            s_im = jnp.where(sub >= shift, pltpu.roll(e_im, shift, 0), 0.0)
            a_re, a_im = cmul(j_re, j_im, s_re, s_im)
            e_re, e_im = e_re + a_re, e_im + a_im
            s_re = jnp.where(sub < CHUNKS - shift, pltpu.roll(f_re, CHUNKS - shift, 0), 0.0)
            s_im = jnp.where(sub < CHUNKS - shift, pltpu.roll(f_im, CHUNKS - shift, 0), 0.0)
            a_re, a_im = cmul(j_re, j_im, s_re, s_im)
            f_re, f_im = f_re + a_re, f_im + a_im
        return e_re, e_im, f_re, f_im

    def send_totals(slot, prefix):
        e_re, e_im, f_re, f_im = prefix
        last, first = slice(CHUNKS - 1, CHUNKS), slice(0, 1)
        for tile in range(p // 128):
            cols = slice(tile * 128, tile * 128 + 128)
            for row, value, part, at in (
                (tile, e_re, 1, last),
                (p // 128 + tile, e_im, 1, last),
                (tile, f_re, 0, first),
                (p // 128 + tile, f_im, 0, first),
            ):
                send_buf[slot, part, row : row + 1, :] = value[at, cols]
        exchange_start(slot)

    def chunk_carries(slot, prefix, jumps, tables):
        e_re, e_im, f_re, f_im = prefix
        d_re, d_im = jumps[3]
        zero = jnp.zeros((1, p), F32)

        def arrived(q, first):
            rows = range(first, first + p // 128)
            return jnp.concatenate([recv_buf[slot, from_rank(q), r : r + 1, :] for r in rows], axis=1)

        def step(k, carry):
            c_re, c_im, a_re, a_im = carry
            n_re, n_im = cmul(d_re, d_im, c_re, c_im)
            use = k < me
            c_re = jnp.where(use, n_re + arrived(k, 0), c_re)
            c_im = jnp.where(use, n_im + arrived(k, p // 128), c_im)
            back = nseq - 1 - k
            n_re, n_im = cmul(d_re, d_im, a_re, a_im)
            use = back > me
            a_re = jnp.where(use, n_re + arrived(back, 0), a_re)
            a_im = jnp.where(use, n_im + arrived(back, p // 128), a_im)
            return c_re, c_im, a_re, a_im

        c_re, c_im, a_re, a_im = lax.fori_loop(0, nseq, step, (zero,) * 4, unroll=True)
        t_re, t_im = tables[0]
        g_re, g_im = cmul(t_re, t_im, c_re, c_im)
        in_c_re = g_re + jnp.where(sub >= 1, pltpu.roll(e_re, 1, 0), 0.0)
        in_c_im = g_im + jnp.where(sub >= 1, pltpu.roll(e_im, 1, 0), 0.0)
        t_re, t_im = tables[1]
        g_re, g_im = cmul(t_re, t_im, a_re, a_im)
        in_a_re = g_re + jnp.where(sub < CHUNKS - 1, pltpu.roll(f_re, CHUNKS - 1, 0), 0.0)
        in_a_im = g_im + jnp.where(sub < CHUNKS - 1, pltpu.roll(f_im, CHUNKS - 1, 0), 0.0)
        return in_c_re, in_c_im, in_a_re, in_a_im

    def half_blocks(half):
        blocks = []
        for first in range(0, half_cols, 128):
            if inside:
                at = (2 * (first // part_cols) + half) * part_cols + first % part_cols
            else:
                at = half * half_cols + first
            if not isinstance(at, int):
                at = pl.multiple_of(at, 128)
            blocks.append((first, pl.ds(at, 128)))
        return blocks

    def put_line(line, row):
        for col in range(0, width, 128):
            at = line * (width // 128) + col // 128
            small_ref[at : at + 1, :] = row[:, col : col + 128]

    part_cols = width // ndp
    rows_dp = width // ndp
    share = p // nseq

    def own_rows(index):
        return pl.ds(pl.multiple_of(index * rows_dp, 16), rows_dp)

    def cast_c(layer):
        cols = pl.ds(pl.multiple_of(yy * part_cols, 128), part_cols)
        c_ref[layer, core, :, zz, xx, :, cols] = I.c_in[layer].astype(BF16)

    def cast_b(layer):
        b_ref[layer, own_rows(my_dp), :] = I.b_in[layer].astype(BF16)

    def cast_glu(layer):
        glu_ref[layer, own_rows(my_dp), :] = I.glu_in[layer].astype(BF16)

    copies, sem_of = {}, {}

    def start(name, copy):
        copies[name] = copy
        copy.start()

    def finish(name):
        copies.pop(name).wait()

    def ensure(name):
        if name in copies:
            finish(name)

    def y_cols(y):
        return pl.ds(pl.multiple_of(y * part_cols, 128), part_cols)

    def start_all(name, total, pairs):
        if name not in copies:
            sem_of[name] = new_sems(1)
            copies[name] = remote(total, total, sem_of[name], x_peer)
        for block, peer in pairs:
            remote(block, block, sem_of[name], peer).start()

    def z_peers():
        return [{"seq": 2 * lax.rem(zz + k, nz) + xx} for k in range(1, nz)]

    front, back = pl.ds(0, 2), pl.ds(2, 2)
    other_y = 1 - yy

    def c_piece(layer, planes, z, x, y):
        return c_ref.at[layer, core, planes, z, x, :, y_cols(y)]

    def c_to_z(name, layer, planes, y):
        total = c_ref.at[layer, core, planes, pl.ds(0, nz - 1), xx, :, y_cols(y)]
        block = c_piece(layer, planes, zz, xx, y)
        start_all((name, layer), total, [(block, peer) for peer in z_peers()])

    def c_to_x(layer, planes, y, others):
        if planes is front:
            name, total = 3, c_ref.at[layer, core, planes, :, xx]
        else:
            name, total = 13, c_ref.at[layer, core, planes, :, xx, :, y_cols(yy)]
        ranks = [lax.rem(zz + k, nz) for k in range(1, nz)] if others else [zz]
        pairs = [(c_piece(layer, planes, z, xx, y), x_peer) for z in ranks]
        start_all((name, layer), total, pairs)

    def one_copy(name, layer, block, peer):
        start((name, layer), remote(block, block, new_sems(1), peer))

    def to_sibling(layer, block):
        start_all((4, layer), c_ref.at[layer, core], [(block, sibling)])

    def back_to_y(layer, x):
        total = c_ref.at[layer, core, back, :, :, :, y_cols(yy)]
        block = c_ref.at[layer, core, back, :, x, :, y_cols(yy)]
        start_all((14, layer), total, [(block, y_peer)])

    def cya(layer):
        one_copy(0, layer, c_piece(layer, front, zz, xx, yy), y_peer)

    def spoa(layer):
        c_to_z(1, layer, front, yy)

    def xoa(layer):
        c_to_x(layer, front, yy, False)

    def spta(layer):
        ensure((0, layer))
        c_to_z(2, layer, front, other_y)

    def xta(layer):
        ensure((0, layer))
        c_to_x(layer, front, other_y, False)

    def poa(layer):
        ensure((1, layer))
        c_to_x(layer, front, yy, True)

    def pta(layer):
        ensure((2, layer))
        c_to_x(layer, front, other_y, True)

    def caa(layer):
        ensure((1, layer))
        ensure((2, layer))
        to_sibling(layer, c_ref.at[layer, core, front, :, xx])

    def cba(layer):
        ensure((3, layer))
        to_sibling(layer, c_ref.at[layer, core, front, :, 1 - xx])

    def zb(layer):
        c_to_z(12, layer, back, yy)

    def xb(layer):
        c_to_x(layer, back, yy, False)

    def pb(layer):
        ensure((12, layer))
        c_to_x(layer, back, yy, True)

    def yb1(layer):
        ensure((12, layer))
        back_to_y(layer, xx)

    def yb2(layer):
        ensure((13, layer))
        back_to_y(layer, 1 - xx)

    def kb1(layer):
        ensure((12, layer))
        ensure((13, layer))
        to_sibling(layer, c_ref.at[layer, core, back, :, :, :, y_cols(yy)])

    def kb2(layer):
        ensure((14, layer))
        to_sibling(layer, c_ref.at[layer, core, back, :, :, :, y_cols(other_y)])

    def c_stage_5(layer):
        finish((4, layer))

    def row_to_y(ref, layer):
        block = ref.at[layer, own_rows(my_dp), :]
        start((id(ref), 0, layer), remote(block, block, new_sems(1), y_peer))

    def row_to_sibling(ref, layer):
        block = ref.at[layer, own_rows(my_dp), :]
        start_all((id(ref), 1, layer), ref.at[layer, pl.ds(0, 2 * rows_dp), :], [(block, sibling)])

    def row_pass(ref, layer):
        finish((id(ref), 0, layer))
        block = ref.at[layer, own_rows(2 * (1 - yy) + core), :]
        start_all((id(ref), 1, layer), ref.at[layer, pl.ds(0, 2 * rows_dp), :], [(block, sibling)])

    def row_stage_end(ref, layer):
        finish((id(ref), 1, layer))

    def table_stage():
        every, own = S.tab_recv, S.tab_recv.at[0]
        rate, phase = I.rate[...], I.phase[...]
        decay = jnp.exp(-rate)
        twice = 2.0 * rate
        series = 1.0 - twice / 7.0
        for term in (6.0, 5.0, 4.0, 3.0, 2.0):
            series = 1.0 - series * (twice / term)
        loss = jnp.where(twice < 0.25, twice * series, 1.0 - jnp.exp(-twice))
        in_scale = jnp.sqrt(loss)
        every[0] = jnp.zeros((8, 128), F32)
        parts = (decay * jnp.cos(phase), decay * jnp.sin(phase), in_scale, jnp.exp(-twice) / in_scale)
        for row, value in enumerate(parts):
            for layer in range(layers):
                at = 4 * layer + row
                every[0, at : at + 1, 0:share] = value[layer : layer + 1]
        arrived = every.at[pl.ds(1, nseq - 1)]
        sem = new_sems(1)
        copies[8, 8] = remote(arrived, arrived, sem, x_peer)

        def one(k):
            remote(own, every.at[k], sem, {"seq": lax.rem(me + k, nseq)}).start()

        seq_loop(one)

    def table_end():
        finish((8, 8))
        lane = lax.broadcasted_iota(jnp.int32, (8, 128), 1)
        tiles = [jnp.zeros((8, 128), F32) for _ in range(p // 128)]
        for q in range(nseq):
            tile, first = (q * share) // 128, (q * share) % 128
            piece = S.tab_recv[from_rank(q)]
            if first:
                piece = pltpu.roll(piece, first, 1)
            here = (lane >= first) & (lane < first + share)
            tiles[tile] = jnp.where(here, piece, tiles[tile])
            if first + share > 128:
                tiles[tile + 1] = jnp.where(lane < first + share - 128, piece, tiles[tile + 1])
        for layer in range(layers):
            for tile in range(p // 128):
                tab_ref[layer, 0:4, tile * 128 : tile * 128 + 128] = tiles[tile][
                    4 * layer : 4 * layer + 4
                ]

    early = {}
    if inside:
        early = {
            (0, 10): [
                partial(cya, 0),
                partial(row_to_y, b_ref, 0),
                partial(zb, 0),
                table_stage,
                partial(xb, 0),
                partial(row_to_y, glu_ref, 0),
                partial(xoa, 0),
                partial(spoa, 0),
            ],
            (0, 12): [
                partial(pb, 0),
                partial(row_to_sibling, b_ref, 1),
                partial(xb, 1),
                partial(xta, 0),
                partial(cya, 1),
                partial(spta, 0),
                partial(yb1, 0),
                partial(row_to_sibling, b_ref, 0),
                partial(row_pass, b_ref, 0),
                partial(zb, 1),
                partial(spoa, 1),
                table_end,
                partial(poa, 0),
                partial(row_pass, glu_ref, 0),
                partial(yb2, 0),
                partial(pta, 0),
            ],
            (0, 14): [
                partial(row_to_y, b_ref, 1),
                partial(pb, 1),
                partial(kb1, 0),
                partial(spta, 1),
                partial(yb1, 1),
            ],
            (0, 15): [
                partial(xta, 1),
                partial(kb2, 0),
                partial(cba, 0),
                partial(caa, 0),
                partial(xoa, 1),
                partial(yb2, 1),
                partial(row_to_sibling, glu_ref, 0),
                partial(poa, 1),
                partial(row_to_sibling, glu_ref, 1),
            ],
            (0, 16): [
                partial(row_to_y, glu_ref, 1),
            ],
            (0, 19): [
                partial(row_pass, b_ref, 1),
                partial(pta, 1),
            ],
            (0, 20): [
                partial(caa, 1),
            ],
            (1, 14): [
                partial(kb1, 1),
                partial(cba, 1),
                partial(kb2, 1),
            ],
            (1, 15): [
                partial(row_pass, glu_ref, 1),
            ],
        }

    def gather(layer, point):
        for stage in early.get((layer, point), []):
            stage()

    for fetch in reversed(fetches):
        fetch.wait()
    if inside:
        for layer in range(layers):
            cast_c(layer)
            cast_b(layer)
            cast_glu(layer)
    pl.semaphore_wait(barrier, greeted)
    gather(0, 10)
    for col in range(0, width, 128):
        perm[col // 128] = x_ref[:, col : col + 128].astype(F32)

        def place(j, carry, col=col):
            rows = pl.ds(pl.multiple_of(j * CHUNKS, CHUNKS), CHUNKS)
            stream[rows, col : col + 128] = perm[col // 128, pl.ds(j, CHUNKS, stride=steps), :]
            return carry

        lax.fori_loop(0, steps, place, 0, unroll=4)

    for layer in range(layers):
        gain = gain_ref[layer : layer + 1, :]
        bias = bias_ref[layer : layer + 1, :]
        skip = skip_ref[layer : layer + 1, :]

        def norm_rows(rows, first, carry, layer=layer, gain=gain, bias=bias):
            value = stream[rows, :]
            center = value - jnp.mean(value, axis=1, keepdims=True)
            spread = jnp.mean(center * center, axis=1, keepdims=True)
            inv = lax.rsqrt(spread + 1e-05)
            hat = center * inv
            xhat[layer, rows, :] = hat
            rstd[layer, rows, :] = inv
            nlow[layer, rows, :] = (hat * gain + bias).astype(BF16)
            return carry

        row_loop(norm_rows, 0)
        if layer == 0:
            gather(0, 11)
        gather(layer, 12)

        if inside:
            row_stage_end(b_ref, layer)
        in_scale = tab_ref[layer, 2:3, :]
        for col in range(0, 2 * p, 256):
            part = mm_nn(nlow[layer], b_ref[layer, :, col : col + 256])
            for half in range(col, col + 256, 128):
                scale_col = half % p
                drive[layer, :, half : half + 128] = (
                    part[:, half - col : half - col + 128].astype(BF16).astype(F32)
                    * in_scale[:, scale_col : scale_col + 128]
                )

        lam_re, lam_im, jumps = layer_powers(layer, False)
        ends = local_ends(drive.at[layer], 0, 0, lam_re, lam_im)
        prefix = local_prefix(ends, jumps)
        gather(layer, 13)
        send_totals(layer, prefix)
        gather(layer, 14)
        tables = (jump_table(jumps, sub), jump_table(jumps, CHUNKS - 1 - sub))
        exchange_wait(layer)
        gather(layer, 15)
        carries = chunk_carries(layer, prefix, jumps, tables)
        caus[layer, 0:CHUNKS, 0:p] = carries[0]
        caus[layer, 0:CHUNKS, p : 2 * p] = carries[1]
        anti[layer, tok : tok + CHUNKS, 0:p] = carries[2]
        anti[layer, tok : tok + CHUNKS, p : 2 * p] = carries[3]
        l_re = jnp.broadcast_to(lam_re, (CHUNKS, p))
        l_im = jnp.broadcast_to(lam_im, (CHUNKS, p))

        def state_pair(k, carry, layer=layer, l_re=l_re, l_im=l_im):
            s_re, s_im, r_re, r_im = carry
            first = pl.multiple_of(k * 2 * CHUNKS, 2 * CHUNKS)
            kept_re, kept_im = [], []
            for half in range(2):
                rows = pl.ds(first + half * CHUNKS, CHUNKS)
                s_re, s_im = cmul(l_re, l_im, s_re, s_im)
                s_re = s_re + drive[layer, rows, 0:p]
                s_im = s_im + drive[layer, rows, p : 2 * p]
                after = pl.ds(first + (half + 1) * CHUNKS, CHUNKS)
                caus[layer, after, 0:p] = s_re
                caus[layer, after, p : 2 * p] = s_im
                kept_re.append(s_re)
                kept_im.append(s_im)
            both = pl.ds(first, 2 * CHUNKS)
            feat[layer, both, 0:p] = jnp.concatenate(kept_re, axis=0).astype(BF16)
            feat[layer, both, p : 2 * p] = jnp.concatenate(kept_im, axis=0).astype(BF16)
            last = pl.multiple_of(tok - (k + 1) * 2 * CHUNKS, 2 * CHUNKS)
            kept_re, kept_im = [], []
            for half in (1, 0):
                rows = pl.ds(last + half * CHUNKS, CHUNKS)
                r_re, r_im = cmul(l_re, l_im, r_re, r_im)
                r_re = r_re + drive[layer, rows, 0:p]
                r_im = r_im + drive[layer, rows, p : 2 * p]
                anti[layer, rows, 0:p] = r_re
                anti[layer, rows, p : 2 * p] = r_im
                kept_re.insert(0, r_re)
                kept_im.insert(0, r_im)
            both = pl.ds(last, 2 * CHUNKS)
            feat[layer, both, 2 * p : 3 * p] = jnp.concatenate(kept_re, axis=0).astype(BF16)
            feat[layer, both, 3 * p : 4 * p] = jnp.concatenate(kept_im, axis=0).astype(BF16)
            return s_re, s_im, r_re, r_im

        lax.fori_loop(0, steps // 2, state_pair, carries, unroll=4)

        gather(layer, 16)
        for turn in range(2):
            half = (1 - own_half) if turn else own_half
            if inside and turn:
                c_stage_5(layer)
            part = mm_nn(feat[layer], c_ref[layer, half].reshape(4 * p, half_cols))
            for first, block in half_blocks(half):
                temp[:, block] = part[:, first : first + 128]
            gather(layer, 17 + turn)

        def act_rows(rows, first, carry, layer=layer, gain=gain, bias=bias, skip=skip):
            pre = temp[rows, :] + skip * (xhat[layer, rows, :] * gain + bias)
            square = pre * pre
            th = jnp.tanh(GELU_A * pre * (1.0 + GELU_B * square))
            cdf = 0.5 * (1.0 + th)
            out = pre * cdf
            gelu_out[layer, rows, :] = out
            gelu_low[layer, rows, :] = out.astype(BF16)
            gelu_der[layer, rows, :] = cdf + 0.5 * pre * (1.0 - th * th) * (
                GELU_A * (1.0 + 3.0 * GELU_B * square)
            )
            return carry

        row_loop(act_rows, 0)
        gather(layer, 19)
        if inside:
            row_stage_end(glu_ref, layer)
        for col in range(0, width, 256):
            temp[:, col : col + 256] = mm_nn(gelu_low[layer], glu_ref[layer, :, col : col + 256])
        gather(layer, 20)
        glu_bias = glub_ref[layer : layer + 1, :]
        last_layer = layer == layers - 1

        def gate_rows(rows, first, carry, layer=layer, glu_bias=glu_bias, last_layer=last_layer):
            gate = 1.0 / (1.0 + jnp.exp(-(temp[rows, :] + glu_bias)))
            sig[layer, rows, :] = gate
            new = stream[rows, :] + gelu_out[layer, rows, :] * gate
            if not last_layer:
                stream[rows, :] = new
                return carry
            return carry + fold8(new * row_mask(first))

        def row_mask(first):
            row = first + lax.broadcasted_iota(jnp.int32, (TILE, 1), 0)
            position = me * tok + (row & (CHUNKS - 1)) * steps + (row >> 3)
            return jnp.where(position < len_ref[0], 1.0, 0.0).astype(F32)

        pooled_part = row_loop(gate_rows, jnp.zeros((CHUNKS, width), F32) if last_layer else 0)
        gather(layer, 21)

    pool_slot = 2 * layers
    own_sum = jnp.sum(pooled_part, axis=0, keepdims=True)
    for part in range(2):
        for tile in range(width // 128):
            cols = slice(tile * 128, tile * 128 + 128)
            send_buf[pool_slot, part, tile : tile + 1, :] = own_sum[:, cols]
    exchange_start(pool_slot)

    small_ref[...] = jnp.zeros(small_ref.shape, F32)
    head_row = 6 * layers
    heads = []

    def head():
        if heads:
            return
        exchange_wait(pool_slot)

        def add_pool(k, total):
            rows = [recv_buf[pool_slot, from_rank(k), r : r + 1, :] for r in range(width // 128)]
            return total + jnp.where(k == me, 0.0, jnp.concatenate(rows, axis=1))

        pooled_sum = lax.fori_loop(0, nseq, add_pool, own_sum, unroll=True)
        len_row = jnp.full((1, 1), len_ref[0], jnp.int32).astype(F32)
        pooled = pooled_sum / len_row
        logit = [
            jnp.sum(pooled * cw_ref[k : k + 1, :], axis=1, keepdims=True)
            + jnp.full((1, 1), cb_ref[k], F32)
            for k in range(classes)
        ]
        top = logit[0]
        for k in range(1, classes):
            top = jnp.maximum(top, logit[k])
        expo = [jnp.exp(v - top) for v in logit]
        norm = expo[0]
        for k in range(1, classes):
            norm = norm + expo[k]
        hot = [jnp.where(lab_ref[0] == k, 1.0, 0.0).astype(F32) for k in range(classes)]
        cross = top + jnp.log(norm)
        for k in range(classes):
            cross = cross - hot[k] * logit[k]
        excess = [expo[k] / norm - hot[k] for k in range(classes)]
        once = jnp.where(me == 0, 1.0, 0.0).astype(F32)
        lane = lax.broadcasted_iota(jnp.int32, (1, width), 1)
        bias_line = jnp.zeros((1, width), F32)
        for k in range(classes):
            lgrad = len_row * excess[k] * once
            put_line(head_row + k, pooled * lgrad)
            bias_line = jnp.where(lane == k, lgrad, bias_line)
        bias_line = jnp.where(lane == classes, cross * once, bias_line)
        put_line(head_row + classes, bias_line)
        factors = jnp.ones((1, 1), F32)
        row = excess[0] * cw_ref[0:1, :]
        if classes == 2:
            first = expo[0] / norm
            factors = hot[0] * (-expo[1] / norm) + (1.0 - hot[0]) * first
            row = cw_ref[0:1, :] - cw_ref[1:2, :]
        else:
            for k in range(1, classes):
                row = row + excess[k] * cw_ref[k : k + 1, :]
        L.scale[...] = jnp.broadcast_to(factors, (8, 128))
        heads.append(row)

    def factor():
        return L.scale[0:1, 0:1]

    if classes == 2:
        grad_row = cw_ref[0:1, :] - cw_ref[1:2, :]
    else:
        head()
        grad_row = heads[0]

    def scale_small():
        rows = head_row * (width // 128)
        small_ref[0:rows, :] = small_ref[0:rows, :] * factor()

    groups = 4 * nz

    def loop(count, body):
        def one(k, carry):
            body(k)
            return carry

        lax.fori_loop(0, count, one, 0, unroll=4)

    def c_grad_start(layer, part):
        rows = feat[layer, :, part * 2 * p : (part + 1) * 2 * p]
        value = (mm_tn(rows, mlow[layer, 1 - core]) * factor()).reshape(groups, share, half_cols)
        CG.snd1[layer, part] = value.astype(BF16)
        copy = remote(CG.snd1.at[layer, part], CG.rcv1.at[layer, part], new_sems(1), sibling)
        start((6, layer, part), copy)
        value = mm_tn(rows, mlow[layer, core]) * factor()
        CG.acc[layer, part] = value.reshape(groups, share, half_cols)

    def c_grad_first(layer, part):
        finish((6, layer, part))
        acc, rcv = CG.acc.at[layer, part], CG.rcv1.at[layer, part]
        if part == 0:

            def put(dst, cols):
                def one(g):
                    value = acc[g, :, cols] + rcv[g, :, cols].astype(F32)
                    dst[layer, g] = value.astype(dst.dtype)

                loop(groups, one)

            put(CG.snd2a, y_cols(1 - yy))
            copy = remote(CG.snd2a.at[layer], CG.rcv2a.at[layer], new_sems(1), y_peer)
            start((7, layer, part), copy)
            put(CG.acc2a, y_cols(yy))
        else:

            def put(dst, x):
                def one(h):
                    value = acc[2 * h + x] + rcv[2 * h + x].astype(F32)
                    dst[layer, h] = value.astype(dst.dtype)

                loop(groups // 2, one)

            put(CG.snd2b, 1 - xx)
            copy = remote(CG.snd2b.at[layer], CG.rcv2b.at[layer], new_sems(1), x_peer)
            start((7, layer, part), copy)
            put(CG.acc2b, xx)

    def c_grad_second(layer, part):
        finish((7, layer, part))
        if part == 0:

            def put(dst, x):
                def one(h):
                    value = CG.acc2a[layer, 2 * h + x] + CG.rcv2a[layer, 2 * h + x].astype(F32)
                    dst[layer, part, h] = value.astype(dst.dtype)

                loop(groups // 2, one)

            away, keep, peer = 1 - xx, xx, x_peer
        else:

            def put(dst, cols):
                def one(h):
                    value = CG.acc2b[layer, h, :, cols] + CG.rcv2b[layer, h, :, cols].astype(F32)
                    dst[layer, part, h] = value.astype(dst.dtype)

                loop(groups // 2, one)

            away, keep, peer = y_cols(1 - yy), y_cols(yy), y_peer
        put(CG.snd3, away)
        copy = remote(CG.snd3.at[layer, part], CG.rcv3.at[layer, part], new_sems(1), peer)
        start((8, layer, part), copy)
        put(CG.acc3, keep)

    def spread_z(name, src, dst):
        arrived = dst.at[pl.ds(1, nz - 1)]
        sem = new_sems(1)
        copies[name] = remote(arrived, arrived, sem, x_peer)
        for k in range(1, nz):
            peer = lax.rem(zz + k, nz)
            remote(src(peer), dst.at[k], sem, {"seq": 2 * peer + xx}).start()

    def c_grad_third(layer, part):
        finish((8, layer, part))

        def one(h):
            value = CG.acc3[layer, part, h] + CG.rcv3[layer, part, h].astype(F32)
            CG.acc3[layer, part, h] = value
            CG.snd4[layer, part, lax.rem(h, nz), h // nz] = value.astype(BF16)

        loop(groups // 2, one)
        snd = CG.snd4.at[layer, part]
        spread_z((9, layer, part), lambda peer: snd.at[peer], CG.rcv4.at[layer, part])

    def c_grad_end(layer, part):
        finish((9, layer, part))
        for plane in range(2):
            value = CG.acc3[layer, part, plane * nz + zz]
            for k in range(1, nz):
                value = value + CG.rcv4[layer, part, k, plane].astype(F32)
            O.c_out[layer, 2 * part + plane] = value

    def row_grad_start(G, layer):
        if G is GG:
            left, right = gelu_low, ggrad[layer]
        elif G is BA:
            left, right = nlow, dlow[layer, :, 0:p]
        else:
            left, right = nlow, dlow[layer, :, p : 2 * p]
        for y in range(ny):
            block = left[layer, :, own_rows(2 * y + 1 - core)]
            G.snd1[layer, y] = (mm_tn(block, right) * factor()).astype(BF16)
        copy = remote(G.snd1.at[layer], G.rcv1.at[layer], new_sems(1), sibling)
        start((id(G), 0, layer), copy)
        for y in range(ny):
            block = left[layer, :, own_rows(2 * y + core)]
            G.acc[layer, y] = mm_tn(block, right) * factor()

    def row_grad_y(G, layer):
        finish((id(G), 0, layer))
        acc, rcv = G.acc.at[layer], G.rcv1.at[layer]
        cast_rows(G.snd2.at[layer], acc.at[1 - yy], rows_dp, 32, rcv.at[1 - yy])
        copy = remote(G.snd2.at[layer], G.rcv2.at[layer], new_sems(1), y_peer)
        start((id(G), 1, layer), copy)
        cast_rows(G.acc2.at[layer], acc.at[yy], rows_dp, 32, rcv.at[yy])

    piece = rows_dp // nseq

    def row_grad_x(G, layer):
        finish((id(G), 1, layer))

        def put(dst, x):
            def one(z):
                rows = pl.ds(pl.multiple_of((2 * z + x) * piece, 16), piece)
                value = G.acc2[layer, rows, :] + G.rcv2[layer, rows, :].astype(F32)
                dst[layer, z] = value.astype(dst.dtype)

            loop(nz, one)

        put(G.snd3, 1 - xx)
        start((id(G), 2, layer), remote(G.snd3.at[layer], G.rcv3.at[layer], new_sems(1), x_peer))
        put(G.acc3, xx)

    def row_grad_z(G, layer):
        finish((id(G), 2, layer))

        def one(z):
            value = G.acc3[layer, z] + G.rcv3[layer, z].astype(F32)
            G.acc3[layer, z] = value
            G.snd4[layer, z] = value.astype(BF16)

        loop(nz, one)
        snd = G.snd4.at[layer]
        spread_z((id(G), 3, layer), lambda peer: snd.at[peer], G.rcv4.at[layer])

    def row_grad_back_z(G, layer):
        finish((id(G), 3, layer))
        value = G.acc3[layer, zz]
        for k in range(1, nz):
            value = value + G.rcv4[layer, k].astype(F32)
        G.full[layer, zz, xx] = value.astype(BF16)
        block = G.full.at[layer, zz, xx]
        total = G.full.at[layer, pl.ds(0, nz - 1), xx]
        start_all((id(G), 4, layer), total, [(block, peer) for peer in z_peers()])

    def row_grad_back_all(G, layer):
        finish((id(G), 3, layer))
        value = G.acc3[layer, zz]
        for k in range(1, nz):
            value = value + G.rcv4[layer, k].astype(F32)
        G.full[layer, zz, xx] = value.astype(BF16)
        block = G.full.at[layer, zz, xx]
        same = [(block, peer) for peer in z_peers()]
        start_all((id(G), 4, layer), G.full.at[layer, pl.ds(0, nz - 1), xx], same)
        cross = [(block, {"seq": 2 * lax.rem(zz + k, nz) + 1 - xx}) for k in range(nz)]
        start_all((id(G), 5, layer), G.full.at[layer, :, xx], cross)

    def row_grad_back_x(G, layer):
        finish((id(G), 4, layer))
        block = G.full.at[layer, :, xx]
        start((id(G), 5, layer), remote(block, block, new_sems(1), x_peer))

    def row_grad_end(G, layer):
        ensure((id(G), 4, layer))
        finish((id(G), 5, layer))
        out = O.glu_out if G is GG else O.b_out
        cols = pl.ds(p if G is BB else 0, G.full.shape[-1])

        def one(z):
            for x in range(2):
                rows = pl.ds(pl.multiple_of((2 * z + x) * piece, 16), piece)
                out[layer, rows, cols] = G.full[layer, z, x].astype(F32)

        loop(nz, one)

    small_rows = small_ref.shape[0]
    small_piece = small_rows // nseq

    def small_start():
        scale_small()
        start((8, 0), remote(small_ref, S.small_core, new_sems(1), sibling))

    def small_y():
        finish((8, 0))
        S.small_sum[0] = small_ref[...] + S.small_core[...]
        start((8, 1), remote(S.small_sum.at[0], S.small_y, new_sems(1), y_peer))

    def small_part(q):
        return pl.ds(pl.multiple_of(q * small_piece, 8), small_piece)

    def small_spread(name, src, dst, wait_ref):
        sem = new_sems(1)
        copies[name] = remote(wait_ref, wait_ref, sem, x_peer)

        def one(k):
            peer = lax.rem(me + k, nseq)
            remote(src(peer), dst(k), sem, {"seq": peer}).start()

        seq_loop(one)

    def small_scatter():
        finish((8, 1))
        S.small_sum[1] = S.small_sum[0] + S.small_y[...]
        small_spread(
            (8, 2),
            lambda peer: S.small_sum.at[1, small_part(peer), :],
            lambda k: S.small_recv.at[k],
            S.small_recv.at[pl.ds(1, nseq - 1)],
        )

    def small_gather():
        finish((8, 2))
        value = S.small_sum[1, small_part(me), :]
        for k in range(1, nseq):
            value = value + S.small_recv[k]
        S.small_sum[2, small_part(me), :] = value
        block = S.small_sum.at[2, small_part(me), :]
        small_spread(
            (8, 3), lambda peer: block, lambda k: block, S.small_recv.at[pl.ds(1, nseq - 1)]
        )

    def small_end():
        finish((8, 3))
        O.small_out[...] = S.small_sum[2]

    order = {(layers - 1, 3): [head]}
    if inside:
        order = {
            (1, 3): [
                head,
                partial(row_grad_start, GG, 1),
                partial(c_grad_start, 1, 1),
                partial(row_grad_y, GG, 1),
            ],
            (1, 5): [
                partial(row_grad_start, BA, 1),
                partial(c_grad_first, 1, 1),
                partial(row_grad_start, BB, 1),
            ],
            (1, 6): [
                partial(row_grad_y, BA, 1),
            ],
            (0, 1): [
                partial(c_grad_start, 0, 1),
                partial(row_grad_start, GG, 0),
                partial(row_grad_y, BB, 1),
            ],
            (0, 3): [
                partial(row_grad_y, GG, 0),
                partial(c_grad_start, 1, 0),
                partial(row_grad_x, BA, 1),
                partial(c_grad_second, 1, 1),
                partial(row_grad_x, GG, 1),
                partial(c_grad_start, 0, 0),
                partial(row_grad_x, BB, 1),
            ],
            (0, 5): [
                partial(row_grad_start, BB, 0),
                partial(c_grad_first, 0, 1),
                partial(row_grad_z, BA, 1),
                partial(row_grad_start, BA, 0),
                partial(row_grad_y, BB, 0),
                partial(row_grad_z, GG, 1),
                partial(row_grad_x, GG, 0),
                partial(row_grad_y, BA, 0),
                partial(c_grad_first, 0, 0),
                partial(row_grad_z, BB, 1),
            ],
            (0, 6): [
                small_start,
                partial(c_grad_third, 1, 1),
                small_y,
                partial(row_grad_x, BB, 0),
                partial(row_grad_back_z, BA, 1),
            ],
            (0, 7): [
                partial(row_grad_back_z, GG, 1),
                partial(row_grad_x, BA, 0),
                partial(row_grad_z, GG, 0),
                partial(c_grad_first, 1, 0),
                partial(row_grad_z, BB, 0),
                partial(c_grad_second, 0, 1),
                partial(row_grad_back_x, BA, 1),
                partial(row_grad_z, BA, 0),
                partial(row_grad_back_z, BB, 1),
                partial(c_grad_second, 0, 0),
                small_scatter,
                partial(row_grad_back_z, GG, 0),
                partial(row_grad_back_z, BB, 0),
                partial(row_grad_back_x, GG, 1),
                partial(row_grad_end, BA, 1),
                partial(row_grad_back_z, BA, 0),
                partial(c_grad_third, 0, 0),
                partial(c_grad_second, 1, 0),
                small_gather,
                partial(c_grad_third, 0, 1),
                partial(row_grad_back_x, BB, 1),
                partial(row_grad_back_x, GG, 0),
                partial(c_grad_third, 1, 0),
                partial(row_grad_back_x, BB, 0),
                partial(row_grad_back_x, BA, 0),
                partial(c_grad_end, 0, 0),
                partial(row_grad_end, GG, 1),
                partial(c_grad_end, 1, 1),
                partial(row_grad_end, GG, 0),
                small_end,
                partial(row_grad_end, BB, 1),
                partial(c_grad_end, 0, 1),
                partial(row_grad_end, BB, 0),
                partial(row_grad_end, BA, 0),
                partial(c_grad_end, 1, 0),
            ],
        }

    def stages(layer, point):
        for stage in order.get((layer, point), []):
            stage()

    grad = stream

    def first_grad(rows, first, carry):
        grad[rows, :] = row_mask(first) * grad_row
        return carry

    row_loop(first_grad, 0)

    for layer in reversed(range(layers)):
        gain = gain_ref[layer : layer + 1, :]
        bias = bias_ref[layer : layer + 1, :]
        skip = skip_ref[layer : layer + 1, :]
        zero_sum = jnp.zeros((CHUNKS, width), F32)

        def gate_back(rows, first, total, layer=layer):
            gate = sig[layer, rows, :]
            low = (grad[rows, :] * gelu_out[layer, rows, :] * gate * (1.0 - gate)).astype(BF16)
            ggrad[layer, rows, :] = low
            return total + fold8(low.astype(F32))

        total = row_loop(gate_back, zero_sum)
        stages(layer, 0)
        put_line(3 * layers + layer, jnp.sum(total, axis=0, keepdims=True))
        for col in range(0, width, 256):
            temp[:, col : col + 256] = mm_nt(ggrad[layer], glu_ref[layer, col : col + 256, :])

        def mix_back(rows, first, total, layer=layer, gain=gain, bias=bias):
            act = grad[rows, :] * sig[layer, rows, :] + temp[rows, :]
            value = act * gelu_der[layer, rows, :]
            mix[rows, :] = value
            for h in range(2):
                for first, block in half_blocks(h):
                    at = block.start
                    mlow[layer, h, rows, first : first + 128] = value[:, at : at + 128].astype(BF16)
            return total + fold8(value * (xhat[layer, rows, :] * gain + bias))

        total = row_loop(mix_back, zero_sum)
        put_line(2 * layers + layer, jnp.sum(total, axis=0, keepdims=True))
        stages(layer, 1)
        for plane in range(0, 4, 2):
            rows = [c_ref[layer, h, plane : plane + 2].reshape(2 * p, half_cols) for h in range(2)]
            wide[:, plane * p : (plane + 2) * p] = mm_nt(mlow[layer, 0], rows[0]) + mm_nt(
                mlow[layer, 1], rows[1]
            )

        lam_re, lam_im, jumps = layer_powers(layer, True)
        ends = local_ends(wide, 2 * p, 0, lam_re, lam_im)
        prefix = local_prefix(ends, jumps)
        stages(layer, 2)
        slot = layers + layer
        send_totals(slot, prefix)
        stages(layer, 3)
        if not inside:
            for h in range(2):
                for col in range(0, 4 * p, 2 * p):
                    value = mm_tn(feat[layer, :, col : col + 2 * p], mlow[layer, h]) * factor()
                    cols = slice(h * half_cols, (h + 1) * half_cols)
                    O.c_out[layer, col : col + 2 * p, cols] = value.astype(BF16)
            for col in range(0, width, 256):
                value = mm_tn(gelu_low[layer, :, col : col + 256], ggrad[layer]) * factor()
                O.glu_out[layer, col : col + 256, :] = value.astype(BF16)
        tables = (jump_table(jumps, sub), jump_table(jumps, CHUNKS - 1 - sub))
        exchange_wait(slot)
        stages(layer, 4)
        carries = chunk_carries(slot, prefix, jumps, tables)
        l_re = jnp.broadcast_to(lam_re, (CHUNKS, p))
        l_im = jnp.broadcast_to(lam_im, (CHUNKS, p))
        zero = jnp.zeros((CHUNKS, p), F32)

        def anti_grad(j, carry, layer=layer, l_re=l_re, l_im=l_im):
            r_re, r_im, d_re, d_im = carry
            rows = pl.ds(pl.multiple_of(j * CHUNKS, CHUNKS), CHUNKS)
            after = pl.ds(pl.multiple_of((j + 1) * CHUNKS, CHUNKS), CHUNKS)
            r_re, r_im = cmul(l_re, l_im, r_re, r_im)
            r_re = r_re + wide[rows, 2 * p : 3 * p]
            r_im = r_im + wide[rows, 3 * p : 4 * p]
            wide[rows, 2 * p : 3 * p] = r_re
            wide[rows, 3 * p : 4 * p] = r_im
            q_re = anti[layer, after, 0:p]
            q_im = anti[layer, after, p : 2 * p]
            return r_re, r_im, d_re + (r_re * q_re + r_im * q_im), d_im + (r_im * q_re - r_re * q_im)

        _, _, d_re, d_im = lax.fori_loop(
            0, steps, anti_grad, (carries[0], carries[1], zero, zero), unroll=4
        )
        in_scale = jnp.broadcast_to(tab_ref[layer, 2:3, :], (CHUNKS, p))

        def caus_grad(k, carry, layer=layer, l_re=l_re, l_im=l_im, in_scale=in_scale):
            a_re, a_im, d_re, d_im, s_sum = carry
            last = pl.multiple_of(tok - (k + 1) * 2 * CHUNKS, 2 * CHUNKS)
            kept_re, kept_im = [], []
            for half in (1, 0):
                rows = pl.ds(last + half * CHUNKS, CHUNKS)
                a_re, a_im = cmul(l_re, l_im, a_re, a_im)
                a_re = a_re + wide[rows, 0:p]
                a_im = a_im + wide[rows, p : 2 * p]
                q_re = caus[layer, rows, 0:p]
                q_im = caus[layer, rows, p : 2 * p]
                d_re = d_re + (a_re * q_re + a_im * q_im)
                d_im = d_im + (a_im * q_re - a_re * q_im)
                t_re = a_re + wide[rows, 2 * p : 3 * p]
                t_im = a_im + wide[rows, 3 * p : 4 * p]
                s_sum = s_sum + (
                    t_re * drive[layer, rows, 0:p] + t_im * drive[layer, rows, p : 2 * p]
                )
                kept_re.insert(0, t_re * in_scale)
                kept_im.insert(0, t_im * in_scale)
            both = pl.ds(last, 2 * CHUNKS)
            dlow[layer, both, 0:p] = jnp.concatenate(kept_re, axis=0).astype(BF16)
            dlow[layer, both, p : 2 * p] = jnp.concatenate(kept_im, axis=0).astype(BF16)
            return a_re, a_im, d_re, d_im, s_sum

        _, _, d_re, d_im, s_sum = lax.fori_loop(
            0, steps // 2, caus_grad, (carries[2], carries[3], d_re, d_im, zero), unroll=2
        )
        d_re = jnp.sum(d_re, axis=0, keepdims=True)
        d_im = jnp.sum(d_im, axis=0, keepdims=True)
        s_sum = jnp.sum(s_sum, axis=0, keepdims=True) / tab_ref[layer, 2:3, :]
        true_re = tab_ref[layer, 0:1, :]
        true_im = tab_ref[layer, 1:2, :]
        pad = jnp.zeros((1, width - p), F32)
        rate_part = s_sum * tab_ref[layer, 3:4, :] - d_re * true_re - d_im * true_im
        put_line(4 * layers + layer, jnp.concatenate([rate_part, pad], axis=1))
        phase_part = d_im * true_re - d_re * true_im
        put_line(5 * layers + layer, jnp.concatenate([phase_part, pad], axis=1))

        stages(layer, 5)
        if not inside:
            for col in range(0, width, 256):
                value = mm_tn(nlow[layer, :, col : col + 256], dlow[layer]) * factor()
                O.b_out[layer, col : col + 256, :] = value.astype(BF16)
        for col in range(0, width, 256):
            temp[:, col : col + 256] = mm_nt(dlow[layer], b_ref[layer, col : col + 256, :])

        def norm_back(rows, first, carry, layer=layer, gain=gain, skip=skip):
            gain_sum, bias_sum = carry
            ngrad = mix[rows, :] * skip + temp[rows, :]
            hat = xhat[layer, rows, :]
            q = ngrad * gain
            mean_q = jnp.mean(q, axis=1, keepdims=True)
            mean_x = jnp.mean(q * hat, axis=1, keepdims=True)
            grad[rows, :] = grad[rows, :] + (q - mean_q - hat * mean_x) * rstd[layer, rows, :]
            return gain_sum + fold8(ngrad * hat), bias_sum + fold8(ngrad)

        gain_sum, bias_sum = row_loop(norm_back, (zero_sum, zero_sum))
        put_line(layer, jnp.sum(gain_sum, axis=0, keepdims=True))
        put_line(layers + layer, jnp.sum(bias_sum, axis=0, keepdims=True))
        stages(layer, 6)

    if not inside:
        scale_small()
    for col in range(0, width, 128):
        perm[col // 128] = grad[:, col : col + 128] * factor()

        def unplace(k, carry, col=col):
            first = k * CHUNKS
            chunk = first // steps
            rows = pl.ds((first - chunk * steps) * CHUNKS + chunk, CHUNKS, stride=CHUNKS)
            out = pl.ds(pl.multiple_of(first, CHUNKS), CHUNKS)
            gin_ref[out, col : col + 128] = perm[col // 128, rows, :]
            return carry

        lax.fori_loop(0, steps, unplace, 0, unroll=4)

    stages(0, 7)


def run_model(dims, inside, operands):
    layers, tok, width, states, classes, ndp, nseq = dims
    vmem = pl.BlockSpec(memory_space=pltpu.VMEM)
    smem = pl.BlockSpec(memory_space=pltpu.SMEM)
    hbm = pl.BlockSpec(memory_space=pltpu.HBM)
    lines = -(-(6 * layers + classes + 1) // 8) * 8
    small_shape = (lines * width // 128, 128)
    slots = 2 * layers + 1
    share, rows_dp = states // nseq, width // ndp
    per_layer = lambda cols, kind, rows=tok: pltpu.VMEM((layers, rows, cols), kind)
    if inside:
        b_shape, g_shape = (layers, rows_dp, 2 * states), (layers, rows_dp, width)
        c_shape, kind = (layers, 4, share, width // ndp), F32
    else:
        b_shape, g_shape = (layers, width, 2 * states), (layers, width, width)
        c_shape, kind = (layers, 4 * states, width), BF16
    scratch = [pltpu.VMEM(a.shape, a.dtype) for a in operands[3:]]
    scratch += [
        pltpu.SemaphoreType.DMA((len(operands) - 3,)),
        pltpu.VMEM((tok, width), F32),
        per_layer(width, F32),
        per_layer(1, F32),
        per_layer(width, BF16),
        per_layer(2 * states, F32),
        per_layer(2 * states, F32, tok + CHUNKS),
        per_layer(2 * states, F32, tok + CHUNKS),
        per_layer(4 * states, BF16),
        per_layer(width, F32),
        per_layer(width, BF16),
        per_layer(width, F32),
        per_layer(width, F32),
        pltpu.VMEM((tok, 4 * states), F32),
        pltpu.VMEM((tok, width), F32),
        pltpu.VMEM((tok, width), F32),
        pltpu.VMEM((layers, 2, tok, width // 2), BF16),
        per_layer(width, BF16),
        per_layer(2 * states, BF16),
        pltpu.VMEM((8, 128), F32),
        pltpu.VMEM((width // 128, tok, 128), F32),
        pltpu.VMEM((slots, 2, 8, 128), F32),
        pltpu.VMEM((slots, nseq, 8, 128), F32),
        pltpu.SemaphoreType.DMA((slots,)),
        pltpu.SemaphoreType.DMA((slots,)),
    ]
    if inside:
        ny, nz, part, half = ndp // 2, nseq // 2, width // ndp, width // 2
        copies = 81
        scratch += [
            pltpu.VMEM((layers, 8, states), F32),
            pltpu.VMEM((nseq, 8, 128), F32),
            per_layer(2 * states, BF16, width),
            per_layer(width, BF16, width),
            pltpu.VMEM((layers, 2, 4, nz, 2, share, half), BF16),
            pltpu.SemaphoreType.DMA((copies,)),
            pltpu.SemaphoreType.DMA((copies,)),
            pltpu.VMEM(small_shape, F32),
            pltpu.VMEM(small_shape, F32),
            pltpu.VMEM(small_shape, F32),
            pltpu.VMEM((3,) + small_shape, F32),
            pltpu.VMEM((nseq, small_shape[0] // nseq, 128), F32),
        ]
        for cols in (states, states, width):
            scratch += [
                pltpu.VMEM((layers, ny, rows_dp, cols), BF16),
                pltpu.VMEM((layers, ny, rows_dp, cols), BF16),
                pltpu.VMEM((layers, ny, rows_dp, cols), F32),
                per_layer(cols, BF16, rows_dp),
                per_layer(cols, BF16, rows_dp),
                per_layer(cols, F32, rows_dp),
                pltpu.VMEM((layers, nz, rows_dp // nseq, cols), BF16),
                pltpu.VMEM((layers, nz, rows_dp // nseq, cols), BF16),
                pltpu.VMEM((layers, nz, rows_dp // nseq, cols), F32),
                pltpu.VMEM((layers, nz, rows_dp // nseq, cols), BF16),
                pltpu.VMEM((layers, nz, rows_dp // nseq, cols), BF16),
                pltpu.VMEM((layers, nz, 2, rows_dp // nseq, cols), BF16),
            ]
        scratch += [
            pltpu.VMEM((layers, 2, 4 * nz, share, half), BF16),
            pltpu.VMEM((layers, 2, 4 * nz, share, half), BF16),
            pltpu.VMEM((layers, 2, 4 * nz, share, half), F32),
            pltpu.VMEM((layers, 4 * nz, share, part), BF16),
            pltpu.VMEM((layers, 4 * nz, share, part), BF16),
            pltpu.VMEM((layers, 4 * nz, share, part), F32),
            pltpu.VMEM((layers, 2 * nz, share, half), BF16),
            pltpu.VMEM((layers, 2 * nz, share, half), BF16),
            pltpu.VMEM((layers, 2 * nz, share, half), F32),
            pltpu.VMEM((layers, 2, 2 * nz, share, part), BF16),
            pltpu.VMEM((layers, 2, 2 * nz, share, part), BF16),
            pltpu.VMEM((layers, 2, 2 * nz, share, part), F32),
            pltpu.VMEM((layers, 2, nz, 2, share, part), BF16),
            pltpu.VMEM((layers, 2, nz, 2, share, part), BF16),
        ]
    return pl.pallas_call(
        partial(model_kernel, dims, inside),
        out_shape=(
            jax.ShapeDtypeStruct((tok, width), F32),
            jax.ShapeDtypeStruct(small_shape, F32),
            jax.ShapeDtypeStruct(b_shape, kind),
            jax.ShapeDtypeStruct(g_shape, kind),
            jax.ShapeDtypeStruct(c_shape, kind),
        ),
        in_specs=[smem] * 3 + [hbm] * (len(operands) - 3),
        out_specs=[vmem] * 5,
        scratch_shapes=scratch,
        compiler_params=pltpu.CompilerParams(
            collective_id=0, has_side_effects=True, vmem_limit_bytes=48 * 1024 * 1024
        ),
        cost_estimate=pl.CostEstimate(
            flops=6 * layers * tok * width * (6 * states + width),
            bytes_accessed=16 * 1024 * 1024,
            transcendentals=2 * layers * tok * width,
        ),
    )(*operands[:3], *[pltpu.with_memory_space_constraint(a, pltpu.HBM) for a in operands[3:]])


def finish_kernel(dims, *refs):
    layers, tok, width, states, classes, ndp, nseq = dims
    small = refs[4]
    loss, gain, bias, rate, phase, skip, glub, head_w, head_b = refs[9:18]
    sems = refs[18]
    outward = [pltpu.make_async_copy(refs[k], refs[5 + k], sems.at[k]) for k in range(4)]
    for copy in outward:
        copy.start()
    tiles = width // 128

    def line(row, count=tiles):
        parts = [small[row * tiles + t : row * tiles + t + 1, :] for t in range(count)]
        return jnp.concatenate(parts, axis=1)

    for layer in range(layers):
        at = slice(layer, layer + 1)
        gain[at, :] = line(layer)
        bias[at, :] = line(layers + layer)
        skip[at, :] = line(2 * layers + layer)
        glub[at, :] = line(3 * layers + layer)
    share = states // nseq
    me = lax.axis_index("seq")
    for first, out in ((4 * layers, rate), (5 * layers, phase)):
        every = jnp.concatenate([line(first + layer) for layer in range(layers)], axis=0)
        mine = every[:, 0:share]
        for q in range(1, nseq):
            mine = jnp.where(me == q, every[:, q * share : (q + 1) * share], mine)
        out[...] = mine
    head = 6 * layers
    for k in range(classes):
        head_w[k : k + 1, :] = line(head + k)
    last = line(head + classes)
    head_b[...] = last[:, 0:classes]
    loss[...] = last[:, classes : classes + 1] / ndp
    for copy in outward:
        copy.wait()


def finish_outputs(dims, grad_inputs, small, b_grad, g_grad, c_grad):
    layers, tok, width, states, classes, ndp, nseq = dims
    vmem = pl.BlockSpec(memory_space=pltpu.VMEM)
    anywhere = pl.BlockSpec(memory_space=pl.ANY)
    large = (grad_inputs, b_grad, g_grad, c_grad)
    share = states // nseq
    rows = (layers, width)
    shapes = [(1, 1), rows, rows, (layers, share), (layers, share), rows, rows, (classes, width)]
    shapes.append((1, classes))
    results = pl.pallas_call(
        partial(finish_kernel, dims),
        out_shape=[jax.ShapeDtypeStruct(a.shape, F32) for a in large]
        + [jax.ShapeDtypeStruct(shape, F32) for shape in shapes],
        in_specs=[vmem] * 5,
        out_specs=[anywhere] * 4 + [vmem] * 9,
        scratch_shapes=[pltpu.SemaphoreType.DMA((4,))],
        compiler_params=pltpu.CompilerParams(vmem_limit_bytes=8 * 1024 * 1024),
    )(*large, small)
    gin, b_share, g_share, c_share, loss, gain, bias, rate, phase, skip, glub, head_w, head_b = results
    return (
        loss.reshape(()),
        gin[None],
        gain,
        bias,
        b_share,
        rate,
        phase,
        c_share,
        skip,
        g_share,
        glub,
        head_w.T,
        head_b.reshape(classes),
    )


def per_device(
    inputs,
    lengths,
    labels,
    norm_gain,
    norm_bias,
    b_proj,
    rate,
    phase,
    c_proj,
    skip,
    glu_weight,
    glu_bias,
    class_weight,
    class_bias,
):
    layers, width = norm_gain.shape
    tok = inputs.shape[1]
    ndp = lax.axis_size("dp")
    nseq = lax.axis_size("seq")
    states = c_proj.shape[2] * nseq
    classes = class_bias.shape[0]
    dims = (layers, tok, width, states, classes, ndp, nseq)
    share = states // nseq
    inside = (
        ndp == 4
        and nseq % 2 == 0
        and share % 16 == 0
        and (width // ndp) % 128 == 0
        and (width // ndp) % (16 * nseq) == 0
        and 4 * layers == 8
    )
    if inside:
        tables = (rate, phase)
        weights = (b_proj, glu_weight, c_proj)
    else:
        decay = jnp.exp(-rate)
        in_scale = jnp.sqrt(-jnp.expm1(-2.0 * rate))
        rows = [
            decay * jnp.cos(phase),
            decay * jnp.sin(phase),
            in_scale,
            jnp.exp(-2.0 * rate) / in_scale,
        ]
        table = lax.all_gather(jnp.stack(rows, axis=1), "seq", axis=2, tiled=True)
        tables = (table, phase)
        b_full = lax.all_gather(b_proj.astype(BF16), "dp", axis=1, tiled=True)
        g_full = lax.all_gather(glu_weight.astype(BF16), "dp", axis=1, tiled=True)
        c_half = lax.all_gather(c_proj.astype(BF16), "dp", axis=3, tiled=True)
        c_full = lax.all_gather(c_half, "seq", axis=2, tiled=True)
        c_full = c_full.reshape(layers, 4, states, 2, width // 2)
        c_full = jnp.moveaxis(c_full, 3, 1)
        weights = (b_full, g_full, c_full)
    grad_inputs, small, b_grad, g_grad, c_grad = run_model(
        dims,
        inside,
        (
            lengths,
            labels,
            class_bias,
            inputs[0],
            norm_gain,
            norm_bias,
            skip,
            glu_bias,
            *tables,
            class_weight.T,
            *weights,
        ),
    )
    if inside:
        return finish_outputs(dims, grad_inputs, small, b_grad, g_grad, c_grad)
    else:
        b_share = lax.psum_scatter(b_grad, "dp", scatter_dimension=1, tiled=True)
        g_share = lax.psum_scatter(g_grad, "dp", scatter_dimension=1, tiled=True)
        b_share = lax.psum(b_share, "seq").astype(F32)
        g_share = lax.psum(g_share, "seq").astype(F32)
        c_grad = c_grad.reshape(layers, 4, states, width)
        c_share = lax.psum_scatter(c_grad, "seq", scatter_dimension=2, tiled=True)
        c_share = lax.psum_scatter(c_share, "dp", scatter_dimension=3, tiled=True).astype(F32)
        small = lax.psum(small, ("dp", "seq"))
    small = small.reshape(-1, width)
    own = lax.axis_index("seq") * (states // nseq)

    def state_rows(first):
        return lax.dynamic_slice(small[first : first + layers], (0, own), (layers, states // nseq))

    head = 6 * layers
    return (
        small[head + classes, classes] / ndp,
        grad_inputs[None],
        small[0:layers],
        small[layers : 2 * layers],
        b_share,
        state_rows(4 * layers),
        state_rows(5 * layers),
        c_share,
        small[2 * layers : 3 * layers],
        g_share,
        small[3 * layers : 4 * layers],
        small[head : head + classes].T,
        small[head + classes, 0:classes],
    )


def solution(mesh):
    return jax.shard_map(
        per_device,
        mesh=mesh,
        in_specs=(
            P("dp", "seq", None),
            P("dp"),
            P("dp"),
            P(),
            P(),
            P(None, "dp", None),
            P(None, "seq"),
            P(None, "seq"),
            P(None, None, "seq", "dp"),
            P(),
            P(None, "dp", None),
            P(),
            P(),
            P(),
        ),
        out_specs=(
            P(),
            P("dp", "seq", None),
            P(),
            P(),
            P(None, "dp", None),
            P(None, "seq"),
            P(None, "seq"),
            P(None, None, "seq", "dp"),
            P(),
            P(None, "dp", None),
            P(),
            P(),
            P(),
        ),
        check_vma=False,
    )
```
